32 devices in a mesh: groups: 2 (over x), space: 16 (over z, y, core).
Axes of the slice: x: 2, y: 2, z: 4, core: 2. Of those that a mesh axis runs over, the one named last changes fastest.
Arguments:
- features: bfloat16 [1024, 64, 512], P(('groups', 'space')), parts along dimension 0, may hold values from -6 to 6
- counts: int32 [32], P(('groups', 'space')), parts along dimension 0, may hold values from 1 to 32, as said below
- neighbors: int32 [1024, 6], P(('groups', 'space')), parts along dimension 0, may hold values from -1 to 511, as said below
- parents: int32 [1024, 2], P(('groups', 'space')), parts along dimension 0, may hold values from 0 to 63, as said below
- w_conv: bfloat16 [7, 64, 64], replicated, may hold values from -0.25 to 0.25
- w_restrict: bfloat16 [8, 128, 64], replicated, may hold values from -0.25 to 0.25
- w_mix: bfloat16 [128, 128], replicated, may hold values from -0.5 to 0.5
- cotangent: bfloat16 [128, 128, 512], P(('groups', 'space')), parts along dimension 0, may hold values from -6 to 6
Outputs:
- coarse_out: bfloat16 [128, 128, 512], P(('groups', 'space')), parts along dimension 0
- grad_conv: float32 [14, 64, 64], P('groups'), parts along dimension 0
- grad_restrict: float32 [16, 128, 64], P('groups'), parts along dimension 0
- grad_mix: float32 [256, 128], P('groups'), parts along dimension 0
The draws below stay inside these ranges and needn't reach their ends.
There are 2 independent parts, one for each index of `groups`. The reference program is written for one: setup_inputs(seed, part) draws one part's arguments, and reference() takes and returns one part's arrays. A program takes and returns all parts, laid end to end along the dimension named above; an argument that names none is the same for every part. Nothing has to cross between parts.
Inputs may be any that keep to these rules, and one draw needn't show every extreme that they name: The live fine bricks of device i are its slots 0 to counts[i] - 1; counts[i] plus the count of the device half the space axis away is at most 40. neighbors[g, d] is the global slot of the live brick across face d of live brick g (directions as in the reference program), else -1; the relation is symmetric and dead slots hold -1 in every entry. Across face 0 the neighbor is on the same device or the next along space, across face 1 on the same or the previous, across faces 2 to 5 on the same device. At most 8 bricks of one device have a face-0 neighbor on the next device, and at most 8 a face-1 neighbor on the previous. parents[g, 0] is a global coarse slot, owned by device parents[g, 0] div 4; parents[g, 1] is an octant. Each coarse slot has exactly one fine brick in each of the 8 octants, all 8 on one device. The fine bricks of one device point to at most the larger of 1 and 4 divided by the devices along space coarse slots of any one owner.
All inputs are finite; a program needn't handle non-finite values.
Results may differ from the reference program's by a relative error of at most 0.0058.
Values may be sent and summed in bfloat16 or wider, within the bound.
No kernel may reach another device: no remote copies, remote signals or barrier semaphores. Data moves between devices by JAX's collectives and lax.ppermute only.
A program may use at most 192 MiB of HBM per device.

```python
import math
import jax
import jax.numpy as jnp
from jax import lax

C1 = 64
C2 = 128
EDGE = 8
RX = 4
RY = 4
RZ = 2
FB = 32
CB = 4
WORK = 20
VOX = 512
OCT_VOX = 64
BRICKS = 512
CBRICKS = 64
N_SPACE = 16


def distinct_order(key, row_count, col_count):
    scores = jax.random.randint(key, (row_count, col_count), 0, 1 << 20) * col_count + jnp.arange(col_count)[None, :]
    return jnp.argsort(scores, axis=1).astype(jnp.int32)


def build_scene(key):
    key_list = jax.random.split(key, 7)
    devices = N_SPACE
    half_count = max(devices // 2, 1)
    heavy_load = FB - jax.random.randint(key_list[0], (half_count,), 0, FB // 4 + 1)
    first_pair = jax.random.randint(key_list[1], (), 0, max(half_count - 1, 1))
    pair_ids = jnp.arange(half_count)
    forced = (pair_ids == first_pair) | (pair_ids == first_pair + 1)
    heavy_load = jnp.where(forced, FB, heavy_load)
    light_load = jax.random.randint(key_list[2], (half_count,), 1, 2 * WORK - heavy_load + 1)
    lower_heavy = (jax.random.randint(key_list[3], (half_count,), 0, 2) == 1) | forced
    counts = jnp.concatenate([jnp.where(lower_heavy, heavy_load, light_load), jnp.where(lower_heavy, light_load, heavy_load)]).astype(jnp.int32)
    group_order = distinct_order(key_list[4], devices, CB)
    octant_order = distinct_order(key_list[5], devices * CB, 8).reshape(devices, CB, 8)
    slot_ids = jnp.arange(FB)
    group_of = slot_ids // 8
    coarse_of = group_order[:, group_of]
    octant_of = octant_order[:, group_of, slot_ids % 8]
    half_y = RY // 2
    half_z = RZ // 2
    coarse_a = coarse_of // (half_y * half_z)
    coarse_b = coarse_of // half_z % half_y
    coarse_c = coarse_of % half_z
    fine_a = 2 * coarse_a + octant_of // 4
    fine_b = 2 * coarse_b + octant_of // 2 % 2
    fine_c = 2 * coarse_c + octant_of % 2
    local_pos = (fine_a * RY + fine_b) * RZ + fine_c
    device_ids = jnp.arange(devices)[:, None]
    inverse = jnp.zeros((devices, FB), jnp.int32).at[jnp.broadcast_to(device_ids, (devices, FB)), local_pos].set(jnp.broadcast_to(slot_ids[None, :], (devices, FB)).astype(jnp.int32))
    alive_mask = slot_ids[None, :] < counts[:, None]
    steps_a = [1, -1, 0, 0, 0, 0]
    steps_b = [0, 0, 1, -1, 0, 0]
    steps_c = [0, 0, 0, 0, 1, -1]
    columns = []
    for face_dir in range(6):
        glob_a = device_ids * RX + fine_a + steps_a[face_dir]
        near_b = fine_b + steps_b[face_dir]
        near_c = fine_c + steps_c[face_dir]
        inside = (glob_a >= 0) & (glob_a < devices * RX) & (near_b >= 0) & (near_b < RY) & (near_c >= 0) & (near_c < RZ)
        other_dev = jnp.clip(glob_a // RX, 0, devices - 1)
        other_pos = (glob_a % RX * RY + jnp.clip(near_b, 0, RY - 1)) * RZ + jnp.clip(near_c, 0, RZ - 1)
        other_slot = inverse[other_dev, other_pos]
        other_alive = other_slot < counts[other_dev]
        columns.append(jnp.where(inside & alive_mask & other_alive, other_dev * FB + other_slot, -1))
    neighbors = jnp.stack(columns, axis=-1).reshape(devices * FB, 6).astype(jnp.int32)
    spread = max(CB, devices)
    offsets = distinct_order(key_list[6], 1, spread)[0, :CB] % devices
    owner_dev = (device_ids + offsets[coarse_of]) % devices
    parents = jnp.stack([owner_dev * CB + coarse_of, octant_of], axis=-1).reshape(devices * FB, 2).astype(jnp.int32)
    return (counts, neighbors, parents)


def draw_counts(key, part):
    return build_scene(key)[0]


def draw_neighbors(key, part):
    return build_scene(key)[1]


def draw_parents(key, part):
    return build_scene(key)[2]


def steps_of(rng, extent, cuts, smallest, high):
    gain, own = 1.0, jax.random.fold_in(rng, 6)
    for dim, shards_of in cuts:
        steps = jnp.exp(jax.random.uniform(jax.random.fold_in(own, dim), (shards_of,), jnp.float32, smallest / len(cuts), high / len(cuts)))
        gain = gain * jnp.repeat(steps, extent[dim] // shards_of).reshape([-1 if axis == dim else 1 for axis in range(len(extent))])
    return gain


def normal_values(key, extent, scale, limit, pieces=(), kind=jnp.bfloat16):
    result = scale * jax.random.normal(key, extent, jnp.float32)
    if pieces:
        result = result * steps_of(key, extent, pieces, -0.22, 0.18)
    return jnp.clip(result, -limit, limit).astype(kind)


def setup_inputs(seed: int = 0, part: int = 0) -> dict:
    keys = jax.random.split(jax.random.key(seed), 9)
    own_keys = jax.random.split(jax.random.fold_in(keys[8], part), 9)
    return {
        "features": normal_values(own_keys[0], (BRICKS, C1, VOX), 1.0, 6.0, ((0, 16),)),
        "counts": draw_counts(jax.random.fold_in(jax.random.fold_in(keys[8], part), 71), part),
        "neighbors": draw_neighbors(jax.random.fold_in(jax.random.fold_in(keys[8], part), 71), part),
        "parents": draw_parents(jax.random.fold_in(jax.random.fold_in(keys[8], part), 71), part),
        "w_conv": normal_values(keys[4], (7, C1, C1), (7 * C1) ** -0.5, 0.25),
        "w_restrict": normal_values(keys[5], (8, C2, C1), (8 * C1) ** -0.5, 0.25),
        "w_mix": normal_values(keys[6], (C2, C2), C2 ** -0.5, 0.5),
        "cotangent": normal_values(own_keys[7], (CBRICKS, C2, VOX), 1.0, 6.0, ((0, 16),)),
    }


def side_planes(blocks):
    return jnp.stack([blocks[:, :, -1], blocks[:, :, 0], blocks[:, :, :, -1], blocks[:, :, :, 0], blocks[:, :, :, :, -1], blocks[:, :, :, :, 0]], axis=1)

def shifted_views(blocks, shells):
    views = [jnp.concatenate([blocks[:, :, 1:], shells[:, 0][:, :, None]], axis=2), jnp.concatenate([shells[:, 1][:, :, None], blocks[:, :, :-1]], axis=2), jnp.concatenate([blocks[:, :, :, 1:], shells[:, 2][:, :, :, None]], axis=3), jnp.concatenate([shells[:, 3][:, :, :, None], blocks[:, :, :, :-1]], axis=3), jnp.concatenate([blocks[:, :, :, :, 1:], shells[:, 4][:, :, :, :, None]], axis=4), jnp.concatenate([shells[:, 5][:, :, :, :, None], blocks[:, :, :, :, :-1]], axis=4), blocks]
    return [shifted.reshape(blocks.shape[0], blocks.shape[1], VOX) for shifted in views]

def stride_split(fine_rows):
    half_edge = EDGE // 2
    lattice = fine_rows.reshape(fine_rows.shape[0], fine_rows.shape[1], half_edge, 2, half_edge, 2, half_edge, 2)
    return lattice.transpose(0, 3, 5, 7, 1, 2, 4, 6).reshape(fine_rows.shape[0], 8, fine_rows.shape[1], half_edge ** 3)

def stride_join(part_rows):
    half_edge = EDGE // 2
    lattice = part_rows.reshape(part_rows.shape[0], 2, 2, 2, part_rows.shape[2], half_edge, half_edge, half_edge)
    return lattice.transpose(0, 4, 5, 1, 6, 2, 7, 3).reshape(part_rows.shape[0], part_rows.shape[2], VOX)

def to_voxel(octant_rows):
    half_edge = EDGE // 2
    lattice = octant_rows.reshape(octant_rows.shape[0], 2, 2, 2, octant_rows.shape[2], half_edge, half_edge, half_edge)
    return lattice.transpose(0, 4, 1, 5, 2, 6, 3, 7).reshape(octant_rows.shape[0], octant_rows.shape[2], VOX)

def from_voxel(voxel_rows):
    half_edge = EDGE // 2
    lattice = voxel_rows.reshape(voxel_rows.shape[0], voxel_rows.shape[1], 2, half_edge, 2, half_edge, 2, half_edge)
    return lattice.transpose(0, 2, 4, 6, 1, 3, 5, 7).reshape(voxel_rows.shape[0], 8, voxel_rows.shape[1], half_edge ** 3)

def silu_slope(values):
    sigmoid_part = jax.nn.sigmoid(values)
    return sigmoid_part * (1.0 + values * (1.0 - sigmoid_part))

def reference(features, counts, neighbors, parents, w_conv, w_restrict, w_mix, cotangent):
    slot_ids = jnp.arange(BRICKS, dtype=jnp.int32)
    alive_mask = slot_ids % FB < counts[slot_ids // FB]
    masked = features * alive_mask[:, None, None].astype(jnp.bfloat16)
    blocks = masked.reshape(BRICKS, C1, EDGE, EDGE, EDGE)
    planes = side_planes(blocks)
    present = neighbors >= 0
    safe_index = jnp.where(present, neighbors, 0)
    shells = jnp.stack([planes[safe_index[:, face_dir], face_dir ^ 1] * present[:, face_dir, None, None, None].astype(jnp.bfloat16) for face_dir in range(6)], axis=1)
    conv_weights = w_conv.astype(jnp.float32)
    restrict_weights = w_restrict.astype(jnp.float32)
    mix_weights = w_mix.astype(jnp.float32)
    block_cubes = blocks.reshape(N_SPACE, FB, C1, EDGE, EDGE, EDGE)
    block_shells = shells.reshape(N_SPACE, FB, 6, C1, EDGE, EDGE)

    def convolve(cubes, shell_rows):
        summed = jnp.zeros((cubes.shape[0], C1, VOX), jnp.float32)
        for offset, shifted in enumerate(shifted_views(cubes, shell_rows)):
            summed = summed + jnp.einsum('oi,biv->bov', conv_weights[offset], shifted.astype(jnp.float32))
        return summed

    def forward_block(pair_rows):
        cubes, shell_rows = pair_rows
        fine_act = jax.nn.silu(convolve(cubes, shell_rows)).astype(jnp.bfloat16)
        restricted = jnp.einsum('toi,btiv->bov', restrict_weights, stride_split(fine_act).astype(jnp.float32)).astype(jnp.bfloat16)
        return (fine_act, restricted)
    fine_act, restricted = lax.map(forward_block, (block_cubes, block_shells))
    restricted = restricted.reshape(BRICKS, C2, OCT_VOX)
    coarse_oct = jnp.zeros((CBRICKS, 8, C2, OCT_VOX), jnp.bfloat16).at[parents[:, 0], parents[:, 1]].set(restricted)
    coarse = to_voxel(coarse_oct)
    coarse_wide = coarse.astype(jnp.float32)
    cotangent_wide = cotangent.astype(jnp.float32)
    coarse_out = jnp.einsum('oi,biv->bov', mix_weights, coarse_wide).astype(jnp.bfloat16)
    norm_scale = 1.0 / math.sqrt(CBRICKS * VOX)
    grad_mix = norm_scale * jnp.einsum('bov,biv->oi', cotangent_wide, coarse_wide)
    grad_coarse = (norm_scale * jnp.einsum('oi,bov->biv', mix_weights, cotangent_wide)).astype(jnp.bfloat16)
    grad_fine = from_voxel(grad_coarse)[parents[:, 0], parents[:, 1]]
    block_grads = grad_fine.reshape(N_SPACE, FB, C2, OCT_VOX)
    block_alive = alive_mask.reshape(N_SPACE, FB)

    def backward_block(rows_in):
        cubes, shell_rows, grad_rows, act_rows, alive_rows = rows_in
        hidden = convolve(cubes, shell_rows)
        split_act = stride_split(act_rows).astype(jnp.float32)
        grad_wide = grad_rows.astype(jnp.float32)
        restrict_part = jnp.einsum('bov,btiv->toi', grad_wide, split_act)
        grad_act = stride_join(jnp.einsum('toi,bov->btiv', restrict_weights, grad_wide))
        grad_hidden = (grad_act * silu_slope(hidden)).astype(jnp.bfloat16) * alive_rows[:, None, None].astype(jnp.bfloat16)
        hidden_wide = grad_hidden.astype(jnp.float32)
        conv_part = jnp.stack([jnp.einsum('bov,biv->oi', hidden_wide, shifted.astype(jnp.float32)) for shifted in shifted_views(cubes, shell_rows)])
        return (conv_part, restrict_part)
    conv_parts, restrict_parts = lax.map(backward_block, (block_cubes, block_shells, block_grads, fine_act, block_alive))
    return (coarse_out, lax.optimization_barrier(jnp.sum(conv_parts, axis=0)), lax.optimization_barrier(jnp.sum(restrict_parts, axis=0)), grad_mix)
```

```python
import functools
import math

import jax
import jax.numpy as jnp
import numpy as np
from jax import lax
from jax.experimental import pallas as pl
from jax.experimental.pallas import tpu as pltpu
from jax.sharding import PartitionSpec as P

EDGE = 8
HALF = EDGE // 2
VOX = EDGE**3
LANES = 128
ROWS = 16
SEND = 8
BF16 = jnp.bfloat16
F32 = jnp.float32
VMEM_BYTES = 40 * 1024 * 1024


def split_matrix():
    lattice = np.arange(VOX).reshape(HALF, 2, HALF, 2, HALF, 2)
    order = lattice.transpose(1, 3, 5, 0, 2, 4).reshape(-1)
    picked = np.zeros((VOX, VOX), np.float32)
    picked[order, np.arange(VOX)] = 1.0
    return picked


def octant_matrix():
    lattice = np.arange(VOX).reshape(2, HALF, 2, HALF, 2, HALF)
    order = lattice.transpose(0, 2, 4, 1, 3, 5).reshape(-1)
    picked = np.zeros((VOX, VOX), np.float32)
    picked[np.arange(VOX), order] = 1.0
    return picked


def dot(a, b):
    return jnp.dot(a, b, preferred_element_type=F32)


def dot_nt(a, b):
    return lax.dot_general(a, b, (((1,), (1,)), ((), ())), preferred_element_type=F32)


def pack_kernel(lane_tiles, idx, feat, cot, label, up, down, msg, sem):
    devices = msg.shape[0]
    slots = cot.shape[0]
    copies = []
    for r in range(SEND):
        copies.append(
            pltpu.make_async_copy(
                feat.at[idx[r], :, pl.ds(VOX - LANES, LANES)], up.at[r], sem.at[r]
            )
        )
        copies.append(
            pltpu.make_async_copy(
                feat.at[idx[SEND + r], :, pl.ds(0, LANES)], down.at[r], sem.at[SEND + r]
            )
        )
    for copy in copies:
        copy.start()
    per_row = VOX // (LANES * lane_tiles)
    for j in range(devices):
        chan, part = j // per_row, j % per_row
        for q in range(slots):
            for lt in range(lane_tiles):
                lane = (part * lane_tiles + lt) * LANES
                msg[j, q * lane_tiles + lt] = cot[
                    q, chan * ROWS : (chan + 1) * ROWS, lane : lane + LANES
                ]
        msg[j, slots * lane_tiles] = label[...]
    for copy in copies:
        copy.wait()


def load_bricks(feat, above, below, bricks, sem):
    count = feat.shape[0]
    copies = [
        pltpu.make_async_copy(feat, bricks.at[pl.ds(0, count)], sem.at[0]),
        pltpu.make_async_copy(
            above, bricks.at[pl.ds(count, SEND), :, pl.ds(0, LANES)], sem.at[1]
        ),
        pltpu.make_async_copy(
            below, bricks.at[pl.ds(count, SEND), :, pl.ds(VOX - LANES, LANES)], sem.at[2]
        ),
    ]
    for copy in copies:
        copy.start()
    bricks[count + SEND] = jnp.zeros(bricks.shape[1:], BF16)
    for copy in copies:
        copy.wait()


def shift_into(tab, base, bricks, views, col):
    chans = bricks.shape[1]
    tiles = VOX // LANES
    lane = lax.broadcasted_iota(jnp.int32, (chans, LANES), 1)
    low = lane < LANES // 2
    b = (lane // EDGE) % EDGE
    c = lane % EDGE
    own = tab[base + 6]
    near = [tab[base + d] for d in range(6)]

    def tile(slot, t):
        return bricks[slot, :, t * LANES : (t + 1) * LANES]

    x = [tile(own, t) for t in range(tiles)]
    after = x[1:] + [tile(near[0], 0)]
    before = [tile(near[1], tiles - 1)] + x[:-1]
    for t in range(tiles):
        y = [None, None] + [tile(near[d], t) for d in range(2, 6)]
        out = [
            pltpu.roll(jnp.where(low, after[t], x[t]), LANES // 2, 1),
            pltpu.roll(jnp.where(low, x[t], before[t]), LANES // 2, 1),
            jnp.where(b < EDGE - 1, pltpu.roll(x[t], LANES - 8, 1), pltpu.roll(y[2], 56, 1)),
            jnp.where(b > 0, pltpu.roll(x[t], 8, 1), pltpu.roll(y[3], LANES - 56, 1)),
            jnp.where(c < EDGE - 1, pltpu.roll(x[t], LANES - 1, 1), pltpu.roll(y[4], 7, 1)),
            jnp.where(c > 0, pltpu.roll(x[t], 1, 1), pltpu.roll(y[5], LANES - 7, 1)),
            x[t],
        ]
        for d in range(7):
            views[d * chans : (d + 1) * chans, col + t * LANES : col + (t + 1) * LANES] = out[d]


def forward_kernel(
    lane_tiles, tab, feat, above, below, w_conv, split, place, w_res, w_mix,
    parts_out, slope_out, coarse_out, piece_out, bricks, views, high, rest, sem,
):
    q = pl.program_id(0)
    chans = feat.shape[1]

    @pl.when(q == 0)
    def _():
        load_bricks(feat, above, below, bricks, sem)

    @pl.loop(0, 4)
    def _(pair):
        for k in range(2):
            shift_into(tab, (q * 8 + pair * 2 + k) * 7, bricks, views, k * VOX)
        hidden = dot(w_conv[...], views[...])
        top = hidden.astype(BF16)
        low = (hidden - top.astype(F32)).astype(BF16)
        for k in range(2):
            row = pl.multiple_of((pair * 2 + k) * chans, chans)
            high[pl.ds(row, chans), :] = top[:, k * VOX : (k + 1) * VOX]
            rest[pl.ds(row, chans), :] = low[:, k * VOX : (k + 1) * VOX]

    low_half = lax.broadcasted_iota(jnp.int32, (chans, LANES), 1) < LANES // 2
    for r in range(4):
        rows = slice(r * 2 * chans, (r + 1) * 2 * chans)
        hidden = dot(high[rows, :], split[...]) + dot(rest[rows, :], split[...])
        sig = 1.0 / (1.0 + jnp.exp(-hidden))
        slope_out[0, rows, :] = sig * (1.0 + hidden * (1.0 - sig))
        act = hidden * sig
        for t in range(4):
            lanes = slice(t * LANES, (t + 1) * LANES)
            one = act[:chans, lanes]
            two = act[chans:, lanes]
            cols = slice(r * LANES, (r + 1) * LANES)
            parts_out[0, 2 * t * chans : (2 * t + 1) * chans, cols] = jnp.where(
                low_half, one, pltpu.roll(two, LANES // 2, 1)
            ).astype(BF16)
            parts_out[0, (2 * t + 1) * chans : (2 * t + 2) * chans, cols] = jnp.where(
                low_half, pltpu.roll(one, LANES // 2, 1), two
            ).astype(BF16)
    by_octant = dot(w_res[...], parts_out[0]).astype(BF16)
    coarse = dot(by_octant, place[...]).astype(BF16)
    coarse_out[0] = coarse
    mixed = dot(w_mix[...], coarse).astype(BF16)
    per_row = VOX // (LANES * lane_tiles)
    for j in range(piece_out.shape[0]):
        chan, part = j // per_row, j % per_row
        for lt in range(lane_tiles):
            lane = (part * lane_tiles + lt) * LANES
            piece_out[j, 0, lt] = mixed[chan * ROWS : (chan + 1) * ROWS, lane : lane + LANES]


def backward_kernel(
    lane_tiles, scale, tab, feat, above, below, pieces, parts, slope, coarse, w_mix_t, w_res_t,
    unplace, unsplit, packed,
    bricks, views, cot, grad_parts, grad_rows, conv_sum, res_sum, mix_sum, sem,
):
    q = pl.program_id(0)
    chans = feat.shape[1]
    wide = coarse.shape[1]

    @pl.when(q == 0)
    def _():
        load_bricks(feat, above, below, bricks, sem)
        conv_sum[...] = jnp.zeros_like(conv_sum)
        res_sum[...] = jnp.zeros_like(res_sum)
        mix_sum[...] = jnp.zeros_like(mix_sum)

    per_row = VOX // (LANES * lane_tiles)
    for j in range(pieces.shape[0]):
        chan, part = j // per_row, j % per_row
        for lt in range(lane_tiles):
            lane = (part * lane_tiles + lt) * LANES
            cot[chan * ROWS : (chan + 1) * ROWS, lane : lane + LANES] = pieces[j, 0, lt]
    cots = cot[...]
    grad_coarse = (scale * dot(w_mix_t[...], cots)).astype(BF16)
    grad_fine = dot(grad_coarse, unplace[...]).astype(BF16)
    mix_sum[...] += dot_nt(cots, coarse[0])
    res_sum[...] += dot_nt(grad_fine, parts[0])
    grad_parts[...] = dot(w_res_t[...], grad_fine)
    low_half = lax.broadcasted_iota(jnp.int32, (chans, LANES), 1) < LANES // 2
    for r in range(4):
        for t in range(4):
            cols = slice(r * LANES, (r + 1) * LANES)
            lanes = slice(t * LANES, (t + 1) * LANES)
            one = grad_parts[2 * t * chans : (2 * t + 1) * chans, cols]
            two = grad_parts[(2 * t + 1) * chans : (2 * t + 2) * chans, cols]
            first = slice(2 * r * chans, (2 * r + 1) * chans)
            second = slice((2 * r + 1) * chans, (2 * r + 2) * chans)
            grad_rows[first, lanes] = (
                jnp.where(low_half, one, pltpu.roll(two, LANES // 2, 1)) * slope[0, first, lanes]
            ).astype(BF16)
            grad_rows[second, lanes] = (
                jnp.where(low_half, pltpu.roll(one, LANES // 2, 1), two) * slope[0, second, lanes]
            ).astype(BF16)
    for r in range(4):
        rows = slice(r * 2 * chans, (r + 1) * 2 * chans)
        grad_rows[rows, :] = dot(grad_rows[rows, :], unsplit[...]).astype(BF16)

    @pl.loop(0, 4)
    def _(pair):
        total = None
        for k in range(2):
            shift_into(tab, (q * 8 + pair * 2 + k) * 7, bricks, views, k * VOX)
        for k in range(2):
            row = pl.multiple_of((pair * 2 + k) * chans, chans)
            term = dot_nt(grad_rows[pl.ds(row, chans), :], views[:, k * VOX : (k + 1) * VOX])
            total = term if total is None else total + term
        conv_sum[:, : 7 * chans] += total

    @pl.when(q == pl.num_programs(0) - 1)
    def _():
        packed[0:wide] = (scale * mix_sum[...]).astype(BF16)
        at = wide
        for t in range(4):
            packed[at : at + wide] = res_sum[:, t * LANES : (t + 1) * LANES].astype(BF16)
            at += wide
        for t in range(4):
            packed[at : at + chans] = conv_sum[:, t * LANES : (t + 1) * LANES].astype(BF16)
            at += chans
        if at < packed.shape[0]:
            packed[at:] = jnp.zeros((packed.shape[0] - at, LANES), BF16)


def unpack_kernel(lane_tiles, packed, pieces, coarse_out, conv, res, mix):
    wide = mix.shape[0]
    chans = conv.shape[1]
    half = LANES // 2
    mix[...] = packed[0:wide].astype(F32)
    at = wide
    for t in range(4):
        block = packed[at : at + wide].astype(F32)
        res[2 * t] = block[:, :half]
        res[2 * t + 1] = block[:, half:]
        at += wide
    for t in range(4):
        block = packed[at : at + chans].astype(F32)
        conv[2 * t] = block[:, :half]
        if 2 * t + 1 < 7:
            conv[2 * t + 1] = block[:, half:]
        at += chans
    per_row = VOX // (LANES * lane_tiles)
    for j in range(pieces.shape[0]):
        chan, part = j // per_row, j % per_row
        for q in range(coarse_out.shape[0]):
            for lt in range(lane_tiles):
                lane = (part * lane_tiles + lt) * LANES
                coarse_out[q, chan * ROWS : (chan + 1) * ROWS, lane : lane + LANES] = pieces[
                    j, q, lt
                ]


def brick_tables(counts, neighbors, parents, position):
    count = neighbors.shape[0]
    slot = jnp.arange(count, dtype=jnp.int32)
    local = neighbors - position * count
    present = neighbors >= 0
    zero_slot = count + SEND
    goes_up = present[:, 0] & (local[:, 0] >= count)
    goes_down = present[:, 1] & (local[:, 1] < 0)

    def listed(flags):
        rank = jnp.sum((flags[None, :] & (slot[None, :] < slot[:, None])).astype(jnp.int32), axis=1)
        hit = flags[None, :] & (rank[None, :] == jnp.arange(SEND, dtype=jnp.int32)[:, None])
        return jnp.sum(jnp.where(hit, slot[None, :], 0), axis=1)

    def arrival(flags, ids):
        earlier = flags[None, :] & (ids[None, :] < ids[:, None])
        return count + jnp.sum(earlier.astype(jnp.int32), axis=1)

    place = jnp.where(present, local, zero_slot)
    columns = [
        jnp.where(goes_up, arrival(goes_up, neighbors[:, 0]), place[:, 0]),
        jnp.where(goes_down, arrival(goes_down, neighbors[:, 1]), place[:, 1]),
    ] + [place[:, d] for d in range(2, 6)]
    columns.append(jnp.where(slot < counts[0], slot, zero_slot))
    sources = jnp.stack(columns, axis=1)

    ids, octant = parents[:, 0], parents[:, 1]
    first = octant == 0
    rank = jnp.sum((first[None, :] & (ids[None, :] < ids[:, None])).astype(jnp.int32), axis=1)
    key = rank * 8 + octant
    at_key = key[None, :] == slot[:, None]
    table = jnp.sum(jnp.where(at_key[:, :, None], sources[None], 0), axis=1)
    kids = jnp.sum(jnp.where(at_key[::8], ids[None, :], 0), axis=1)
    return jnp.concatenate([listed(goes_up), listed(goes_down)]), table.reshape(-1), kids


def kernel_call(kernel, out_shape, grid_spec, flops, moved):
    return pl.pallas_call(
        kernel,
        out_shape=out_shape,
        grid_spec=grid_spec,
        compiler_params=pltpu.CompilerParams(vmem_limit_bytes=VMEM_BYTES),
        cost_estimate=pl.CostEstimate(flops=flops, bytes_accessed=moved, transcendentals=0),
    )


def body(features, counts, neighbors, parents, w_conv, w_restrict, w_mix, cotangent):
    devices = lax.axis_size("space")
    position = lax.axis_index("space")
    slots, wide = cotangent.shape[:2]
    count, chans = features.shape[:2]
    lane_tiles = VOX * 8 // devices // LANES
    tiles = slots * lane_tiles
    groups = count // 8
    whole = lambda shape: pl.BlockSpec(shape, lambda *_: (0,) * len(shape))
    any_spec = pl.BlockSpec(memory_space=pl.ANY)

    send_idx, table, kids = brick_tables(counts, neighbors, parents, position)
    label = jnp.zeros((ROWS, LANES), BF16).at[:, :slots].set(kids.astype(BF16)[None, :])

    plane = jax.ShapeDtypeStruct((SEND, chans, LANES), BF16)
    up, down, message = kernel_call(
        functools.partial(pack_kernel, lane_tiles),
        (plane, plane, jax.ShapeDtypeStruct((devices, tiles + 1, ROWS, LANES), BF16)),
        pltpu.PrefetchScalarGridSpec(
            num_scalar_prefetch=1,
            grid=(1,),
            in_specs=[any_spec, whole(cotangent.shape), whole(label.shape)],
            out_specs=[whole(plane.shape), whole(plane.shape),
                       whole((devices, tiles + 1, ROWS, LANES))],
            scratch_shapes=[pltpu.SemaphoreType.DMA((2 * SEND,))],
        ),
        1000, 2 * 2**20,
    )(send_idx, features, cotangent, label)

    below = lax.ppermute(up, "space", [(i, i + 1) for i in range(devices - 1)])
    above = lax.ppermute(down, "space", [(i + 1, i) for i in range(devices - 1)])
    spread = lax.all_to_all(message, "space", split_axis=0, concat_axis=0, tiled=True)

    split = split_matrix()
    place = octant_matrix()
    const = lambda array: jnp.asarray(array, BF16)
    conv_cat = w_conv.transpose(1, 0, 2).reshape(chans, 7 * chans)
    res_cat = w_restrict.transpose(1, 0, 2).reshape(wide, 8 * chans)
    brick_scratch = pltpu.VMEM((count + SEND + 1, chans, VOX), BF16)
    view_scratch = pltpu.VMEM((7 * chans, 2 * VOX), BF16)
    per_group = lambda *shape: pl.BlockSpec((1,) + shape, lambda q, *_: (q,) + (0,) * len(shape))
    piece_shape = (devices, groups, lane_tiles, ROWS, LANES)
    piece_spec = pl.BlockSpec(
        (devices, 1, lane_tiles, ROWS, LANES), lambda q, *_: (0, q, 0, 0, 0)
    )
    parts, slope, coarse, pieces = kernel_call(
        functools.partial(forward_kernel, lane_tiles),
        (
            jax.ShapeDtypeStruct((groups, 8 * chans, VOX), BF16),
            jax.ShapeDtypeStruct((groups, 8 * chans, VOX), F32),
            jax.ShapeDtypeStruct((groups, wide, VOX), BF16),
            jax.ShapeDtypeStruct(piece_shape, BF16),
        ),
        pltpu.PrefetchScalarGridSpec(
            num_scalar_prefetch=1,
            grid=(groups,),
            in_specs=[any_spec, any_spec, any_spec, whole(conv_cat.shape), whole(split.shape),
                      whole(place.shape), whole(res_cat.shape), whole(w_mix.shape)],
            out_specs=[per_group(8 * chans, VOX), per_group(8 * chans, VOX),
                       per_group(wide, VOX), piece_spec],
            scratch_shapes=[brick_scratch, view_scratch, pltpu.VMEM((8 * chans, VOX), BF16),
                            pltpu.VMEM((8 * chans, VOX), BF16), pltpu.SemaphoreType.DMA((3,))],
        ),
        4 * 10**9, 16 * 2**20,
    )(table, features, above, below, conv_cat, const(split), const(place), res_cat, w_mix)

    lane_ids = jnp.arange(lane_tiles, dtype=jnp.int32)
    all_kids = spread[:, tiles, 0, :groups].astype(jnp.int32)
    kid_tiles = (all_kids // slots) * (tiles + 1) + (all_kids % slots) * lane_tiles
    forward_tiles = jnp.take(
        spread.reshape(devices * (tiles + 1), ROWS, LANES),
        (kid_tiles[:, :, None] + lane_ids).reshape(-1), axis=0, mode="clip",
    ).reshape(piece_shape)
    cot_pieces = lax.all_to_all(forward_tiles, "space", split_axis=0, concat_axis=0, tiled=True)

    returned = lax.all_to_all(pieces, "space", split_axis=0, concat_axis=0, tiled=True)
    flat_kids = all_kids.reshape(-1)
    number = jnp.arange(devices * groups, dtype=jnp.int32)
    source = jnp.sum(jnp.where(flat_kids[None, :] == number[:, None], number[None, :], 0), axis=1)
    owner_tiles = jnp.take(
        returned.reshape(devices * groups, lane_tiles, ROWS, LANES), source, axis=0, mode="clip"
    ).reshape(devices, slots, lane_tiles, ROWS, LANES)
    out_pieces = lax.all_to_all(owner_tiles, "space", split_axis=0, concat_axis=0, tiled=True)

    scale = 1.0 / math.sqrt(devices * slots * VOX)
    used = wide + 4 * wide + 4 * chans
    rows = -(-used // (devices * ROWS)) * ROWS
    packed = kernel_call(
        functools.partial(backward_kernel, lane_tiles, scale),
        jax.ShapeDtypeStruct((devices * rows, LANES), BF16),
        pltpu.PrefetchScalarGridSpec(
            num_scalar_prefetch=1,
            grid=(groups,),
            in_specs=[any_spec, any_spec, any_spec, piece_spec, per_group(8 * chans, VOX),
                      per_group(8 * chans, VOX), per_group(wide, VOX), whole(w_mix.shape),
                      whole((8 * chans, wide)), whole(place.shape), whole(split.shape)],
            out_specs=whole((devices * rows, LANES)),
            scratch_shapes=[
                brick_scratch, view_scratch, pltpu.VMEM((wide, VOX), BF16),
                pltpu.VMEM((8 * chans, VOX), F32), pltpu.VMEM((8 * chans, VOX), BF16),
                pltpu.VMEM((chans, 8 * chans), F32), pltpu.VMEM((wide, 8 * chans), F32),
                pltpu.VMEM((wide, wide), F32), pltpu.SemaphoreType.DMA((3,)),
            ],
        ),
        4 * 10**9, 16 * 2**20,
    )(table, features, above, below, cot_pieces, parts, slope, coarse, w_mix.T, res_cat.T,
      const(place.T), const(split.T))

    shares = lax.all_to_all(
        packed.reshape(devices, rows, LANES), "space", split_axis=0, concat_axis=0, tiled=True
    )
    summed = jnp.sum(shares.astype(F32), axis=0).astype(BF16)
    totals = lax.all_to_all(
        jnp.broadcast_to(summed[None], (devices, rows, LANES)),
        "space", split_axis=0, concat_axis=0, tiled=True,
    ).reshape(devices * rows, LANES)

    return kernel_call(
        functools.partial(unpack_kernel, lane_tiles),
        (
            jax.ShapeDtypeStruct((slots, wide, VOX), BF16),
            jax.ShapeDtypeStruct((7, chans, chans), F32),
            jax.ShapeDtypeStruct((8, wide, chans), F32),
            jax.ShapeDtypeStruct((wide, wide), F32),
        ),
        pl.GridSpec(
            grid=(1,),
            in_specs=[whole(totals.shape), whole(out_pieces.shape)],
            out_specs=[whole((slots, wide, VOX)), whole((7, chans, chans)),
                       whole((8, wide, chans)), whole((wide, wide))],
        ),
        1000, 2 * 2**20,
    )(totals, out_pieces)


def solution(mesh):
    return jax.shard_map(
        body,
        mesh=mesh,
        in_specs=(
            P(("groups", "space"), None, None),
            P(("groups", "space")),
            P(("groups", "space"), None),
            P(("groups", "space"), None),
            P(),
            P(),
            P(),
            P(("groups", "space"), None, None),
        ),
        out_specs=(
            P(("groups", "space"), None, None),
            P("groups", None, None),
            P("groups", None, None),
            P("groups", None),
        ),
        check_vma=False,
    )
```

```python
import functools
import math

import jax
import jax.numpy as jnp
from jax import lax
from jax.experimental import pallas as pl
from jax.experimental.pallas import tpu as pltpu
from jax.sharding import PartitionSpec as P

EDGE = 8
HALF = EDGE // 2
VOX = EDGE**3
LANES = 128
ROWS = 16
SEND = 8
BF16 = jnp.bfloat16
F32 = jnp.float32
VMEM_BYTES = 60 * 1024 * 1024


def bits_of(value):
    return [(value >> (8 - k)) & 1 for k in range(9)]


def join_bits(bits):
    value = bits[0]
    for bit in bits[1:]:
        value = value * 2 + bit
    return value


def split_voxel(column):
    ta, tb, tc, a1, a0, b1, b0, c1, c0 = bits_of(column)
    return join_bits([a1, a0, ta, b1, b0, tb, c1, c0, tc])


def octant_voxel(column):
    oa, ob, oc, a1, a0, b1, b0, c1, c0 = bits_of(column)
    return join_bits([oa, a1, a0, ob, b1, b0, oc, c1, c0])


def picker(voxel_of, voxel_axis):
    voxel = lax.broadcasted_iota(jnp.int32, (VOX, VOX), voxel_axis)
    column = lax.broadcasted_iota(jnp.int32, (VOX, VOX), 1 - voxel_axis)
    return (voxel == voxel_of(column)).astype(BF16)


def dot(a, b):
    return jnp.dot(a, b, preferred_element_type=F32)


def dot_nt(a, b):
    return lax.dot_general(a, b, (((1,), (1,)), ((), ())), preferred_element_type=F32)


def pack_kernel(lane_tiles, parents, cot, msg, kids_out, kids):
    devices = msg.shape[0]
    slots = cot.shape[0]
    per_row = VOX // (LANES * lane_tiles)
    for j in range(devices):
        chan, part = j // per_row, j % per_row
        for q in range(slots):
            for lt in range(lane_tiles):
                lane = (part * lane_tiles + lt) * LANES
                msg[j, q * lane_tiles + lt] = cot[
                    q, chan * ROWS : (chan + 1) * ROWS, lane : lane + LANES
                ]

    def find(g, found):
        kids[found] = parents[0, g]
        return found + (parents[1, g] == 0).astype(jnp.int32)

    lax.fori_loop(0, parents.shape[1], find, jnp.int32(0))
    lane = lax.broadcasted_iota(jnp.int32, (ROWS, LANES), 1)
    label = jnp.zeros((ROWS, LANES), jnp.int32)
    for q in range(kids_out.shape[0]):
        kids_out[q] = kids[q]
        label = jnp.where(lane == q, kids[q], label)
    label = label.astype(F32).astype(BF16)
    for j in range(devices):
        msg[j, slots * lane_tiles] = label


def table_kernel(
    place, counts, kids, neighbors, parents, feat, up, down, table,
    slot_at, up_idx, up_far, up_place, down_idx, down_far, down_place, sem,
):
    count = neighbors.shape[1]
    base = place[0] * count
    zero_slot = count + SEND
    for r in range(SEND + 1):
        up_idx[r] = 0
        down_idx[r] = 0
        up_far[r] = 2 * count
        down_far[r] = 2 * count

    def scan(g, found):
        n_up, n_down = found
        q = jnp.int32(0)
        for k in range(1, kids.shape[0]):
            q += jnp.where(kids[k] == parents[0, g], k, 0)
        slot_at[q * 8 + parents[1, g]] = g
        near_up, near_down = neighbors[0, g], neighbors[1, g]
        far_up, far_down = near_up - base - count, near_down - base + count
        goes_up = (near_up >= 0) & (far_up >= 0)
        goes_down = (near_down >= 0) & (far_down < count)
        up_idx[n_up] = g
        up_far[n_up] = jnp.where(goes_up, far_up, 2 * count)
        down_idx[n_down] = g
        down_far[n_down] = jnp.where(goes_down, far_down, 2 * count)
        return n_up + goes_up.astype(jnp.int32), n_down + goes_down.astype(jnp.int32)

    lax.fori_loop(0, count, scan, (jnp.int32(0), jnp.int32(0)))
    copies = []
    for r in range(SEND):
        copies.append(
            pltpu.make_async_copy(
                feat.at[up_idx[r], :, pl.ds(VOX - LANES, LANES)], up.at[r], sem.at[r]
            )
        )
        copies.append(
            pltpu.make_async_copy(
                feat.at[down_idx[r], :, pl.ds(0, LANES)], down.at[r], sem.at[SEND + r]
            )
        )
    for copy in copies:
        copy.start()

    def rank(r, carry):
        for far, idx, put in ((up_far, up_idx, up_place), (down_far, down_idx, down_place)):
            earlier = jnp.int32(0)
            for other in range(SEND):
                earlier += (far[other] < far[r]).astype(jnp.int32)

            @pl.when(far[r] < count)
            def _():
                put[idx[r]] = count + earlier

        return carry

    lax.fori_loop(0, SEND, rank, jnp.int32(0))

    def fill(k, carry):
        g = slot_at[k]
        for d in range(6):
            near = neighbors[d, g]
            local = near - base
            if d == 0:
                local = jnp.where(local >= count, up_place[g], local)
            if d == 1:
                local = jnp.where(local < 0, down_place[g], local)
            table[k * 7 + d] = jnp.where(near >= 0, local, zero_slot)
        table[k * 7 + 6] = jnp.where(g < counts[0], g, zero_slot)
        return carry

    lax.fori_loop(0, count, fill, jnp.int32(0))
    for copy in copies:
        copy.wait()


def load_bricks(feat, above, below, bricks, sem):
    count = feat.shape[0]
    copies = [
        pltpu.make_async_copy(feat, bricks.at[pl.ds(0, count)], sem.at[0]),
        pltpu.make_async_copy(
            above, bricks.at[pl.ds(count, SEND), :, pl.ds(0, LANES)], sem.at[1]
        ),
        pltpu.make_async_copy(
            below, bricks.at[pl.ds(count, SEND), :, pl.ds(VOX - LANES, LANES)], sem.at[2]
        ),
    ]
    for copy in copies:
        copy.start()
    bricks[count + SEND] = jnp.zeros(bricks.shape[1:], BF16)
    for copy in copies:
        copy.wait()


def shift_into(tab, base, bricks, views, col):
    chans = bricks.shape[1]
    tiles = VOX // LANES
    lane = lax.broadcasted_iota(jnp.int32, (chans, LANES), 1)
    low = lane < LANES // 2
    b = (lane // EDGE) % EDGE
    c = lane % EDGE
    own = tab[base + 6]
    near = [tab[base + d] for d in range(6)]

    def tile(slot, t):
        return bricks[slot, :, t * LANES : (t + 1) * LANES]

    x = [tile(own, t) for t in range(tiles)]
    after = x[1:] + [tile(near[0], 0)]
    before = [tile(near[1], tiles - 1)] + x[:-1]
    for t in range(tiles):
        y = [None, None] + [tile(near[d], t) for d in range(2, 6)]
        out = [
            pltpu.roll(jnp.where(low, after[t], x[t]), LANES // 2, 1),
            pltpu.roll(jnp.where(low, x[t], before[t]), LANES // 2, 1),
            jnp.where(b < EDGE - 1, pltpu.roll(x[t], LANES - 8, 1), pltpu.roll(y[2], 56, 1)),
            jnp.where(b > 0, pltpu.roll(x[t], 8, 1), pltpu.roll(y[3], LANES - 56, 1)),
            jnp.where(c < EDGE - 1, pltpu.roll(x[t], LANES - 1, 1), pltpu.roll(y[4], 7, 1)),
            jnp.where(c > 0, pltpu.roll(x[t], 1, 1), pltpu.roll(y[5], LANES - 7, 1)),
            x[t],
        ]
        for d in range(7):
            views[d * chans : (d + 1) * chans, col + t * LANES : col + (t + 1) * LANES] = out[d]


def forward_kernel(
    lane_tiles, start, tab, feat, above, below, w_conv, split, place, w_res, w_mix, *refs
):
    parts_out, slope_out, coarse_out, piece_out, bricks, views, high, rest, sem = refs[-9:]
    q = pl.program_id(0) + start
    chans = feat.shape[1]

    @pl.when(pl.program_id(0) == 0)
    def _():
        load_bricks(feat, above, below, bricks, sem)

    @pl.loop(0, 4)
    def _(pair):
        for k in range(2):
            shift_into(tab, (q * 8 + pair * 2 + k) * 7, bricks, views, k * VOX)
        hidden = dot(w_conv[...], views[...])
        top = hidden.astype(BF16)
        low = (hidden - top.astype(F32)).astype(BF16)
        for k in range(2):
            row = pl.multiple_of((pair * 2 + k) * chans, chans)
            high[pl.ds(row, chans), :] = top[:, k * VOX : (k + 1) * VOX]
            rest[pl.ds(row, chans), :] = low[:, k * VOX : (k + 1) * VOX]

    low_half = lax.broadcasted_iota(jnp.int32, (chans, LANES), 1) < LANES // 2
    for r in range(4):
        rows = slice(r * 2 * chans, (r + 1) * 2 * chans)
        hidden = dot(high[rows, :], split[...]) + dot(rest[rows, :], split[...])
        sig = 1.0 / (1.0 + jnp.exp(-hidden))
        slope_out[0, rows, :] = sig * (1.0 + hidden * (1.0 - sig))
        act = hidden * sig
        for t in range(4):
            lanes = slice(t * LANES, (t + 1) * LANES)
            one = act[:chans, lanes]
            two = act[chans:, lanes]
            cols = slice(r * LANES, (r + 1) * LANES)
            parts_out[0, 2 * t * chans : (2 * t + 1) * chans, cols] = jnp.where(
                low_half, one, pltpu.roll(two, LANES // 2, 1)
            ).astype(BF16)
            parts_out[0, (2 * t + 1) * chans : (2 * t + 2) * chans, cols] = jnp.where(
                low_half, pltpu.roll(one, LANES // 2, 1), two
            ).astype(BF16)
    by_octant = dot(w_res[...], parts_out[0]).astype(BF16)
    coarse = dot(by_octant, place[...]).astype(BF16)
    coarse_out[0] = coarse
    mixed = dot(w_mix[...], coarse).astype(BF16)
    per_row = VOX // (LANES * lane_tiles)
    for j in range(piece_out.shape[0]):
        chan, part = j // per_row, j % per_row
        for lt in range(lane_tiles):
            lane = (part * lane_tiles + lt) * LANES
            piece_out[j, 0, lt] = mixed[chan * ROWS : (chan + 1) * ROWS, lane : lane + LANES]


def backward_kernel(
    lane_tiles, scale, tab, feat, above, below, pieces, parts, slope, coarse, w_mix_t, w_res_t,
    unplace, unsplit, packed,
    bricks, views, cot, grad_parts, grad_rows, conv_sum, res_sum, mix_sum, sem,
):
    q = pl.program_id(0)
    chans = feat.shape[1]
    wide = coarse.shape[1]

    @pl.when(q == 0)
    def _():
        load_bricks(feat, above, below, bricks, sem)
        conv_sum[...] = jnp.zeros_like(conv_sum)
        res_sum[...] = jnp.zeros_like(res_sum)
        mix_sum[...] = jnp.zeros_like(mix_sum)

    per_row = VOX // (LANES * lane_tiles)
    for j in range(pieces.shape[0]):
        chan, part = j // per_row, j % per_row
        for lt in range(lane_tiles):
            lane = (part * lane_tiles + lt) * LANES
            cot[chan * ROWS : (chan + 1) * ROWS, lane : lane + LANES] = pieces[j, 0, lt]
    cots = cot[...]
    grad_coarse = (scale * dot(w_mix_t[...], cots)).astype(BF16)
    grad_fine = dot(grad_coarse, unplace[...]).astype(BF16)
    mix_sum[...] += dot_nt(cots, coarse[0])
    res_sum[...] += dot_nt(parts[0], grad_fine)
    grad_parts[...] = dot(w_res_t[...], grad_fine)
    low_half = lax.broadcasted_iota(jnp.int32, (chans, LANES), 1) < LANES // 2
    for r in range(4):
        for t in range(4):
            cols = slice(r * LANES, (r + 1) * LANES)
            lanes = slice(t * LANES, (t + 1) * LANES)
            one = grad_parts[2 * t * chans : (2 * t + 1) * chans, cols]
            two = grad_parts[(2 * t + 1) * chans : (2 * t + 2) * chans, cols]
            first = slice(2 * r * chans, (2 * r + 1) * chans)
            second = slice((2 * r + 1) * chans, (2 * r + 2) * chans)
            grad_rows[first, lanes] = (
                jnp.where(low_half, one, pltpu.roll(two, LANES // 2, 1)) * slope[0, first, lanes]
            ).astype(BF16)
            grad_rows[second, lanes] = (
                jnp.where(low_half, pltpu.roll(one, LANES // 2, 1), two) * slope[0, second, lanes]
            ).astype(BF16)
    for r in range(4):
        rows = slice(r * 2 * chans, (r + 1) * 2 * chans)
        grad_rows[rows, :] = dot(grad_rows[rows, :], unsplit[...]).astype(BF16)

    @pl.loop(0, 4)
    def _(pair):
        total = None
        for k in range(2):
            shift_into(tab, (q * 8 + pair * 2 + k) * 7, bricks, views, k * VOX)
        for k in range(2):
            row = pl.multiple_of((pair * 2 + k) * chans, chans)
            term = dot_nt(grad_rows[pl.ds(row, chans), :], views[:, k * VOX : (k + 1) * VOX])
            total = term if total is None else total + term
        conv_sum[:, : 7 * chans] += total

    @pl.when(q == pl.num_programs(0) - 1)
    def _():
        packed[0:wide] = (scale * mix_sum[...]).astype(BF16)
        at = wide
        packed[at : at + 8 * chans] = res_sum[...].astype(BF16)
        at += 8 * chans
        for t in range(4):
            packed[at : at + chans] = conv_sum[:, t * LANES : (t + 1) * LANES].astype(BF16)
            at += chans
        if at < packed.shape[0]:
            packed[at:] = jnp.zeros((packed.shape[0] - at, LANES), BF16)


def unpack_kernel(lane_tiles, packed, pieces, coarse_out, conv, res, mix):
    wide = mix.shape[0]
    chans = conv.shape[1]
    half = LANES // 2
    mix[...] = packed[0:wide].astype(F32)
    at = wide
    for t in range(8):
        res[t] = packed[at : at + chans].astype(F32)
        at += chans
    for t in range(4):
        block = packed[at : at + chans].astype(F32)
        conv[2 * t] = block[:, :half]
        if 2 * t + 1 < 7:
            conv[2 * t + 1] = block[:, half:]
        at += chans
    per_row = VOX // (LANES * lane_tiles)
    for j in range(pieces.shape[0]):
        chan, part = j // per_row, j % per_row
        for q in range(coarse_out.shape[0]):
            for lt in range(lane_tiles):
                lane = (part * lane_tiles + lt) * LANES
                coarse_out[q, chan * ROWS : (chan + 1) * ROWS, lane : lane + LANES] = pieces[
                    j, q, lt
                ]


def kernel_call(kernel, out_shape, grid_spec, flops, moved):
    return pl.pallas_call(
        kernel,
        out_shape=out_shape,
        grid_spec=grid_spec,
        compiler_params=pltpu.CompilerParams(vmem_limit_bytes=VMEM_BYTES),
        cost_estimate=pl.CostEstimate(flops=flops, bytes_accessed=moved, transcendentals=0),
    )


def body(features, counts, neighbors, parents, w_conv, w_restrict, w_mix, cotangent):
    devices = lax.axis_size("space")
    position = lax.axis_index("space").astype(jnp.int32).reshape(1)
    slots, wide = cotangent.shape[:2]
    count, chans = features.shape[:2]
    lane_tiles = VOX * 8 // devices // LANES
    tiles = slots * lane_tiles
    groups = count // 8
    first = groups // 2
    whole = lambda shape: pl.BlockSpec(shape, lambda *_: (0,) * len(shape))
    any_spec = pl.BlockSpec(memory_space=pl.ANY)
    smem_spec = pl.BlockSpec(memory_space=pltpu.SMEM)
    smem = lambda size: pltpu.SMEM((size,), jnp.int32)

    message_shape = (devices, tiles + 1, ROWS, LANES)
    message, kids = kernel_call(
        functools.partial(pack_kernel, lane_tiles),
        (
            jax.ShapeDtypeStruct(message_shape, BF16),
            jax.ShapeDtypeStruct((groups,), jnp.int32),
        ),
        pl.GridSpec(
            grid=(1,),
            in_specs=[smem_spec, whole(cotangent.shape)],
            out_specs=[whole(message_shape), smem_spec],
            scratch_shapes=[smem(groups + 1)],
        ),
        1000, 2**20,
    )(parents.T, cotangent)
    spread = lax.all_to_all(message, "space", split_axis=0, concat_axis=0, tiled=True)

    plane = jax.ShapeDtypeStruct((SEND, chans, LANES), BF16)
    up, down, table = kernel_call(
        table_kernel,
        (plane, plane, jax.ShapeDtypeStruct((count * 7,), jnp.int32)),
        pl.GridSpec(
            grid=(1,),
            in_specs=[smem_spec] * 5 + [any_spec],
            out_specs=[whole(plane.shape), whole(plane.shape), smem_spec],
            scratch_shapes=[smem(count)]
            + [smem(SEND + 1), smem(SEND + 1), smem(count)] * 2
            + [pltpu.SemaphoreType.DMA((2 * SEND,))],
        ),
        1000, 2**20,
    )(position, counts, kids, neighbors.T, parents.T, features)
    below = lax.ppermute(up, "space", [(i, i + 1) for i in range(devices - 1)])
    above = lax.ppermute(down, "space", [(i + 1, i) for i in range(devices - 1)])

    conv_cat = w_conv.transpose(1, 0, 2).reshape(chans, 7 * chans)
    res_rows = w_restrict.transpose(0, 2, 1).reshape(8 * chans, wide)
    brick_scratch = pltpu.VMEM((count + SEND + 1, chans, VOX), BF16)
    view_scratch = pltpu.VMEM((7 * chans, 2 * VOX), BF16)
    piece_shape = (devices, groups, lane_tiles, ROWS, LANES)

    def per_group(shape, start=0):
        return pl.BlockSpec((1,) + shape, lambda q, *_: (q + start,) + (0,) * len(shape))

    def piece_spec(start=0):
        return pl.BlockSpec(
            (devices, 1, lane_tiles, ROWS, LANES), lambda q, *_: (0, q + start, 0, 0, 0)
        )

    split = picker(split_voxel, 0)
    place = picker(octant_voxel, 1)
    fixed = (conv_cat, split, place, res_rows.T, w_mix)

    def forward(start, steps, before):
        operands = (table, features, above, below) + fixed + before
        return pl.pallas_call(
            functools.partial(forward_kernel, lane_tiles, start),
            out_shape=(
                jax.ShapeDtypeStruct((groups, 8 * chans, VOX), BF16),
                jax.ShapeDtypeStruct((groups, 8 * chans, VOX), F32),
                jax.ShapeDtypeStruct((groups, wide, VOX), BF16),
                jax.ShapeDtypeStruct(piece_shape, BF16),
            ),
            grid_spec=pltpu.PrefetchScalarGridSpec(
                num_scalar_prefetch=1,
                grid=(steps,),
                in_specs=[any_spec] * 3 + [whole(x.shape) for x in fixed]
                + [any_spec] * len(before),
                out_specs=[per_group((8 * chans, VOX), start), per_group((8 * chans, VOX), start),
                           per_group((wide, VOX), start), piece_spec(start)],
                scratch_shapes=[
                    brick_scratch, view_scratch, pltpu.VMEM((8 * chans, VOX), BF16),
                    pltpu.VMEM((8 * chans, VOX), BF16), pltpu.SemaphoreType.DMA((3,)),
                ],
            ),
            input_output_aliases={len(operands) - len(before) + k: k for k in range(len(before))},
            compiler_params=pltpu.CompilerParams(vmem_limit_bytes=VMEM_BYTES),
            cost_estimate=pl.CostEstimate(
                flops=8 * 10**9, bytes_accessed=16 * 2**20, transcendentals=0
            ),
        )(*operands)

    half = forward(0, first, ())

    spread, half = lax.optimization_barrier((spread, half))
    lane_ids = jnp.arange(lane_tiles, dtype=jnp.int32)
    all_kids = spread[:, tiles, 0, :groups].astype(jnp.int32)
    kid_tiles = (all_kids // slots) * (tiles + 1) + (all_kids % slots) * lane_tiles
    forward_tiles = jnp.take(
        spread.reshape(devices * (tiles + 1), ROWS, LANES),
        (kid_tiles[:, :, None] + lane_ids).reshape(-1), axis=0, mode="clip",
    ).reshape(piece_shape)
    cot_pieces = lax.all_to_all(forward_tiles, "space", split_axis=0, concat_axis=0, tiled=True)

    parts, slope, coarse, pieces = forward(first, groups - first, tuple(half))
    returned = lax.all_to_all(pieces, "space", split_axis=0, concat_axis=0, tiled=True)

    scale = 1.0 / math.sqrt(devices * slots * VOX)
    used = wide + 8 * chans + 4 * chans
    rows = -(-used // (devices * ROWS)) * ROWS
    packed = kernel_call(
        functools.partial(backward_kernel, lane_tiles, scale),
        jax.ShapeDtypeStruct((devices * rows, LANES), BF16),
        pltpu.PrefetchScalarGridSpec(
            num_scalar_prefetch=1,
            grid=(groups,),
            in_specs=[any_spec, any_spec, any_spec, piece_spec(), per_group((8 * chans, VOX)),
                      per_group((8 * chans, VOX)), per_group((wide, VOX)), whole(w_mix.shape),
                      whole((8 * chans, wide)), whole(place.shape), whole(split.shape)],
            out_specs=whole((devices * rows, LANES)),
            scratch_shapes=[
                brick_scratch, view_scratch, pltpu.VMEM((wide, VOX), BF16),
                pltpu.VMEM((8 * chans, VOX), F32), pltpu.VMEM((8 * chans, VOX), BF16),
                pltpu.VMEM((chans, 8 * chans), F32), pltpu.VMEM((8 * chans, wide), F32),
                pltpu.VMEM((wide, wide), F32), pltpu.SemaphoreType.DMA((3,)),
            ],
        ),
        16 * 10**9, 16 * 2**20,
    )(table, features, above, below, cot_pieces, parts, slope, coarse, w_mix.T, res_rows,
      picker(octant_voxel, 0), picker(split_voxel, 1))

    shares = lax.all_to_all(
        packed.reshape(devices, rows, LANES), "space", split_axis=0, concat_axis=0, tiled=True
    )

    returned, _ = lax.optimization_barrier((returned, packed))
    flat_kids = all_kids.reshape(-1)
    number = jnp.arange(devices * groups, dtype=jnp.int32)
    source = jnp.sum(jnp.where(flat_kids[None, :] == number[:, None], number[None, :], 0), axis=1)
    owner_tiles = jnp.take(
        returned.reshape(devices * groups, lane_tiles, ROWS, LANES), source, axis=0, mode="clip"
    ).reshape(devices, slots, lane_tiles, ROWS, LANES)
    out_pieces = lax.all_to_all(owner_tiles, "space", split_axis=0, concat_axis=0, tiled=True)

    summed = jnp.sum(shares.astype(F32), axis=0).astype(BF16)
    totals = lax.all_to_all(
        jnp.broadcast_to(summed[None], (devices, rows, LANES)),
        "space", split_axis=0, concat_axis=0, tiled=True,
    ).reshape(devices * rows, LANES)

    coarse_out, grad_conv, grad_res, grad_mix = kernel_call(
        functools.partial(unpack_kernel, lane_tiles),
        (
            jax.ShapeDtypeStruct((slots, wide, VOX), BF16),
            jax.ShapeDtypeStruct((7, chans, chans), F32),
            jax.ShapeDtypeStruct((8, chans, wide), F32),
            jax.ShapeDtypeStruct((wide, wide), F32),
        ),
        pl.GridSpec(
            grid=(1,),
            in_specs=[whole(totals.shape), whole(out_pieces.shape)],
            out_specs=[whole((slots, wide, VOX)), whole((7, chans, chans)),
                       whole((8, chans, wide)), whole((wide, wide))],
        ),
        1000, 2 * 2**20,
    )(totals, out_pieces)
    return coarse_out, grad_conv, grad_res.transpose(0, 2, 1), grad_mix


def solution(mesh):
    return jax.shard_map(
        body,
        mesh=mesh,
        in_specs=(
            P(("groups", "space"), None, None),
            P(("groups", "space")),
            P(("groups", "space"), None),
            P(("groups", "space"), None),
            P(),
            P(),
            P(),
            P(("groups", "space"), None, None),
        ),
        out_specs=(
            P(("groups", "space"), None, None),
            P("groups", None, None),
            P("groups", None, None),
            P("groups", None),
        ),
        check_vma=False,
    )
```

```python
import functools
import math

import jax
import jax.numpy as jnp
from jax import lax
from jax.experimental import pallas as pl
from jax.experimental.pallas import tpu as pltpu
from jax.sharding import PartitionSpec as P

EDGE = 8
HALF = EDGE // 2
VOX = EDGE**3
LANES = 128
ROWS = 16
SEND = 8
STEP = 4
BF16 = jnp.bfloat16
F32 = jnp.float32
VMEM_BYTES = 60 * 1024 * 1024


def bits_of(value):
    return [(value >> (8 - k)) & 1 for k in range(9)]


def join_bits(bits):
    value = bits[0]
    for bit in bits[1:]:
        value = value * 2 + bit
    return value


def split_voxel(column):
    ta, tb, tc, a1, a0, b1, b0, c1, c0 = bits_of(column)
    return join_bits([a1, a0, ta, b1, b0, tb, c1, c0, tc])


def octant_voxel(column):
    oa, ob, oc, a1, a0, b1, b0, c1, c0 = bits_of(column)
    return join_bits([oa, a1, a0, ob, b1, b0, oc, c1, c0])


def picker(voxel_of, voxel_axis):
    voxel = lax.broadcasted_iota(jnp.int32, (VOX, VOX), voxel_axis)
    column = lax.broadcasted_iota(jnp.int32, (VOX, VOX), 1 - voxel_axis)
    return (voxel == voxel_of(column)).astype(BF16)


def dot(a, b):
    return jnp.dot(a, b, preferred_element_type=F32)


def dot_nt(a, b):
    return lax.dot_general(a, b, (((1,), (1,)), ((), ())), preferred_element_type=F32)


def pack_kernel(lane_tiles, parents, cot_hbm, msg, kids_out, kids, cot, sem):
    devices = msg.shape[0]
    slots = cot.shape[0]
    fetch = pltpu.make_async_copy(cot_hbm, cot, sem)
    fetch.start()

    def find(g, found):
        kids[found] = parents[0, g]
        return found + (parents[1, g] == 0).astype(jnp.int32)

    lax.fori_loop(0, parents.shape[1], find, jnp.int32(0), unroll=4)
    lane = lax.broadcasted_iota(jnp.int32, (ROWS, LANES), 1)
    label = jnp.zeros((ROWS, LANES), jnp.int32)
    for q in range(kids_out.shape[0]):
        kids_out[q] = kids[q]
        label = jnp.where(lane == q, kids[q], label)
    label = label.astype(F32).astype(BF16)
    for j in range(devices):
        msg[j, slots * lane_tiles] = label
    fetch.wait()
    per_row = VOX // (LANES * lane_tiles)
    for j in range(devices):
        chan, part = j // per_row, j % per_row
        for q in range(slots):
            for lt in range(lane_tiles):
                lane = (part * lane_tiles + lt) * LANES
                msg[j, q * lane_tiles + lt] = cot[
                    q, chan * ROWS : (chan + 1) * ROWS, lane : lane + LANES
                ]


def table_kernel(
    place, kids, neighbors, parents, feat, up, down, slot_at, up_place, down_place,
    up_idx, up_far, down_idx, down_far, sem,
):
    count = neighbors.shape[1]
    base = place[0] * count
    for r in range(SEND + 1):
        up_idx[r] = 0
        down_idx[r] = 0
        up_far[r] = 2 * count
        down_far[r] = 2 * count

    def scan(g, found):
        n_up, n_down = found
        near_up, near_down = neighbors[0, g], neighbors[1, g]
        far_up, far_down = near_up - base - count, near_down - base + count
        goes_up = (near_up >= 0) & (far_up >= 0)
        goes_down = (near_down >= 0) & (far_down < count)
        up_idx[n_up] = g
        up_far[n_up] = jnp.where(goes_up, far_up, 2 * count)
        down_idx[n_down] = g
        down_far[n_down] = jnp.where(goes_down, far_down, 2 * count)
        return n_up + goes_up.astype(jnp.int32), n_down + goes_down.astype(jnp.int32)

    lax.fori_loop(0, count, scan, (jnp.int32(0), jnp.int32(0)), unroll=4)
    copies = []
    for r in range(SEND):
        copies.append(
            pltpu.make_async_copy(
                feat.at[up_idx[r], :, pl.ds(VOX - LANES, LANES)], up.at[r], sem.at[r]
            )
        )
        copies.append(
            pltpu.make_async_copy(
                feat.at[down_idx[r], :, pl.ds(0, LANES)], down.at[r], sem.at[SEND + r]
            )
        )
    for copy in copies:
        copy.start()

    def order(g, carry):
        q = jnp.int32(0)
        for k in range(1, kids.shape[0]):
            q += jnp.where(kids[k] == parents[0, g], k, 0)
        slot_at[q * 8 + parents[1, g]] = g
        return carry

    lax.fori_loop(0, count, order, jnp.int32(0), unroll=4)

    def rank(r, carry):
        for far, idx, put in ((up_far, up_idx, up_place), (down_far, down_idx, down_place)):
            earlier = jnp.int32(0)
            for other in range(SEND):
                earlier += (far[other] < far[r]).astype(jnp.int32)

            @pl.when(far[r] < count)
            def _():
                put[idx[r]] = count + earlier

        return carry

    lax.fori_loop(0, SEND, rank, jnp.int32(0))
    for copy in copies:
        copy.wait()


def start_bricks(feat, above, below, bricks, sem):
    count = feat.shape[0]
    copies = [
        pltpu.make_async_copy(feat, bricks.at[pl.ds(0, count)], sem.at[0]),
        pltpu.make_async_copy(
            above, bricks.at[pl.ds(count, SEND), :, pl.ds(0, LANES)], sem.at[1]
        ),
        pltpu.make_async_copy(
            below, bricks.at[pl.ds(count, SEND), :, pl.ds(VOX - LANES, LANES)], sem.at[2]
        ),
    ]
    for copy in copies:
        copy.start()
    bricks[count + SEND] = jnp.zeros(bricks.shape[1:], BF16)
    return copies


def sources(scalars, number):
    place, counts, neighbors, slot_at, up_place, down_place = scalars
    count = neighbors.shape[1]
    zero_slot = count + SEND
    g = slot_at[number]
    found = []
    for d in range(6):
        near = neighbors[d, g]
        local = near - place[0] * count
        if d == 0:
            local = jnp.where(local >= count, up_place[g], local)
        if d == 1:
            local = jnp.where(local < 0, down_place[g], local)
        found.append(jnp.where(near >= 0, local, zero_slot))
    found.append(jnp.where(g < counts[0], g, zero_slot))
    return found


def shift_into(slots, bricks, views):
    chans = bricks.shape[1]
    tiles = VOX // LANES
    lane = lax.broadcasted_iota(jnp.int32, (chans, LANES), 1)
    low = lane < LANES // 2
    b = (lane // EDGE) % EDGE
    c = lane % EDGE

    def tile(slot, t):
        return bricks[slot, :, t * LANES : (t + 1) * LANES]

    x = [tile(slots[6], t) for t in range(tiles)]
    after = x[1:] + [tile(slots[0], 0)]
    before = [tile(slots[1], tiles - 1)] + x[:-1]
    for t in range(tiles):
        y = [None, None] + [tile(slots[d], t) for d in range(2, 6)]
        out = [
            pltpu.roll(jnp.where(low, after[t], x[t]), LANES // 2, 1),
            pltpu.roll(jnp.where(low, x[t], before[t]), LANES // 2, 1),
            jnp.where(b < EDGE - 1, pltpu.roll(x[t], LANES - 8, 1), pltpu.roll(y[2], 56, 1)),
            jnp.where(b > 0, pltpu.roll(x[t], 8, 1), pltpu.roll(y[3], LANES - 56, 1)),
            jnp.where(c < EDGE - 1, pltpu.roll(x[t], LANES - 1, 1), pltpu.roll(y[4], 7, 1)),
            jnp.where(c > 0, pltpu.roll(x[t], 1, 1), pltpu.roll(y[5], LANES - 7, 1)),
            x[t],
        ]
        for d in range(7):
            views[d * chans : (d + 1) * chans, t * LANES : (t + 1) * LANES] = out[d]


def low_lanes(rows):
    return lax.broadcasted_iota(jnp.int32, (rows, LANES), 1) < LANES // 2


def forward_kernel(
    lane_tiles, place_no, counts, neighbors, slot_at, up_place, down_place,
    feat, above, below, w_conv, w_res, w_mix,
    parts_out, slope_out, coarse_out, piece_out,
    bricks, views, hidden_parts, split, place, conv_cat, res_cat, sem,
):
    q = pl.program_id(0)
    chans = feat.shape[1]
    scalars = (place_no, counts, neighbors, slot_at, up_place, down_place)

    @pl.when(q == 0)
    def _():
        copies = start_bricks(feat, above, below, bricks, sem)
        picked = picker(split_voxel, 0)
        split[:VOX] = picked
        split[VOX:] = picked
        place[...] = picker(octant_voxel, 1)
        for d in range(7):
            conv_cat[:, d * chans : (d + 1) * chans] = w_conv[d]
        res_cat[...] = w_res[...].T
        for copy in copies:
            copy.wait()

    @pl.loop(0, 8 // STEP)
    def _(step):
        for k in range(STEP):
            shift_into(sources(scalars, q * 8 + step * STEP + k), bricks, views.at[k])
        for k in range(STEP):
            hidden = dot(conv_cat[...], views[k])
            top = hidden.astype(BF16)
            row = pl.multiple_of((step * STEP + k) * chans, chans)
            hidden_parts[pl.ds(row, chans), :VOX] = top
            hidden_parts[pl.ds(row, chans), VOX:] = (hidden - top.astype(F32)).astype(BF16)

    low_half = low_lanes(chans)
    for r in range(4):
        rows = slice(r * 2 * chans, (r + 1) * 2 * chans)
        hidden = dot(hidden_parts[rows, :], split[...])
        sig = 0.5 + 0.5 * jnp.tanh(0.5 * hidden)
        act = hidden * sig
        slope_out[0, rows, :] = (sig + act * (1.0 - sig)).astype(BF16)
        act = act.astype(BF16)
        for t in range(4):
            lanes = slice(t * LANES, (t + 1) * LANES)
            one = act[:chans, lanes]
            two = act[chans:, lanes]
            cols = slice(r * LANES, (r + 1) * LANES)
            parts_out[0, 2 * t * chans : (2 * t + 1) * chans, cols] = jnp.where(
                low_half, one, pltpu.roll(two, LANES // 2, 1)
            )
            parts_out[0, (2 * t + 1) * chans : (2 * t + 2) * chans, cols] = jnp.where(
                low_half, pltpu.roll(one, LANES // 2, 1), two
            )
    by_octant = dot(res_cat[...], parts_out[0]).astype(BF16)
    coarse = dot(by_octant, place[...]).astype(BF16)
    coarse_out[0] = coarse
    mixed = dot(w_mix[...], coarse).astype(BF16)
    per_row = VOX // (LANES * lane_tiles)
    for j in range(piece_out.shape[0]):
        chan, part = j // per_row, j % per_row
        for lt in range(lane_tiles):
            lane = (part * lane_tiles + lt) * LANES
            piece_out[j, 0, lt] = mixed[chan * ROWS : (chan + 1) * ROWS, lane : lane + LANES]


def backward_kernel(
    lane_tiles, scale, place_no, counts, neighbors, slot_at, up_place, down_place,
    feat, above, below, pieces, parts, slope, coarse, w_mix, w_res, packed,
    bricks, views, cot, grad_parts, grad_rows, grad_cols, split, unplace, mix_t,
    conv_sum, res_sum, mix_sum, sem,
):
    q = pl.program_id(0)
    chans = feat.shape[1]
    wide = coarse.shape[1]
    scalars = (place_no, counts, neighbors, slot_at, up_place, down_place)

    @pl.when(q == 0)
    def _():
        copies = start_bricks(feat, above, below, bricks, sem)
        split[...] = picker(split_voxel, 0)
        unplace[...] = picker(octant_voxel, 0)
        mix_t[...] = w_mix[...].T
        conv_sum[...] = jnp.zeros_like(conv_sum)
        res_sum[...] = jnp.zeros_like(res_sum)
        mix_sum[...] = jnp.zeros_like(mix_sum)
        for copy in copies:
            copy.wait()

    per_row = VOX // (LANES * lane_tiles)
    for j in range(pieces.shape[0]):
        chan, part = j // per_row, j % per_row
        for lt in range(lane_tiles):
            lane = (part * lane_tiles + lt) * LANES
            cot[chan * ROWS : (chan + 1) * ROWS, lane : lane + LANES] = pieces[j, 0, lt]
    cots = cot[...]
    grad_coarse = (scale * dot(mix_t[...], cots)).astype(BF16)
    grad_fine = dot(grad_coarse, unplace[...]).astype(BF16)
    mix_sum[...] += dot_nt(cots, coarse[0])
    res_sum[...] += dot_nt(parts[0], grad_fine)
    grad_parts[...] = dot(w_res[...], grad_fine)
    low_half = low_lanes(chans)
    for r in range(4):
        for t in range(4):
            cols = slice(r * LANES, (r + 1) * LANES)
            lanes = slice(t * LANES, (t + 1) * LANES)
            one = grad_parts[2 * t * chans : (2 * t + 1) * chans, cols]
            two = grad_parts[(2 * t + 1) * chans : (2 * t + 2) * chans, cols]
            first = slice(2 * r * chans, (2 * r + 1) * chans)
            second = slice((2 * r + 1) * chans, (2 * r + 2) * chans)
            grad_rows[first, lanes] = (
                jnp.where(low_half, one, pltpu.roll(two, LANES // 2, 1))
                * slope[0, first, lanes].astype(F32)
            ).astype(BF16)
            grad_rows[second, lanes] = (
                jnp.where(low_half, pltpu.roll(one, LANES // 2, 1), two)
                * slope[0, second, lanes].astype(F32)
            ).astype(BF16)
    for r in range(4):
        rows = slice(r * 2 * chans, (r + 1) * 2 * chans)
        grad_cols[r] = dot_nt(split[...], grad_rows[rows, :]).astype(BF16)

    low_half = low_lanes(7 * chans)

    @pl.loop(0, 8 // STEP)
    def _(step):
        for k in range(STEP):
            shift_into(sources(scalars, q * 8 + step * STEP + k), bricks, views.at[k])
        total = None
        for k in range(0, STEP, 2):
            grads = grad_cols[step * (STEP // 2) + k // 2]
            term = jnp.where(low_half, dot(views[k], grads), dot(views[k + 1], grads))
            total = term if total is None else total + term
        conv_sum[...] += total

    @pl.when(q == pl.num_programs(0) - 1)
    def _():
        packed[0:wide] = (scale * mix_sum[...]).astype(BF16)
        at = wide
        packed[at : at + 8 * chans] = res_sum[...].astype(BF16)
        at += 8 * chans
        total = conv_sum[...] + pltpu.roll(conv_sum[...], LANES // 2, 1)
        low = low_lanes(chans)
        for t in range(4):
            one = total[2 * t * chans : (2 * t + 1) * chans]
            two = total[(2 * t + 1) * chans : (2 * t + 2) * chans] if t < 3 else one
            packed[at : at + chans] = jnp.where(low, one, two).astype(BF16)
            at += chans
        if at < packed.shape[0]:
            packed[at:] = jnp.zeros((packed.shape[0] - at, LANES), BF16)


def unpack_kernel(lane_tiles, packed, pieces, coarse_out, conv, res, mix):
    wide = mix.shape[0]
    chans = conv.shape[1]
    half = LANES // 2
    mix[...] = packed[0:wide].astype(F32)
    at = wide
    for t in range(8):
        res[t] = packed[at : at + chans].astype(F32)
        at += chans
    for t in range(4):
        block = packed[at : at + chans].astype(F32)
        block = block.T
        conv[2 * t] = block[:half]
        if 2 * t + 1 < 7:
            conv[2 * t + 1] = block[half:]
        at += chans
    per_row = VOX // (LANES * lane_tiles)
    for j in range(pieces.shape[0]):
        chan, part = j // per_row, j % per_row
        for q in range(coarse_out.shape[0]):
            for lt in range(lane_tiles):
                lane = (part * lane_tiles + lt) * LANES
                coarse_out[q, chan * ROWS : (chan + 1) * ROWS, lane : lane + LANES] = pieces[
                    j, q, lt
                ]


def kernel_call(kernel, out_shape, grid_spec, flops, moved):
    return pl.pallas_call(
        kernel,
        out_shape=out_shape,
        grid_spec=grid_spec,
        compiler_params=pltpu.CompilerParams(vmem_limit_bytes=VMEM_BYTES),
        cost_estimate=pl.CostEstimate(flops=flops, bytes_accessed=moved, transcendentals=0),
    )


def body(features, counts, neighbors, parents, w_conv, w_restrict, w_mix, cotangent):
    devices = lax.axis_size("space")
    position = lax.axis_index("space").astype(jnp.int32).reshape(1)
    slots, wide = cotangent.shape[:2]
    count, chans = features.shape[:2]
    lane_tiles = VOX * 8 // devices // LANES
    tiles = slots * lane_tiles
    groups = count // 8
    whole = lambda shape: pl.BlockSpec(shape, lambda *_: (0,) * len(shape))
    any_spec = pl.BlockSpec(memory_space=pl.ANY)
    smem_spec = pl.BlockSpec(memory_space=pltpu.SMEM)
    smem = lambda size: pltpu.SMEM((size,), jnp.int32)
    vmem = pltpu.VMEM
    ints = lambda size: jax.ShapeDtypeStruct((size,), jnp.int32)

    message_shape = (devices, tiles + 1, ROWS, LANES)
    message, kids = kernel_call(
        functools.partial(pack_kernel, lane_tiles),
        (jax.ShapeDtypeStruct(message_shape, BF16), ints(groups)),
        pl.GridSpec(
            grid=(1,),
            in_specs=[smem_spec, any_spec],
            out_specs=[whole(message_shape), smem_spec],
            scratch_shapes=[
                smem(groups + 1), vmem(cotangent.shape, BF16), pltpu.SemaphoreType.DMA,
            ],
        ),
        1000, 2**20,
    )(parents.T, cotangent)
    spread = lax.all_to_all(message, "space", split_axis=0, concat_axis=0, tiled=True)

    plane = jax.ShapeDtypeStruct((SEND, chans, LANES), BF16)
    up, down, slot_at, up_place, down_place = kernel_call(
        table_kernel,
        (plane, plane, ints(count), ints(count), ints(count)),
        pl.GridSpec(
            grid=(1,),
            in_specs=[smem_spec] * 4 + [any_spec],
            out_specs=[whole(plane.shape)] * 2 + [smem_spec] * 3,
            scratch_shapes=[smem(SEND + 1)] * 4 + [pltpu.SemaphoreType.DMA((2 * SEND,))],
        ),
        1000, 2**20,
    )(position, kids, neighbors.T, parents.T, features)
    below = lax.ppermute(up, "space", [(i, i + 1) for i in range(devices - 1)])
    above = lax.ppermute(down, "space", [(i + 1, i) for i in range(devices - 1)])

    lane_ids = jnp.arange(lane_tiles, dtype=jnp.int32)
    all_kids = spread[:, tiles, 0, :groups].astype(jnp.int32)
    kid_tiles = (all_kids // slots) * (tiles + 1) + (all_kids % slots) * lane_tiles
    piece_shape = (devices, groups, lane_tiles, ROWS, LANES)
    forward_tiles = jnp.take(
        spread.reshape(devices * (tiles + 1), ROWS, LANES),
        (kid_tiles[:, :, None] + lane_ids).reshape(-1), axis=0, mode="clip",
    ).reshape(piece_shape)
    forward_tiles, above, below = lax.optimization_barrier((forward_tiles, above, below))
    cot_pieces = lax.all_to_all(forward_tiles, "space", split_axis=0, concat_axis=0, tiled=True)

    res_rows = w_restrict.transpose(0, 2, 1).reshape(8 * chans, wide)
    scalars = (position, counts, neighbors.T, slot_at, up_place, down_place)
    brick_scratch = vmem((count + SEND + 1, chans, VOX), BF16)
    view_scratch = vmem((STEP, 7 * chans, VOX), BF16)
    per_group = lambda *shape: pl.BlockSpec((1,) + shape, lambda q: (q,) + (0,) * len(shape))
    piece_spec = pl.BlockSpec((devices, 1, lane_tiles, ROWS, LANES), lambda q: (0, q, 0, 0, 0))
    square = vmem((8 * chans, VOX), BF16)
    parts, slope, coarse, pieces = kernel_call(
        functools.partial(forward_kernel, lane_tiles),
        (
            jax.ShapeDtypeStruct((groups, 8 * chans, VOX), BF16),
            jax.ShapeDtypeStruct((groups, 8 * chans, VOX), BF16),
            jax.ShapeDtypeStruct((groups, wide, VOX), BF16),
            jax.ShapeDtypeStruct(piece_shape, BF16),
        ),
        pl.GridSpec(
            grid=(groups,),
            in_specs=[smem_spec] * 6 + [any_spec] * 3
            + [whole(w_conv.shape), whole(res_rows.shape), whole(w_mix.shape)],
            out_specs=[per_group(8 * chans, VOX), per_group(8 * chans, VOX),
                       per_group(wide, VOX), piece_spec],
            scratch_shapes=[
                brick_scratch, view_scratch, vmem((8 * chans, 2 * VOX), BF16),
                vmem((2 * VOX, VOX), BF16), vmem((VOX, VOX), BF16),
                vmem((chans, 7 * chans), BF16), vmem((wide, 8 * chans), BF16),
                pltpu.SemaphoreType.DMA((3,)),
            ],
        ),
        16 * 10**9, 16 * 2**20,
    )(*scalars, features, above, below, w_conv, res_rows, w_mix)
    returned = lax.all_to_all(pieces, "space", split_axis=0, concat_axis=0, tiled=True)

    scale = 1.0 / math.sqrt(devices * slots * VOX)
    used = wide + 8 * chans + 4 * chans
    rows = -(-used // (devices * ROWS)) * ROWS
    packed = kernel_call(
        functools.partial(backward_kernel, lane_tiles, scale),
        jax.ShapeDtypeStruct((devices * rows, LANES), BF16),
        pl.GridSpec(
            grid=(groups,),
            in_specs=[smem_spec] * 6 + [any_spec] * 3
            + [piece_spec, per_group(8 * chans, VOX), per_group(8 * chans, VOX),
               per_group(wide, VOX), whole(w_mix.shape), whole(res_rows.shape)],
            out_specs=whole((devices * rows, LANES)),
            scratch_shapes=[
                brick_scratch, view_scratch, vmem((wide, VOX), BF16),
                vmem((8 * chans, VOX), F32), square, vmem((4, VOX, 2 * chans), BF16),
                vmem((VOX, VOX), BF16), vmem((VOX, VOX), BF16), vmem((wide, wide), BF16),
                vmem((7 * chans, 2 * chans), F32), vmem((8 * chans, wide), F32),
                vmem((wide, wide), F32), pltpu.SemaphoreType.DMA((3,)),
            ],
        ),
        16 * 10**9, 16 * 2**20,
    )(*scalars, features, above, below, cot_pieces, parts, slope, coarse, w_mix, res_rows)

    shares = lax.all_to_all(
        packed.reshape(devices, rows, LANES), "space", split_axis=0, concat_axis=0, tiled=True
    )
    summed = jnp.sum(shares.astype(F32), axis=0).astype(BF16)
    totals = lax.all_gather(summed, "space", axis=0, tiled=True)

    returned, _ = lax.optimization_barrier((returned, packed))
    flat_kids = all_kids.reshape(-1)
    number = jnp.arange(devices * groups, dtype=jnp.int32)
    source = jnp.sum(jnp.where(flat_kids[None, :] == number[:, None], number[None, :], 0), axis=1)
    owner_tiles = jnp.take(
        returned.reshape(devices * groups, lane_tiles, ROWS, LANES), source, axis=0, mode="clip"
    ).reshape(devices, slots, lane_tiles, ROWS, LANES)
    out_pieces = lax.all_to_all(owner_tiles, "space", split_axis=0, concat_axis=0, tiled=True)

    coarse_out, grad_conv, grad_res, grad_mix = kernel_call(
        functools.partial(unpack_kernel, lane_tiles),
        (
            jax.ShapeDtypeStruct((slots, wide, VOX), BF16),
            jax.ShapeDtypeStruct((7, chans, chans), F32),
            jax.ShapeDtypeStruct((8, chans, wide), F32),
            jax.ShapeDtypeStruct((wide, wide), F32),
        ),
        pl.GridSpec(
            grid=(1,),
            in_specs=[whole(totals.shape), whole(out_pieces.shape)],
            out_specs=[whole((slots, wide, VOX)), whole((7, chans, chans)),
                       whole((8, chans, wide)), whole((wide, wide))],
        ),
        1000, 2 * 2**20,
    )(totals, out_pieces)
    return coarse_out, grad_conv, grad_res.transpose(0, 2, 1), grad_mix


def solution(mesh):
    return jax.shard_map(
        body,
        mesh=mesh,
        in_specs=(
            P(("groups", "space"), None, None),
            P(("groups", "space")),
            P(("groups", "space"), None),
            P(("groups", "space"), None),
            P(),
            P(),
            P(),
            P(("groups", "space"), None, None),
        ),
        out_specs=(
            P(("groups", "space"), None, None),
            P("groups", None, None),
            P("groups", None, None),
            P("groups", None),
        ),
        check_vma=False,
    )
```

```python
import functools
import math

import jax
import jax.numpy as jnp
from jax import lax
from jax.experimental import pallas as pl
from jax.experimental.pallas import tpu as pltpu
from jax.sharding import PartitionSpec as P

EDGE = 8
HALF = EDGE // 2
VOX = EDGE**3
LANES = 128
ROWS = 16
SEND = 8
STEP = 4
BF16 = jnp.bfloat16
F32 = jnp.float32
VMEM_BYTES = 60 * 1024 * 1024


def bits_of(value):
    return [(value >> (8 - k)) & 1 for k in range(9)]


def join_bits(bits):
    value = bits[0]
    for bit in bits[1:]:
        value = value * 2 + bit
    return value


def split_voxel(column):
    ta, tb, tc, a1, a0, b1, b0, c1, c0 = bits_of(column)
    return join_bits([a1, a0, ta, b1, b0, tb, c1, c0, tc])


def octant_voxel(column):
    oa, ob, oc, a1, a0, b1, b0, c1, c0 = bits_of(column)
    return join_bits([oa, a1, a0, ob, b1, b0, oc, c1, c0])


def picker(voxel_of, shape=(VOX, VOX), start=(0, 0), flip=False):
    row = lax.broadcasted_iota(jnp.int32, shape, 0) + start[0]
    column = lax.broadcasted_iota(jnp.int32, shape, 1) + start[1]
    return (column == voxel_of(row) if flip else row == voxel_of(column)).astype(BF16)


def dot(a, b):
    return jnp.dot(a, b, preferred_element_type=F32)


def dot_nt(a, b):
    return lax.dot_general(a, b, (((1,), (1,)), ((), ())), preferred_element_type=F32)


def pack_kernel(lane_tiles, parents, cot, msg, kids_out, kids):
    devices = msg.shape[0]
    slots = cot.shape[0]

    def find(g, found):
        kids[found] = parents[0, g]
        return found + (parents[1, g] == 0).astype(jnp.int32)

    lax.fori_loop(0, parents.shape[1], find, jnp.int32(0), unroll=4)
    lane = lax.broadcasted_iota(jnp.int32, (ROWS, LANES), 1)
    label = jnp.zeros((ROWS, LANES), jnp.int32)
    for q in range(kids_out.shape[0]):
        kids_out[q] = kids[q]
        label = jnp.where(lane == q, kids[q], label)
    label = label.astype(F32).astype(BF16)
    for j in range(devices):
        msg[j, slots * lane_tiles] = label
    per_row = VOX // (LANES * lane_tiles)
    for j in range(devices):
        chan, part = j // per_row, j % per_row
        for q in range(slots):
            for lt in range(lane_tiles):
                lane = (part * lane_tiles + lt) * LANES
                msg[j, q * lane_tiles + lt] = cot[
                    q, chan * ROWS : (chan + 1) * ROWS, lane : lane + LANES
                ]


def table_kernel(
    place, kids, neighbors, parents, feat, up, down, slot_at, up_place, down_place,
    up_idx, up_far, down_idx, down_far, sem,
):
    count = neighbors.shape[1]
    base = place[0] * count
    for r in range(SEND + 1):
        up_idx[r] = 0
        down_idx[r] = 0
        up_far[r] = 2 * count
        down_far[r] = 2 * count

    def scan(g, found):
        n_up, n_down = found
        near_up, near_down = neighbors[0, g], neighbors[1, g]
        far_up, far_down = near_up - base - count, near_down - base + count
        goes_up = (near_up >= 0) & (far_up >= 0)
        goes_down = (near_down >= 0) & (far_down < count)
        up_idx[n_up] = g
        up_far[n_up] = jnp.where(goes_up, far_up, 2 * count)
        down_idx[n_down] = g
        down_far[n_down] = jnp.where(goes_down, far_down, 2 * count)
        return n_up + goes_up.astype(jnp.int32), n_down + goes_down.astype(jnp.int32)

    lax.fori_loop(0, count, scan, (jnp.int32(0), jnp.int32(0)), unroll=4)
    copies = []
    for r in range(SEND):
        copies.append(
            pltpu.make_async_copy(
                feat.at[up_idx[r], :, pl.ds(VOX - LANES, LANES)], up.at[r], sem.at[r]
            )
        )
        copies.append(
            pltpu.make_async_copy(
                feat.at[down_idx[r], :, pl.ds(0, LANES)], down.at[r], sem.at[SEND + r]
            )
        )
    for copy in copies:
        copy.start()

    def order(g, carry):
        q = jnp.int32(0)
        for k in range(1, kids.shape[0]):
            q += jnp.where(kids[k] == parents[0, g], k, 0)
        slot_at[q * 8 + parents[1, g]] = g
        return carry

    lax.fori_loop(0, count, order, jnp.int32(0), unroll=4)

    def rank(r, carry):
        for far, idx, put in ((up_far, up_idx, up_place), (down_far, down_idx, down_place)):
            earlier = jnp.int32(0)
            for other in range(SEND):
                earlier += (far[other] < far[r]).astype(jnp.int32)

            @pl.when(far[r] < count)
            def _():
                put[idx[r]] = count + earlier

        return carry

    lax.fori_loop(0, SEND, rank, jnp.int32(0))
    for copy in copies:
        copy.wait()


def order_kernel(feat, out, split):
    @pl.when(pl.program_id(0) == 0)
    def _():
        split[...] = picker(split_voxel)

    bricks, chans = feat.shape[:2]
    rows = feat[...].reshape(bricks * chans, VOX)
    out[...] = dot(rows, split[...]).astype(BF16).reshape(out.shape)


def place_arrivals(above, below, bricks, count):
    chans = bricks.shape[1]
    half = VOX // 2
    shape = (LANES, half)
    first = dot(above[...].reshape(SEND * chans, LANES), picker(split_voxel, shape))
    last = dot(
        below[...].reshape(SEND * chans, LANES), picker(split_voxel, shape, (VOX - LANES, half))
    )
    bricks[count : count + SEND, :, :half] = first.astype(BF16).reshape(SEND, chans, half)
    bricks[count : count + SEND, :, half:] = last.astype(BF16).reshape(SEND, chans, half)
    bricks[count + SEND] = jnp.zeros(bricks.shape[1:], BF16)


def sources(scalars, number):
    place, counts, neighbors, slot_at, up_place, down_place = scalars
    count = neighbors.shape[1]
    zero_slot = count + SEND
    g = slot_at[number]
    found = []
    for d in range(6):
        near = neighbors[d, g]
        local = near - place[0] * count
        if d == 0:
            local = jnp.where(local >= count, up_place[g], local)
        if d == 1:
            local = jnp.where(local < 0, down_place[g], local)
        found.append(jnp.where(near >= 0, local, zero_slot))
    found.append(jnp.where(g < counts[0], g, zero_slot))
    return found


def shift_into(slots, bricks, views):
    chans = bricks.shape[1]
    tiles = VOX // LANES
    lane = lax.broadcasted_iota(jnp.int32, (chans, LANES), 1)
    low = lane < LANES // 2
    a = (lane // 16) % HALF
    b = (lane // 4) % HALF
    c = lane % HALF

    def tile(slot, t):
        return bricks[slot, :, t * LANES : (t + 1) * LANES]

    def turn(value, by):
        return pltpu.roll(value, by % LANES, 1)

    x = [tile(slots[6], t) for t in range(tiles)]
    for t in range(tiles):
        lanes = slice(t * LANES, (t + 1) * LANES)
        if t < 2:
            plus_a = x[t + 2]
            minus_a = jnp.where(a > 0, turn(x[t + 2], 16), turn(tile(slots[1], t + 2), -48))
        else:
            plus_a = jnp.where(a < HALF - 1, turn(x[t - 2], -16), turn(tile(slots[0], t - 2), 48))
            minus_a = x[t - 2]
        if t % 2 == 0:
            plus_b = x[t + 1]
            minus_b = jnp.where(b > 0, turn(x[t + 1], 4), turn(tile(slots[3], t + 1), -12))
        else:
            plus_b = jnp.where(b < HALF - 1, turn(x[t - 1], -4), turn(tile(slots[2], t - 1), 12))
            minus_b = x[t - 1]
        swapped = turn(x[t], 64)
        plus_c = jnp.where(c < HALF - 1, turn(x[t], 63), turn(tile(slots[4], t), 67))
        minus_c = jnp.where(c > 0, turn(x[t], -63), turn(tile(slots[5], t), -67))
        out = [plus_a, minus_a, plus_b, minus_b, jnp.where(low, swapped, plus_c),
               jnp.where(low, minus_c, swapped), x[t]]
        for d in range(7):
            views[d * chans : (d + 1) * chans, lanes] = out[d]


def low_lanes(rows):
    return lax.broadcasted_iota(jnp.int32, (rows, LANES), 1) < LANES // 2


def forward_kernel(
    lane_tiles, place_no, counts, neighbors, slot_at, up_place, down_place,
    feat, w_conv_hbm, w_res_hbm, w_mix_hbm, above, below,
    parts_out, slope_out, coarse_out, piece_out,
    bricks, views, place, w_conv, w_res, w_mix, conv_cat, res_cat, sem,
):
    q = pl.program_id(0)
    count, chans = feat.shape[:2]
    scalars = (place_no, counts, neighbors, slot_at, up_place, down_place)

    @pl.when(q == 0)
    def _():
        copies = [
            pltpu.make_async_copy(source, target, sem.at[k])
            for k, (source, target) in enumerate((
                (w_conv_hbm, w_conv), (w_res_hbm, w_res), (w_mix_hbm, w_mix),
                (feat, bricks.at[pl.ds(0, count)]),
            ))
        ]
        for copy in copies:
            copy.start()
        place_arrivals(above, below, bricks, count)
        place[...] = picker(octant_voxel, flip=True)
        for copy in copies[:3]:
            copy.wait()
        for d in range(7):
            conv_cat[:, d * chans : (d + 1) * chans] = w_conv[d]
        res_cat[...] = w_res[...].T
        copies[3].wait()

    low_half = low_lanes(chans)

    @pl.loop(0, 8 // STEP)
    def _(step):
        for k in range(STEP):
            shift_into(sources(scalars, q * 8 + step * STEP + k), bricks, views.at[k])
        acts = []
        for k in range(STEP):
            hidden = dot(conv_cat[...], views[k])
            sig = 0.5 + 0.5 * jnp.tanh(0.5 * hidden)
            act = hidden * sig
            row = pl.multiple_of((step * STEP + k) * chans, chans)
            slope_out[0, pl.ds(row, chans), :] = (sig + act * (1.0 - sig)).astype(BF16)
            acts.append(act.astype(BF16))
        for k in range(0, STEP, 2):
            column = pl.multiple_of((step * STEP + k) * (LANES // 2), LANES)
            for t in range(4):
                one = acts[k][:, t * LANES : (t + 1) * LANES]
                two = acts[k + 1][:, t * LANES : (t + 1) * LANES]
                parts_out[0, 2 * t * chans : (2 * t + 1) * chans, pl.ds(column, LANES)] = (
                    jnp.where(low_half, one, pltpu.roll(two, LANES // 2, 1))
                )
                parts_out[0, (2 * t + 1) * chans : (2 * t + 2) * chans, pl.ds(column, LANES)] = (
                    jnp.where(low_half, pltpu.roll(one, LANES // 2, 1), two)
                )

    by_octant = dot(res_cat[...], parts_out[0]).astype(BF16)
    coarse = dot(by_octant, place[...]).astype(BF16)
    coarse_out[0] = coarse
    mixed = dot(w_mix[...], coarse).astype(BF16)
    per_row = VOX // (LANES * lane_tiles)
    for j in range(piece_out.shape[0]):
        chan, part = j // per_row, j % per_row
        for lt in range(lane_tiles):
            lane = (part * lane_tiles + lt) * LANES
            piece_out[j, 0, lt] = mixed[chan * ROWS : (chan + 1) * ROWS, lane : lane + LANES]


def backward_kernel(
    lane_tiles, scale, place_no, counts, neighbors, slot_at, up_place, down_place,
    feat, above, below, pieces, parts, slope, coarse, w_mix, w_res, packed,
    bricks, views, cot, grad_parts, grad_rows, unplace, mix_t, conv_sum, res_sum, mix_sum, sem,
):
    q = pl.program_id(0)
    count, chans = feat.shape[:2]
    wide = coarse.shape[1]
    scalars = (place_no, counts, neighbors, slot_at, up_place, down_place)
    fetch = pltpu.make_async_copy(feat, bricks.at[pl.ds(0, count)], sem)

    @pl.when(q == 0)
    def _():
        fetch.start()
        place_arrivals(above, below, bricks, count)
        unplace[...] = picker(octant_voxel)
        mix_t[...] = w_mix[...].T
        conv_sum[...] = jnp.zeros_like(conv_sum)
        res_sum[...] = jnp.zeros_like(res_sum)
        mix_sum[...] = jnp.zeros_like(mix_sum)

    per_row = VOX // (LANES * lane_tiles)
    for j in range(pieces.shape[0]):
        chan, part = j // per_row, j % per_row
        for lt in range(lane_tiles):
            lane = (part * lane_tiles + lt) * LANES
            cot[chan * ROWS : (chan + 1) * ROWS, lane : lane + LANES] = pieces[j, 0, lt]
    cots = cot[...]
    grad_coarse = (scale * dot(mix_t[...], cots)).astype(BF16)
    grad_fine = dot(grad_coarse, unplace[...]).astype(BF16)
    mix_sum[...] += dot_nt(cots, coarse[0])
    res_sum[...] += dot_nt(parts[0], grad_fine)
    grad_parts[...] = dot(w_res[...], grad_fine)
    low_half = low_lanes(chans)
    for r in range(4):
        for t in range(4):
            cols = slice(r * LANES, (r + 1) * LANES)
            lanes = slice(t * LANES, (t + 1) * LANES)
            one = grad_parts[2 * t * chans : (2 * t + 1) * chans, cols]
            two = grad_parts[(2 * t + 1) * chans : (2 * t + 2) * chans, cols]
            first = slice(2 * r * chans, (2 * r + 1) * chans)
            second = slice((2 * r + 1) * chans, (2 * r + 2) * chans)
            grad_rows[first, lanes] = (
                jnp.where(low_half, one, pltpu.roll(two, LANES // 2, 1))
                * slope[0, first, lanes].astype(F32)
            ).astype(BF16)
            grad_rows[second, lanes] = (
                jnp.where(low_half, pltpu.roll(one, LANES // 2, 1), two)
                * slope[0, second, lanes].astype(F32)
            ).astype(BF16)

    @pl.when(q == 0)
    def _():
        fetch.wait()

    @pl.loop(0, 8 // STEP)
    def _(step):
        for k in range(STEP):
            shift_into(sources(scalars, q * 8 + step * STEP + k), bricks, views.at[k])
        total = None
        for k in range(STEP):
            row = pl.multiple_of((step * STEP + k) * chans, chans)
            term = dot_nt(grad_rows[pl.ds(row, chans), :], views[k])
            total = term if total is None else total + term
        conv_sum[:, : 7 * chans] += total

    @pl.when(q == pl.num_programs(0) - 1)
    def _():
        packed[0:wide] = (scale * mix_sum[...]).astype(BF16)
        at = wide
        packed[at : at + 8 * chans] = res_sum[...].astype(BF16)
        at += 8 * chans
        for t in range(4):
            packed[at : at + chans] = conv_sum[:, t * LANES : (t + 1) * LANES].astype(BF16)
            at += chans
        if at < packed.shape[0]:
            packed[at:] = jnp.zeros((packed.shape[0] - at, LANES), BF16)


def join_kernel(kids, shares, pieces, msg):
    devices, groups, lane_tiles = pieces.shape[:3]
    slots = groups
    body_rows = slots * lane_tiles * ROWS
    for s in range(devices):
        for q in range(groups):
            kid = kids[s * groups + q]
            owner, slot = kid // slots, kid % slots
            for lt in range(lane_tiles):
                row = pl.multiple_of((slot * lane_tiles + lt) * ROWS, ROWS)
                msg[owner, pl.ds(row, ROWS), :] = pieces[s, q, lt]
    total = jnp.sum(shares[...].astype(F32), axis=0).astype(BF16)
    for j in range(devices):
        msg[j, body_rows:] = total


def unpack_kernel(lane_tiles, msg, coarse_out, conv, res, mix, packed):
    devices, rows = msg.shape[:2]
    slots = coarse_out.shape[0]
    wide = mix.shape[0]
    chans = conv.shape[1]
    half = LANES // 2
    body_rows = slots * lane_tiles * ROWS
    share = rows - body_rows
    for j in range(devices):
        packed[j * share : (j + 1) * share] = msg[j, body_rows:].astype(F32)
    mix[...] = packed[0:wide]
    at = wide
    for t in range(8):
        res[t] = packed[at : at + chans]
        at += chans
    for t in range(4):
        block = packed[at : at + chans]
        conv[2 * t] = block[:, :half]
        if 2 * t + 1 < 7:
            conv[2 * t + 1] = block[:, half:]
        at += chans
    per_row = VOX // (LANES * lane_tiles)
    for j in range(devices):
        chan, part = j // per_row, j % per_row
        for q in range(slots):
            for lt in range(lane_tiles):
                row = (q * lane_tiles + lt) * ROWS
                lane = (part * lane_tiles + lt) * LANES
                coarse_out[q, chan * ROWS : (chan + 1) * ROWS, lane : lane + LANES] = msg[
                    j, row : row + ROWS
                ]


def kernel_call(kernel, out_shape, grid_spec, flops, moved):
    return pl.pallas_call(
        kernel,
        out_shape=out_shape,
        grid_spec=grid_spec,
        compiler_params=pltpu.CompilerParams(vmem_limit_bytes=VMEM_BYTES),
        cost_estimate=pl.CostEstimate(flops=flops, bytes_accessed=moved, transcendentals=0),
    )


def body(features, counts, neighbors, parents, w_conv, w_restrict, w_mix, cotangent):
    devices = lax.axis_size("space")
    position = lax.axis_index("space").astype(jnp.int32).reshape(1)
    slots, wide = cotangent.shape[:2]
    count, chans = features.shape[:2]
    lane_tiles = VOX * 8 // devices // LANES
    tiles = slots * lane_tiles
    groups = count // 8
    whole = lambda shape: pl.BlockSpec(shape, lambda *_: (0,) * len(shape))
    any_spec = pl.BlockSpec(memory_space=pl.ANY)
    smem_spec = pl.BlockSpec(memory_space=pltpu.SMEM)
    smem = lambda size: pltpu.SMEM((size,), jnp.int32)
    vmem = pltpu.VMEM
    ints = lambda size: jax.ShapeDtypeStruct((size,), jnp.int32)

    message_shape = (devices, tiles + 1, ROWS, LANES)
    message, kids = kernel_call(
        functools.partial(pack_kernel, lane_tiles),
        (jax.ShapeDtypeStruct(message_shape, BF16), ints(groups)),
        pl.GridSpec(
            grid=(1,),
            in_specs=[smem_spec, whole(cotangent.shape)],
            out_specs=[whole(message_shape), smem_spec],
            scratch_shapes=[smem(groups + 1)],
        ),
        1000, 2**20,
    )(parents.T, cotangent)
    spread = lax.all_to_all(message, "space", split_axis=0, concat_axis=0, tiled=True)

    plane = jax.ShapeDtypeStruct((SEND, chans, LANES), BF16)
    up, down, slot_at, up_place, down_place = kernel_call(
        table_kernel,
        (plane, plane, ints(count), ints(count), ints(count)),
        pl.GridSpec(
            grid=(1,),
            in_specs=[smem_spec] * 4 + [any_spec],
            out_specs=[whole(plane.shape)] * 2 + [smem_spec] * 3,
            scratch_shapes=[smem(SEND + 1)] * 4 + [pltpu.SemaphoreType.DMA((2 * SEND,))],
        ),
        1000, 2**20,
    )(position, kids, neighbors.T, parents.T, features)
    below = lax.ppermute(up, "space", [(i, i + 1) for i in range(devices - 1)])
    above = lax.ppermute(down, "space", [(i + 1, i) for i in range(devices - 1)])

    ordered = kernel_call(
        order_kernel,
        jax.ShapeDtypeStruct(features.shape, BF16),
        pl.GridSpec(
            grid=(groups,),
            in_specs=[pl.BlockSpec((8, chans, VOX), lambda q: (q, 0, 0))],
            out_specs=pl.BlockSpec((8, chans, VOX), lambda q: (q, 0, 0)),
            scratch_shapes=[vmem((VOX, VOX), BF16)],
        ),
        1000, 2**20,
    )(features)

    lane_ids = jnp.arange(lane_tiles, dtype=jnp.int32)
    all_kids = spread[:, tiles, 0, :groups].astype(jnp.int32)
    kid_tiles = (all_kids // slots) * (tiles + 1) + (all_kids % slots) * lane_tiles
    piece_shape = (devices, groups, lane_tiles, ROWS, LANES)
    forward_tiles = jnp.take(
        spread.reshape(devices * (tiles + 1), ROWS, LANES),
        (kid_tiles[:, :, None] + lane_ids).reshape(-1), axis=0, mode="clip",
    ).reshape(piece_shape)
    forward_tiles, above, below = lax.optimization_barrier((forward_tiles, above, below))
    cot_pieces = lax.all_to_all(forward_tiles, "space", split_axis=0, concat_axis=0, tiled=True)

    res_rows = w_restrict.transpose(0, 2, 1).reshape(8 * chans, wide)
    scalars = (position, counts, neighbors.T, slot_at, up_place, down_place)
    brick_scratch = vmem((count + SEND + 1, chans, VOX), BF16)
    view_scratch = vmem((STEP, 7 * chans, VOX), BF16)
    per_group = lambda *shape: pl.BlockSpec((1,) + shape, lambda q: (q,) + (0,) * len(shape))
    piece_spec = pl.BlockSpec((devices, 1, lane_tiles, ROWS, LANES), lambda q: (0, q, 0, 0, 0))
    parts, slope, coarse, pieces = kernel_call(
        functools.partial(forward_kernel, lane_tiles),
        (
            jax.ShapeDtypeStruct((groups, 8 * chans, VOX), BF16),
            jax.ShapeDtypeStruct((groups, 8 * chans, VOX), BF16),
            jax.ShapeDtypeStruct((groups, wide, VOX), BF16),
            jax.ShapeDtypeStruct(piece_shape, BF16),
        ),
        pl.GridSpec(
            grid=(groups,),
            in_specs=[smem_spec] * 6 + [any_spec] * 4 + [whole(plane.shape)] * 2,
            out_specs=[per_group(8 * chans, VOX), per_group(8 * chans, VOX),
                       per_group(wide, VOX), piece_spec],
            scratch_shapes=[
                brick_scratch, view_scratch, vmem((VOX, VOX), BF16), vmem(w_conv.shape, BF16),
                vmem(res_rows.shape, BF16), vmem(w_mix.shape, BF16),
                vmem((chans, 7 * chans), BF16), vmem((wide, 8 * chans), BF16),
                pltpu.SemaphoreType.DMA((4,)),
            ],
        ),
        16 * 10**9, 16 * 2**20,
    )(*scalars, ordered, w_conv, res_rows, w_mix, above, below)
    returned = lax.all_to_all(pieces, "space", split_axis=0, concat_axis=0, tiled=True)

    scale = 1.0 / math.sqrt(devices * slots * VOX)
    used = wide + 8 * chans + 4 * chans
    rows = -(-used // (devices * 8)) * 8
    packed = kernel_call(
        functools.partial(backward_kernel, lane_tiles, scale),
        jax.ShapeDtypeStruct((devices * rows, LANES), BF16),
        pl.GridSpec(
            grid=(groups,),
            in_specs=[smem_spec] * 6 + [any_spec] + [whole(plane.shape)] * 2
            + [piece_spec, per_group(8 * chans, VOX), per_group(8 * chans, VOX),
               per_group(wide, VOX), whole(w_mix.shape), whole(res_rows.shape)],
            out_specs=whole((devices * rows, LANES)),
            scratch_shapes=[
                brick_scratch, view_scratch, vmem((wide, VOX), BF16),
                vmem((8 * chans, VOX), F32), vmem((8 * chans, VOX), BF16), vmem((VOX, VOX), BF16),
                vmem((wide, wide), BF16), vmem((chans, 8 * chans), F32),
                vmem((8 * chans, wide), F32), vmem((wide, wide), F32), pltpu.SemaphoreType.DMA,
            ],
        ),
        16 * 10**9, 16 * 2**20,
    )(*scalars, ordered, above, below, cot_pieces, parts, slope, coarse, w_mix, res_rows)

    shares = lax.all_to_all(
        packed.reshape(devices, rows, LANES), "space", split_axis=0, concat_axis=0, tiled=True
    )
    joined_shape = (devices, tiles * ROWS + rows, LANES)
    joined = kernel_call(
        join_kernel,
        jax.ShapeDtypeStruct(joined_shape, BF16),
        pl.GridSpec(
            grid=(1,),
            in_specs=[smem_spec, whole(shares.shape), whole(piece_shape)],
            out_specs=whole(joined_shape),
        ),
        1000, 2**20,
    )(all_kids.reshape(-1), shares, returned)
    finished = lax.all_to_all(joined, "space", split_axis=0, concat_axis=0, tiled=True)

    coarse_out, grad_conv, grad_res, grad_mix = kernel_call(
        functools.partial(unpack_kernel, lane_tiles),
        (
            jax.ShapeDtypeStruct((slots, wide, VOX), BF16),
            jax.ShapeDtypeStruct((7, chans, chans), F32),
            jax.ShapeDtypeStruct((8, chans, wide), F32),
            jax.ShapeDtypeStruct((wide, wide), F32),
        ),
        pl.GridSpec(
            grid=(1,),
            in_specs=[whole(joined_shape)],
            out_specs=[whole((slots, wide, VOX)), whole((7, chans, chans)),
                       whole((8, chans, wide)), whole((wide, wide))],
            scratch_shapes=[vmem((devices * rows, LANES), F32)],
        ),
        1000, 2 * 2**20,
    )(finished)
    return coarse_out, grad_conv, grad_res.transpose(0, 2, 1), grad_mix


def solution(mesh):
    return jax.shard_map(
        body,
        mesh=mesh,
        in_specs=(
            P(("groups", "space"), None, None),
            P(("groups", "space")),
            P(("groups", "space"), None),
            P(("groups", "space"), None),
            P(),
            P(),
            P(),
            P(("groups", "space"), None, None),
        ),
        out_specs=(
            P(("groups", "space"), None, None),
            P("groups", None, None),
            P("groups", None, None),
            P("groups", None),
        ),
        check_vma=False,
    )
```

```python
import functools
import math

import jax
import jax.numpy as jnp
from jax import lax
from jax.experimental import pallas as pl
from jax.experimental.pallas import tpu as pltpu
from jax.sharding import PartitionSpec as P

EDGE = 8
HALF = EDGE // 2
VOX = EDGE**3
LANES = 128
ROWS = 16
SEND = 8
STEP = 4
BF16 = jnp.bfloat16
F32 = jnp.float32
VMEM_BYTES = 60 * 1024 * 1024


def bits_of(value):
    return [(value >> (8 - k)) & 1 for k in range(9)]


def join_bits(bits):
    value = bits[0]
    for bit in bits[1:]:
        value = value * 2 + bit
    return value


def split_voxel(column):
    ta, tb, tc, a1, a0, b1, b0, c1, c0 = bits_of(column)
    return join_bits([a1, a0, ta, b1, b0, tb, c1, c0, tc])


def octant_voxel(column):
    oa, ob, oc, a1, a0, b1, b0, c1, c0 = bits_of(column)
    return join_bits([oa, a1, a0, ob, b1, b0, oc, c1, c0])


def picker(voxel_of, shape=(VOX, VOX), start=(0, 0), flip=False):
    row = lax.broadcasted_iota(jnp.int32, shape, 0) + start[0]
    column = lax.broadcasted_iota(jnp.int32, shape, 1) + start[1]
    return (column == voxel_of(row) if flip else row == voxel_of(column)).astype(BF16)


def dot(a, b):
    return jnp.dot(a, b, preferred_element_type=F32)


def dot_nt(a, b):
    return lax.dot_general(a, b, (((1,), (1,)), ((), ())), preferred_element_type=F32)


def pack_kernel(lane_tiles, parents, cot, msg, kids_out, kids):
    devices = msg.shape[0]
    slots = cot.shape[0]

    def find(g, found):
        kids[found] = parents[0, g]
        return found + (parents[1, g] == 0).astype(jnp.int32)

    lax.fori_loop(0, parents.shape[1], find, jnp.int32(0), unroll=4)
    lane = lax.broadcasted_iota(jnp.int32, (ROWS, LANES), 1)
    label = jnp.zeros((ROWS, LANES), jnp.int32)
    for q in range(kids_out.shape[0]):
        kids_out[q] = kids[q]
        label = jnp.where(lane == q, kids[q], label)
    label = label.astype(F32).astype(BF16)
    for j in range(devices):
        msg[j, slots * lane_tiles] = label
    per_row = VOX // (LANES * lane_tiles)
    for j in range(devices):
        chan, part = j // per_row, j % per_row
        for q in range(slots):
            for lt in range(lane_tiles):
                lane = (part * lane_tiles + lt) * LANES
                msg[j, q * lane_tiles + lt] = cot[
                    q, chan * ROWS : (chan + 1) * ROWS, lane : lane + LANES
                ]


def table_kernel(
    place, kids, neighbors, parents, feat, up, down, slot_at, up_place, down_place,
    up_idx, up_far, down_idx, down_far, sem,
):
    count = neighbors.shape[1]
    base = place[0] * count
    for r in range(SEND + 1):
        up_idx[r] = 0
        down_idx[r] = 0
        up_far[r] = 2 * count
        down_far[r] = 2 * count

    def scan(g, found):
        n_up, n_down = found
        near_up, near_down = neighbors[0, g], neighbors[1, g]
        far_up, far_down = near_up - base - count, near_down - base + count
        goes_up = (near_up >= 0) & (far_up >= 0)
        goes_down = (near_down >= 0) & (far_down < count)
        up_idx[n_up] = g
        up_far[n_up] = jnp.where(goes_up, far_up, 2 * count)
        down_idx[n_down] = g
        down_far[n_down] = jnp.where(goes_down, far_down, 2 * count)
        return n_up + goes_up.astype(jnp.int32), n_down + goes_down.astype(jnp.int32)

    lax.fori_loop(0, count, scan, (jnp.int32(0), jnp.int32(0)), unroll=4)
    copies = []
    for r in range(SEND):
        copies.append(
            pltpu.make_async_copy(
                feat.at[up_idx[r], :, pl.ds(VOX - LANES, LANES)], up.at[r], sem.at[r]
            )
        )
        copies.append(
            pltpu.make_async_copy(
                feat.at[down_idx[r], :, pl.ds(0, LANES)], down.at[r], sem.at[SEND + r]
            )
        )
    for copy in copies:
        copy.start()

    def order(g, carry):
        q = jnp.int32(0)
        for k in range(1, kids.shape[0]):
            q += jnp.where(kids[k] == parents[0, g], k, 0)
        slot_at[q * 8 + parents[1, g]] = g
        return carry

    lax.fori_loop(0, count, order, jnp.int32(0), unroll=4)

    def rank(r, carry):
        for far, idx, put in ((up_far, up_idx, up_place), (down_far, down_idx, down_place)):
            earlier = jnp.int32(0)
            for other in range(SEND):
                earlier += (far[other] < far[r]).astype(jnp.int32)

            @pl.when(far[r] < count)
            def _():
                put[idx[r]] = count + earlier

        return carry

    lax.fori_loop(0, SEND, rank, jnp.int32(0))
    for copy in copies:
        copy.wait()


def order_kernel(feat, out, split):
    @pl.when(pl.program_id(0) == 0)
    def _():
        split[...] = picker(split_voxel)

    bricks, chans = feat.shape[:2]
    rows = feat[...].reshape(bricks * chans, VOX)
    out[...] = dot(rows, split[...]).astype(BF16).reshape(out.shape)


def place_arrivals(above, below, bricks, count):
    chans = bricks.shape[1]
    half = VOX // 2
    shape = (LANES, half)
    first = dot(above[...].reshape(SEND * chans, LANES), picker(split_voxel, shape))
    last = dot(
        below[...].reshape(SEND * chans, LANES), picker(split_voxel, shape, (VOX - LANES, half))
    )
    bricks[count : count + SEND, :, :half] = first.astype(BF16).reshape(SEND, chans, half)
    bricks[count : count + SEND, :, half:] = last.astype(BF16).reshape(SEND, chans, half)
    bricks[count + SEND] = jnp.zeros(bricks.shape[1:], BF16)


def sources(scalars, number):
    place, counts, neighbors, slot_at, up_place, down_place = scalars
    count = neighbors.shape[1]
    zero_slot = count + SEND
    g = slot_at[number]
    found = []
    for d in range(6):
        near = neighbors[d, g]
        local = near - place[0] * count
        if d == 0:
            local = jnp.where(local >= count, up_place[g], local)
        if d == 1:
            local = jnp.where(local < 0, down_place[g], local)
        found.append(jnp.where(near >= 0, local, zero_slot))
    found.append(jnp.where(g < counts[0], g, zero_slot))
    return found


def shift_into(slots, bricks, views):
    chans = bricks.shape[1]
    tiles = VOX // LANES
    lane = lax.broadcasted_iota(jnp.int32, (chans, LANES), 1)
    low = lane < LANES // 2
    a = (lane // 16) % HALF
    b = (lane // 4) % HALF
    c = lane % HALF

    def tile(slot, t):
        return bricks[slot, :, t * LANES : (t + 1) * LANES]

    def turn(value, by):
        return pltpu.roll(value, by % LANES, 1)

    x = [tile(slots[6], t) for t in range(tiles)]
    for t in range(tiles):
        lanes = slice(t * LANES, (t + 1) * LANES)
        if t < 2:
            plus_a = x[t + 2]
            minus_a = jnp.where(a > 0, turn(x[t + 2], 16), turn(tile(slots[1], t + 2), -48))
        else:
            plus_a = jnp.where(a < HALF - 1, turn(x[t - 2], -16), turn(tile(slots[0], t - 2), 48))
            minus_a = x[t - 2]
        if t % 2 == 0:
            plus_b = x[t + 1]
            minus_b = jnp.where(b > 0, turn(x[t + 1], 4), turn(tile(slots[3], t + 1), -12))
        else:
            plus_b = jnp.where(b < HALF - 1, turn(x[t - 1], -4), turn(tile(slots[2], t - 1), 12))
            minus_b = x[t - 1]
        swapped = turn(x[t], 64)
        plus_c = jnp.where(c < HALF - 1, turn(x[t], 63), turn(tile(slots[4], t), 67))
        minus_c = jnp.where(c > 0, turn(x[t], -63), turn(tile(slots[5], t), -67))
        out = [plus_a, minus_a, plus_b, minus_b, jnp.where(low, swapped, plus_c),
               jnp.where(low, minus_c, swapped), x[t]]
        for d in range(7):
            views[d * chans : (d + 1) * chans, lanes] = out[d]


def low_lanes(rows):
    return lax.broadcasted_iota(jnp.int32, (rows, LANES), 1) < LANES // 2


def forward_kernel(
    lane_tiles, place_no, counts, neighbors, slot_at, up_place, down_place,
    feat, w_conv_hbm, w_res_hbm, w_mix_hbm, above, below,
    parts_out, slope_out, coarse_out, piece_out,
    bricks, views, place, w_conv, w_res, w_mix, conv_cat, res_cat, sem,
):
    q = pl.program_id(0)
    count, chans = feat.shape[:2]
    scalars = (place_no, counts, neighbors, slot_at, up_place, down_place)

    @pl.when(q == 0)
    def _():
        copies = [
            pltpu.make_async_copy(source, target, sem.at[k])
            for k, (source, target) in enumerate((
                (w_conv_hbm, w_conv), (w_res_hbm, w_res), (w_mix_hbm, w_mix),
                (feat, bricks.at[pl.ds(0, count)]),
            ))
        ]
        for copy in copies:
            copy.start()
        place_arrivals(above, below, bricks, count)
        place[...] = picker(octant_voxel, flip=True)
        for copy in copies[:3]:
            copy.wait()
        for d in range(7):
            conv_cat[:, d * chans : (d + 1) * chans] = w_conv[d]
        res_cat[...] = w_res[...].T
        copies[3].wait()

    low_half = low_lanes(chans)

    @pl.loop(0, 8 // STEP)
    def _(step):
        for k in range(STEP):
            shift_into(sources(scalars, q * 8 + step * STEP + k), bricks, views.at[k])
        acts = []
        for k in range(STEP):
            hidden = dot(conv_cat[...], views[k])
            sig = 0.5 + 0.5 * jnp.tanh(0.5 * hidden)
            act = hidden * sig
            row = pl.multiple_of((step * STEP + k) * chans, chans)
            slope_out[0, pl.ds(row, chans), :] = (sig + act * (1.0 - sig)).astype(BF16)
            acts.append(act.astype(BF16))
        for k in range(0, STEP, 2):
            column = pl.multiple_of((step * STEP + k) * (LANES // 2), LANES)
            for t in range(4):
                one = acts[k][:, t * LANES : (t + 1) * LANES]
                two = acts[k + 1][:, t * LANES : (t + 1) * LANES]
                parts_out[0, 2 * t * chans : (2 * t + 1) * chans, pl.ds(column, LANES)] = (
                    jnp.where(low_half, one, pltpu.roll(two, LANES // 2, 1))
                )
                parts_out[0, (2 * t + 1) * chans : (2 * t + 2) * chans, pl.ds(column, LANES)] = (
                    jnp.where(low_half, pltpu.roll(one, LANES // 2, 1), two)
                )

    by_octant = dot(res_cat[...], parts_out[0]).astype(BF16)
    coarse = dot(by_octant, place[...]).astype(BF16)
    coarse_out[0] = coarse
    mixed = dot(w_mix[...], coarse).astype(BF16)
    per_row = VOX // (LANES * lane_tiles)
    for j in range(piece_out.shape[0]):
        chan, part = j // per_row, j % per_row
        for lt in range(lane_tiles):
            lane = (part * lane_tiles + lt) * LANES
            piece_out[j, 0, lt] = mixed[chan * ROWS : (chan + 1) * ROWS, lane : lane + LANES]


def backward_kernel(
    lane_tiles, scale, place_no, counts, neighbors, slot_at, up_place, down_place,
    feat, above, below, pieces, parts, slope, coarse, w_mix, w_res, packed,
    bricks, views, cot, grad_parts, grad_rows, unplace, mix_t, conv_sum, res_sum, mix_sum, sem,
):
    q = pl.program_id(0)
    count, chans = feat.shape[:2]
    wide = coarse.shape[1]
    scalars = (place_no, counts, neighbors, slot_at, up_place, down_place)
    fetch = pltpu.make_async_copy(feat, bricks.at[pl.ds(0, count)], sem)

    @pl.when(q == 0)
    def _():
        fetch.start()
        place_arrivals(above, below, bricks, count)
        unplace[...] = picker(octant_voxel)
        mix_t[...] = w_mix[...].T
        conv_sum[...] = jnp.zeros_like(conv_sum)
        res_sum[...] = jnp.zeros_like(res_sum)
        mix_sum[...] = jnp.zeros_like(mix_sum)

    per_row = VOX // (LANES * lane_tiles)
    for j in range(pieces.shape[0]):
        chan, part = j // per_row, j % per_row
        for lt in range(lane_tiles):
            lane = (part * lane_tiles + lt) * LANES
            cot[chan * ROWS : (chan + 1) * ROWS, lane : lane + LANES] = pieces[j, 0, lt]
    cots = cot[...]
    grad_coarse = (scale * dot(mix_t[...], cots)).astype(BF16)
    grad_fine = dot(grad_coarse, unplace[...]).astype(BF16)
    mix_sum[...] += dot_nt(cots, coarse[0])
    res_sum[...] += dot_nt(parts[0], grad_fine)
    grad_parts[...] = dot(w_res[...], grad_fine)
    low_half = low_lanes(chans)
    for r in range(4):
        for t in range(4):
            cols = slice(r * LANES, (r + 1) * LANES)
            lanes = slice(t * LANES, (t + 1) * LANES)
            one = grad_parts[2 * t * chans : (2 * t + 1) * chans, cols]
            two = grad_parts[(2 * t + 1) * chans : (2 * t + 2) * chans, cols]
            first = slice(2 * r * chans, (2 * r + 1) * chans)
            second = slice((2 * r + 1) * chans, (2 * r + 2) * chans)
            grad_rows[first, lanes] = (
                jnp.where(low_half, one, pltpu.roll(two, LANES // 2, 1))
                * slope[0, first, lanes].astype(F32)
            ).astype(BF16)
            grad_rows[second, lanes] = (
                jnp.where(low_half, pltpu.roll(one, LANES // 2, 1), two)
                * slope[0, second, lanes].astype(F32)
            ).astype(BF16)

    @pl.when(q == 0)
    def _():
        fetch.wait()

    @pl.loop(0, 8 // STEP)
    def _(step):
        for k in range(STEP):
            shift_into(sources(scalars, q * 8 + step * STEP + k), bricks, views.at[k])
        total = None
        for k in range(STEP):
            row = pl.multiple_of((step * STEP + k) * chans, chans)
            term = dot_nt(grad_rows[pl.ds(row, chans), :], views[k])
            total = term if total is None else total + term
        conv_sum[:, : 7 * chans] += total

    @pl.when(q == pl.num_programs(0) - 1)
    def _():
        packed[0:wide] = scale * mix_sum[...]
        at = wide
        packed[at : at + 8 * chans] = res_sum[...]
        at += 8 * chans
        for t in range(4):
            packed[at : at + chans] = conv_sum[:, t * LANES : (t + 1) * LANES]
            at += chans


def join_kernel(kids, pieces, msg):
    devices, groups, lane_tiles = pieces.shape[:3]
    slots = groups
    for s in range(devices):
        for q in range(groups):
            kid = kids[s * groups + q]
            owner, slot = kid // slots, kid % slots
            for lt in range(lane_tiles):
                row = pl.multiple_of((slot * lane_tiles + lt) * ROWS, ROWS)
                msg[owner, pl.ds(row, ROWS), :] = pieces[s, q, lt]


def unpack_kernel(lane_tiles, msg, packed, coarse_out, conv, res, mix):
    devices = msg.shape[0]
    slots = coarse_out.shape[0]
    wide = mix.shape[0]
    chans = conv.shape[1]
    half = LANES // 2
    mix[...] = packed[0:wide]
    at = wide
    for t in range(8):
        res[t] = packed[at : at + chans]
        at += chans
    for t in range(4):
        block = packed[at : at + chans]
        conv[2 * t] = block[:, :half]
        if 2 * t + 1 < 7:
            conv[2 * t + 1] = block[:, half:]
        at += chans
    per_row = VOX // (LANES * lane_tiles)
    for j in range(devices):
        chan, part = j // per_row, j % per_row
        for q in range(slots):
            for lt in range(lane_tiles):
                row = (q * lane_tiles + lt) * ROWS
                lane = (part * lane_tiles + lt) * LANES
                coarse_out[q, chan * ROWS : (chan + 1) * ROWS, lane : lane + LANES] = msg[
                    j, row : row + ROWS
                ]


def kernel_call(kernel, out_shape, grid_spec, flops, moved):
    return pl.pallas_call(
        kernel,
        out_shape=out_shape,
        grid_spec=grid_spec,
        compiler_params=pltpu.CompilerParams(vmem_limit_bytes=VMEM_BYTES),
        cost_estimate=pl.CostEstimate(flops=flops, bytes_accessed=moved, transcendentals=0),
    )


def body(features, counts, neighbors, parents, w_conv, w_restrict, w_mix, cotangent):
    devices = lax.axis_size("space")
    position = lax.axis_index("space").astype(jnp.int32).reshape(1)
    slots, wide = cotangent.shape[:2]
    count, chans = features.shape[:2]
    lane_tiles = VOX * 8 // devices // LANES
    tiles = slots * lane_tiles
    groups = count // 8
    whole = lambda shape: pl.BlockSpec(shape, lambda *_: (0,) * len(shape))
    any_spec = pl.BlockSpec(memory_space=pl.ANY)
    smem_spec = pl.BlockSpec(memory_space=pltpu.SMEM)
    smem = lambda size: pltpu.SMEM((size,), jnp.int32)
    vmem = pltpu.VMEM
    ints = lambda size: jax.ShapeDtypeStruct((size,), jnp.int32)

    message_shape = (devices, tiles + 1, ROWS, LANES)
    message, kids = kernel_call(
        functools.partial(pack_kernel, lane_tiles),
        (jax.ShapeDtypeStruct(message_shape, BF16), ints(groups)),
        pl.GridSpec(
            grid=(1,),
            in_specs=[smem_spec, whole(cotangent.shape)],
            out_specs=[whole(message_shape), smem_spec],
            scratch_shapes=[smem(groups + 1)],
        ),
        1000, 2**20,
    )(parents.T, cotangent)
    spread = lax.all_to_all(message, "space", split_axis=0, concat_axis=0, tiled=True)

    plane = jax.ShapeDtypeStruct((SEND, chans, LANES), BF16)
    up, down, slot_at, up_place, down_place = kernel_call(
        table_kernel,
        (plane, plane, ints(count), ints(count), ints(count)),
        pl.GridSpec(
            grid=(1,),
            in_specs=[smem_spec] * 4 + [any_spec],
            out_specs=[whole(plane.shape)] * 2 + [smem_spec] * 3,
            scratch_shapes=[smem(SEND + 1)] * 4 + [pltpu.SemaphoreType.DMA((2 * SEND,))],
        ),
        1000, 2**20,
    )(position, kids, neighbors.T, parents.T, features)
    below = lax.ppermute(up, "space", [(i, i + 1) for i in range(devices - 1)])
    above = lax.ppermute(down, "space", [(i + 1, i) for i in range(devices - 1)])

    ordered = kernel_call(
        order_kernel,
        jax.ShapeDtypeStruct(features.shape, BF16),
        pl.GridSpec(
            grid=(groups,),
            in_specs=[pl.BlockSpec((8, chans, VOX), lambda q: (q, 0, 0))],
            out_specs=pl.BlockSpec((8, chans, VOX), lambda q: (q, 0, 0)),
            scratch_shapes=[vmem((VOX, VOX), BF16)],
        ),
        1000, 2**20,
    )(features)

    lane_ids = jnp.arange(lane_tiles, dtype=jnp.int32)
    all_kids = spread[:, tiles, 0, :groups].astype(jnp.int32)
    kid_tiles = (all_kids // slots) * (tiles + 1) + (all_kids % slots) * lane_tiles
    piece_shape = (devices, groups, lane_tiles, ROWS, LANES)
    forward_tiles = jnp.take(
        spread.reshape(devices * (tiles + 1), ROWS, LANES),
        (kid_tiles[:, :, None] + lane_ids).reshape(-1), axis=0, mode="clip",
    ).reshape(piece_shape)
    forward_tiles, above, below = lax.optimization_barrier((forward_tiles, above, below))
    cot_pieces = lax.all_to_all(forward_tiles, "space", split_axis=0, concat_axis=0, tiled=True)

    res_rows = w_restrict.transpose(0, 2, 1).reshape(8 * chans, wide)
    scalars = (position, counts, neighbors.T, slot_at, up_place, down_place)
    brick_scratch = vmem((count + SEND + 1, chans, VOX), BF16)
    view_scratch = vmem((STEP, 7 * chans, VOX), BF16)
    per_group = lambda *shape: pl.BlockSpec((1,) + shape, lambda q: (q,) + (0,) * len(shape))
    piece_spec = pl.BlockSpec((devices, 1, lane_tiles, ROWS, LANES), lambda q: (0, q, 0, 0, 0))
    parts, slope, coarse, pieces = kernel_call(
        functools.partial(forward_kernel, lane_tiles),
        (
            jax.ShapeDtypeStruct((groups, 8 * chans, VOX), BF16),
            jax.ShapeDtypeStruct((groups, 8 * chans, VOX), BF16),
            jax.ShapeDtypeStruct((groups, wide, VOX), BF16),
            jax.ShapeDtypeStruct(piece_shape, BF16),
        ),
        pl.GridSpec(
            grid=(groups,),
            in_specs=[smem_spec] * 6 + [any_spec] * 4 + [whole(plane.shape)] * 2,
            out_specs=[per_group(8 * chans, VOX), per_group(8 * chans, VOX),
                       per_group(wide, VOX), piece_spec],
            scratch_shapes=[
                brick_scratch, view_scratch, vmem((VOX, VOX), BF16), vmem(w_conv.shape, BF16),
                vmem(res_rows.shape, BF16), vmem(w_mix.shape, BF16),
                vmem((chans, 7 * chans), BF16), vmem((wide, 8 * chans), BF16),
                pltpu.SemaphoreType.DMA((4,)),
            ],
        ),
        16 * 10**9, 16 * 2**20,
    )(*scalars, ordered, w_conv, res_rows, w_mix, above, below)
    returned = lax.all_to_all(pieces, "space", split_axis=0, concat_axis=0, tiled=True)

    scale = 1.0 / math.sqrt(devices * slots * VOX)
    used = wide + 8 * chans + 4 * chans
    packed = kernel_call(
        functools.partial(backward_kernel, lane_tiles, scale),
        jax.ShapeDtypeStruct((used, LANES), F32),
        pl.GridSpec(
            grid=(groups,),
            in_specs=[smem_spec] * 6 + [any_spec] + [whole(plane.shape)] * 2
            + [piece_spec, per_group(8 * chans, VOX), per_group(8 * chans, VOX),
               per_group(wide, VOX), whole(w_mix.shape), whole(res_rows.shape)],
            out_specs=whole((used, LANES)),
            scratch_shapes=[
                brick_scratch, view_scratch, vmem((wide, VOX), BF16),
                vmem((8 * chans, VOX), F32), vmem((8 * chans, VOX), BF16), vmem((VOX, VOX), BF16),
                vmem((wide, wide), BF16), vmem((chans, 8 * chans), F32),
                vmem((8 * chans, wide), F32), vmem((wide, wide), F32), pltpu.SemaphoreType.DMA,
            ],
        ),
        16 * 10**9, 16 * 2**20,
    )(*scalars, ordered, above, below, cot_pieces, parts, slope, coarse, w_mix, res_rows)

    totals = lax.psum(packed, "space")

    returned, _ = lax.optimization_barrier((returned, packed))
    joined_shape = (devices, tiles * ROWS, LANES)
    joined = kernel_call(
        join_kernel,
        jax.ShapeDtypeStruct(joined_shape, BF16),
        pl.GridSpec(
            grid=(1,),
            in_specs=[smem_spec, whole(piece_shape)],
            out_specs=whole(joined_shape),
        ),
        1000, 2**20,
    )(all_kids.reshape(-1), returned)
    finished = lax.all_to_all(joined, "space", split_axis=0, concat_axis=0, tiled=True)

    coarse_out, grad_conv, grad_res, grad_mix = kernel_call(
        functools.partial(unpack_kernel, lane_tiles),
        (
            jax.ShapeDtypeStruct((slots, wide, VOX), BF16),
            jax.ShapeDtypeStruct((7, chans, chans), F32),
            jax.ShapeDtypeStruct((8, chans, wide), F32),
            jax.ShapeDtypeStruct((wide, wide), F32),
        ),
        pl.GridSpec(
            grid=(1,),
            in_specs=[whole(joined_shape), whole(totals.shape)],
            out_specs=[whole((slots, wide, VOX)), whole((7, chans, chans)),
                       whole((8, chans, wide)), whole((wide, wide))],
        ),
        1000, 2 * 2**20,
    )(finished, totals)
    return coarse_out, grad_conv, grad_res.transpose(0, 2, 1), grad_mix


def solution(mesh):
    return jax.shard_map(
        body,
        mesh=mesh,
        in_specs=(
            P(("groups", "space"), None, None),
            P(("groups", "space")),
            P(("groups", "space"), None),
            P(("groups", "space"), None),
            P(),
            P(),
            P(),
            P(("groups", "space"), None, None),
        ),
        out_specs=(
            P(("groups", "space"), None, None),
            P("groups", None, None),
            P("groups", None, None),
            P("groups", None),
        ),
        check_vma=False,
    )
```

```python
import functools
import math

import jax
import jax.numpy as jnp
from jax import lax
from jax.experimental import pallas as pl
from jax.experimental.pallas import tpu as pltpu
from jax.sharding import PartitionSpec as P

EDGE = 8
HALF = EDGE // 2
VOX = EDGE**3
LANES = 128
ROWS = 16
SEND = 8
BF16 = jnp.bfloat16
F32 = jnp.float32
VMEM_BYTES = 60 * 1024 * 1024
SMALL_VMEM_BYTES = 16 * 1024 * 1024


def bits_of(value):
    return [(value >> (8 - k)) & 1 for k in range(9)]


def join_bits(bits):
    value = bits[0]
    for bit in bits[1:]:
        value = value * 2 + bit
    return value


def split_voxel(column):
    ta, tb, tc, a1, a0, b1, b0, c1, c0 = bits_of(column)
    return join_bits([a1, a0, ta, b1, b0, tb, c1, c0, tc])


def octant_voxel(column):
    oa, ob, oc, a1, a0, b1, b0, c1, c0 = bits_of(column)
    return join_bits([oa, a1, a0, ob, b1, b0, oc, c1, c0])


def picker(voxel_of, shape=(VOX, VOX), start=(0, 0), flip=False):
    row = lax.broadcasted_iota(jnp.int32, shape, 0) + start[0]
    column = lax.broadcasted_iota(jnp.int32, shape, 1) + start[1]
    return (column == voxel_of(row) if flip else row == voxel_of(column)).astype(BF16)


def dot(a, b):
    return jnp.dot(a, b, preferred_element_type=F32)


def dot_nt(a, b):
    return lax.dot_general(a, b, (((1,), (1,)), ((), ())), preferred_element_type=F32)


def pack_kernel(lane_tiles, parents, cot, msg, kids_out, kids):
    devices = msg.shape[0]
    slots = cot.shape[0]

    def find(g, found):
        kids[found] = parents[0, g]
        return found + (parents[1, g] == 0).astype(jnp.int32)

    lax.fori_loop(0, parents.shape[1], find, jnp.int32(0), unroll=4)
    lane = lax.broadcasted_iota(jnp.int32, (ROWS, LANES), 1)
    label = jnp.zeros((ROWS, LANES), jnp.int32)
    for q in range(kids_out.shape[0]):
        kids_out[q] = kids[q]
        label = jnp.where(lane == q, kids[q], label)
    label = label.astype(F32).astype(BF16)
    for j in range(devices):
        msg[j, slots * lane_tiles] = label
    per_row = VOX // (LANES * lane_tiles)
    for j in range(devices):
        chan, part = j // per_row, j % per_row
        for q in range(slots):
            for lt in range(lane_tiles):
                lane = (part * lane_tiles + lt) * LANES
                msg[j, q * lane_tiles + lt] = cot[
                    q, chan * ROWS : (chan + 1) * ROWS, lane : lane + LANES
                ]


def table_kernel(
    place, kids, neighbors, parents, feat, up, down, slot_at, up_place, down_place,
    up_idx, up_far, down_idx, down_far, sem,
):
    count = neighbors.shape[1]
    base = place[0] * count
    for r in range(SEND + 1):
        up_idx[r] = 0
        down_idx[r] = 0
        up_far[r] = 2 * count
        down_far[r] = 2 * count

    def scan(g, found):
        n_up, n_down = found
        near_up, near_down = neighbors[0, g], neighbors[1, g]
        far_up, far_down = near_up - base - count, near_down - base + count
        goes_up = (near_up >= 0) & (far_up >= 0)
        goes_down = (near_down >= 0) & (far_down < count)
        up_idx[n_up] = g
        up_far[n_up] = jnp.where(goes_up, far_up, 2 * count)
        down_idx[n_down] = g
        down_far[n_down] = jnp.where(goes_down, far_down, 2 * count)
        return n_up + goes_up.astype(jnp.int32), n_down + goes_down.astype(jnp.int32)

    lax.fori_loop(0, count, scan, (jnp.int32(0), jnp.int32(0)), unroll=4)
    copies = []
    for r in range(SEND):
        copies.append(
            pltpu.make_async_copy(
                feat.at[up_idx[r], :, pl.ds(VOX - LANES, LANES)], up.at[r], sem.at[r]
            )
        )
        copies.append(
            pltpu.make_async_copy(
                feat.at[down_idx[r], :, pl.ds(0, LANES)], down.at[r], sem.at[SEND + r]
            )
        )
    for copy in copies:
        copy.start()

    def order(g, carry):
        q = jnp.int32(0)
        for k in range(1, kids.shape[0]):
            q += jnp.where(kids[k] == parents[0, g], k, 0)
        slot_at[q * 8 + parents[1, g]] = g
        return carry

    lax.fori_loop(0, count, order, jnp.int32(0), unroll=4)

    def rank(r, carry):
        for far, idx, put in ((up_far, up_idx, up_place), (down_far, down_idx, down_place)):
            earlier = jnp.int32(0)
            for other in range(SEND):
                earlier += (far[other] < far[r]).astype(jnp.int32)

            @pl.when(far[r] < count)
            def _():
                put[idx[r]] = count + earlier

        return carry

    lax.fori_loop(0, SEND, rank, jnp.int32(0))
    for copy in copies:
        copy.wait()


def order_kernel(feat, out, split):
    @pl.when(pl.program_id(0) == 0)
    def _():
        split[...] = picker(split_voxel)

    bricks, chans = feat.shape[:2]
    rows = feat[...].reshape(bricks * chans, VOX)
    out[...] = dot(rows, split[...]).astype(BF16).reshape(out.shape)


def place_arrivals(above, below, bricks, count):
    chans = bricks.shape[1]
    half = VOX // 2
    shape = (LANES, half)
    first = dot(above[...].reshape(SEND * chans, LANES), picker(split_voxel, shape))
    last = dot(
        below[...].reshape(SEND * chans, LANES), picker(split_voxel, shape, (VOX - LANES, half))
    )
    bricks[count : count + SEND, :, :half] = first.astype(BF16).reshape(SEND, chans, half)
    bricks[count : count + SEND, :, half:] = last.astype(BF16).reshape(SEND, chans, half)
    bricks[count + SEND] = jnp.zeros(bricks.shape[1:], BF16)


def sources(scalars, number):
    place, counts, neighbors, slot_at, up_place, down_place = scalars
    count = neighbors.shape[1]
    zero_slot = count + SEND
    g = slot_at[number]
    found = []
    for d in range(6):
        near = neighbors[d, g]
        local = near - place[0] * count
        if d == 0:
            local = jnp.where(local >= count, up_place[g], local)
        if d == 1:
            local = jnp.where(local < 0, down_place[g], local)
        found.append(jnp.where(near >= 0, local, zero_slot))
    found.append(jnp.where(g < counts[0], g, zero_slot))
    return found


def shift_into(slots, bricks, views):
    chans = bricks.shape[1]
    tiles = VOX // LANES
    lane = lax.broadcasted_iota(jnp.int32, (chans, LANES), 1)
    low = lane < LANES // 2
    a = (lane // 16) % HALF
    b = (lane // 4) % HALF
    c = lane % HALF

    def tile(slot, t):
        return bricks[slot, :, t * LANES : (t + 1) * LANES]

    def turn(value, by):
        return pltpu.roll(value, by % LANES, 1)

    x = [tile(slots[6], t) for t in range(tiles)]
    for t in range(tiles):
        lanes = slice(t * LANES, (t + 1) * LANES)
        if t < 2:
            plus_a = x[t + 2]
            minus_a = jnp.where(a > 0, turn(x[t + 2], 16), turn(tile(slots[1], t + 2), -48))
        else:
            plus_a = jnp.where(a < HALF - 1, turn(x[t - 2], -16), turn(tile(slots[0], t - 2), 48))
            minus_a = x[t - 2]
        if t % 2 == 0:
            plus_b = x[t + 1]
            minus_b = jnp.where(b > 0, turn(x[t + 1], 4), turn(tile(slots[3], t + 1), -12))
        else:
            plus_b = jnp.where(b < HALF - 1, turn(x[t - 1], -4), turn(tile(slots[2], t - 1), 12))
            minus_b = x[t - 1]
        swapped = turn(x[t], 64)
        plus_c = jnp.where(c < HALF - 1, turn(x[t], 63), turn(tile(slots[4], t), 67))
        minus_c = jnp.where(c > 0, turn(x[t], -63), turn(tile(slots[5], t), -67))
        out = [plus_a, minus_a, plus_b, minus_b, jnp.where(low, swapped, plus_c),
               jnp.where(low, minus_c, swapped), x[t]]
        for d in range(7):
            views[d * chans : (d + 1) * chans, lanes] = out[d]


def low_lanes(rows):
    return lax.broadcasted_iota(jnp.int32, (rows, LANES), 1) < LANES // 2


def forward_kernel(
    lane_tiles, place_no, counts, neighbors, slot_at, up_place, down_place,
    feat, w_conv_hbm, w_res_hbm, w_mix_hbm, above, below,
    parts_out, slope_out, coarse_out, piece_out,
    bricks, views, place, w_conv, w_res, w_mix, conv_cat, res_cat, sem,
):
    q = pl.program_id(0)
    count, chans = feat.shape[:2]
    scalars = (place_no, counts, neighbors, slot_at, up_place, down_place)

    @pl.when(q == 0)
    def _():
        copies = [
            pltpu.make_async_copy(source, target, sem.at[k])
            for k, (source, target) in enumerate((
                (w_conv_hbm, w_conv), (w_res_hbm, w_res), (w_mix_hbm, w_mix),
                (feat, bricks.at[pl.ds(0, count)]),
            ))
        ]
        for copy in copies:
            copy.start()
        place_arrivals(above, below, bricks, count)
        place[...] = picker(octant_voxel, flip=True)
        for copy in copies[:3]:
            copy.wait()
        for d in range(7):
            conv_cat[:, d * chans : (d + 1) * chans] = w_conv[d]
        res_cat[...] = w_res[...].T
        copies[3].wait()

    low_half = low_lanes(chans)

    by_octant = []
    for first in (0, 4):
        acts = []
        for k in range(first, first + 4):
            shift_into(sources(scalars, q * 8 + k), bricks, views.at[k])
            hidden = dot(conv_cat[...], views[k])
            sig = 0.5 + 0.5 * jnp.tanh(0.5 * hidden)
            act = hidden * sig
            slope_out[0, k * chans : (k + 1) * chans, :] = (sig + act * (1.0 - sig)).astype(BF16)
            acts.append(act.astype(BF16))
        for k in range(0, 4, 2):
            lanes = slice((first + k) * (LANES // 2), (first + k + 2) * (LANES // 2))
            for t in range(4):
                one = acts[k][:, t * LANES : (t + 1) * LANES]
                two = acts[k + 1][:, t * LANES : (t + 1) * LANES]
                parts_out[0, 2 * t * chans : (2 * t + 1) * chans, lanes] = jnp.where(
                    low_half, one, pltpu.roll(two, LANES // 2, 1)
                )
                parts_out[0, (2 * t + 1) * chans : (2 * t + 2) * chans, lanes] = jnp.where(
                    low_half, pltpu.roll(one, LANES // 2, 1), two
                )
        lanes = slice(first * (LANES // 2), (first + 4) * (LANES // 2))
        by_octant.append(dot(res_cat[...], parts_out[0, :, lanes]).astype(BF16))
    by_octant = jnp.concatenate(by_octant, axis=1)
    coarse = dot(by_octant, place[...]).astype(BF16)
    coarse_out[0] = coarse
    mixed = dot(w_mix[...], coarse).astype(BF16)
    per_row = VOX // (LANES * lane_tiles)
    for j in range(piece_out.shape[0]):
        chan, part = j // per_row, j % per_row
        for lt in range(lane_tiles):
            lane = (part * lane_tiles + lt) * LANES
            piece_out[j, 0, lt] = mixed[chan * ROWS : (chan + 1) * ROWS, lane : lane + LANES]


def backward_kernel(
    lane_tiles, scale, place_no, counts, neighbors, slot_at, up_place, down_place,
    feat, above, below, pieces, parts, slope, coarse, w_mix, w_res, packed,
    bricks, views, cot, grad_parts, grad_rows, unplace, mix_t, conv_sum, res_sum, mix_sum, sem,
):
    q = pl.program_id(0)
    count, chans = feat.shape[:2]
    wide = coarse.shape[1]
    scalars = (place_no, counts, neighbors, slot_at, up_place, down_place)
    fetch = pltpu.make_async_copy(feat, bricks.at[pl.ds(0, count)], sem)

    @pl.when(q == 0)
    def _():
        fetch.start()
        place_arrivals(above, below, bricks, count)
        unplace[...] = picker(octant_voxel)
        mix_t[...] = w_mix[...].T
        conv_sum[...] = jnp.zeros_like(conv_sum)
        res_sum[...] = jnp.zeros_like(res_sum)
        mix_sum[...] = jnp.zeros_like(mix_sum)
        fetch.wait()

    per_row = VOX // (LANES * lane_tiles)
    for j in range(pieces.shape[0]):
        chan, part = j // per_row, j % per_row
        for lt in range(lane_tiles):
            lane = (part * lane_tiles + lt) * LANES
            cot[chan * ROWS : (chan + 1) * ROWS, lane : lane + LANES] = pieces[j, 0, lt]
    cots = cot[...]
    grad_coarse = (scale * dot(mix_t[...], cots)).astype(BF16)
    grad_fine = dot(grad_coarse, unplace[...]).astype(BF16)
    mix_sum[...] += dot_nt(cots, coarse[0])
    res_sum[...] += dot_nt(parts[0], grad_fine)
    grad_parts[...] = dot(w_res[...], grad_fine)
    low_half = low_lanes(chans)
    for r in range(4):
        for t in range(4):
            cols = slice(r * LANES, (r + 1) * LANES)
            lanes = slice(t * LANES, (t + 1) * LANES)
            one = grad_parts[2 * t * chans : (2 * t + 1) * chans, cols]
            two = grad_parts[(2 * t + 1) * chans : (2 * t + 2) * chans, cols]
            first = slice(2 * r * chans, (2 * r + 1) * chans)
            second = slice((2 * r + 1) * chans, (2 * r + 2) * chans)
            grad_rows[first, lanes] = (
                jnp.where(low_half, one, pltpu.roll(two, LANES // 2, 1))
                * slope[0, first, lanes].astype(F32)
            ).astype(BF16)
            grad_rows[second, lanes] = (
                jnp.where(low_half, pltpu.roll(one, LANES // 2, 1), two)
                * slope[0, second, lanes].astype(F32)
            ).astype(BF16)

    total = None
    for k in range(8):
        shift_into(sources(scalars, q * 8 + k), bricks, views.at[k])
        term = dot_nt(grad_rows[k * chans : (k + 1) * chans, :], views[k])
        total = term if total is None else total + term
    conv_sum[:, : 7 * chans] += total

    @pl.when(q == pl.num_programs(0) - 1)
    def _():
        packed[0:wide] = (scale * mix_sum[...]).astype(BF16)
        at = wide
        packed[at : at + 8 * chans] = res_sum[...].astype(BF16)
        at += 8 * chans
        for t in range(4):
            packed[at : at + chans] = conv_sum[:, t * LANES : (t + 1) * LANES].astype(BF16)
            at += chans
        if at < packed.shape[0]:
            packed[at:] = jnp.zeros((packed.shape[0] - at, LANES), BF16)


def join_kernel(kids, shares, pieces, msg):
    devices, groups, lane_tiles = pieces.shape[:3]
    slots = groups
    body_rows = slots * lane_tiles * ROWS
    for s in range(devices):
        for q in range(groups):
            kid = kids[s * groups + q]
            owner, slot = kid // slots, kid % slots
            for lt in range(lane_tiles):
                row = pl.multiple_of((slot * lane_tiles + lt) * ROWS, ROWS)
                msg[owner, pl.ds(row, ROWS), :] = pieces[s, q, lt]
    total = jnp.sum(shares[...].astype(F32), axis=0).astype(BF16)
    for j in range(devices):
        msg[j, body_rows:] = total


def unpack_kernel(lane_tiles, msg, coarse_out, conv, res, mix, packed):
    devices, rows = msg.shape[:2]
    slots = coarse_out.shape[0]
    wide = mix.shape[0]
    chans = conv.shape[1]
    half = LANES // 2
    body_rows = slots * lane_tiles * ROWS
    share = rows - body_rows
    for j in range(devices):
        packed[j * share : (j + 1) * share] = msg[j, body_rows:].astype(F32)
    mix[...] = packed[0:wide]
    at = wide
    for t in range(8):
        res[t] = packed[at : at + chans]
        at += chans
    for t in range(4):
        block = packed[at : at + chans]
        conv[2 * t] = block[:, :half]
        if 2 * t + 1 < 7:
            conv[2 * t + 1] = block[:, half:]
        at += chans
    per_row = VOX // (LANES * lane_tiles)
    for j in range(devices):
        chan, part = j // per_row, j % per_row
        for q in range(slots):
            for lt in range(lane_tiles):
                row = (q * lane_tiles + lt) * ROWS
                lane = (part * lane_tiles + lt) * LANES
                coarse_out[q, chan * ROWS : (chan + 1) * ROWS, lane : lane + LANES] = msg[
                    j, row : row + ROWS
                ]


def kernel_call(kernel, out_shape, grid_spec, flops, moved, vmem=VMEM_BYTES):
    return pl.pallas_call(
        kernel,
        out_shape=out_shape,
        grid_spec=grid_spec,
        compiler_params=pltpu.CompilerParams(vmem_limit_bytes=vmem),
        cost_estimate=pl.CostEstimate(flops=flops, bytes_accessed=moved, transcendentals=0),
    )


def body(features, counts, neighbors, parents, w_conv, w_restrict, w_mix, cotangent):
    devices = lax.axis_size("space")
    position = lax.axis_index("space").astype(jnp.int32).reshape(1)
    slots, wide = cotangent.shape[:2]
    count, chans = features.shape[:2]
    lane_tiles = VOX * 8 // devices // LANES
    tiles = slots * lane_tiles
    groups = count // 8
    whole = lambda shape: pl.BlockSpec(shape, lambda *_: (0,) * len(shape))
    any_spec = pl.BlockSpec(memory_space=pl.ANY)
    smem_spec = pl.BlockSpec(memory_space=pltpu.SMEM)
    smem = lambda size: pltpu.SMEM((size,), jnp.int32)
    vmem = pltpu.VMEM
    ints = lambda size: jax.ShapeDtypeStruct((size,), jnp.int32)

    message_shape = (devices, tiles + 1, ROWS, LANES)
    message, kids = kernel_call(
        functools.partial(pack_kernel, lane_tiles),
        (jax.ShapeDtypeStruct(message_shape, BF16), ints(groups)),
        pl.GridSpec(
            grid=(1,),
            in_specs=[smem_spec, whole(cotangent.shape)],
            out_specs=[whole(message_shape), smem_spec],
            scratch_shapes=[smem(groups + 1)],
        ),
        1000, 2**20,
    )(parents.T, cotangent)
    spread = lax.all_to_all(message, "space", split_axis=0, concat_axis=0, tiled=True)

    plane = jax.ShapeDtypeStruct((SEND, chans, LANES), BF16)
    up, down, slot_at, up_place, down_place = kernel_call(
        table_kernel,
        (plane, plane, ints(count), ints(count), ints(count)),
        pl.GridSpec(
            grid=(1,),
            in_specs=[smem_spec] * 4 + [any_spec],
            out_specs=[whole(plane.shape)] * 2 + [smem_spec] * 3,
            scratch_shapes=[smem(SEND + 1)] * 4 + [pltpu.SemaphoreType.DMA((2 * SEND,))],
        ),
        1000, 2**20,
    )(position, kids, neighbors.T, parents.T, features)
    below = lax.ppermute(up, "space", [(i, i + 1) for i in range(devices - 1)])
    above = lax.ppermute(down, "space", [(i + 1, i) for i in range(devices - 1)])

    ordered = kernel_call(
        order_kernel,
        jax.ShapeDtypeStruct(features.shape, BF16),
        pl.GridSpec(
            grid=(groups,),
            in_specs=[pl.BlockSpec((8, chans, VOX), lambda q: (q, 0, 0))],
            out_specs=pl.BlockSpec((8, chans, VOX), lambda q: (q, 0, 0)),
            scratch_shapes=[vmem((VOX, VOX), BF16)],
        ),
        1000, 2**20,
    )(features)

    lane_ids = jnp.arange(lane_tiles, dtype=jnp.int32)
    all_kids = spread[:, tiles, 0, :groups].astype(jnp.int32)
    kid_tiles = (all_kids // slots) * (tiles + 1) + (all_kids % slots) * lane_tiles
    piece_shape = (devices, groups, lane_tiles, ROWS, LANES)
    forward_tiles = jnp.take(
        spread.reshape(devices * (tiles + 1), ROWS, LANES),
        (kid_tiles[:, :, None] + lane_ids).reshape(-1), axis=0, mode="clip",
    ).reshape(piece_shape)
    forward_tiles, above, below = lax.optimization_barrier((forward_tiles, above, below))
    cot_pieces = lax.all_to_all(forward_tiles, "space", split_axis=0, concat_axis=0, tiled=True)

    res_rows = w_restrict.transpose(0, 2, 1).reshape(8 * chans, wide)
    scalars = (position, counts, neighbors.T, slot_at, up_place, down_place)
    brick_scratch = vmem((count + SEND + 1, chans, VOX), BF16)
    view_scratch = vmem((8, 7 * chans, VOX), BF16)
    per_group = lambda *shape: pl.BlockSpec((1,) + shape, lambda q: (q,) + (0,) * len(shape))
    piece_spec = pl.BlockSpec((devices, 1, lane_tiles, ROWS, LANES), lambda q: (0, q, 0, 0, 0))
    parts, slope, coarse, pieces = kernel_call(
        functools.partial(forward_kernel, lane_tiles),
        (
            jax.ShapeDtypeStruct((groups, 8 * chans, VOX), BF16),
            jax.ShapeDtypeStruct((groups, 8 * chans, VOX), BF16),
            jax.ShapeDtypeStruct((groups, wide, VOX), BF16),
            jax.ShapeDtypeStruct(piece_shape, BF16),
        ),
        pl.GridSpec(
            grid=(groups,),
            in_specs=[smem_spec] * 6 + [any_spec] * 4 + [whole(plane.shape)] * 2,
            out_specs=[per_group(8 * chans, VOX), per_group(8 * chans, VOX),
                       per_group(wide, VOX), piece_spec],
            scratch_shapes=[
                brick_scratch, view_scratch, vmem((VOX, VOX), BF16), vmem(w_conv.shape, BF16),
                vmem(res_rows.shape, BF16), vmem(w_mix.shape, BF16),
                vmem((chans, 7 * chans), BF16), vmem((wide, 8 * chans), BF16),
                pltpu.SemaphoreType.DMA((4,)),
            ],
        ),
        16 * 10**9, 16 * 2**20,
    )(*scalars, ordered, w_conv, res_rows, w_mix, above, below)
    returned = lax.all_to_all(pieces, "space", split_axis=0, concat_axis=0, tiled=True)

    scale = 1.0 / math.sqrt(devices * slots * VOX)
    used = wide + 8 * chans + 4 * chans
    rows = -(-used // (devices * 8)) * 8
    packed = kernel_call(
        functools.partial(backward_kernel, lane_tiles, scale),
        jax.ShapeDtypeStruct((devices * rows, LANES), BF16),
        pl.GridSpec(
            grid=(groups,),
            in_specs=[smem_spec] * 6 + [any_spec] + [whole(plane.shape)] * 2
            + [piece_spec, per_group(8 * chans, VOX), per_group(8 * chans, VOX),
               per_group(wide, VOX), whole(w_mix.shape), whole(res_rows.shape)],
            out_specs=whole((devices * rows, LANES)),
            scratch_shapes=[
                brick_scratch, view_scratch, vmem((wide, VOX), BF16),
                vmem((8 * chans, VOX), F32), vmem((8 * chans, VOX), BF16), vmem((VOX, VOX), BF16),
                vmem((wide, wide), BF16), vmem((chans, 8 * chans), F32),
                vmem((8 * chans, wide), F32), vmem((wide, wide), F32), pltpu.SemaphoreType.DMA,
            ],
        ),
        16 * 10**9, 16 * 2**20,
    )(*scalars, ordered, above, below, cot_pieces, parts, slope, coarse, w_mix, res_rows)

    shares = lax.all_to_all(
        packed.reshape(devices, rows, LANES), "space", split_axis=0, concat_axis=0, tiled=True
    )
    joined_shape = (devices, tiles * ROWS + rows, LANES)
    joined = kernel_call(
        join_kernel,
        jax.ShapeDtypeStruct(joined_shape, BF16),
        pl.GridSpec(
            grid=(1,),
            in_specs=[smem_spec, whole(shares.shape), whole(piece_shape)],
            out_specs=whole(joined_shape),
        ),
        1000, 2**20, SMALL_VMEM_BYTES,
    )(all_kids.reshape(-1), shares, returned)
    finished = lax.all_to_all(joined, "space", split_axis=0, concat_axis=0, tiled=True)

    coarse_out, grad_conv, grad_res, grad_mix = kernel_call(
        functools.partial(unpack_kernel, lane_tiles),
        (
            jax.ShapeDtypeStruct((slots, wide, VOX), BF16),
            jax.ShapeDtypeStruct((7, chans, chans), F32),
            jax.ShapeDtypeStruct((8, chans, wide), F32),
            jax.ShapeDtypeStruct((wide, wide), F32),
        ),
        pl.GridSpec(
            grid=(1,),
            in_specs=[whole(joined_shape)],
            out_specs=[whole((slots, wide, VOX)), whole((7, chans, chans)),
                       whole((8, chans, wide)), whole((wide, wide))],
            scratch_shapes=[vmem((devices * rows, LANES), F32)],
        ),
        1000, 2 * 2**20, SMALL_VMEM_BYTES,
    )(finished)
    return coarse_out, grad_conv, grad_res.transpose(0, 2, 1), grad_mix


def solution(mesh):
    return jax.shard_map(
        body,
        mesh=mesh,
        in_specs=(
            P(("groups", "space"), None, None),
            P(("groups", "space")),
            P(("groups", "space"), None),
            P(("groups", "space"), None),
            P(),
            P(),
            P(),
            P(("groups", "space"), None, None),
        ),
        out_specs=(
            P(("groups", "space"), None, None),
            P("groups", None, None),
            P("groups", None, None),
            P("groups", None),
        ),
        check_vma=False,
    )
```

```python
import functools
import math

import jax
import jax.numpy as jnp
from jax import lax
from jax.experimental import pallas as pl
from jax.experimental.pallas import tpu as pltpu
from jax.sharding import PartitionSpec as P

EDGE = 8
HALF = EDGE // 2
VOX = EDGE**3
LANES = 128
ROWS = 16
LABEL_ROWS = 8
SEND = 8
BF16 = jnp.bfloat16
F32 = jnp.float32
VMEM_BYTES = 60 * 1024 * 1024
SMALL_VMEM_BYTES = 16 * 1024 * 1024


def bits_of(value):
    return [(value >> (8 - k)) & 1 for k in range(9)]


def join_bits(bits):
    value = bits[0]
    for bit in bits[1:]:
        value = value * 2 + bit
    return value


def split_voxel(column):
    ta, tb, tc, a1, a0, b1, b0, c1, c0 = bits_of(column)
    return join_bits([a1, a0, ta, b1, b0, tb, c1, c0, tc])


def octant_voxel(column):
    oa, ob, oc, a1, a0, b1, b0, c1, c0 = bits_of(column)
    return join_bits([oa, a1, a0, ob, b1, b0, oc, c1, c0])


def picker(voxel_of, shape=(VOX, VOX), start=(0, 0), flip=False):
    row = lax.broadcasted_iota(jnp.int32, shape, 0) + start[0]
    column = lax.broadcasted_iota(jnp.int32, shape, 1) + start[1]
    return (column == voxel_of(row) if flip else row == voxel_of(column)).astype(BF16)


def dot(a, b):
    return jnp.dot(a, b, preferred_element_type=F32)


def dot_nt(a, b):
    return lax.dot_general(a, b, (((1,), (1,)), ((), ())), preferred_element_type=F32)


def pack_kernel(lane_tiles, parents, cot, msg, kids_out, kids):
    devices = msg.shape[0]
    slots = cot.shape[0]

    def find(g, found):
        kids[found] = parents[0, g]
        return found + (parents[1, g] == 0).astype(jnp.int32)

    lax.fori_loop(0, parents.shape[1], find, jnp.int32(0), unroll=4)
    lane = lax.broadcasted_iota(jnp.int32, (LABEL_ROWS, LANES), 1)
    label = jnp.zeros((LABEL_ROWS, LANES), jnp.int32)
    for q in range(kids_out.shape[0]):
        kids_out[q] = kids[q]
        label = jnp.where(lane == q, kids[q], label)
    label = label.astype(F32).astype(BF16)
    for j in range(devices):
        msg[j, slots * lane_tiles * ROWS :] = label
    per_row = VOX // (LANES * lane_tiles)
    for j in range(devices):
        chan, part = j // per_row, j % per_row
        for q in range(slots):
            for lt in range(lane_tiles):
                lane = (part * lane_tiles + lt) * LANES
                row = (q * lane_tiles + lt) * ROWS
                msg[j, row : row + ROWS] = cot[
                    q, chan * ROWS : (chan + 1) * ROWS, lane : lane + LANES
                ]


def table_kernel(
    place, kids, neighbors, parents, feat, up, down, slot_at, up_place, down_place,
    up_idx, up_far, down_idx, down_far, sem,
):
    count = neighbors.shape[1]
    base = place[0] * count
    for r in range(SEND + 1):
        up_idx[r] = 0
        down_idx[r] = 0
        up_far[r] = 2 * count
        down_far[r] = 2 * count

    def scan(g, found):
        n_up, n_down = found
        near_up, near_down = neighbors[0, g], neighbors[1, g]
        far_up, far_down = near_up - base - count, near_down - base + count
        goes_up = (near_up >= 0) & (far_up >= 0)
        goes_down = (near_down >= 0) & (far_down < count)
        up_idx[n_up] = g
        up_far[n_up] = jnp.where(goes_up, far_up, 2 * count)
        down_idx[n_down] = g
        down_far[n_down] = jnp.where(goes_down, far_down, 2 * count)
        return n_up + goes_up.astype(jnp.int32), n_down + goes_down.astype(jnp.int32)

    lax.fori_loop(0, count, scan, (jnp.int32(0), jnp.int32(0)), unroll=4)
    copies = []
    for r in range(SEND):
        copies.append(
            pltpu.make_async_copy(
                feat.at[up_idx[r], :, pl.ds(VOX - LANES, LANES)], up.at[r], sem.at[r]
            )
        )
        copies.append(
            pltpu.make_async_copy(
                feat.at[down_idx[r], :, pl.ds(0, LANES)], down.at[r], sem.at[SEND + r]
            )
        )
    for copy in copies:
        copy.start()

    def order(g, carry):
        q = jnp.int32(0)
        for k in range(1, kids.shape[0]):
            q += jnp.where(kids[k] == parents[0, g], k, 0)
        slot_at[q * 8 + parents[1, g]] = g
        return carry

    lax.fori_loop(0, count, order, jnp.int32(0), unroll=4)

    def rank(r, carry):
        for far, idx, put in ((up_far, up_idx, up_place), (down_far, down_idx, down_place)):
            earlier = jnp.int32(0)
            for other in range(SEND):
                earlier += (far[other] < far[r]).astype(jnp.int32)

            @pl.when(far[r] < count)
            def _():
                put[idx[r]] = count + earlier

        return carry

    lax.fori_loop(0, SEND, rank, jnp.int32(0))
    for copy in copies:
        copy.wait()


def order_kernel(feat, out, split):
    @pl.when(pl.program_id(0) == 0)
    def _():
        split[...] = picker(split_voxel)

    bricks, chans = feat.shape[:2]
    rows = feat[...].reshape(bricks * chans, VOX)
    out[...] = dot(rows, split[...]).astype(BF16).reshape(out.shape)


def route_kernel(kids, msg, pieces):
    devices, groups, lane_tiles = pieces.shape[:3]
    slots = groups
    for s in range(devices):
        for q in range(groups):
            kid = kids[s * groups + q]
            owner, slot = kid // slots, kid % slots
            for lt in range(lane_tiles):
                row = pl.multiple_of((slot * lane_tiles + lt) * ROWS, ROWS)
                pieces[s, q, lt] = msg[owner, pl.ds(row, ROWS), :]


def place_arrivals(above, below, bricks, count):
    chans = bricks.shape[1]
    half = VOX // 2
    shape = (LANES, half)
    first = dot(above[...].reshape(SEND * chans, LANES), picker(split_voxel, shape))
    last = dot(
        below[...].reshape(SEND * chans, LANES), picker(split_voxel, shape, (VOX - LANES, half))
    )
    bricks[count : count + SEND, :, :half] = first.astype(BF16).reshape(SEND, chans, half)
    bricks[count : count + SEND, :, half:] = last.astype(BF16).reshape(SEND, chans, half)
    bricks[count + SEND] = jnp.zeros(bricks.shape[1:], BF16)


def sources(scalars, number):
    place, counts, neighbors, slot_at, up_place, down_place = scalars
    count = neighbors.shape[1]
    zero_slot = count + SEND
    g = slot_at[number]
    found = []
    for d in range(6):
        near = neighbors[d, g]
        local = near - place[0] * count
        if d == 0:
            local = jnp.where(local >= count, up_place[g], local)
        if d == 1:
            local = jnp.where(local < 0, down_place[g], local)
        found.append(jnp.where(near >= 0, local, zero_slot))
    found.append(jnp.where(g < counts[0], g, zero_slot))
    return found


def shift_into(slots, bricks, views):
    chans = bricks.shape[1]
    tiles = VOX // LANES
    lane = lax.broadcasted_iota(jnp.int32, (chans, LANES), 1)
    low = lane < LANES // 2
    a = (lane // 16) % HALF
    b = (lane // 4) % HALF
    c = lane % HALF

    def tile(slot, t):
        return bricks[slot, :, t * LANES : (t + 1) * LANES]

    def turn(value, by):
        return pltpu.roll(value, by % LANES, 1)

    x = [tile(slots[6], t) for t in range(tiles)]
    for t in range(tiles):
        lanes = slice(t * LANES, (t + 1) * LANES)
        if t < 2:
            plus_a = x[t + 2]
            minus_a = jnp.where(a > 0, turn(x[t + 2], 16), turn(tile(slots[1], t + 2), -48))
        else:
            plus_a = jnp.where(a < HALF - 1, turn(x[t - 2], -16), turn(tile(slots[0], t - 2), 48))
            minus_a = x[t - 2]
        if t % 2 == 0:
            plus_b = x[t + 1]
            minus_b = jnp.where(b > 0, turn(x[t + 1], 4), turn(tile(slots[3], t + 1), -12))
        else:
            plus_b = jnp.where(b < HALF - 1, turn(x[t - 1], -4), turn(tile(slots[2], t - 1), 12))
            minus_b = x[t - 1]
        swapped = turn(x[t], 64)
        plus_c = jnp.where(c < HALF - 1, turn(x[t], 63), turn(tile(slots[4], t), 67))
        minus_c = jnp.where(c > 0, turn(x[t], -63), turn(tile(slots[5], t), -67))
        out = [plus_a, minus_a, plus_b, minus_b, jnp.where(low, swapped, plus_c),
               jnp.where(low, minus_c, swapped), x[t]]
        for d in range(7):
            views[d * chans : (d + 1) * chans, lanes] = out[d]


def low_lanes(rows):
    return lax.broadcasted_iota(jnp.int32, (rows, LANES), 1) < LANES // 2


def forward_kernel(
    lane_tiles, place_no, counts, neighbors, slot_at, up_place, down_place,
    feat, w_conv_hbm, w_res_hbm, w_mix_hbm, above, below,
    parts_out, slope_out, coarse_out, piece_out,
    bricks, views, place, w_conv, w_res, w_mix, conv_cat, res_cat, octants, sem,
):
    q = pl.program_id(0)
    groups = pl.num_programs(0) - 1
    count, chans = feat.shape[:2]
    scalars = (place_no, counts, neighbors, slot_at, up_place, down_place)

    @pl.when(q == 0)
    def _():
        copies = [
            pltpu.make_async_copy(source, target, sem.at[k])
            for k, (source, target) in enumerate((
                (w_conv_hbm, w_conv), (w_res_hbm, w_res), (w_mix_hbm, w_mix),
                (feat, bricks.at[pl.ds(0, count)]),
            ))
        ]
        for copy in copies:
            copy.start()
        place_arrivals(above, below, bricks, count)
        place[...] = picker(octant_voxel, flip=True)
        for copy in copies[:3]:
            copy.wait()
        for d in range(7):
            conv_cat[:, d * chans : (d + 1) * chans] = w_conv[d]
        res_cat[...] = w_res[...].T
        copies[3].wait()

    low_half = low_lanes(chans)

    def finish():
        coarse = dot(octants[...], place[...]).astype(BF16)
        coarse_out[0] = coarse
        mixed = dot(w_mix[...], coarse).astype(BF16)
        per_row = VOX // (LANES * lane_tiles)
        for j in range(piece_out.shape[0]):
            chan, part = j // per_row, j % per_row
            for lt in range(lane_tiles):
                lane = (part * lane_tiles + lt) * LANES
                piece_out[j, 0, lt] = mixed[chan * ROWS : (chan + 1) * ROWS, lane : lane + LANES]

    def restrict(first):
        acts = []
        for k in range(first, first + 4):
            shift_into(sources(scalars, q * 8 + k), bricks, views.at[k])
            hidden = dot(conv_cat[...], views[k])
            sig = 0.5 + 0.5 * jnp.tanh(0.5 * hidden)
            act = hidden * sig
            slope_out[0, k * chans : (k + 1) * chans, :] = (sig + act * (1.0 - sig)).astype(BF16)
            acts.append(act.astype(BF16))
        for k in range(0, 4, 2):
            lanes = slice((first + k) * (LANES // 2), (first + k + 2) * (LANES // 2))
            for t in range(4):
                one = acts[k][:, t * LANES : (t + 1) * LANES]
                two = acts[k + 1][:, t * LANES : (t + 1) * LANES]
                parts_out[0, 2 * t * chans : (2 * t + 1) * chans, lanes] = jnp.where(
                    low_half, one, pltpu.roll(two, LANES // 2, 1)
                )
                parts_out[0, (2 * t + 1) * chans : (2 * t + 2) * chans, lanes] = jnp.where(
                    low_half, pltpu.roll(one, LANES // 2, 1), two
                )
        lanes = slice(first * (LANES // 2), (first + 4) * (LANES // 2))
        return dot(res_cat[...], parts_out[0, :, lanes]).astype(BF16)

    @pl.when(q < groups)
    def _():
        finish()
        halves = [restrict(0), restrict(4)]
        octants[...] = jnp.concatenate(halves, axis=1)

    @pl.when(q == groups)
    def _():
        finish()


def backward_kernel(
    lane_tiles, scale, place_no, counts, neighbors, slot_at, up_place, down_place,
    feat, above, below, pieces, parts, slope, coarse, w_mix, w_res, packed,
    bricks, views, cot, grad_parts, grad_rows, unplace, mix_t, conv_sum, res_sum, mix_sum, sem,
):
    q = pl.program_id(0)
    count, chans = feat.shape[:2]
    wide = coarse.shape[1]
    scalars = (place_no, counts, neighbors, slot_at, up_place, down_place)
    fetch = pltpu.make_async_copy(feat, bricks.at[pl.ds(0, count)], sem)

    @pl.when(q == 0)
    def _():
        fetch.start()
        place_arrivals(above, below, bricks, count)
        unplace[...] = picker(octant_voxel)
        mix_t[...] = w_mix[...].T
        conv_sum[...] = jnp.zeros_like(conv_sum)
        res_sum[...] = jnp.zeros_like(res_sum)
        mix_sum[...] = jnp.zeros_like(mix_sum)
        fetch.wait()

    per_row = VOX // (LANES * lane_tiles)
    for j in range(pieces.shape[0]):
        chan, part = j // per_row, j % per_row
        for lt in range(lane_tiles):
            lane = (part * lane_tiles + lt) * LANES
            cot[chan * ROWS : (chan + 1) * ROWS, lane : lane + LANES] = pieces[j, 0, lt]
    cots = cot[...]
    grad_coarse = (scale * dot(mix_t[...], cots)).astype(BF16)
    grad_fine = dot(grad_coarse, unplace[...]).astype(BF16)
    mix_sum[...] += dot_nt(cots, coarse[0])
    res_sum[...] += dot_nt(parts[0], grad_fine)
    grad_parts[...] = dot(w_res[...], grad_fine)
    low_half = low_lanes(chans)
    for r in range(4):
        for t in range(4):
            cols = slice(r * LANES, (r + 1) * LANES)
            lanes = slice(t * LANES, (t + 1) * LANES)
            one = grad_parts[2 * t * chans : (2 * t + 1) * chans, cols]
            two = grad_parts[(2 * t + 1) * chans : (2 * t + 2) * chans, cols]
            first = slice(2 * r * chans, (2 * r + 1) * chans)
            second = slice((2 * r + 1) * chans, (2 * r + 2) * chans)
            grad_rows[first, lanes] = (
                jnp.where(low_half, one, pltpu.roll(two, LANES // 2, 1))
                * slope[0, first, lanes].astype(F32)
            ).astype(BF16)
            grad_rows[second, lanes] = (
                jnp.where(low_half, pltpu.roll(one, LANES // 2, 1), two)
                * slope[0, second, lanes].astype(F32)
            ).astype(BF16)

    total = None
    for k in range(8):
        shift_into(sources(scalars, q * 8 + k), bricks, views.at[k])
        term = dot_nt(grad_rows[k * chans : (k + 1) * chans, :], views[k])
        total = term if total is None else total + term
    conv_sum[:, : 7 * chans] += total

    @pl.when(q == pl.num_programs(0) - 1)
    def _():
        packed[0:wide] = (scale * mix_sum[...]).astype(BF16)
        at = wide
        packed[at : at + 8 * chans] = res_sum[...].astype(BF16)
        at += 8 * chans
        for t in range(4):
            packed[at : at + chans] = conv_sum[:, t * LANES : (t + 1) * LANES].astype(BF16)
            at += chans
        if at < packed.shape[0]:
            packed[at:] = jnp.zeros((packed.shape[0] - at, LANES), BF16)


def join_kernel(kids, shares, pieces, msg):
    devices, groups, lane_tiles = pieces.shape[:3]
    slots = groups
    body_rows = slots * lane_tiles * ROWS
    for s in range(devices):
        for q in range(groups):
            kid = kids[s * groups + q]
            owner, slot = kid // slots, kid % slots
            for lt in range(lane_tiles):
                row = pl.multiple_of((slot * lane_tiles + lt) * ROWS, ROWS)
                msg[owner, pl.ds(row, ROWS), :] = pieces[s, q, lt]
    total = jnp.sum(shares[...].astype(F32), axis=0).astype(BF16)
    for j in range(devices):
        msg[j, body_rows:] = total


def unpack_kernel(lane_tiles, msg, coarse_out, conv, res, mix, packed):
    devices, rows = msg.shape[:2]
    slots = coarse_out.shape[0]
    wide = mix.shape[0]
    chans = conv.shape[1]
    half = LANES // 2
    body_rows = slots * lane_tiles * ROWS
    share = rows - body_rows
    for j in range(devices):
        packed[j * share : (j + 1) * share] = msg[j, body_rows:].astype(F32)
    mix[...] = packed[0:wide]
    at = wide
    for t in range(8):
        res[t] = packed[at : at + chans]
        at += chans
    for t in range(4):
        block = packed[at : at + chans]
        conv[2 * t] = block[:, :half]
        if 2 * t + 1 < 7:
            conv[2 * t + 1] = block[:, half:]
        at += chans
    per_row = VOX // (LANES * lane_tiles)
    for j in range(devices):
        chan, part = j // per_row, j % per_row
        for q in range(slots):
            for lt in range(lane_tiles):
                row = (q * lane_tiles + lt) * ROWS
                lane = (part * lane_tiles + lt) * LANES
                coarse_out[q, chan * ROWS : (chan + 1) * ROWS, lane : lane + LANES] = msg[
                    j, row : row + ROWS
                ]


def kernel_call(kernel, out_shape, grid_spec, flops, moved, vmem=VMEM_BYTES):
    return pl.pallas_call(
        kernel,
        out_shape=out_shape,
        grid_spec=grid_spec,
        compiler_params=pltpu.CompilerParams(vmem_limit_bytes=vmem),
        cost_estimate=pl.CostEstimate(flops=flops, bytes_accessed=moved, transcendentals=0),
    )


def body(features, counts, neighbors, parents, w_conv, w_restrict, w_mix, cotangent):
    devices = lax.axis_size("space")
    position = lax.axis_index("space").astype(jnp.int32).reshape(1)
    slots, wide = cotangent.shape[:2]
    count, chans = features.shape[:2]
    lane_tiles = VOX * 8 // devices // LANES
    tiles = slots * lane_tiles
    groups = count // 8
    whole = lambda shape: pl.BlockSpec(shape, lambda *_: (0,) * len(shape))
    any_spec = pl.BlockSpec(memory_space=pl.ANY)
    smem_spec = pl.BlockSpec(memory_space=pltpu.SMEM)
    smem = lambda size: pltpu.SMEM((size,), jnp.int32)
    vmem = pltpu.VMEM
    ints = lambda size: jax.ShapeDtypeStruct((size,), jnp.int32)

    message_shape = (devices, tiles * ROWS + LABEL_ROWS, LANES)
    message, kids = kernel_call(
        functools.partial(pack_kernel, lane_tiles),
        (jax.ShapeDtypeStruct(message_shape, BF16), ints(groups)),
        pl.GridSpec(
            grid=(1,),
            in_specs=[smem_spec, whole(cotangent.shape)],
            out_specs=[whole(message_shape), smem_spec],
            scratch_shapes=[smem(groups + 1)],
        ),
        1000, 2**20,
    )(parents.T, cotangent)
    spread = lax.all_to_all(message, "space", split_axis=0, concat_axis=0, tiled=True)

    plane = jax.ShapeDtypeStruct((SEND, chans, LANES), BF16)
    up, down, slot_at, up_place, down_place = kernel_call(
        table_kernel,
        (plane, plane, ints(count), ints(count), ints(count)),
        pl.GridSpec(
            grid=(1,),
            in_specs=[smem_spec] * 4 + [any_spec],
            out_specs=[whole(plane.shape)] * 2 + [smem_spec] * 3,
            scratch_shapes=[smem(SEND + 1)] * 4 + [pltpu.SemaphoreType.DMA((2 * SEND,))],
        ),
        1000, 2**20,
    )(position, kids, neighbors.T, parents.T, features)
    below = lax.ppermute(up, "space", [(i, i + 1) for i in range(devices - 1)])
    above = lax.ppermute(down, "space", [(i + 1, i) for i in range(devices - 1)])

    ordered = kernel_call(
        order_kernel,
        jax.ShapeDtypeStruct(features.shape, BF16),
        pl.GridSpec(
            grid=(groups,),
            in_specs=[pl.BlockSpec((8, chans, VOX), lambda q: (q, 0, 0))],
            out_specs=pl.BlockSpec((8, chans, VOX), lambda q: (q, 0, 0)),
            scratch_shapes=[vmem((VOX, VOX), BF16)],
        ),
        1000, 2**20,
    )(features)

    all_kids = spread[:, tiles * ROWS, :groups].astype(jnp.int32).reshape(-1)
    piece_shape = (devices, groups, lane_tiles, ROWS, LANES)
    forward_tiles = kernel_call(
        route_kernel,
        jax.ShapeDtypeStruct(piece_shape, BF16),
        pl.GridSpec(
            grid=(1,),
            in_specs=[smem_spec, whole(message_shape)],
            out_specs=whole(piece_shape),
        ),
        1000, 2**20, SMALL_VMEM_BYTES,
    )(all_kids, spread)
    forward_tiles, above, below = lax.optimization_barrier((forward_tiles, above, below))
    cot_pieces = lax.all_to_all(forward_tiles, "space", split_axis=0, concat_axis=0, tiled=True)

    res_rows = w_restrict.transpose(0, 2, 1).reshape(8 * chans, wide)
    scalars = (position, counts, neighbors.T, slot_at, up_place, down_place)
    brick_scratch = vmem((count + SEND + 1, chans, VOX), BF16)
    view_scratch = vmem((8, 7 * chans, VOX), BF16)
    per_group = lambda *shape: pl.BlockSpec((1,) + shape, lambda q: (q,) + (0,) * len(shape))
    piece_spec = pl.BlockSpec((devices, 1, lane_tiles, ROWS, LANES), lambda q: (0, q, 0, 0, 0))
    parts, slope, coarse, pieces = kernel_call(
        functools.partial(forward_kernel, lane_tiles),
        (
            jax.ShapeDtypeStruct((groups, 8 * chans, VOX), BF16),
            jax.ShapeDtypeStruct((groups, 8 * chans, VOX), BF16),
            jax.ShapeDtypeStruct((groups, wide, VOX), BF16),
            jax.ShapeDtypeStruct(piece_shape, BF16),
        ),
        pl.GridSpec(
            grid=(groups + 1,),
            in_specs=[smem_spec] * 6 + [any_spec] * 4 + [whole(plane.shape)] * 2,
            out_specs=[
                pl.BlockSpec((1, 8 * chans, VOX), lambda q: (jnp.minimum(q, groups - 1), 0, 0)),
                pl.BlockSpec((1, 8 * chans, VOX), lambda q: (jnp.minimum(q, groups - 1), 0, 0)),
                pl.BlockSpec((1, wide, VOX), lambda q: (jnp.maximum(q - 1, 0), 0, 0)),
                pl.BlockSpec(
                    (devices, 1, lane_tiles, ROWS, LANES),
                    lambda q: (0, jnp.maximum(q - 1, 0), 0, 0, 0),
                ),
            ],
            scratch_shapes=[
                brick_scratch, view_scratch, vmem((VOX, VOX), BF16), vmem(w_conv.shape, BF16),
                vmem(res_rows.shape, BF16), vmem(w_mix.shape, BF16),
                vmem((chans, 7 * chans), BF16), vmem((wide, 8 * chans), BF16),
                vmem((wide, VOX), BF16), pltpu.SemaphoreType.DMA((4,)),
            ],
        ),
        16 * 10**9, 16 * 2**20,
    )(*scalars, ordered, w_conv, res_rows, w_mix, above, below)
    returned = lax.all_to_all(pieces, "space", split_axis=0, concat_axis=0, tiled=True)

    scale = 1.0 / math.sqrt(devices * slots * VOX)
    used = wide + 8 * chans + 4 * chans
    rows = -(-used // (devices * 8)) * 8
    packed = kernel_call(
        functools.partial(backward_kernel, lane_tiles, scale),
        jax.ShapeDtypeStruct((devices * rows, LANES), BF16),
        pl.GridSpec(
            grid=(groups,),
            in_specs=[smem_spec] * 6 + [any_spec] + [whole(plane.shape)] * 2
            + [piece_spec, per_group(8 * chans, VOX), per_group(8 * chans, VOX),
               per_group(wide, VOX), whole(w_mix.shape), whole(res_rows.shape)],
            out_specs=whole((devices * rows, LANES)),
            scratch_shapes=[
                brick_scratch, view_scratch, vmem((wide, VOX), BF16),
                vmem((8 * chans, VOX), F32), vmem((8 * chans, VOX), BF16), vmem((VOX, VOX), BF16),
                vmem((wide, wide), BF16), vmem((chans, 8 * chans), F32),
                vmem((8 * chans, wide), F32), vmem((wide, wide), F32), pltpu.SemaphoreType.DMA,
            ],
        ),
        16 * 10**9, 16 * 2**20,
    )(*scalars, ordered, above, below, cot_pieces, parts, slope, coarse, w_mix, res_rows)

    shares = lax.all_to_all(
        packed.reshape(devices, rows, LANES), "space", split_axis=0, concat_axis=0, tiled=True
    )
    joined_shape = (devices, tiles * ROWS + rows, LANES)
    joined = kernel_call(
        join_kernel,
        jax.ShapeDtypeStruct(joined_shape, BF16),
        pl.GridSpec(
            grid=(1,),
            in_specs=[smem_spec, whole(shares.shape), whole(piece_shape)],
            out_specs=whole(joined_shape),
        ),
        1000, 2**20, SMALL_VMEM_BYTES,
    )(all_kids, shares, returned)
    finished = lax.all_to_all(joined, "space", split_axis=0, concat_axis=0, tiled=True)

    coarse_out, grad_conv, grad_res, grad_mix = kernel_call(
        functools.partial(unpack_kernel, lane_tiles),
        (
            jax.ShapeDtypeStruct((slots, wide, VOX), BF16),
            jax.ShapeDtypeStruct((7, chans, chans), F32),
            jax.ShapeDtypeStruct((8, chans, wide), F32),
            jax.ShapeDtypeStruct((wide, wide), F32),
        ),
        pl.GridSpec(
            grid=(1,),
            in_specs=[whole(joined_shape)],
            out_specs=[whole((slots, wide, VOX)), whole((7, chans, chans)),
                       whole((8, chans, wide)), whole((wide, wide))],
            scratch_shapes=[vmem((devices * rows, LANES), F32)],
        ),
        1000, 2 * 2**20, SMALL_VMEM_BYTES,
    )(finished)
    return coarse_out, grad_conv, grad_res.transpose(0, 2, 1), grad_mix


def solution(mesh):
    return jax.shard_map(
        body,
        mesh=mesh,
        in_specs=(
            P(("groups", "space"), None, None),
            P(("groups", "space")),
            P(("groups", "space"), None),
            P(("groups", "space"), None),
            P(),
            P(),
            P(),
            P(("groups", "space"), None, None),
        ),
        out_specs=(
            P(("groups", "space"), None, None),
            P("groups", None, None),
            P("groups", None, None),
            P("groups", None),
        ),
        check_vma=False,
    )
```

```python
import functools
import math

import jax
import jax.numpy as jnp
from jax import lax
from jax.experimental import pallas as pl
from jax.experimental.pallas import tpu as pltpu
from jax.sharding import PartitionSpec as P

EDGE = 8
HALF = EDGE // 2
VOX = EDGE**3
LANES = 128
ROWS = 16
LABEL_ROWS = 8
SEND = 8
BF16 = jnp.bfloat16
F32 = jnp.float32
VMEM_BYTES = 60 * 1024 * 1024
SMALL_VMEM_BYTES = 16 * 1024 * 1024


def bits_of(value):
    return [(value >> (8 - k)) & 1 for k in range(9)]


def join_bits(bits):
    value = bits[0]
    for bit in bits[1:]:
        value = value * 2 + bit
    return value


def split_voxel(column):
    ta, tb, tc, a1, a0, b1, b0, c1, c0 = bits_of(column)
    return join_bits([a1, a0, ta, b1, b0, tb, c1, c0, tc])


def octant_voxel(column):
    oa, ob, oc, a1, a0, b1, b0, c1, c0 = bits_of(column)
    return join_bits([oa, a1, a0, ob, b1, b0, oc, c1, c0])


def picker(voxel_of, shape=(VOX, VOX), start=(0, 0), flip=False):
    row = lax.broadcasted_iota(jnp.int32, shape, 0) + start[0]
    column = lax.broadcasted_iota(jnp.int32, shape, 1) + start[1]
    return (column == voxel_of(row) if flip else row == voxel_of(column)).astype(BF16)


def dot(a, b):
    return jnp.dot(a, b, preferred_element_type=F32)


def dot_nt(a, b):
    return lax.dot_general(a, b, (((1,), (1,)), ((), ())), preferred_element_type=F32)


def table_kernel(
    place, neighbors, parents, feat, up, down, label_out, kids_out, slot_at, up_place, down_place,
    kids, up_idx, up_far, down_idx, down_far, sem,
):
    count = neighbors.shape[1]
    base = place[0] * count
    for r in range(SEND + 1):
        up_idx[r] = 0
        down_idx[r] = 0
        up_far[r] = 2 * count
        down_far[r] = 2 * count

    def scan(g, found):
        n_up, n_down = found
        near_up, near_down = neighbors[0, g], neighbors[1, g]
        far_up, far_down = near_up - base - count, near_down - base + count
        goes_up = (near_up >= 0) & (far_up >= 0)
        goes_down = (near_down >= 0) & (far_down < count)
        up_idx[n_up] = g
        up_far[n_up] = jnp.where(goes_up, far_up, 2 * count)
        down_idx[n_down] = g
        down_far[n_down] = jnp.where(goes_down, far_down, 2 * count)
        return n_up + goes_up.astype(jnp.int32), n_down + goes_down.astype(jnp.int32)

    lax.fori_loop(0, count, scan, (jnp.int32(0), jnp.int32(0)), unroll=4)
    copies = []
    for r in range(SEND):
        copies.append(
            pltpu.make_async_copy(
                feat.at[up_idx[r], :, pl.ds(VOX - LANES, LANES)], up.at[r], sem.at[r]
            )
        )
        copies.append(
            pltpu.make_async_copy(
                feat.at[down_idx[r], :, pl.ds(0, LANES)], down.at[r], sem.at[SEND + r]
            )
        )
    for copy in copies:
        copy.start()

    def find(g, found):
        kids[found] = parents[0, g]
        return found + (parents[1, g] == 0).astype(jnp.int32)

    lax.fori_loop(0, count, find, jnp.int32(0), unroll=4)
    lane = lax.broadcasted_iota(jnp.int32, label_out.shape, 2)
    label = jnp.zeros(label_out.shape, jnp.int32)
    for q in range(kids_out.shape[0]):
        kids_out[q] = kids[q]
        label = jnp.where(lane == q, kids[q], label)
    label_out[...] = label

    def order(g, carry):
        q = jnp.int32(0)
        for k in range(1, kids_out.shape[0]):
            q += jnp.where(kids[k] == parents[0, g], k, 0)
        slot_at[q * 8 + parents[1, g]] = g
        return carry

    lax.fori_loop(0, count, order, jnp.int32(0), unroll=4)

    def rank(r, carry):
        for far, idx, put in ((up_far, up_idx, up_place), (down_far, down_idx, down_place)):
            earlier = jnp.int32(0)
            for other in range(SEND):
                earlier += (far[other] < far[r]).astype(jnp.int32)

            @pl.when(far[r] < count)
            def _():
                put[idx[r]] = count + earlier

        return carry

    lax.fori_loop(0, SEND, rank, jnp.int32(0))
    for copy in copies:
        copy.wait()


def order_kernel(feat, out, split):
    @pl.when(pl.program_id(0) == 0)
    def _():
        split[...] = picker(split_voxel)

    bricks, chans = feat.shape[:2]
    rows = feat[...].reshape(bricks * chans, VOX)
    out[...] = dot(rows, split[...]).astype(BF16).reshape(out.shape)


def place_arrivals(above, below, bricks, count):
    chans = bricks.shape[1]
    half = VOX // 2
    shape = (LANES, half)
    first = dot(above[...].reshape(SEND * chans, LANES), picker(split_voxel, shape))
    last = dot(
        below[...].reshape(SEND * chans, LANES), picker(split_voxel, shape, (VOX - LANES, half))
    )
    bricks[count : count + SEND, :, :half] = first.astype(BF16).reshape(SEND, chans, half)
    bricks[count : count + SEND, :, half:] = last.astype(BF16).reshape(SEND, chans, half)
    bricks[count + SEND] = jnp.zeros(bricks.shape[1:], BF16)


def sources(scalars, number):
    place, counts, neighbors, slot_at, up_place, down_place = scalars
    count = neighbors.shape[1]
    zero_slot = count + SEND
    g = slot_at[number]
    found = []
    for d in range(6):
        near = neighbors[d, g]
        local = near - place[0] * count
        if d == 0:
            local = jnp.where(local >= count, up_place[g], local)
        if d == 1:
            local = jnp.where(local < 0, down_place[g], local)
        found.append(jnp.where(near >= 0, local, zero_slot))
    found.append(jnp.where(g < counts[0], g, zero_slot))
    return found


def shift_into(slots, bricks, views):
    chans = bricks.shape[1]
    tiles = VOX // LANES
    lane = lax.broadcasted_iota(jnp.int32, (chans, LANES), 1)
    low = lane < LANES // 2
    a = (lane // 16) % HALF
    b = (lane // 4) % HALF
    c = lane % HALF

    def tile(slot, t):
        return bricks[slot, :, t * LANES : (t + 1) * LANES]

    def turn(value, by):
        return pltpu.roll(value, by % LANES, 1)

    x = [tile(slots[6], t) for t in range(tiles)]
    for t in range(tiles):
        lanes = slice(t * LANES, (t + 1) * LANES)
        if t < 2:
            plus_a = x[t + 2]
            minus_a = jnp.where(a > 0, turn(x[t + 2], 16), turn(tile(slots[1], t + 2), -48))
        else:
            plus_a = jnp.where(a < HALF - 1, turn(x[t - 2], -16), turn(tile(slots[0], t - 2), 48))
            minus_a = x[t - 2]
        if t % 2 == 0:
            plus_b = x[t + 1]
            minus_b = jnp.where(b > 0, turn(x[t + 1], 4), turn(tile(slots[3], t + 1), -12))
        else:
            plus_b = jnp.where(b < HALF - 1, turn(x[t - 1], -4), turn(tile(slots[2], t - 1), 12))
            minus_b = x[t - 1]
        swapped = turn(x[t], 64)
        plus_c = jnp.where(c < HALF - 1, turn(x[t], 63), turn(tile(slots[4], t), 67))
        minus_c = jnp.where(c > 0, turn(x[t], -63), turn(tile(slots[5], t), -67))
        out = [plus_a, minus_a, plus_b, minus_b, jnp.where(low, swapped, plus_c),
               jnp.where(low, minus_c, swapped), x[t]]
        for d in range(7):
            views[d * chans : (d + 1) * chans, lanes] = out[d]


def low_lanes(rows):
    return lax.broadcasted_iota(jnp.int32, (rows, LANES), 1) < LANES // 2


def forward_kernel(
    lane_tiles, place_no, counts, neighbors, slot_at, up_place, down_place,
    feat, w_conv_hbm, w_res_hbm, w_mix_hbm, above, below,
    parts_out, slope_out, coarse_out, piece_out,
    bricks, views, place, w_conv, w_res, w_mix, conv_cat, res_cat, octants, sem,
):
    q = pl.program_id(0)
    groups = pl.num_programs(0) - 1
    count, chans = feat.shape[:2]
    scalars = (place_no, counts, neighbors, slot_at, up_place, down_place)

    @pl.when(q == 0)
    def _():
        copies = [
            pltpu.make_async_copy(source, target, sem.at[k])
            for k, (source, target) in enumerate((
                (w_conv_hbm, w_conv), (w_res_hbm, w_res), (w_mix_hbm, w_mix),
                (feat, bricks.at[pl.ds(0, count)]),
            ))
        ]
        for copy in copies:
            copy.start()
        place_arrivals(above, below, bricks, count)
        place[...] = picker(octant_voxel, flip=True)
        for copy in copies[:3]:
            copy.wait()
        for d in range(7):
            conv_cat[:, d * chans : (d + 1) * chans] = w_conv[d]
        res_cat[...] = w_res[...].T
        copies[3].wait()

    low_half = low_lanes(chans)

    def finish():
        coarse = dot(octants[...], place[...]).astype(BF16)
        coarse_out[0] = coarse
        mixed = dot(w_mix[...], coarse).astype(BF16)
        per_row = VOX // (LANES * lane_tiles)
        for j in range(piece_out.shape[0]):
            chan, part = j // per_row, j % per_row
            for lt in range(lane_tiles):
                lane = (part * lane_tiles + lt) * LANES
                piece_out[j, 0, lt] = mixed[chan * ROWS : (chan + 1) * ROWS, lane : lane + LANES]

    def restrict(first):
        acts = []
        for k in range(first, first + 4):
            shift_into(sources(scalars, q * 8 + k), bricks, views.at[k])
            hidden = dot(conv_cat[...], views[k])
            sig = 0.5 + 0.5 * jnp.tanh(0.5 * hidden)
            act = hidden * sig
            slope_out[0, k * chans : (k + 1) * chans, :] = (sig + act * (1.0 - sig)).astype(BF16)
            acts.append(act.astype(BF16))
        for k in range(0, 4, 2):
            lanes = slice((first + k) * (LANES // 2), (first + k + 2) * (LANES // 2))
            for t in range(4):
                one = acts[k][:, t * LANES : (t + 1) * LANES]
                two = acts[k + 1][:, t * LANES : (t + 1) * LANES]
                parts_out[0, 2 * t * chans : (2 * t + 1) * chans, lanes] = jnp.where(
                    low_half, one, pltpu.roll(two, LANES // 2, 1)
                )
                parts_out[0, (2 * t + 1) * chans : (2 * t + 2) * chans, lanes] = jnp.where(
                    low_half, pltpu.roll(one, LANES // 2, 1), two
                )
        lanes = slice(first * (LANES // 2), (first + 4) * (LANES // 2))
        return dot(res_cat[...], parts_out[0, :, lanes]).astype(BF16)

    @pl.when(q < groups)
    def _():
        finish()
        halves = [restrict(0), restrict(4)]
        octants[...] = jnp.concatenate(halves, axis=1)

    @pl.when(q == groups)
    def _():
        finish()


def backward_kernel(
    scale, kids, place_no, counts, neighbors, slot_at, up_place, down_place,
    feat, above, below, cot, parts, slope, coarse, w_mix, w_res, packed,
    bricks, views, grad_parts, grad_rows, unplace, mix_t, conv_sum, res_sum, mix_sum, sem,
):
    q = pl.program_id(0)
    count, chans = feat.shape[:2]
    wide = coarse.shape[1]
    scalars = (place_no, counts, neighbors, slot_at, up_place, down_place)
    fetch = pltpu.make_async_copy(feat, bricks.at[pl.ds(0, count)], sem)

    @pl.when(q == 0)
    def _():
        fetch.start()
        place_arrivals(above, below, bricks, count)
        unplace[...] = picker(octant_voxel)
        mix_t[...] = w_mix[...].T
        conv_sum[...] = jnp.zeros_like(conv_sum)
        res_sum[...] = jnp.zeros_like(res_sum)
        mix_sum[...] = jnp.zeros_like(mix_sum)
        fetch.wait()

    cots = cot[0]
    grad_coarse = (scale * dot(mix_t[...], cots)).astype(BF16)
    grad_fine = dot(grad_coarse, unplace[...]).astype(BF16)
    mix_sum[...] += dot_nt(cots, coarse[0])
    res_sum[...] += dot_nt(parts[0], grad_fine)
    grad_parts[...] = dot(w_res[...], grad_fine)
    low_half = low_lanes(chans)
    for r in range(4):
        for t in range(4):
            cols = slice(r * LANES, (r + 1) * LANES)
            lanes = slice(t * LANES, (t + 1) * LANES)
            one = grad_parts[2 * t * chans : (2 * t + 1) * chans, cols]
            two = grad_parts[(2 * t + 1) * chans : (2 * t + 2) * chans, cols]
            first = slice(2 * r * chans, (2 * r + 1) * chans)
            second = slice((2 * r + 1) * chans, (2 * r + 2) * chans)
            grad_rows[first, lanes] = (
                jnp.where(low_half, one, pltpu.roll(two, LANES // 2, 1))
                * slope[0, first, lanes].astype(F32)
            ).astype(BF16)
            grad_rows[second, lanes] = (
                jnp.where(low_half, pltpu.roll(one, LANES // 2, 1), two)
                * slope[0, second, lanes].astype(F32)
            ).astype(BF16)

    total = None
    for k in range(8):
        shift_into(sources(scalars, q * 8 + k), bricks, views.at[k])
        term = dot_nt(grad_rows[k * chans : (k + 1) * chans, :], views[k])
        total = term if total is None else total + term
    conv_sum[:, : 7 * chans] += total

    @pl.when(q == pl.num_programs(0) - 1)
    def _():
        packed[0:wide] = (scale * mix_sum[...]).astype(BF16)
        at = wide
        packed[at : at + 8 * chans] = res_sum[...].astype(BF16)
        at += 8 * chans
        for t in range(4):
            packed[at : at + chans] = conv_sum[:, t * LANES : (t + 1) * LANES].astype(BF16)
            at += chans
        if at < packed.shape[0]:
            packed[at:] = jnp.zeros((packed.shape[0] - at, LANES), BF16)


def sort_kernel(kids, pieces, msg):
    devices, groups, lane_tiles = pieces.shape[:3]
    slots = groups
    for s in range(devices):
        for q in range(groups):
            kid = kids[s * groups + q]
            owner, slot = kid // slots, kid % slots
            for lt in range(lane_tiles):
                row = pl.multiple_of((slot * lane_tiles + lt) * ROWS, ROWS)
                msg[owner, pl.ds(row, ROWS), :] = pieces[s, q, lt]


def sum_kernel(shares, sums):
    total = jnp.sum(shares[...].astype(F32), axis=0).astype(BF16)
    for j in range(sums.shape[0]):
        sums[j] = total


def unpack_kernel(lane_tiles, msg, sums, coarse_out, conv, res, mix, packed):
    devices = msg.shape[0]
    slots = coarse_out.shape[0]
    wide = mix.shape[0]
    chans = conv.shape[1]
    half = LANES // 2
    share = sums.shape[1]
    for j in range(devices):
        packed[j * share : (j + 1) * share] = sums[j].astype(F32)
    mix[...] = packed[0:wide]
    at = wide
    for t in range(8):
        res[t] = packed[at : at + chans]
        at += chans
    for t in range(4):
        block = packed[at : at + chans]
        conv[2 * t] = block[:, :half]
        if 2 * t + 1 < 7:
            conv[2 * t + 1] = block[:, half:]
        at += chans
    per_row = VOX // (LANES * lane_tiles)
    for j in range(devices):
        chan, part = j // per_row, j % per_row
        for q in range(slots):
            for lt in range(lane_tiles):
                row = (q * lane_tiles + lt) * ROWS
                lane = (part * lane_tiles + lt) * LANES
                coarse_out[q, chan * ROWS : (chan + 1) * ROWS, lane : lane + LANES] = msg[
                    j, row : row + ROWS
                ]


def kernel_call(kernel, out_shape, grid_spec, flops, moved, vmem=VMEM_BYTES):
    return pl.pallas_call(
        kernel,
        out_shape=out_shape,
        grid_spec=grid_spec,
        compiler_params=pltpu.CompilerParams(vmem_limit_bytes=vmem),
        cost_estimate=pl.CostEstimate(flops=flops, bytes_accessed=moved, transcendentals=0),
    )


def body(features, counts, neighbors, parents, w_conv, w_restrict, w_mix, cotangent):
    devices = lax.axis_size("space")
    position = lax.axis_index("space").astype(jnp.int32).reshape(1)
    slots, wide = cotangent.shape[:2]
    count, chans = features.shape[:2]
    lane_tiles = VOX * 8 // devices // LANES
    tiles = slots * lane_tiles
    groups = count // 8
    whole = lambda shape: pl.BlockSpec(shape, lambda *_: (0,) * len(shape))
    any_spec = pl.BlockSpec(memory_space=pl.ANY)
    smem_spec = pl.BlockSpec(memory_space=pltpu.SMEM)
    smem = lambda size: pltpu.SMEM((size,), jnp.int32)
    vmem = pltpu.VMEM
    ints = lambda size: jax.ShapeDtypeStruct((size,), jnp.int32)

    gathered = lax.all_gather(cotangent, "space", axis=0, tiled=True)
    piece_shape = (devices, groups, lane_tiles, ROWS, LANES)

    plane = jax.ShapeDtypeStruct((SEND, chans, LANES), BF16)
    label_shape = (devices, 8, LANES)
    up, down, labels, kids, slot_at, up_place, down_place = kernel_call(
        table_kernel,
        (plane, plane, jax.ShapeDtypeStruct(label_shape, jnp.int32), ints(groups),
         ints(count), ints(count), ints(count)),
        pl.GridSpec(
            grid=(1,),
            in_specs=[smem_spec] * 3 + [any_spec],
            out_specs=[whole(plane.shape)] * 2 + [whole(label_shape)] + [smem_spec] * 4,
            scratch_shapes=[smem(groups + 1)] + [smem(SEND + 1)] * 4
            + [pltpu.SemaphoreType.DMA((2 * SEND,))],
        ),
        1000, 2**20,
    )(position, neighbors.T, parents.T, features)
    below = lax.ppermute(up, "space", [(i, i + 1) for i in range(devices - 1)])
    above = lax.ppermute(down, "space", [(i + 1, i) for i in range(devices - 1)])

    ordered = kernel_call(
        order_kernel,
        jax.ShapeDtypeStruct(features.shape, BF16),
        pl.GridSpec(
            grid=(groups,),
            in_specs=[pl.BlockSpec((8, chans, VOX), lambda q: (q, 0, 0))],
            out_specs=pl.BlockSpec((8, chans, VOX), lambda q: (q, 0, 0)),
            scratch_shapes=[vmem((VOX, VOX), BF16)],
        ),
        1000, 2**20,
    )(features)

    labels = lax.all_to_all(labels, "space", split_axis=0, concat_axis=0, tiled=True)
    all_kids = labels[:, 0, :groups].reshape(-1)

    res_rows = w_restrict.transpose(0, 2, 1).reshape(8 * chans, wide)
    scalars = (position, counts, neighbors.T, slot_at, up_place, down_place)
    brick_scratch = vmem((count + SEND + 1, chans, VOX), BF16)
    view_scratch = vmem((8, 7 * chans, VOX), BF16)
    per_group = lambda *shape: pl.BlockSpec((1,) + shape, lambda q: (q,) + (0,) * len(shape))
    piece_spec = pl.BlockSpec((devices, 1, lane_tiles, ROWS, LANES), lambda q: (0, q, 0, 0, 0))
    parts, slope, coarse, pieces = kernel_call(
        functools.partial(forward_kernel, lane_tiles),
        (
            jax.ShapeDtypeStruct((groups, 8 * chans, VOX), BF16),
            jax.ShapeDtypeStruct((groups, 8 * chans, VOX), BF16),
            jax.ShapeDtypeStruct((groups, wide, VOX), BF16),
            jax.ShapeDtypeStruct(piece_shape, BF16),
        ),
        pl.GridSpec(
            grid=(groups + 1,),
            in_specs=[smem_spec] * 6 + [any_spec] * 4 + [whole(plane.shape)] * 2,
            out_specs=[
                pl.BlockSpec((1, 8 * chans, VOX), lambda q: (jnp.minimum(q, groups - 1), 0, 0)),
                pl.BlockSpec((1, 8 * chans, VOX), lambda q: (jnp.minimum(q, groups - 1), 0, 0)),
                pl.BlockSpec((1, wide, VOX), lambda q: (jnp.maximum(q - 1, 0), 0, 0)),
                pl.BlockSpec(
                    (devices, 1, lane_tiles, ROWS, LANES),
                    lambda q: (0, jnp.maximum(q - 1, 0), 0, 0, 0),
                ),
            ],
            scratch_shapes=[
                brick_scratch, view_scratch, vmem((VOX, VOX), BF16), vmem(w_conv.shape, BF16),
                vmem(res_rows.shape, BF16), vmem(w_mix.shape, BF16),
                vmem((chans, 7 * chans), BF16), vmem((wide, 8 * chans), BF16),
                vmem((wide, VOX), BF16), pltpu.SemaphoreType.DMA((4,)),
            ],
        ),
        16 * 10**9, 16 * 2**20,
    )(*scalars, ordered, w_conv, res_rows, w_mix, above, below)
    returned = lax.all_to_all(pieces, "space", split_axis=0, concat_axis=0, tiled=True)

    scale = 1.0 / math.sqrt(devices * slots * VOX)
    used = wide + 8 * chans + 4 * chans
    rows = -(-used // (devices * 8)) * 8
    per_group = lambda *shape: pl.BlockSpec((1,) + shape, lambda q, _: (q,) + (0,) * len(shape))
    packed = kernel_call(
        functools.partial(backward_kernel, scale),
        jax.ShapeDtypeStruct((devices * rows, LANES), BF16),
        pltpu.PrefetchScalarGridSpec(
            num_scalar_prefetch=1,
            grid=(groups,),
            in_specs=[smem_spec] * 6 + [any_spec] + [whole(plane.shape)] * 2
            + [pl.BlockSpec((1, wide, VOX), lambda q, kids: (kids[q], 0, 0)),
               per_group(8 * chans, VOX), per_group(8 * chans, VOX),
               per_group(wide, VOX), whole(w_mix.shape), whole(res_rows.shape)],
            out_specs=whole((devices * rows, LANES)),
            scratch_shapes=[
                brick_scratch, view_scratch,
                vmem((8 * chans, VOX), F32), vmem((8 * chans, VOX), BF16), vmem((VOX, VOX), BF16),
                vmem((wide, wide), BF16), vmem((chans, 8 * chans), F32),
                vmem((8 * chans, wide), F32), vmem((wide, wide), F32), pltpu.SemaphoreType.DMA,
            ],
        ),
        16 * 10**9, 16 * 2**20,
    )(kids, *scalars, ordered, above, below, gathered, parts, slope, coarse, w_mix, res_rows)

    shares = lax.all_to_all(
        packed.reshape(devices, rows, LANES), "space", split_axis=0, concat_axis=0, tiled=True
    )
    sum_shape = (devices, rows, LANES)
    sums = kernel_call(
        sum_kernel,
        jax.ShapeDtypeStruct(sum_shape, BF16),
        pl.GridSpec(grid=(1,), in_specs=[whole(sum_shape)], out_specs=whole(sum_shape)),
        1000, 2**20, SMALL_VMEM_BYTES,
    )(shares)
    sums = lax.all_to_all(sums, "space", split_axis=0, concat_axis=0, tiled=True)

    joined_shape = (devices, tiles * ROWS, LANES)
    joined = kernel_call(
        sort_kernel,
        jax.ShapeDtypeStruct(joined_shape, BF16),
        pl.GridSpec(
            grid=(1,),
            in_specs=[smem_spec, whole(piece_shape)],
            out_specs=whole(joined_shape),
        ),
        1000, 2**20, SMALL_VMEM_BYTES,
    )(all_kids, returned)
    finished = lax.all_to_all(joined, "space", split_axis=0, concat_axis=0, tiled=True)

    coarse_out, grad_conv, grad_res, grad_mix = kernel_call(
        functools.partial(unpack_kernel, lane_tiles),
        (
            jax.ShapeDtypeStruct((slots, wide, VOX), BF16),
            jax.ShapeDtypeStruct((7, chans, chans), F32),
            jax.ShapeDtypeStruct((8, chans, wide), F32),
            jax.ShapeDtypeStruct((wide, wide), F32),
        ),
        pl.GridSpec(
            grid=(1,),
            in_specs=[whole(joined_shape), whole(sum_shape)],
            out_specs=[whole((slots, wide, VOX)), whole((7, chans, chans)),
                       whole((8, chans, wide)), whole((wide, wide))],
            scratch_shapes=[vmem((devices * rows, LANES), F32)],
        ),
        1000, 2 * 2**20, SMALL_VMEM_BYTES,
    )(finished, sums)
    return coarse_out, grad_conv, grad_res.transpose(0, 2, 1), grad_mix


def solution(mesh):
    return jax.shard_map(
        body,
        mesh=mesh,
        in_specs=(
            P(("groups", "space"), None, None),
            P(("groups", "space")),
            P(("groups", "space"), None),
            P(("groups", "space"), None),
            P(),
            P(),
            P(),
            P(("groups", "space"), None, None),
        ),
        out_specs=(
            P(("groups", "space"), None, None),
            P("groups", None, None),
            P("groups", None, None),
            P("groups", None),
        ),
        check_vma=False,
    )
```

```python
import functools
import math

import jax
import jax.numpy as jnp
from jax import lax
from jax.experimental import pallas as pl
from jax.experimental.pallas import tpu as pltpu
from jax.sharding import PartitionSpec as P

EDGE = 8
HALF = EDGE // 2
VOX = EDGE**3
LANES = 128
ROWS = 16
LABEL_ROWS = 8
SEND = 8
BF16 = jnp.bfloat16
F32 = jnp.float32
VMEM_BYTES = 60 * 1024 * 1024
SMALL_VMEM_BYTES = 16 * 1024 * 1024


def bits_of(value):
    return [(value >> (8 - k)) & 1 for k in range(9)]


def join_bits(bits):
    value = bits[0]
    for bit in bits[1:]:
        value = value * 2 + bit
    return value


def split_voxel(column):
    ta, tb, tc, a1, a0, b1, b0, c1, c0 = bits_of(column)
    return join_bits([a1, a0, ta, b1, b0, tb, c1, c0, tc])


def octant_voxel(column):
    oa, ob, oc, a1, a0, b1, b0, c1, c0 = bits_of(column)
    return join_bits([oa, a1, a0, ob, b1, b0, oc, c1, c0])


def picker(voxel_of, shape=(VOX, VOX), start=(0, 0), flip=False):
    row = lax.broadcasted_iota(jnp.int32, shape, 0) + start[0]
    column = lax.broadcasted_iota(jnp.int32, shape, 1) + start[1]
    return (column == voxel_of(row) if flip else row == voxel_of(column)).astype(BF16)


def dot(a, b):
    return jnp.dot(a, b, preferred_element_type=F32)


def dot_nt(a, b):
    return lax.dot_general(a, b, (((1,), (1,)), ((), ())), preferred_element_type=F32)


def pack_kernel(lane_tiles, parents, cot, msg, kids_out, kids):
    devices = msg.shape[0]
    slots = cot.shape[0]

    def find(g, found):
        kids[found] = parents[0, g]
        return found + (parents[1, g] == 0).astype(jnp.int32)

    lax.fori_loop(0, parents.shape[1], find, jnp.int32(0), unroll=4)
    lane = lax.broadcasted_iota(jnp.int32, (LABEL_ROWS, LANES), 1)
    label = jnp.zeros((LABEL_ROWS, LANES), jnp.int32)
    for q in range(kids_out.shape[0]):
        kids_out[q] = kids[q]
        label = jnp.where(lane == q, kids[q], label)
    label = label.astype(F32).astype(BF16)
    for j in range(devices):
        msg[j, slots * lane_tiles * ROWS :] = label
    per_row = VOX // (LANES * lane_tiles)
    for j in range(devices):
        chan, part = j // per_row, j % per_row
        for q in range(slots):
            for lt in range(lane_tiles):
                lane = (part * lane_tiles + lt) * LANES
                row = (q * lane_tiles + lt) * ROWS
                msg[j, row : row + ROWS] = cot[
                    q, chan * ROWS : (chan + 1) * ROWS, lane : lane + LANES
                ]


def table_kernel(
    place, counts, kids, neighbors, parents, feat, up, down, table,
    up_idx, up_far, down_idx, down_far, up_tile, down_tile, sem,
):
    count = neighbors.shape[1]
    base = place[0] * count
    table[4 * count] = place[0]
    for r in range(SEND + 1):
        up_idx[r] = 0
        down_idx[r] = 0
        up_far[r] = 2 * count
        down_far[r] = 2 * count

    def scan(g, found):
        n_up, n_down = found
        near_up, near_down = neighbors[0, g], neighbors[1, g]
        far_up, far_down = near_up - base - count, near_down - base + count
        goes_up = (near_up >= 0) & (far_up >= 0)
        goes_down = (near_down >= 0) & (far_down < count)
        up_idx[n_up] = g
        up_far[n_up] = jnp.where(goes_up, far_up, 2 * count)
        down_idx[n_down] = g
        down_far[n_down] = jnp.where(goes_down, far_down, 2 * count)
        return n_up + goes_up.astype(jnp.int32), n_down + goes_down.astype(jnp.int32)

    lax.fori_loop(0, count, scan, (jnp.int32(0), jnp.int32(0)), unroll=4)
    copies = []
    for r in range(SEND):
        copies.append(
            pltpu.make_async_copy(
                feat.at[up_idx[r], :, pl.ds(VOX - LANES, LANES)], up_tile.at[r], sem.at[r]
            )
        )
        copies.append(
            pltpu.make_async_copy(
                feat.at[down_idx[r], :, pl.ds(0, LANES)], down_tile.at[r], sem.at[SEND + r]
            )
        )
    for copy in copies:
        copy.start()

    def order(g, carry):
        q = jnp.int32(0)
        for k in range(1, kids.shape[0]):
            q += jnp.where(kids[k] == parents[0, g], k, 0)
        number = q * 8 + parents[1, g]
        table[number] = g
        table[count + number] = jnp.where(g < counts[0], g, count + SEND)
        return carry

    lax.fori_loop(0, count, order, jnp.int32(0), unroll=4)

    def rank(r, carry):
        for start, far, idx in ((2 * count, up_far, up_idx), (3 * count, down_far, down_idx)):
            earlier = jnp.int32(0)
            for other in range(SEND):
                earlier += (far[other] < far[r]).astype(jnp.int32)

            @pl.when(far[r] < count)
            def _():
                table[start + idx[r]] = count + earlier

        return carry

    lax.fori_loop(0, SEND, rank, jnp.int32(0))
    for copy in copies:
        copy.wait()
    low = low_lanes(feat.shape[1])
    for r in range(SEND // 2):
        other = r + SEND // 2
        up[r] = jnp.where(low, pltpu.roll(up_tile[r], LANES // 2, 1), up_tile[other])
        down[r] = jnp.where(low, down_tile[r], pltpu.roll(down_tile[other], LANES // 2, 1))


def order_kernel(feat, out, split):
    @pl.when(pl.program_id(0) == 0)
    def _():
        split[...] = picker(split_voxel)

    bricks, chans = feat.shape[:2]
    for k in range(0, bricks, 2):
        rows = feat[k : k + 2].reshape(2 * chans, VOX)
        for lane in range(0, VOX, VOX // 2):
            cols = slice(lane, lane + VOX // 2)
            done = dot(rows, split[:, cols]).astype(BF16)
            out[k : k + 2, :, cols] = done.reshape(2, chans, VOX // 2)


def route_kernel(kids, msg, pieces, sem):
    devices, groups, rows = pieces.shape[:3]
    slots = groups
    copies = []
    for s in range(devices):
        for q in range(groups):
            kid = kids[s * groups + q]
            row = pl.multiple_of((kid % slots) * rows, rows)
            copies.append(
                pltpu.make_async_copy(
                    msg.at[kid // slots, pl.ds(row, rows), :], pieces.at[s, q],
                    sem.at[s * groups + q],
                )
            )
            copies[-1].start()
    for copy in copies:
        copy.wait()


def place_arrivals(above, below, bricks, count):
    chans = bricks.shape[1]
    half = VOX // 2
    side = LANES // 2
    shape = (LANES, half)
    pairs = SEND // 2
    for k, shift in ((0, 0), (pairs, -side)):
        slots = slice(count + k, count + k + pairs)
        first = dot(
            above[...].reshape(pairs * chans, LANES), picker(split_voxel, shape, (shift, 0))
        )
        last = dot(
            below[...].reshape(pairs * chans, LANES),
            picker(split_voxel, shape, (VOX - side + shift, half)),
        )
        bricks[slots, :, :half] = first.astype(BF16).reshape(pairs, chans, half)
        bricks[slots, :, half:] = last.astype(BF16).reshape(pairs, chans, half)
    bricks[count + SEND] = jnp.zeros(bricks.shape[1:], BF16)


def sources(table, neighbors, number):
    count = neighbors.shape[1]
    g = table[number]
    found = []
    for d in range(6):
        near = neighbors[d, g]
        local = near - table[4 * count] * count
        if d == 0:
            local = jnp.where(local >= count, table[2 * count + g], local)
        if d == 1:
            local = jnp.where(local < 0, table[3 * count + g], local)
        found.append(jnp.where(near >= 0, local, count + SEND))
    found.append(table[count + number])
    return found


def shift_into(slots, bricks, views):
    chans = bricks.shape[1]
    tiles = VOX // LANES
    lane = lax.broadcasted_iota(jnp.int32, (chans, LANES), 1)
    low = lane < LANES // 2
    a = (lane // 16) % HALF
    b = (lane // 4) % HALF
    c = lane % HALF

    def tile(slot, t):
        return bricks[slot, :, t * LANES : (t + 1) * LANES]

    def turn(value, by):
        return pltpu.roll(value, by % LANES, 1)

    x = [tile(slots[6], t) for t in range(tiles)]
    for t in range(tiles):
        lanes = slice(t * LANES, (t + 1) * LANES)
        if t < 2:
            plus_a = x[t + 2]
            minus_a = jnp.where(a > 0, turn(x[t + 2], 16), turn(tile(slots[1], t + 2), -48))
        else:
            plus_a = jnp.where(a < HALF - 1, turn(x[t - 2], -16), turn(tile(slots[0], t - 2), 48))
            minus_a = x[t - 2]
        if t % 2 == 0:
            plus_b = x[t + 1]
            minus_b = jnp.where(b > 0, turn(x[t + 1], 4), turn(tile(slots[3], t + 1), -12))
        else:
            plus_b = jnp.where(b < HALF - 1, turn(x[t - 1], -4), turn(tile(slots[2], t - 1), 12))
            minus_b = x[t - 1]
        swapped = turn(x[t], 64)
        plus_c = jnp.where(c < HALF - 1, turn(x[t], 63), turn(tile(slots[4], t), 67))
        minus_c = jnp.where(c > 0, turn(x[t], -63), turn(tile(slots[5], t), -67))
        out = [plus_a, minus_a, plus_b, minus_b, jnp.where(low, swapped, plus_c),
               jnp.where(low, minus_c, swapped), x[t]]
        for d in range(7):
            views[d * chans : (d + 1) * chans, lanes] = out[d]


def low_lanes(rows):
    return lax.broadcasted_iota(jnp.int32, (rows, LANES), 1) < LANES // 2


def forward_kernel(
    lane_tiles, table, neighbors, feat, w_conv_hbm, w_res_hbm, w_mix_hbm, above, below,
    parts_out, slope_out, coarse_out, piece_out,
    bricks, views, place, w_conv, w_res, w_mix, conv_cat, res_cat, octants, sem,
):
    q = pl.program_id(0)
    groups = pl.num_programs(0) - 1
    count, chans = feat.shape[:2]

    @pl.when(q == 0)
    def _():
        copies = [
            pltpu.make_async_copy(source, target, sem.at[k])
            for k, (source, target) in enumerate((
                (w_conv_hbm, w_conv), (w_res_hbm, w_res), (w_mix_hbm, w_mix),
                (feat, bricks.at[pl.ds(0, count)]),
            ))
        ]
        for copy in copies:
            copy.start()
        place_arrivals(above, below, bricks, count)
        place[...] = picker(octant_voxel, flip=True)
        for copy in copies[:3]:
            copy.wait()
        for d in range(7):
            conv_cat[:, d * chans : (d + 1) * chans] = w_conv[d]
        res_cat[...] = w_res[...].T
        copies[3].wait()

    low_half = low_lanes(chans)

    def finish():
        coarse = dot(octants[...], place[...]).astype(BF16)
        coarse_out[0] = coarse
        mixed = dot(w_mix[...], coarse).astype(BF16)
        per_row = VOX // (LANES * lane_tiles)
        for j in range(piece_out.shape[0]):
            chan, part = j // per_row, j % per_row
            for lt in range(lane_tiles):
                lane = (part * lane_tiles + lt) * LANES
                piece_out[j, 0, lt] = mixed[chan * ROWS : (chan + 1) * ROWS, lane : lane + LANES]

    def restrict(first):
        acts = []
        for k in range(first, first + 4):
            shift_into(sources(table, neighbors, q * 8 + k), bricks, views.at[k])
            hidden = dot(conv_cat[...], views[k])
            sig = 0.5 + 0.5 * jnp.tanh(0.5 * hidden)
            act = hidden * sig
            slope_out[0, k * chans : (k + 1) * chans, :] = (sig + act * (1.0 - sig)).astype(BF16)
            acts.append(act.astype(BF16))
        for k in range(0, 4, 2):
            lanes = slice((first + k) * (LANES // 2), (first + k + 2) * (LANES // 2))
            for t in range(4):
                one = acts[k][:, t * LANES : (t + 1) * LANES]
                two = acts[k + 1][:, t * LANES : (t + 1) * LANES]
                parts_out[0, 2 * t * chans : (2 * t + 1) * chans, lanes] = jnp.where(
                    low_half, one, pltpu.roll(two, LANES // 2, 1)
                )
                parts_out[0, (2 * t + 1) * chans : (2 * t + 2) * chans, lanes] = jnp.where(
                    low_half, pltpu.roll(one, LANES // 2, 1), two
                )
        lanes = slice(first * (LANES // 2), (first + 4) * (LANES // 2))
        return dot(res_cat[...], parts_out[0, :, lanes]).astype(BF16)

    @pl.when(q < groups)
    def _():
        finish()
        halves = [restrict(0), restrict(4)]
        octants[...] = jnp.concatenate(halves, axis=1)

    @pl.when(q == groups)
    def _():
        finish()


def backward_kernel(
    lane_tiles, scale, table, neighbors, feat, above, below, pieces, parts, slope, coarse, w_mix, w_res, packed,
    bricks, views, cot, grad_parts, grad_rows, unplace, mix_t, conv_sum, res_sum, mix_sum, sem,
):
    q = pl.program_id(0)
    count, chans = feat.shape[:2]
    wide = coarse.shape[1]
    fetch = pltpu.make_async_copy(feat, bricks.at[pl.ds(0, count)], sem)

    @pl.when(q == 0)
    def _():
        fetch.start()
        place_arrivals(above, below, bricks, count)
        unplace[...] = picker(octant_voxel)
        mix_t[...] = w_mix[...].T
        conv_sum[...] = jnp.zeros_like(conv_sum)
        res_sum[...] = jnp.zeros_like(res_sum)
        mix_sum[...] = jnp.zeros_like(mix_sum)
        fetch.wait()

    per_row = VOX // (LANES * lane_tiles)
    for j in range(pieces.shape[0]):
        chan, part = j // per_row, j % per_row
        for lt in range(lane_tiles):
            lane = (part * lane_tiles + lt) * LANES
            cot[chan * ROWS : (chan + 1) * ROWS, lane : lane + LANES] = pieces[j, 0, lt]
    cots = cot[...]
    grad_coarse = (scale * dot(mix_t[...], cots)).astype(BF16)
    grad_fine = dot(grad_coarse, unplace[...]).astype(BF16)
    mix_sum[...] += dot_nt(cots, coarse[0])
    res_sum[...] += dot_nt(parts[0], grad_fine)
    grad_parts[...] = dot(w_res[...], grad_fine)
    low_half = low_lanes(chans)
    for r in range(4):
        for t in range(4):
            cols = slice(r * LANES, (r + 1) * LANES)
            lanes = slice(t * LANES, (t + 1) * LANES)
            one = grad_parts[2 * t * chans : (2 * t + 1) * chans, cols]
            two = grad_parts[(2 * t + 1) * chans : (2 * t + 2) * chans, cols]
            first = slice(2 * r * chans, (2 * r + 1) * chans)
            second = slice((2 * r + 1) * chans, (2 * r + 2) * chans)
            grad_rows[first, lanes] = (
                jnp.where(low_half, one, pltpu.roll(two, LANES // 2, 1))
                * slope[0, first, lanes].astype(F32)
            ).astype(BF16)
            grad_rows[second, lanes] = (
                jnp.where(low_half, pltpu.roll(one, LANES // 2, 1), two)
                * slope[0, second, lanes].astype(F32)
            ).astype(BF16)

    total = None
    for k in range(8):
        shift_into(sources(table, neighbors, q * 8 + k), bricks, views.at[k])
        term = dot_nt(grad_rows[k * chans : (k + 1) * chans, :], views[k])
        total = term if total is None else total + term
    conv_sum[:, : 7 * chans] += total

    @pl.when(q == pl.num_programs(0) - 1)
    def _():
        packed[0:wide] = (scale * mix_sum[...]).astype(BF16)
        at = wide
        packed[at : at + 8 * chans] = res_sum[...].astype(BF16)
        at += 8 * chans
        for t in range(4):
            packed[at : at + chans] = conv_sum[:, t * LANES : (t + 1) * LANES].astype(BF16)
            at += chans
        if at < packed.shape[0]:
            packed[at:] = jnp.zeros((packed.shape[0] - at, LANES), BF16)


def join_kernel(kids, shares, pieces, msg):
    devices, groups, lane_tiles = pieces.shape[:3]
    slots = groups
    body_rows = slots * lane_tiles * ROWS
    for s in range(devices):
        for q in range(groups):
            kid = kids[s * groups + q]
            owner, slot = kid // slots, kid % slots
            for lt in range(lane_tiles):
                row = pl.multiple_of((slot * lane_tiles + lt) * ROWS, ROWS)
                msg[owner, pl.ds(row, ROWS), :] = pieces[s, q, lt]
    total = jnp.sum(shares[...].astype(F32), axis=0).astype(BF16)
    for j in range(devices):
        msg[j, body_rows:] = total


def unpack_kernel(lane_tiles, msg, coarse_out, conv, res, mix, packed):
    devices, rows = msg.shape[:2]
    slots = coarse_out.shape[0]
    wide = mix.shape[0]
    chans = conv.shape[1]
    half = LANES // 2
    body_rows = slots * lane_tiles * ROWS
    share = rows - body_rows
    for j in range(devices):
        packed[j * share : (j + 1) * share] = msg[j, body_rows:].astype(F32)
    mix[...] = packed[0:wide]
    at = wide
    for t in range(8):
        res[t] = packed[at : at + chans]
        at += chans
    for t in range(4):
        block = packed[at : at + chans]
        conv[2 * t] = block[:, :half]
        if 2 * t + 1 < 7:
            conv[2 * t + 1] = block[:, half:]
        at += chans
    per_row = VOX // (LANES * lane_tiles)
    for j in range(devices):
        chan, part = j // per_row, j % per_row
        for q in range(slots):
            for lt in range(lane_tiles):
                row = (q * lane_tiles + lt) * ROWS
                lane = (part * lane_tiles + lt) * LANES
                coarse_out[q, chan * ROWS : (chan + 1) * ROWS, lane : lane + LANES] = msg[
                    j, row : row + ROWS
                ]


def kernel_call(kernel, out_shape, grid_spec, flops, moved, vmem=VMEM_BYTES):
    return pl.pallas_call(
        kernel,
        out_shape=out_shape,
        grid_spec=grid_spec,
        compiler_params=pltpu.CompilerParams(vmem_limit_bytes=vmem),
        cost_estimate=pl.CostEstimate(flops=flops, bytes_accessed=moved, transcendentals=0),
    )


def body(features, counts, neighbors, parents, w_conv, w_restrict, w_mix, cotangent):
    devices = lax.axis_size("space")
    position = lax.axis_index("space").astype(jnp.int32).reshape(1)
    slots, wide = cotangent.shape[:2]
    count, chans = features.shape[:2]
    lane_tiles = VOX * 8 // devices // LANES
    tiles = slots * lane_tiles
    groups = count // 8
    whole = lambda shape: pl.BlockSpec(shape, lambda *_: (0,) * len(shape))
    any_spec = pl.BlockSpec(memory_space=pl.ANY)
    smem_spec = pl.BlockSpec(memory_space=pltpu.SMEM)
    smem = lambda size: pltpu.SMEM((size,), jnp.int32)
    vmem = pltpu.VMEM
    ints = lambda size: jax.ShapeDtypeStruct((size,), jnp.int32)

    message_shape = (devices, tiles * ROWS + LABEL_ROWS, LANES)
    message, kids = kernel_call(
        functools.partial(pack_kernel, lane_tiles),
        (jax.ShapeDtypeStruct(message_shape, BF16), ints(groups)),
        pl.GridSpec(
            grid=(1,),
            in_specs=[smem_spec, whole(cotangent.shape)],
            out_specs=[whole(message_shape), smem_spec],
            scratch_shapes=[smem(groups + 1)],
        ),
        1000, 2**20, SMALL_VMEM_BYTES,
    )(parents.T, cotangent)
    spread = lax.all_to_all(message, "space", split_axis=0, concat_axis=0, tiled=True)

    plane = jax.ShapeDtypeStruct((SEND // 2, chans, LANES), BF16)
    tile_scratch = vmem((SEND, chans, LANES), BF16)
    up, down, table = kernel_call(
        table_kernel,
        (plane, plane, ints(4 * count + 1)),
        pl.GridSpec(
            grid=(1,),
            in_specs=[smem_spec] * 5 + [any_spec],
            out_specs=[whole(plane.shape)] * 2 + [smem_spec],
            scratch_shapes=[smem(SEND + 1)] * 4
            + [tile_scratch, tile_scratch, pltpu.SemaphoreType.DMA((2 * SEND,))],
        ),
        1000, 2**20,
    )(position, counts, kids, neighbors.T, parents.T, features)
    below = lax.ppermute(up, "space", [(i, i + 1) for i in range(devices - 1)])
    above = lax.ppermute(down, "space", [(i + 1, i) for i in range(devices - 1)])

    ordered = kernel_call(
        order_kernel,
        jax.ShapeDtypeStruct(features.shape, BF16),
        pl.GridSpec(
            grid=(groups,),
            in_specs=[pl.BlockSpec((8, chans, VOX), lambda q: (q, 0, 0))],
            out_specs=pl.BlockSpec((8, chans, VOX), lambda q: (q, 0, 0)),
            scratch_shapes=[vmem((VOX, VOX), BF16)],
        ),
        1000, 2**20,
    )(features)

    all_kids = spread[:, tiles * ROWS, :groups].astype(jnp.int32).reshape(-1)
    piece_shape = (devices, groups, lane_tiles, ROWS, LANES)
    forward_tiles = kernel_call(
        route_kernel,
        jax.ShapeDtypeStruct((devices, groups, lane_tiles * ROWS, LANES), BF16),
        pl.GridSpec(
            grid=(1,),
            in_specs=[smem_spec, any_spec],
            out_specs=any_spec,
            scratch_shapes=[pltpu.SemaphoreType.DMA((devices * groups,))],
        ),
        1000, 2**20, SMALL_VMEM_BYTES,
    )(all_kids, spread).reshape(piece_shape)
    forward_tiles, above, below = lax.optimization_barrier((forward_tiles, above, below))
    cot_pieces = lax.all_to_all(forward_tiles, "space", split_axis=0, concat_axis=0, tiled=True)

    res_rows = w_restrict.transpose(0, 2, 1).reshape(8 * chans, wide)
    scalars = (table, neighbors.T)
    brick_scratch = vmem((count + SEND + 1, chans, VOX), BF16)
    view_scratch = vmem((8, 7 * chans, VOX), BF16)
    per_group = lambda *shape: pl.BlockSpec((1,) + shape, lambda q: (q,) + (0,) * len(shape))
    piece_spec = pl.BlockSpec((devices, 1, lane_tiles, ROWS, LANES), lambda q: (0, q, 0, 0, 0))
    parts, slope, coarse, pieces = kernel_call(
        functools.partial(forward_kernel, lane_tiles),
        (
            jax.ShapeDtypeStruct((groups, 8 * chans, VOX), BF16),
            jax.ShapeDtypeStruct((groups, 8 * chans, VOX), BF16),
            jax.ShapeDtypeStruct((groups, wide, VOX), BF16),
            jax.ShapeDtypeStruct(piece_shape, BF16),
        ),
        pl.GridSpec(
            grid=(groups + 1,),
            in_specs=[smem_spec] * 2 + [any_spec] * 4 + [whole(plane.shape)] * 2,
            out_specs=[
                pl.BlockSpec((1, 8 * chans, VOX), lambda q: (jnp.minimum(q, groups - 1), 0, 0)),
                pl.BlockSpec((1, 8 * chans, VOX), lambda q: (jnp.minimum(q, groups - 1), 0, 0)),
                pl.BlockSpec((1, wide, VOX), lambda q: (jnp.maximum(q - 1, 0), 0, 0)),
                pl.BlockSpec(
                    (devices, 1, lane_tiles, ROWS, LANES),
                    lambda q: (0, jnp.maximum(q - 1, 0), 0, 0, 0),
                ),
            ],
            scratch_shapes=[
                brick_scratch, view_scratch, vmem((VOX, VOX), BF16), vmem(w_conv.shape, BF16),
                vmem(res_rows.shape, BF16), vmem(w_mix.shape, BF16),
                vmem((chans, 7 * chans), BF16), vmem((wide, 8 * chans), BF16),
                vmem((wide, VOX), BF16), pltpu.SemaphoreType.DMA((4,)),
            ],
        ),
        16 * 10**9, 16 * 2**20,
    )(*scalars, ordered, w_conv, res_rows, w_mix, above, below)
    returned = lax.all_to_all(pieces, "space", split_axis=0, concat_axis=0, tiled=True)

    scale = 1.0 / math.sqrt(devices * slots * VOX)
    used = wide + 8 * chans + 4 * chans
    rows = -(-used // (devices * 8)) * 8
    packed = kernel_call(
        functools.partial(backward_kernel, lane_tiles, scale),
        jax.ShapeDtypeStruct((devices * rows, LANES), BF16),
        pl.GridSpec(
            grid=(groups,),
            in_specs=[smem_spec] * 2 + [any_spec] + [whole(plane.shape)] * 2
            + [piece_spec, per_group(8 * chans, VOX), per_group(8 * chans, VOX),
               per_group(wide, VOX), whole(w_mix.shape), whole(res_rows.shape)],
            out_specs=whole((devices * rows, LANES)),
            scratch_shapes=[
                brick_scratch, view_scratch, vmem((wide, VOX), BF16),
                vmem((8 * chans, VOX), F32), vmem((8 * chans, VOX), BF16), vmem((VOX, VOX), BF16),
                vmem((wide, wide), BF16), vmem((chans, 8 * chans), F32),
                vmem((8 * chans, wide), F32), vmem((wide, wide), F32), pltpu.SemaphoreType.DMA,
            ],
        ),
        16 * 10**9, 16 * 2**20,
    )(*scalars, ordered, above, below, cot_pieces, parts, slope, coarse, w_mix, res_rows)

    shares = lax.all_to_all(
        packed.reshape(devices, rows, LANES), "space", split_axis=0, concat_axis=0, tiled=True
    )
    joined_shape = (devices, tiles * ROWS + rows, LANES)
    joined = kernel_call(
        join_kernel,
        jax.ShapeDtypeStruct(joined_shape, BF16),
        pl.GridSpec(
            grid=(1,),
            in_specs=[smem_spec, whole(shares.shape), whole(piece_shape)],
            out_specs=whole(joined_shape),
        ),
        1000, 2**20, SMALL_VMEM_BYTES,
    )(all_kids, shares, returned)
    finished = lax.all_to_all(joined, "space", split_axis=0, concat_axis=0, tiled=True)

    coarse_out, grad_conv, grad_res, grad_mix = kernel_call(
        functools.partial(unpack_kernel, lane_tiles),
        (
            jax.ShapeDtypeStruct((slots, wide, VOX), BF16),
            jax.ShapeDtypeStruct((7, chans, chans), F32),
            jax.ShapeDtypeStruct((8, chans, wide), F32),
            jax.ShapeDtypeStruct((wide, wide), F32),
        ),
        pl.GridSpec(
            grid=(1,),
            in_specs=[whole(joined_shape)],
            out_specs=[whole((slots, wide, VOX)), whole((7, chans, chans)),
                       whole((8, chans, wide)), whole((wide, wide))],
            scratch_shapes=[vmem((devices * rows, LANES), F32)],
        ),
        1000, 2 * 2**20, SMALL_VMEM_BYTES,
    )(finished)
    return coarse_out, grad_conv, grad_res.transpose(0, 2, 1), grad_mix


def solution(mesh):
    return jax.shard_map(
        body,
        mesh=mesh,
        in_specs=(
            P(("groups", "space"), None, None),
            P(("groups", "space")),
            P(("groups", "space"), None),
            P(("groups", "space"), None),
            P(),
            P(),
            P(),
            P(("groups", "space"), None, None),
        ),
        out_specs=(
            P(("groups", "space"), None, None),
            P("groups", None, None),
            P("groups", None, None),
            P("groups", None),
        ),
        check_vma=False,
    )
```

```python
import functools
import math

import jax
import jax.numpy as jnp
from jax import lax
from jax.experimental import pallas as pl
from jax.experimental.pallas import tpu as pltpu
from jax.sharding import PartitionSpec as P

EDGE = 8
HALF = EDGE // 2
VOX = EDGE**3
LANES = 128
ROWS = 16
LABEL_ROWS = 8
SEND = 8
PARTS = 4
BF16 = jnp.bfloat16
F32 = jnp.float32
VMEM_BYTES = 60 * 1024 * 1024
SMALL_VMEM_BYTES = 16 * 1024 * 1024


def bits_of(value):
    return [(value >> (8 - k)) & 1 for k in range(9)]


def join_bits(bits):
    value = bits[0]
    for bit in bits[1:]:
        value = value * 2 + bit
    return value


def split_voxel(column):
    ta, tb, tc, a1, a0, b1, b0, c1, c0 = bits_of(column)
    return join_bits([a1, a0, ta, b1, b0, tb, c1, c0, tc])


def octant_voxel(column):
    oa, ob, oc, a1, a0, b1, b0, c1, c0 = bits_of(column)
    return join_bits([oa, a1, a0, ob, b1, b0, oc, c1, c0])


def picker(voxel_of, shape=(VOX, VOX), start=(0, 0), flip=False):
    row = lax.broadcasted_iota(jnp.int32, shape, 0) + start[0]
    column = lax.broadcasted_iota(jnp.int32, shape, 1) + start[1]
    return (column == voxel_of(row) if flip else row == voxel_of(column)).astype(BF16)


def dot(a, b):
    return jnp.dot(a, b, preferred_element_type=F32)


def dot_nt(a, b):
    return lax.dot_general(a, b, (((1,), (1,)), ((), ())), preferred_element_type=F32)


def pack_kernel(lane_tiles, parents, cot, msg, kids_out, kids):
    devices = msg.shape[0]
    slots = cot.shape[0]

    def find(g, found):
        kids[found] = parents[0, g]
        return found + (parents[1, g] == 0).astype(jnp.int32)

    lax.fori_loop(0, parents.shape[1], find, jnp.int32(0), unroll=4)
    lane = lax.broadcasted_iota(jnp.int32, (LABEL_ROWS, LANES), 1)
    label = jnp.zeros((LABEL_ROWS, LANES), jnp.int32)
    for q in range(kids_out.shape[0]):
        kids_out[q] = kids[q]
        label = jnp.where(lane == q, kids[q], label)
    label = label.astype(F32).astype(BF16)
    for j in range(devices):
        msg[j, slots * lane_tiles * ROWS :] = label
    per_row = VOX // (LANES * lane_tiles)
    for j in range(devices):
        chan, part = j // per_row, j % per_row
        for q in range(slots):
            for lt in range(lane_tiles):
                lane = (part * lane_tiles + lt) * LANES
                row = (q * lane_tiles + lt) * ROWS
                msg[j, row : row + ROWS] = cot[
                    q, chan * ROWS : (chan + 1) * ROWS, lane : lane + LANES
                ]


def table_kernel(
    place, counts, kids, neighbors, parents, feat, up, down, table, ordered,
    up_idx, up_far, down_idx, down_far, bricks, done, split, in_sem, out_sem,
):
    count, chans = feat.shape[:2]
    part = count // PARTS
    fetches = [
        pltpu.make_async_copy(
            feat.at[pl.ds(k * part, part)], bricks.at[pl.ds(k * part, part)], in_sem.at[k]
        )
        for k in range(PARTS)
    ]
    for fetch in fetches:
        fetch.start()
    base = place[0] * count
    table[4 * count] = place[0]
    for r in range(SEND + 1):
        up_idx[r] = 0
        down_idx[r] = 0
        up_far[r] = 2 * count
        down_far[r] = 2 * count
    split[...] = picker(split_voxel)

    def scan(g, found):
        n_up, n_down = found
        near_up, near_down = neighbors[0, g], neighbors[1, g]
        far_up, far_down = near_up - base - count, near_down - base + count
        goes_up = (near_up >= 0) & (far_up >= 0)
        goes_down = (near_down >= 0) & (far_down < count)
        up_idx[n_up] = g
        up_far[n_up] = jnp.where(goes_up, far_up, 2 * count)
        down_idx[n_down] = g
        down_far[n_down] = jnp.where(goes_down, far_down, 2 * count)
        q = jnp.int32(0)
        for k in range(1, kids.shape[0]):
            q += jnp.where(kids[k] == parents[0, g], k, 0)
        number = q * 8 + parents[1, g]
        table[number] = g
        table[count + number] = jnp.where(g < counts[0], g, count + SEND)
        return n_up + goes_up.astype(jnp.int32), n_down + goes_down.astype(jnp.int32)

    lax.fori_loop(0, count, scan, (jnp.int32(0), jnp.int32(0)), unroll=4)

    def rank(r, carry):
        for start, far, idx in ((2 * count, up_far, up_idx), (3 * count, down_far, down_idx)):
            earlier = jnp.int32(0)
            for other in range(SEND):
                earlier += (far[other] < far[r]).astype(jnp.int32)

            @pl.when(far[r] < count)
            def _():
                table[start + idx[r]] = count + earlier

        return carry

    lax.fori_loop(0, SEND, rank, jnp.int32(0))
    sends = []
    for k in range(PARTS):
        fetches[k].wait()
        rows = bricks[k * part : (k + 1) * part].reshape(part * chans, VOX)
        done[k * part : (k + 1) * part] = (
            dot(rows, split[...]).astype(BF16).reshape(part, chans, VOX)
        )
        sends.append(
            pltpu.make_async_copy(
                done.at[pl.ds(k * part, part)], ordered.at[pl.ds(k * part, part)], out_sem.at[k]
            )
        )
        sends[-1].start()
    low = low_lanes(chans)
    for r in range(SEND // 2):
        other = r + SEND // 2
        top = slice(VOX - LANES, VOX)
        up[r] = jnp.where(
            low,
            pltpu.roll(bricks[up_idx[r], :, top], LANES // 2, 1),
            bricks[up_idx[other], :, top],
        )
        down[r] = jnp.where(
            low,
            bricks[down_idx[r], :, :LANES],
            pltpu.roll(bricks[down_idx[other], :, :LANES], LANES // 2, 1),
        )
    for send in sends:
        send.wait()


def route_kernel(kids, msg, pieces):
    devices, groups, lane_tiles = pieces.shape[:3]
    slots = groups
    for s in range(devices):
        for q in range(groups):
            kid = kids[s * groups + q]
            owner, slot = kid // slots, kid % slots
            for lt in range(lane_tiles):
                row = pl.multiple_of((slot * lane_tiles + lt) * ROWS, ROWS)
                pieces[s, q, lt] = msg[owner, pl.ds(row, ROWS), :]


def place_arrivals(above, below, bricks, count):
    chans = bricks.shape[1]
    half = VOX // 2
    side = LANES // 2
    shape = (LANES, half)
    pairs = SEND // 2
    for k, shift in ((0, 0), (pairs, -side)):
        slots = slice(count + k, count + k + pairs)
        first = dot(
            above[...].reshape(pairs * chans, LANES), picker(split_voxel, shape, (shift, 0))
        )
        last = dot(
            below[...].reshape(pairs * chans, LANES),
            picker(split_voxel, shape, (VOX - side + shift, half)),
        )
        bricks[slots, :, :half] = first.astype(BF16).reshape(pairs, chans, half)
        bricks[slots, :, half:] = last.astype(BF16).reshape(pairs, chans, half)
    bricks[count + SEND] = jnp.zeros(bricks.shape[1:], BF16)


def sources(table, neighbors, number):
    count = neighbors.shape[1]
    g = table[number]
    found = []
    for d in range(6):
        near = neighbors[d, g]
        local = near - table[4 * count] * count
        if d == 0:
            local = jnp.where(local >= count, table[2 * count + g], local)
        if d == 1:
            local = jnp.where(local < 0, table[3 * count + g], local)
        found.append(jnp.where(near >= 0, local, count + SEND))
    found.append(table[count + number])
    return found


def shift_into(slots, bricks, views):
    chans = bricks.shape[1]
    tiles = VOX // LANES
    lane = lax.broadcasted_iota(jnp.int32, (chans, LANES), 1)
    low = lane < LANES // 2
    a = (lane // 16) % HALF
    b = (lane // 4) % HALF
    c = lane % HALF

    def tile(slot, t):
        return bricks[slot, :, t * LANES : (t + 1) * LANES]

    def turn(value, by):
        return pltpu.roll(value, by % LANES, 1)

    x = [tile(slots[6], t) for t in range(tiles)]
    for t in range(tiles):
        lanes = slice(t * LANES, (t + 1) * LANES)
        if t < 2:
            plus_a = x[t + 2]
            minus_a = jnp.where(a > 0, turn(x[t + 2], 16), turn(tile(slots[1], t + 2), -48))
        else:
            plus_a = jnp.where(a < HALF - 1, turn(x[t - 2], -16), turn(tile(slots[0], t - 2), 48))
            minus_a = x[t - 2]
        if t % 2 == 0:
            plus_b = x[t + 1]
            minus_b = jnp.where(b > 0, turn(x[t + 1], 4), turn(tile(slots[3], t + 1), -12))
        else:
            plus_b = jnp.where(b < HALF - 1, turn(x[t - 1], -4), turn(tile(slots[2], t - 1), 12))
            minus_b = x[t - 1]
        swapped = turn(x[t], 64)
        plus_c = jnp.where(c < HALF - 1, turn(x[t], 63), turn(tile(slots[4], t), 67))
        minus_c = jnp.where(c > 0, turn(x[t], -63), turn(tile(slots[5], t), -67))
        out = [plus_a, minus_a, plus_b, minus_b, jnp.where(low, swapped, plus_c),
               jnp.where(low, minus_c, swapped), x[t]]
        for d in range(7):
            views[d * chans : (d + 1) * chans, lanes] = out[d]


def low_lanes(rows):
    return lax.broadcasted_iota(jnp.int32, (rows, LANES), 1) < LANES // 2


def forward_kernel(
    lane_tiles, table_hbm, neighbors_hbm, feat, w_conv_hbm, w_res_hbm, w_mix_hbm,
    above_hbm, below_hbm,
    parts_out, slope_out, coarse_out, piece_out,
    bricks, views, place, w_conv, w_res, w_mix, conv_cat, res_cat, octants,
    table, neighbors, above, below, sem,
):
    q = pl.program_id(0)
    groups = pl.num_programs(0) - 1
    count, chans = feat.shape[:2]

    @pl.when(q == 0)
    def _():
        copies = [
            pltpu.make_async_copy(source, target, sem.at[k])
            for k, (source, target) in enumerate((
                (above_hbm, above), (below_hbm, below), (w_conv_hbm, w_conv),
                (w_res_hbm, w_res), (w_mix_hbm, w_mix), (table_hbm, table),
                (neighbors_hbm, neighbors), (feat, bricks.at[pl.ds(0, count)]),
            ))
        ]
        for copy in copies:
            copy.start()
        place[...] = picker(octant_voxel, flip=True)
        for copy in copies[:-1]:
            copy.wait()
        place_arrivals(above, below, bricks, count)
        for d in range(7):
            conv_cat[:, d * chans : (d + 1) * chans] = w_conv[d]
        res_cat[...] = w_res[...].T
        copies[-1].wait()

    low_half = low_lanes(chans)

    def finish():
        coarse = dot(octants[...], place[...]).astype(BF16)
        coarse_out[0] = coarse
        mixed = dot(w_mix[...], coarse).astype(BF16)
        per_row = VOX // (LANES * lane_tiles)
        for j in range(piece_out.shape[0]):
            chan, part = j // per_row, j % per_row
            for lt in range(lane_tiles):
                lane = (part * lane_tiles + lt) * LANES
                piece_out[j, 0, lt] = mixed[chan * ROWS : (chan + 1) * ROWS, lane : lane + LANES]

    def restrict(first):
        acts = []
        for k in range(first, first + 4):
            shift_into(sources(table, neighbors, q * 8 + k), bricks, views.at[k])
            hidden = dot(conv_cat[...], views[k])
            sig = 0.5 + 0.5 * jnp.tanh(0.5 * hidden)
            act = hidden * sig
            slope_out[0, k * chans : (k + 1) * chans, :] = (sig + act * (1.0 - sig)).astype(BF16)
            acts.append(act.astype(BF16))
        for k in range(0, 4, 2):
            lanes = slice((first + k) * (LANES // 2), (first + k + 2) * (LANES // 2))
            for t in range(4):
                one = acts[k][:, t * LANES : (t + 1) * LANES]
                two = acts[k + 1][:, t * LANES : (t + 1) * LANES]
                parts_out[0, 2 * t * chans : (2 * t + 1) * chans, lanes] = jnp.where(
                    low_half, one, pltpu.roll(two, LANES // 2, 1)
                )
                parts_out[0, (2 * t + 1) * chans : (2 * t + 2) * chans, lanes] = jnp.where(
                    low_half, pltpu.roll(one, LANES // 2, 1), two
                )
        lanes = slice(first * (LANES // 2), (first + 4) * (LANES // 2))
        return dot(res_cat[...], parts_out[0, :, lanes]).astype(BF16)

    @pl.when(q < groups)
    def _():
        finish()
        halves = [restrict(0), restrict(4)]
        octants[...] = jnp.concatenate(halves, axis=1)

    @pl.when(q == groups)
    def _():
        finish()


def backward_kernel(
    lane_tiles, scale, table, neighbors, feat, above, below, pieces, parts, slope, coarse, w_mix, w_res, packed,
    bricks, views, cot, grad_parts, grad_rows, unplace, mix_t, conv_sum, res_sum, mix_sum, sem,
):
    q = pl.program_id(0)
    count, chans = feat.shape[:2]
    wide = coarse.shape[1]
    fetch = pltpu.make_async_copy(feat, bricks.at[pl.ds(0, count)], sem)

    @pl.when(q == 0)
    def _():
        fetch.start()
        place_arrivals(above, below, bricks, count)
        unplace[...] = picker(octant_voxel)
        mix_t[...] = w_mix[...].T
        conv_sum[...] = jnp.zeros_like(conv_sum)
        res_sum[...] = jnp.zeros_like(res_sum)
        mix_sum[...] = jnp.zeros_like(mix_sum)
        fetch.wait()

    per_row = VOX // (LANES * lane_tiles)
    for j in range(pieces.shape[0]):
        chan, part = j // per_row, j % per_row
        for lt in range(lane_tiles):
            lane = (part * lane_tiles + lt) * LANES
            cot[chan * ROWS : (chan + 1) * ROWS, lane : lane + LANES] = pieces[j, 0, lt]
    cots = cot[...]
    grad_coarse = (scale * dot(mix_t[...], cots)).astype(BF16)
    grad_fine = dot(grad_coarse, unplace[...]).astype(BF16)
    mix_sum[...] += dot_nt(cots, coarse[0])
    res_sum[...] += dot_nt(parts[0], grad_fine)
    grad_parts[...] = dot(w_res[...], grad_fine)
    low_half = low_lanes(chans)
    for r in range(4):
        for t in range(4):
            cols = slice(r * LANES, (r + 1) * LANES)
            lanes = slice(t * LANES, (t + 1) * LANES)
            one = grad_parts[2 * t * chans : (2 * t + 1) * chans, cols]
            two = grad_parts[(2 * t + 1) * chans : (2 * t + 2) * chans, cols]
            first = slice(2 * r * chans, (2 * r + 1) * chans)
            second = slice((2 * r + 1) * chans, (2 * r + 2) * chans)
            grad_rows[first, lanes] = (
                jnp.where(low_half, one, pltpu.roll(two, LANES // 2, 1))
                * slope[0, first, lanes].astype(F32)
            ).astype(BF16)
            grad_rows[second, lanes] = (
                jnp.where(low_half, pltpu.roll(one, LANES // 2, 1), two)
                * slope[0, second, lanes].astype(F32)
            ).astype(BF16)

    total = None
    for k in range(8):
        shift_into(sources(table, neighbors, q * 8 + k), bricks, views.at[k])
        term = dot_nt(grad_rows[k * chans : (k + 1) * chans, :], views[k])
        total = term if total is None else total + term
    conv_sum[:, : 7 * chans] += total

    @pl.when(q == pl.num_programs(0) - 1)
    def _():
        packed[0:wide] = (scale * mix_sum[...]).astype(BF16)
        at = wide
        packed[at : at + 8 * chans] = res_sum[...].astype(BF16)
        at += 8 * chans
        for t in range(4):
            packed[at : at + chans] = conv_sum[:, t * LANES : (t + 1) * LANES].astype(BF16)
            at += chans
        if at < packed.shape[0]:
            packed[at:] = jnp.zeros((packed.shape[0] - at, LANES), BF16)


def join_kernel(kids, shares, pieces, msg):
    devices, groups, lane_tiles = pieces.shape[:3]
    slots = groups
    body_rows = slots * lane_tiles * ROWS
    for s in range(devices):
        for q in range(groups):
            kid = kids[s * groups + q]
            owner, slot = kid // slots, kid % slots
            for lt in range(lane_tiles):
                row = pl.multiple_of((slot * lane_tiles + lt) * ROWS, ROWS)
                msg[owner, pl.ds(row, ROWS), :] = pieces[s, q, lt]
    total = jnp.sum(shares[...].astype(F32), axis=0).astype(BF16)
    for j in range(devices):
        msg[j, body_rows:] = total


def unpack_kernel(lane_tiles, msg, coarse_out, conv, res, mix, packed):
    devices, rows = msg.shape[:2]
    slots = coarse_out.shape[0]
    wide = mix.shape[0]
    chans = conv.shape[1]
    half = LANES // 2
    body_rows = slots * lane_tiles * ROWS
    share = rows - body_rows
    for j in range(devices):
        packed[j * share : (j + 1) * share] = msg[j, body_rows:].astype(F32)
    mix[...] = packed[0:wide]
    at = wide
    for t in range(8):
        res[t] = packed[at : at + chans]
        at += chans
    for t in range(4):
        block = packed[at : at + chans]
        conv[2 * t] = block[:, :half]
        if 2 * t + 1 < 7:
            conv[2 * t + 1] = block[:, half:]
        at += chans
    per_row = VOX // (LANES * lane_tiles)
    for j in range(devices):
        chan, part = j // per_row, j % per_row
        for q in range(slots):
            for lt in range(lane_tiles):
                row = (q * lane_tiles + lt) * ROWS
                lane = (part * lane_tiles + lt) * LANES
                coarse_out[q, chan * ROWS : (chan + 1) * ROWS, lane : lane + LANES] = msg[
                    j, row : row + ROWS
                ]


def kernel_call(kernel, out_shape, grid_spec, flops, moved, vmem=VMEM_BYTES):
    return pl.pallas_call(
        kernel,
        out_shape=out_shape,
        grid_spec=grid_spec,
        compiler_params=pltpu.CompilerParams(vmem_limit_bytes=vmem),
        cost_estimate=pl.CostEstimate(flops=flops, bytes_accessed=moved, transcendentals=0),
    )


def body(features, counts, neighbors, parents, w_conv, w_restrict, w_mix, cotangent):
    devices = lax.axis_size("space")
    position = lax.axis_index("space").astype(jnp.int32).reshape(1)
    slots, wide = cotangent.shape[:2]
    count, chans = features.shape[:2]
    lane_tiles = VOX * 8 // devices // LANES
    tiles = slots * lane_tiles
    groups = count // 8
    whole = lambda shape: pl.BlockSpec(shape, lambda *_: (0,) * len(shape))
    any_spec = pl.BlockSpec(memory_space=pl.ANY)
    smem_spec = pl.BlockSpec(memory_space=pltpu.SMEM)
    smem = lambda size: pltpu.SMEM((size,), jnp.int32)
    vmem = pltpu.VMEM
    ints = lambda size: jax.ShapeDtypeStruct((size,), jnp.int32)

    message_shape = (devices, tiles * ROWS + LABEL_ROWS, LANES)
    message, kids = kernel_call(
        functools.partial(pack_kernel, lane_tiles),
        (jax.ShapeDtypeStruct(message_shape, BF16), ints(groups)),
        pl.GridSpec(
            grid=(1,),
            in_specs=[smem_spec, whole(cotangent.shape)],
            out_specs=[whole(message_shape), smem_spec],
            scratch_shapes=[smem(groups + 1)],
        ),
        1000, 2**20,
    )(parents.T, cotangent)
    spread = lax.all_to_all(message, "space", split_axis=0, concat_axis=0, tiled=True)

    plane = jax.ShapeDtypeStruct((SEND // 2, chans, LANES), BF16)
    up, down, table, ordered = kernel_call(
        table_kernel,
        (plane, plane, ints(4 * count + 1), jax.ShapeDtypeStruct(features.shape, BF16)),
        pl.GridSpec(
            grid=(1,),
            in_specs=[smem_spec] * 5 + [any_spec],
            out_specs=[whole(plane.shape)] * 2 + [smem_spec, any_spec],
            scratch_shapes=[smem(SEND + 1)] * 4
            + [vmem(features.shape, BF16), vmem(features.shape, BF16), vmem((VOX, VOX), BF16),
               pltpu.SemaphoreType.DMA((PARTS,)), pltpu.SemaphoreType.DMA((PARTS,))],
        ),
        1000, 2**20,
    )(position, counts, kids, neighbors.T, parents.T, features)
    below = lax.ppermute(up, "space", [(i, i + 1) for i in range(devices - 1)])
    above = lax.ppermute(down, "space", [(i + 1, i) for i in range(devices - 1)])

    all_kids = spread[:, tiles * ROWS, :groups].astype(jnp.int32).reshape(-1)
    piece_shape = (devices, groups, lane_tiles, ROWS, LANES)
    forward_tiles = kernel_call(
        route_kernel,
        jax.ShapeDtypeStruct(piece_shape, BF16),
        pl.GridSpec(
            grid=(1,),
            in_specs=[smem_spec, whole(message_shape)],
            out_specs=whole(piece_shape),
        ),
        1000, 2**20, SMALL_VMEM_BYTES,
    )(all_kids, spread)
    forward_tiles, above, below = lax.optimization_barrier((forward_tiles, above, below))
    cot_pieces = lax.all_to_all(forward_tiles, "space", split_axis=0, concat_axis=0, tiled=True)

    res_rows = w_restrict.transpose(0, 2, 1).reshape(8 * chans, wide)
    scalars = (table, neighbors.T)
    brick_scratch = vmem((count + SEND + 1, chans, VOX), BF16)
    view_scratch = vmem((8, 7 * chans, VOX), BF16)
    per_group = lambda *shape: pl.BlockSpec((1,) + shape, lambda q: (q,) + (0,) * len(shape))
    piece_spec = pl.BlockSpec((devices, 1, lane_tiles, ROWS, LANES), lambda q: (0, q, 0, 0, 0))
    parts, slope, coarse, pieces = kernel_call(
        functools.partial(forward_kernel, lane_tiles),
        (
            jax.ShapeDtypeStruct((groups, 8 * chans, VOX), BF16),
            jax.ShapeDtypeStruct((groups, 8 * chans, VOX), BF16),
            jax.ShapeDtypeStruct((groups, wide, VOX), BF16),
            jax.ShapeDtypeStruct(piece_shape, BF16),
        ),
        pl.GridSpec(
            grid=(groups + 1,),
            in_specs=[any_spec] * 8,
            out_specs=[
                pl.BlockSpec((1, 8 * chans, VOX), lambda q: (jnp.minimum(q, groups - 1), 0, 0)),
                pl.BlockSpec((1, 8 * chans, VOX), lambda q: (jnp.minimum(q, groups - 1), 0, 0)),
                pl.BlockSpec((1, wide, VOX), lambda q: (jnp.maximum(q - 1, 0), 0, 0)),
                pl.BlockSpec(
                    (devices, 1, lane_tiles, ROWS, LANES),
                    lambda q: (0, jnp.maximum(q - 1, 0), 0, 0, 0),
                ),
            ],
            scratch_shapes=[
                brick_scratch, view_scratch, vmem((VOX, VOX), BF16), vmem(w_conv.shape, BF16),
                vmem(res_rows.shape, BF16), vmem(w_mix.shape, BF16),
                vmem((chans, 7 * chans), BF16), vmem((wide, 8 * chans), BF16),
                vmem((wide, VOX), BF16), smem(4 * count + 1),
                pltpu.SMEM((6, count), jnp.int32), vmem(plane.shape, BF16),
                vmem(plane.shape, BF16), pltpu.SemaphoreType.DMA((8,)),
            ],
        ),
        16 * 10**9, 16 * 2**20,
    )(*scalars, ordered, w_conv, res_rows, w_mix, above, below)
    returned = lax.all_to_all(pieces, "space", split_axis=0, concat_axis=0, tiled=True)

    scale = 1.0 / math.sqrt(devices * slots * VOX)
    used = wide + 8 * chans + 4 * chans
    rows = -(-used // (devices * 8)) * 8
    packed = kernel_call(
        functools.partial(backward_kernel, lane_tiles, scale),
        jax.ShapeDtypeStruct((devices * rows, LANES), BF16),
        pl.GridSpec(
            grid=(groups,),
            in_specs=[smem_spec] * 2 + [any_spec] + [whole(plane.shape)] * 2
            + [piece_spec, per_group(8 * chans, VOX), per_group(8 * chans, VOX),
               per_group(wide, VOX), whole(w_mix.shape), whole(res_rows.shape)],
            out_specs=whole((devices * rows, LANES)),
            scratch_shapes=[
                brick_scratch, view_scratch, vmem((wide, VOX), BF16),
                vmem((8 * chans, VOX), F32), vmem((8 * chans, VOX), BF16), vmem((VOX, VOX), BF16),
                vmem((wide, wide), BF16), vmem((chans, 8 * chans), F32),
                vmem((8 * chans, wide), F32), vmem((wide, wide), F32), pltpu.SemaphoreType.DMA,
            ],
        ),
        16 * 10**9, 16 * 2**20,
    )(*scalars, ordered, above, below, cot_pieces, parts, slope, coarse, w_mix, res_rows)

    shares = lax.all_to_all(
        packed.reshape(devices, rows, LANES), "space", split_axis=0, concat_axis=0, tiled=True
    )
    joined_shape = (devices, tiles * ROWS + rows, LANES)
    joined = kernel_call(
        join_kernel,
        jax.ShapeDtypeStruct(joined_shape, BF16),
        pl.GridSpec(
            grid=(1,),
            in_specs=[smem_spec, whole(shares.shape), whole(piece_shape)],
            out_specs=whole(joined_shape),
        ),
        1000, 2**20, SMALL_VMEM_BYTES,
    )(all_kids, shares, returned)
    finished = lax.all_to_all(joined, "space", split_axis=0, concat_axis=0, tiled=True)

    coarse_out, grad_conv, grad_res, grad_mix = kernel_call(
        functools.partial(unpack_kernel, lane_tiles),
        (
            jax.ShapeDtypeStruct((slots, wide, VOX), BF16),
            jax.ShapeDtypeStruct((7, chans, chans), F32),
            jax.ShapeDtypeStruct((8, chans, wide), F32),
            jax.ShapeDtypeStruct((wide, wide), F32),
        ),
        pl.GridSpec(
            grid=(1,),
            in_specs=[whole(joined_shape)],
            out_specs=[whole((slots, wide, VOX)), whole((7, chans, chans)),
                       whole((8, chans, wide)), whole((wide, wide))],
            scratch_shapes=[vmem((devices * rows, LANES), F32)],
        ),
        1000, 2 * 2**20, SMALL_VMEM_BYTES,
    )(finished)
    return coarse_out, grad_conv, grad_res.transpose(0, 2, 1), grad_mix


def solution(mesh):
    return jax.shard_map(
        body,
        mesh=mesh,
        in_specs=(
            P(("groups", "space"), None, None),
            P(("groups", "space")),
            P(("groups", "space"), None),
            P(("groups", "space"), None),
            P(),
            P(),
            P(),
            P(("groups", "space"), None, None),
        ),
        out_specs=(
            P(("groups", "space"), None, None),
            P("groups", None, None),
            P("groups", None, None),
            P("groups", None),
        ),
        check_vma=False,
    )
```

```python
import functools
import math

import jax
import jax.numpy as jnp
from jax import lax
from jax.experimental import pallas as pl
from jax.experimental.pallas import tpu as pltpu
from jax.sharding import PartitionSpec as P

EDGE = 8
HALF = EDGE // 2
VOX = EDGE**3
LANES = 128
ROWS = 16
LABEL_ROWS = 8
SEND = 8
PARTS = 4
BF16 = jnp.bfloat16
F32 = jnp.float32
VMEM_BYTES = 60 * 1024 * 1024
SMALL_VMEM_BYTES = 16 * 1024 * 1024


def bits_of(value):
    return [(value >> (8 - k)) & 1 for k in range(9)]


def join_bits(bits):
    value = bits[0]
    for bit in bits[1:]:
        value = value * 2 + bit
    return value


def split_voxel(column):
    ta, tb, tc, a1, a0, b1, b0, c1, c0 = bits_of(column)
    return join_bits([a1, a0, ta, b1, b0, tb, c1, c0, tc])


def octant_voxel(column):
    oa, ob, oc, a1, a0, b1, b0, c1, c0 = bits_of(column)
    return join_bits([oa, a1, a0, ob, b1, b0, oc, c1, c0])


def picker(voxel_of, shape=(VOX, VOX), start=(0, 0), flip=False):
    row = lax.broadcasted_iota(jnp.int32, shape, 0) + start[0]
    column = lax.broadcasted_iota(jnp.int32, shape, 1) + start[1]
    return (column == voxel_of(row) if flip else row == voxel_of(column)).astype(BF16)


def dot(a, b):
    return jnp.dot(a, b, preferred_element_type=F32)


def dot_nt(a, b):
    return lax.dot_general(a, b, (((1,), (1,)), ((), ())), preferred_element_type=F32)


def piece_copies(lane_tiles, bricks, message, sem):
    copies = []
    for part in range(message.shape[1]):
        for q in range(bricks.shape[0]):
            for lt in range(lane_tiles):
                lane = (part * lane_tiles + lt) * LANES
                row = (q * lane_tiles + lt) * ROWS
                copies.append((
                    bricks.at[q, :, :, pl.ds(lane, LANES)],
                    message.at[:, part, pl.ds(row, ROWS), :],
                    sem.at[len(copies)],
                ))
    return copies


def pack_kernel(lane_tiles, parents, cot, msg, kids_out, kids, label, sem, label_sem):
    copies = [
        pltpu.make_async_copy(source, target, at)
        for source, target, at in piece_copies(lane_tiles, cot, msg, sem)
    ]
    for copy in copies:
        copy.start()

    def find(g, found):
        kids[found] = parents[0, g]
        return found + (parents[1, g] == 0).astype(jnp.int32)

    lax.fori_loop(0, parents.shape[1], find, jnp.int32(0), unroll=4)
    lane = lax.broadcasted_iota(jnp.int32, (LABEL_ROWS, LANES), 1)
    listed = jnp.zeros((LABEL_ROWS, LANES), jnp.int32)
    for q in range(kids_out.shape[0]):
        kids_out[q] = kids[q]
        listed = jnp.where(lane == q, kids[q], listed)
    for c in range(label.shape[0]):
        label[c] = listed.astype(F32).astype(BF16)
    row = cot.shape[0] * lane_tiles * ROWS
    for part in range(msg.shape[1]):
        copies.append(
            pltpu.make_async_copy(
                label, msg.at[:, part, pl.ds(row, LABEL_ROWS), :], label_sem.at[part]
            )
        )
        copies[-1].start()
    for copy in copies:
        copy.wait()


def table_kernel(
    place, counts, kids, neighbors, parents, feat, up, down, table, ordered,
    up_idx, up_far, down_idx, down_far, bricks, done, split, in_sem, out_sem,
):
    count, chans = feat.shape[:2]
    part = count // PARTS
    fetches = [
        pltpu.make_async_copy(
            feat.at[pl.ds(k * part, part)], bricks.at[pl.ds(k * part, part)], in_sem.at[k]
        )
        for k in range(PARTS)
    ]
    for fetch in fetches:
        fetch.start()
    base = place[0] * count
    table[4 * count] = place[0]
    for r in range(SEND + 1):
        up_idx[r] = 0
        down_idx[r] = 0
        up_far[r] = 2 * count
        down_far[r] = 2 * count
    split[...] = picker(split_voxel)

    def scan(g, found):
        n_up, n_down = found
        near_up, near_down = neighbors[0, g], neighbors[1, g]
        far_up, far_down = near_up - base - count, near_down - base + count
        goes_up = (near_up >= 0) & (far_up >= 0)
        goes_down = (near_down >= 0) & (far_down < count)
        up_idx[n_up] = g
        up_far[n_up] = jnp.where(goes_up, far_up, 2 * count)
        down_idx[n_down] = g
        down_far[n_down] = jnp.where(goes_down, far_down, 2 * count)
        q = jnp.int32(0)
        for k in range(1, kids.shape[0]):
            q += jnp.where(kids[k] == parents[0, g], k, 0)
        number = q * 8 + parents[1, g]
        table[number] = g
        table[count + number] = jnp.where(g < counts[0], g, count + SEND)
        return n_up + goes_up.astype(jnp.int32), n_down + goes_down.astype(jnp.int32)

    lax.fori_loop(0, count, scan, (jnp.int32(0), jnp.int32(0)), unroll=4)

    def rank(r, carry):
        for start, far, idx in ((2 * count, up_far, up_idx), (3 * count, down_far, down_idx)):
            earlier = jnp.int32(0)
            for other in range(SEND):
                earlier += (far[other] < far[r]).astype(jnp.int32)

            @pl.when(far[r] < count)
            def _():
                table[start + idx[r]] = count + earlier

        return carry

    lax.fori_loop(0, SEND, rank, jnp.int32(0))
    sends = []
    for k in range(PARTS):
        fetches[k].wait()
        rows = bricks[k * part : (k + 1) * part].reshape(part * chans, VOX)
        done[k * part : (k + 1) * part] = (
            dot(rows, split[...]).astype(BF16).reshape(part, chans, VOX)
        )
        sends.append(
            pltpu.make_async_copy(
                done.at[pl.ds(k * part, part)], ordered.at[pl.ds(k * part, part)], out_sem.at[k]
            )
        )
        sends[-1].start()
    low = low_lanes(chans)
    for r in range(SEND // 2):
        other = r + SEND // 2
        top = slice(VOX - LANES, VOX)
        up[r] = jnp.where(
            low,
            pltpu.roll(bricks[up_idx[r], :, top], LANES // 2, 1),
            bricks[up_idx[other], :, top],
        )
        down[r] = jnp.where(
            low,
            bricks[down_idx[r], :, :LANES],
            pltpu.roll(bricks[down_idx[other], :, :LANES], LANES // 2, 1),
        )
    for send in sends:
        send.wait()


def route_kernel(kids, msg, pieces):
    devices, groups, lane_tiles = pieces.shape[:3]
    slots = groups
    for s in range(devices):
        for q in range(groups):
            kid = kids[s * groups + q]
            owner, slot = kid // slots, kid % slots
            for lt in range(lane_tiles):
                row = pl.multiple_of((slot * lane_tiles + lt) * ROWS, ROWS)
                pieces[s, q, lt] = msg[owner, pl.ds(row, ROWS), :]


def place_arrivals(above, below, bricks, count):
    chans = bricks.shape[1]
    half = VOX // 2
    side = LANES // 2
    shape = (LANES, half)
    pairs = SEND // 2
    for k, shift in ((0, 0), (pairs, -side)):
        slots = slice(count + k, count + k + pairs)
        first = dot(
            above[...].reshape(pairs * chans, LANES), picker(split_voxel, shape, (shift, 0))
        )
        last = dot(
            below[...].reshape(pairs * chans, LANES),
            picker(split_voxel, shape, (VOX - side + shift, half)),
        )
        bricks[slots, :, :half] = first.astype(BF16).reshape(pairs, chans, half)
        bricks[slots, :, half:] = last.astype(BF16).reshape(pairs, chans, half)
    bricks[count + SEND] = jnp.zeros(bricks.shape[1:], BF16)


def sources(table, neighbors, number):
    count = neighbors.shape[1]
    g = table[number]
    found = []
    for d in range(6):
        near = neighbors[d, g]
        local = near - table[4 * count] * count
        if d == 0:
            local = jnp.where(local >= count, table[2 * count + g], local)
        if d == 1:
            local = jnp.where(local < 0, table[3 * count + g], local)
        found.append(jnp.where(near >= 0, local, count + SEND))
    found.append(table[count + number])
    return found


def shift_into(slots, bricks, views):
    chans = bricks.shape[1]
    tiles = VOX // LANES
    lane = lax.broadcasted_iota(jnp.int32, (chans, LANES), 1)
    low = lane < LANES // 2
    a = (lane // 16) % HALF
    b = (lane // 4) % HALF
    c = lane % HALF

    def tile(slot, t):
        return bricks[slot, :, t * LANES : (t + 1) * LANES]

    def turn(value, by):
        return pltpu.roll(value, by % LANES, 1)

    x = [tile(slots[6], t) for t in range(tiles)]
    for t in range(tiles):
        lanes = slice(t * LANES, (t + 1) * LANES)
        if t < 2:
            plus_a = x[t + 2]
            minus_a = jnp.where(a > 0, turn(x[t + 2], 16), turn(tile(slots[1], t + 2), -48))
        else:
            plus_a = jnp.where(a < HALF - 1, turn(x[t - 2], -16), turn(tile(slots[0], t - 2), 48))
            minus_a = x[t - 2]
        if t % 2 == 0:
            plus_b = x[t + 1]
            minus_b = jnp.where(b > 0, turn(x[t + 1], 4), turn(tile(slots[3], t + 1), -12))
        else:
            plus_b = jnp.where(b < HALF - 1, turn(x[t - 1], -4), turn(tile(slots[2], t - 1), 12))
            minus_b = x[t - 1]
        swapped = turn(x[t], 64)
        plus_c = jnp.where(c < HALF - 1, turn(x[t], 63), turn(tile(slots[4], t), 67))
        minus_c = jnp.where(c > 0, turn(x[t], -63), turn(tile(slots[5], t), -67))
        out = [plus_a, minus_a, plus_b, minus_b, jnp.where(low, swapped, plus_c),
               jnp.where(low, minus_c, swapped), x[t]]
        for d in range(7):
            views[d * chans : (d + 1) * chans, lanes] = out[d]


def low_lanes(rows):
    return lax.broadcasted_iota(jnp.int32, (rows, LANES), 1) < LANES // 2


def forward_kernel(
    lane_tiles, table_hbm, neighbors_hbm, feat, w_conv_hbm, w_res_hbm, w_mix_hbm,
    above_hbm, below_hbm,
    parts_out, slope_out, coarse_out, piece_out,
    bricks, views, place, w_conv, w_res, w_mix, conv_cat, res_cat, octants,
    table, neighbors, above, below, sem,
):
    q = pl.program_id(0)
    groups = pl.num_programs(0) - 1
    count, chans = feat.shape[:2]

    @pl.when(q == 0)
    def _():
        copies = [
            pltpu.make_async_copy(source, target, sem.at[k])
            for k, (source, target) in enumerate((
                (above_hbm, above), (below_hbm, below), (w_conv_hbm, w_conv),
                (w_res_hbm, w_res), (w_mix_hbm, w_mix), (table_hbm, table),
                (neighbors_hbm, neighbors), (feat, bricks.at[pl.ds(0, count)]),
            ))
        ]
        for copy in copies:
            copy.start()
        place[...] = picker(octant_voxel, flip=True)
        for copy in copies[:-1]:
            copy.wait()
        place_arrivals(above, below, bricks, count)
        for d in range(7):
            conv_cat[:, d * chans : (d + 1) * chans] = w_conv[d]
        res_cat[...] = w_res[...].T
        copies[-1].wait()

    low_half = low_lanes(chans)

    def finish():
        coarse = dot(octants[...], place[...]).astype(BF16)
        coarse_out[0] = coarse
        mixed = dot(w_mix[...], coarse).astype(BF16)
        per_row = VOX // (LANES * lane_tiles)
        for j in range(piece_out.shape[0]):
            chan, part = j // per_row, j % per_row
            for lt in range(lane_tiles):
                lane = (part * lane_tiles + lt) * LANES
                piece_out[j, 0, lt] = mixed[chan * ROWS : (chan + 1) * ROWS, lane : lane + LANES]

    def restrict(first):
        acts = []
        for k in range(first, first + 4):
            shift_into(sources(table, neighbors, q * 8 + k), bricks, views.at[k])
            hidden = dot(conv_cat[...], views[k])
            sig = 0.5 + 0.5 * jnp.tanh(0.5 * hidden)
            act = hidden * sig
            slope_out[0, k * chans : (k + 1) * chans, :] = (sig + act * (1.0 - sig)).astype(BF16)
            acts.append(act.astype(BF16))
        for k in range(0, 4, 2):
            lanes = slice((first + k) * (LANES // 2), (first + k + 2) * (LANES // 2))
            for t in range(4):
                one = acts[k][:, t * LANES : (t + 1) * LANES]
                two = acts[k + 1][:, t * LANES : (t + 1) * LANES]
                parts_out[0, 2 * t * chans : (2 * t + 1) * chans, lanes] = jnp.where(
                    low_half, one, pltpu.roll(two, LANES // 2, 1)
                )
                parts_out[0, (2 * t + 1) * chans : (2 * t + 2) * chans, lanes] = jnp.where(
                    low_half, pltpu.roll(one, LANES // 2, 1), two
                )
        lanes = slice(first * (LANES // 2), (first + 4) * (LANES // 2))
        return dot(res_cat[...], parts_out[0, :, lanes]).astype(BF16)

    @pl.when(q < groups)
    def _():
        finish()
        halves = [restrict(0), restrict(4)]
        octants[...] = jnp.concatenate(halves, axis=1)

    @pl.when(q == groups)
    def _():
        finish()


def backward_kernel(
    lane_tiles, scale, table, neighbors, feat, above, below, pieces, parts, slope, coarse, w_mix, w_res, packed,
    bricks, views, cot, grad_parts, grad_rows, unplace, mix_t, conv_sum, res_sum, mix_sum, sem,
):
    q = pl.program_id(0)
    count, chans = feat.shape[:2]
    wide = coarse.shape[1]
    fetch = pltpu.make_async_copy(feat, bricks.at[pl.ds(0, count)], sem)

    @pl.when(q == 0)
    def _():
        fetch.start()
        place_arrivals(above, below, bricks, count)
        unplace[...] = picker(octant_voxel)
        mix_t[...] = w_mix[...].T
        conv_sum[...] = jnp.zeros_like(conv_sum)
        res_sum[...] = jnp.zeros_like(res_sum)
        mix_sum[...] = jnp.zeros_like(mix_sum)
        fetch.wait()

    per_row = VOX // (LANES * lane_tiles)
    for j in range(pieces.shape[0]):
        chan, part = j // per_row, j % per_row
        for lt in range(lane_tiles):
            lane = (part * lane_tiles + lt) * LANES
            cot[chan * ROWS : (chan + 1) * ROWS, lane : lane + LANES] = pieces[j, 0, lt]
    cots = cot[...]
    grad_coarse = (scale * dot(mix_t[...], cots)).astype(BF16)
    grad_fine = dot(grad_coarse, unplace[...]).astype(BF16)
    mix_sum[...] += dot_nt(cots, coarse[0])
    res_sum[...] += dot_nt(parts[0], grad_fine)
    grad_parts[...] = dot(w_res[...], grad_fine)
    low_half = low_lanes(chans)
    for r in range(4):
        for t in range(4):
            cols = slice(r * LANES, (r + 1) * LANES)
            lanes = slice(t * LANES, (t + 1) * LANES)
            one = grad_parts[2 * t * chans : (2 * t + 1) * chans, cols]
            two = grad_parts[(2 * t + 1) * chans : (2 * t + 2) * chans, cols]
            first = slice(2 * r * chans, (2 * r + 1) * chans)
            second = slice((2 * r + 1) * chans, (2 * r + 2) * chans)
            grad_rows[first, lanes] = (
                jnp.where(low_half, one, pltpu.roll(two, LANES // 2, 1))
                * slope[0, first, lanes].astype(F32)
            ).astype(BF16)
            grad_rows[second, lanes] = (
                jnp.where(low_half, pltpu.roll(one, LANES // 2, 1), two)
                * slope[0, second, lanes].astype(F32)
            ).astype(BF16)

    total = None
    for k in range(8):
        shift_into(sources(table, neighbors, q * 8 + k), bricks, views.at[k])
        term = dot_nt(grad_rows[k * chans : (k + 1) * chans, :], views[k])
        total = term if total is None else total + term
    conv_sum[:, : 7 * chans] += total

    @pl.when(q == pl.num_programs(0) - 1)
    def _():
        packed[0:wide] = (scale * mix_sum[...]).astype(BF16)
        at = wide
        packed[at : at + 8 * chans] = res_sum[...].astype(BF16)
        at += 8 * chans
        for t in range(4):
            packed[at : at + chans] = conv_sum[:, t * LANES : (t + 1) * LANES].astype(BF16)
            at += chans
        if at < packed.shape[0]:
            packed[at:] = jnp.zeros((packed.shape[0] - at, LANES), BF16)


def join_kernel(kids, shares, pieces, msg):
    devices, groups, lane_tiles = pieces.shape[:3]
    slots = groups
    body_rows = slots * lane_tiles * ROWS
    for s in range(devices):
        for q in range(groups):
            kid = kids[s * groups + q]
            owner, slot = kid // slots, kid % slots
            for lt in range(lane_tiles):
                row = pl.multiple_of((slot * lane_tiles + lt) * ROWS, ROWS)
                msg[owner, pl.ds(row, ROWS), :] = pieces[s, q, lt]
    total = jnp.sum(shares[...].astype(F32), axis=0).astype(BF16)
    for j in range(devices):
        msg[j, body_rows:] = total


def unpack_kernel(lane_tiles, msg, coarse_out, conv, res, mix, packed, sem):
    slots = coarse_out.shape[0]
    wide = mix.shape[0]
    chans = conv.shape[1]
    half = LANES // 2
    copies = [
        pltpu.make_async_copy(target, source, at)
        for source, target, at in piece_copies(lane_tiles, coarse_out, msg, sem)
    ]
    for copy in copies:
        copy.start()
    body_rows = slots * lane_tiles * ROWS
    per_row = msg.shape[1]
    share = msg.shape[2] - body_rows
    for j in range(msg.shape[0] * per_row):
        packed[j * share : (j + 1) * share] = msg[j // per_row, j % per_row, body_rows:].astype(F32)
    mix[...] = packed[0:wide]
    at = wide
    for t in range(8):
        res[t] = packed[at : at + chans]
        at += chans
    for t in range(4):
        block = packed[at : at + chans]
        conv[2 * t] = block[:, :half]
        if 2 * t + 1 < 7:
            conv[2 * t + 1] = block[:, half:]
        at += chans
    for copy in copies:
        copy.wait()


def kernel_call(kernel, out_shape, grid_spec, flops, moved, vmem=VMEM_BYTES):
    return pl.pallas_call(
        kernel,
        out_shape=out_shape,
        grid_spec=grid_spec,
        compiler_params=pltpu.CompilerParams(vmem_limit_bytes=vmem),
        cost_estimate=pl.CostEstimate(flops=flops, bytes_accessed=moved, transcendentals=0),
    )


def body(features, counts, neighbors, parents, w_conv, w_restrict, w_mix, cotangent):
    devices = lax.axis_size("space")
    position = lax.axis_index("space").astype(jnp.int32).reshape(1)
    slots, wide = cotangent.shape[:2]
    count, chans = features.shape[:2]
    lane_tiles = VOX * 8 // devices // LANES
    tiles = slots * lane_tiles
    groups = count // 8
    whole = lambda shape: pl.BlockSpec(shape, lambda *_: (0,) * len(shape))
    any_spec = pl.BlockSpec(memory_space=pl.ANY)
    smem_spec = pl.BlockSpec(memory_space=pltpu.SMEM)
    smem = lambda size: pltpu.SMEM((size,), jnp.int32)
    vmem = pltpu.VMEM
    ints = lambda size: jax.ShapeDtypeStruct((size,), jnp.int32)

    parts_of = devices // 8
    message_shape = (devices, tiles * ROWS + LABEL_ROWS, LANES)
    message, kids = kernel_call(
        functools.partial(pack_kernel, lane_tiles),
        (jax.ShapeDtypeStruct((8, parts_of) + message_shape[1:], BF16), ints(groups)),
        pl.GridSpec(
            grid=(1,),
            in_specs=[smem_spec, any_spec],
            out_specs=[any_spec, smem_spec],
            scratch_shapes=[
                smem(groups + 1), vmem((8, LABEL_ROWS, LANES), BF16),
                pltpu.SemaphoreType.DMA((parts_of * tiles,)),
                pltpu.SemaphoreType.DMA((parts_of,)),
            ],
        ),
        1000, 2**20,
    )(parents.T, cotangent.reshape(slots, 8, ROWS, VOX))
    spread = lax.all_to_all(
        message.reshape(message_shape), "space", split_axis=0, concat_axis=0, tiled=True
    )

    plane = jax.ShapeDtypeStruct((SEND // 2, chans, LANES), BF16)
    up, down, table, ordered = kernel_call(
        table_kernel,
        (plane, plane, ints(4 * count + 1), jax.ShapeDtypeStruct(features.shape, BF16)),
        pl.GridSpec(
            grid=(1,),
            in_specs=[smem_spec] * 5 + [any_spec],
            out_specs=[whole(plane.shape)] * 2 + [smem_spec, any_spec],
            scratch_shapes=[smem(SEND + 1)] * 4
            + [vmem(features.shape, BF16), vmem(features.shape, BF16), vmem((VOX, VOX), BF16),
               pltpu.SemaphoreType.DMA((PARTS,)), pltpu.SemaphoreType.DMA((PARTS,))],
        ),
        1000, 2**20,
    )(position, counts, kids, neighbors.T, parents.T, features)
    below = lax.ppermute(up, "space", [(i, i + 1) for i in range(devices - 1)])
    above = lax.ppermute(down, "space", [(i + 1, i) for i in range(devices - 1)])

    all_kids = spread[:, tiles * ROWS, :groups].astype(jnp.int32).reshape(-1)
    piece_shape = (devices, groups, lane_tiles, ROWS, LANES)
    forward_tiles = kernel_call(
        route_kernel,
        jax.ShapeDtypeStruct(piece_shape, BF16),
        pl.GridSpec(
            grid=(1,),
            in_specs=[smem_spec, whole(message_shape)],
            out_specs=whole(piece_shape),
        ),
        1000, 2**20, SMALL_VMEM_BYTES,
    )(all_kids, spread)
    forward_tiles, above, below = lax.optimization_barrier((forward_tiles, above, below))
    cot_pieces = lax.all_to_all(forward_tiles, "space", split_axis=0, concat_axis=0, tiled=True)

    res_rows = w_restrict.transpose(0, 2, 1).reshape(8 * chans, wide)
    scalars = (table, neighbors.T)
    brick_scratch = vmem((count + SEND + 1, chans, VOX), BF16)
    view_scratch = vmem((8, 7 * chans, VOX), BF16)
    per_group = lambda *shape: pl.BlockSpec((1,) + shape, lambda q: (q,) + (0,) * len(shape))
    piece_spec = pl.BlockSpec((devices, 1, lane_tiles, ROWS, LANES), lambda q: (0, q, 0, 0, 0))
    parts, slope, coarse, pieces = kernel_call(
        functools.partial(forward_kernel, lane_tiles),
        (
            jax.ShapeDtypeStruct((groups, 8 * chans, VOX), BF16),
            jax.ShapeDtypeStruct((groups, 8 * chans, VOX), BF16),
            jax.ShapeDtypeStruct((groups, wide, VOX), BF16),
            jax.ShapeDtypeStruct(piece_shape, BF16),
        ),
        pl.GridSpec(
            grid=(groups + 1,),
            in_specs=[any_spec] * 8,
            out_specs=[
                pl.BlockSpec((1, 8 * chans, VOX), lambda q: (jnp.minimum(q, groups - 1), 0, 0)),
                pl.BlockSpec((1, 8 * chans, VOX), lambda q: (jnp.minimum(q, groups - 1), 0, 0)),
                pl.BlockSpec((1, wide, VOX), lambda q: (jnp.maximum(q - 1, 0), 0, 0)),
                pl.BlockSpec(
                    (devices, 1, lane_tiles, ROWS, LANES),
                    lambda q: (0, jnp.maximum(q - 1, 0), 0, 0, 0),
                ),
            ],
            scratch_shapes=[
                brick_scratch, view_scratch, vmem((VOX, VOX), BF16), vmem(w_conv.shape, BF16),
                vmem(res_rows.shape, BF16), vmem(w_mix.shape, BF16),
                vmem((chans, 7 * chans), BF16), vmem((wide, 8 * chans), BF16),
                vmem((wide, VOX), BF16), smem(4 * count + 1),
                pltpu.SMEM((6, count), jnp.int32), vmem(plane.shape, BF16),
                vmem(plane.shape, BF16), pltpu.SemaphoreType.DMA((8,)),
            ],
        ),
        16 * 10**9, 16 * 2**20,
    )(*scalars, ordered, w_conv, res_rows, w_mix, above, below)
    returned = lax.all_to_all(pieces, "space", split_axis=0, concat_axis=0, tiled=True)

    scale = 1.0 / math.sqrt(devices * slots * VOX)
    used = wide + 8 * chans + 4 * chans
    rows = -(-used // (devices * 8)) * 8
    packed = kernel_call(
        functools.partial(backward_kernel, lane_tiles, scale),
        jax.ShapeDtypeStruct((devices * rows, LANES), BF16),
        pl.GridSpec(
            grid=(groups,),
            in_specs=[smem_spec] * 2 + [any_spec] + [whole(plane.shape)] * 2
            + [piece_spec, per_group(8 * chans, VOX), per_group(8 * chans, VOX),
               per_group(wide, VOX), whole(w_mix.shape), whole(res_rows.shape)],
            out_specs=whole((devices * rows, LANES)),
            scratch_shapes=[
                brick_scratch, view_scratch, vmem((wide, VOX), BF16),
                vmem((8 * chans, VOX), F32), vmem((8 * chans, VOX), BF16), vmem((VOX, VOX), BF16),
                vmem((wide, wide), BF16), vmem((chans, 8 * chans), F32),
                vmem((8 * chans, wide), F32), vmem((wide, wide), F32), pltpu.SemaphoreType.DMA,
            ],
        ),
        16 * 10**9, 16 * 2**20,
    )(*scalars, ordered, above, below, cot_pieces, parts, slope, coarse, w_mix, res_rows)

    shares = lax.all_to_all(
        packed.reshape(devices, rows, LANES), "space", split_axis=0, concat_axis=0, tiled=True
    )
    joined_shape = (devices, tiles * ROWS + rows, LANES)
    joined = kernel_call(
        join_kernel,
        jax.ShapeDtypeStruct(joined_shape, BF16),
        pl.GridSpec(
            grid=(1,),
            in_specs=[smem_spec, whole(shares.shape), whole(piece_shape)],
            out_specs=whole(joined_shape),
        ),
        1000, 2**20, SMALL_VMEM_BYTES,
    )(all_kids, shares, returned)
    finished = lax.all_to_all(joined, "space", split_axis=0, concat_axis=0, tiled=True)

    split_shape = (8, parts_of) + joined_shape[1:]
    coarse_out, grad_conv, grad_res, grad_mix = kernel_call(
        functools.partial(unpack_kernel, lane_tiles),
        (
            jax.ShapeDtypeStruct((slots, 8, ROWS, VOX), BF16),
            jax.ShapeDtypeStruct((7, chans, chans), F32),
            jax.ShapeDtypeStruct((8, chans, wide), F32),
            jax.ShapeDtypeStruct((wide, wide), F32),
        ),
        pl.GridSpec(
            grid=(1,),
            in_specs=[whole(split_shape)],
            out_specs=[any_spec, whole((7, chans, chans)),
                       whole((8, chans, wide)), whole((wide, wide))],
            scratch_shapes=[
                vmem((devices * rows, LANES), F32), pltpu.SemaphoreType.DMA((parts_of * tiles,)),
            ],
        ),
        1000, 2 * 2**20, SMALL_VMEM_BYTES,
    )(finished.reshape(split_shape))
    coarse_out = coarse_out.reshape(slots, wide, VOX)
    return coarse_out, grad_conv, grad_res.transpose(0, 2, 1), grad_mix


def solution(mesh):
    return jax.shard_map(
        body,
        mesh=mesh,
        in_specs=(
            P(("groups", "space"), None, None),
            P(("groups", "space")),
            P(("groups", "space"), None),
            P(("groups", "space"), None),
            P(),
            P(),
            P(),
            P(("groups", "space"), None, None),
        ),
        out_specs=(
            P(("groups", "space"), None, None),
            P("groups", None, None),
            P("groups", None, None),
            P("groups", None),
        ),
        check_vma=False,
    )
```

```python
import functools
import math

import jax
import jax.numpy as jnp
from jax import lax
from jax.experimental import pallas as pl
from jax.experimental.pallas import tpu as pltpu
from jax.sharding import PartitionSpec as P

EDGE = 8
HALF = EDGE // 2
VOX = EDGE**3
LANES = 128
ROWS = 16
LABEL_ROWS = 8
SEND = 8
PARTS = 4
BF16 = jnp.bfloat16
F32 = jnp.float32
VMEM_BYTES = 60 * 1024 * 1024
SMALL_VMEM_BYTES = 16 * 1024 * 1024


def bits_of(value):
    return [(value >> (8 - k)) & 1 for k in range(9)]


def join_bits(bits):
    value = bits[0]
    for bit in bits[1:]:
        value = value * 2 + bit
    return value


def split_voxel(column):
    ta, tb, tc, a1, a0, b1, b0, c1, c0 = bits_of(column)
    return join_bits([a1, a0, ta, b1, b0, tb, c1, c0, tc])


def octant_voxel(column):
    oa, ob, oc, a1, a0, b1, b0, c1, c0 = bits_of(column)
    return join_bits([oa, a1, a0, ob, b1, b0, oc, c1, c0])


def picker(voxel_of, shape=(VOX, VOX), start=(0, 0), flip=False):
    row = lax.broadcasted_iota(jnp.int32, shape, 0) + start[0]
    column = lax.broadcasted_iota(jnp.int32, shape, 1) + start[1]
    return (column == voxel_of(row) if flip else row == voxel_of(column)).astype(BF16)


def dot(a, b):
    return jnp.dot(a, b, preferred_element_type=F32)


def dot_nt(a, b):
    return lax.dot_general(a, b, (((1,), (1,)), ((), ())), preferred_element_type=F32)


def pack_kernel(lane_tiles, parents, cot, msg, kids_out, kids):
    devices = msg.shape[0]
    slots = cot.shape[0]

    def find(g, found):
        kids[found] = parents[0, g]
        return found + (parents[1, g] == 0).astype(jnp.int32)

    lax.fori_loop(0, parents.shape[1], find, jnp.int32(0), unroll=4)
    lane = lax.broadcasted_iota(jnp.int32, (LABEL_ROWS, LANES), 1)
    label = jnp.zeros((LABEL_ROWS, LANES), jnp.int32)
    for q in range(kids_out.shape[0]):
        kids_out[q] = kids[q]
        label = jnp.where(lane == q, kids[q], label)
    label = label.astype(F32).astype(BF16)
    for j in range(devices):
        msg[j, slots * lane_tiles * ROWS :] = label
    per_row = VOX // (LANES * lane_tiles)
    for j in range(devices):
        chan, part = j // per_row, j % per_row
        for q in range(slots):
            for lt in range(lane_tiles):
                lane = (part * lane_tiles + lt) * LANES
                row = (q * lane_tiles + lt) * ROWS
                msg[j, row : row + ROWS] = cot[
                    q, chan * ROWS : (chan + 1) * ROWS, lane : lane + LANES
                ]


def table_kernel(
    place, counts, kids, neighbors, parents, feat, up, down, table, ordered,
    up_idx, up_far, down_idx, down_far, bricks, done, split, in_sem, out_sem,
):
    count, chans = feat.shape[:2]
    part = count // PARTS
    fetches = [
        pltpu.make_async_copy(
            feat.at[pl.ds(k * part, part)], bricks.at[pl.ds(k * part, part)], in_sem.at[k]
        )
        for k in range(PARTS)
    ]
    for fetch in fetches:
        fetch.start()
    base = place[0] * count
    table[4 * count] = place[0]
    for r in range(SEND + 1):
        up_idx[r] = 0
        down_idx[r] = 0
        up_far[r] = 2 * count
        down_far[r] = 2 * count
    split[...] = picker(split_voxel)

    def scan(g, found):
        n_up, n_down = found
        near_up, near_down = neighbors[0, g], neighbors[1, g]
        far_up, far_down = near_up - base - count, near_down - base + count
        goes_up = (near_up >= 0) & (far_up >= 0)
        goes_down = (near_down >= 0) & (far_down < count)
        up_idx[n_up] = g
        up_far[n_up] = jnp.where(goes_up, far_up, 2 * count)
        down_idx[n_down] = g
        down_far[n_down] = jnp.where(goes_down, far_down, 2 * count)
        q = jnp.int32(0)
        for k in range(1, kids.shape[0]):
            q += jnp.where(kids[k] == parents[0, g], k, 0)
        number = q * 8 + parents[1, g]
        table[number] = g
        table[count + number] = jnp.where(g < counts[0], g, count + SEND)
        return n_up + goes_up.astype(jnp.int32), n_down + goes_down.astype(jnp.int32)

    lax.fori_loop(0, count, scan, (jnp.int32(0), jnp.int32(0)), unroll=4)

    def rank(r, carry):
        for start, far, idx in ((2 * count, up_far, up_idx), (3 * count, down_far, down_idx)):
            earlier = jnp.int32(0)
            for other in range(SEND):
                earlier += (far[other] < far[r]).astype(jnp.int32)

            @pl.when(far[r] < count)
            def _():
                table[start + idx[r]] = count + earlier

        return carry

    lax.fori_loop(0, SEND, rank, jnp.int32(0))
    sends = []
    for k in range(PARTS):
        fetches[k].wait()
        rows = bricks[k * part : (k + 1) * part].reshape(part * chans, VOX)
        done[k * part : (k + 1) * part] = (
            dot(rows, split[...]).astype(BF16).reshape(part, chans, VOX)
        )
        sends.append(
            pltpu.make_async_copy(
                done.at[pl.ds(k * part, part)], ordered.at[pl.ds(k * part, part)], out_sem.at[k]
            )
        )
        sends[-1].start()
    low = low_lanes(chans)
    for r in range(SEND // 2):
        other = r + SEND // 2
        top = slice(VOX - LANES, VOX)
        up[r] = jnp.where(
            low,
            pltpu.roll(bricks[up_idx[r], :, top], LANES // 2, 1),
            bricks[up_idx[other], :, top],
        )
        down[r] = jnp.where(
            low,
            bricks[down_idx[r], :, :LANES],
            pltpu.roll(bricks[down_idx[other], :, :LANES], LANES // 2, 1),
        )
    for send in sends:
        send.wait()


def route_kernel(kids, msg, pieces):
    devices, groups, lane_tiles = pieces.shape[:3]
    slots = groups
    for s in range(devices):
        for q in range(groups):
            kid = kids[s * groups + q]
            owner, slot = kid // slots, kid % slots
            for lt in range(lane_tiles):
                row = pl.multiple_of((slot * lane_tiles + lt) * ROWS, ROWS)
                pieces[s, q, lt] = msg[owner, pl.ds(row, ROWS), :]


def place_arrivals(above, below, bricks, count):
    chans = bricks.shape[1]
    half = VOX // 2
    side = LANES // 2
    shape = (LANES, half)
    pairs = SEND // 2
    for k, shift in ((0, 0), (pairs, -side)):
        slots = slice(count + k, count + k + pairs)
        first = dot(
            above[...].reshape(pairs * chans, LANES), picker(split_voxel, shape, (shift, 0))
        )
        last = dot(
            below[...].reshape(pairs * chans, LANES),
            picker(split_voxel, shape, (VOX - side + shift, half)),
        )
        bricks[slots, :, :half] = first.astype(BF16).reshape(pairs, chans, half)
        bricks[slots, :, half:] = last.astype(BF16).reshape(pairs, chans, half)
    bricks[count + SEND] = jnp.zeros(bricks.shape[1:], BF16)


def sources(table, neighbors, number):
    count = neighbors.shape[1]
    g = table[number]
    found = []
    for d in range(6):
        near = neighbors[d, g]
        local = near - table[4 * count] * count
        if d == 0:
            local = jnp.where(local >= count, table[2 * count + g], local)
        if d == 1:
            local = jnp.where(local < 0, table[3 * count + g], local)
        found.append(jnp.where(near >= 0, local, count + SEND))
    found.append(table[count + number])
    return found


def shift_into(slots, bricks, views):
    chans = bricks.shape[1]
    tiles = VOX // LANES
    lane = lax.broadcasted_iota(jnp.int32, (chans, LANES), 1)
    low = lane < LANES // 2
    a = (lane // 16) % HALF
    b = (lane // 4) % HALF
    c = lane % HALF

    def tile(slot, t):
        return bricks[slot, :, t * LANES : (t + 1) * LANES]

    def turn(value, by):
        return pltpu.roll(value, by % LANES, 1)

    x = [tile(slots[6], t) for t in range(tiles)]
    for t in range(tiles):
        lanes = slice(t * LANES, (t + 1) * LANES)
        if t < 2:
            plus_a = x[t + 2]
            minus_a = jnp.where(a > 0, turn(x[t + 2], 16), turn(tile(slots[1], t + 2), -48))
        else:
            plus_a = jnp.where(a < HALF - 1, turn(x[t - 2], -16), turn(tile(slots[0], t - 2), 48))
            minus_a = x[t - 2]
        if t % 2 == 0:
            plus_b = x[t + 1]
            minus_b = jnp.where(b > 0, turn(x[t + 1], 4), turn(tile(slots[3], t + 1), -12))
        else:
            plus_b = jnp.where(b < HALF - 1, turn(x[t - 1], -4), turn(tile(slots[2], t - 1), 12))
            minus_b = x[t - 1]
        swapped = turn(x[t], 64)
        plus_c = jnp.where(c < HALF - 1, turn(x[t], 63), turn(tile(slots[4], t), 67))
        minus_c = jnp.where(c > 0, turn(x[t], -63), turn(tile(slots[5], t), -67))
        out = [plus_a, minus_a, plus_b, minus_b, jnp.where(low, swapped, plus_c),
               jnp.where(low, minus_c, swapped), x[t]]
        for d in range(7):
            views[d * chans : (d + 1) * chans, lanes] = out[d]


def low_lanes(rows):
    return lax.broadcasted_iota(jnp.int32, (rows, LANES), 1) < LANES // 2


def forward_kernel(
    lane_tiles, table_hbm, neighbors_hbm, feat, w_conv_hbm, w_res_hbm, w_mix_hbm,
    above_hbm, below_hbm,
    parts_out, slope_out, coarse_out, piece_out,
    bricks, views, place, w_conv, w_res, w_mix, conv_cat, res_cat, octants,
    table, neighbors, above, below, sem,
):
    q = pl.program_id(0)
    groups = pl.num_programs(0) - 1
    count, chans = feat.shape[:2]

    @pl.when(q == 0)
    def _():
        copies = [
            pltpu.make_async_copy(source, target, sem.at[k])
            for k, (source, target) in enumerate((
                (above_hbm, above), (below_hbm, below), (w_conv_hbm, w_conv),
                (w_res_hbm, w_res), (w_mix_hbm, w_mix), (table_hbm, table),
                (neighbors_hbm, neighbors), (feat, bricks.at[pl.ds(0, count)]),
            ))
        ]
        for copy in copies:
            copy.start()
        place[...] = picker(octant_voxel, flip=True)
        for copy in copies[:-1]:
            copy.wait()
        place_arrivals(above, below, bricks, count)
        for d in range(7):
            conv_cat[:, d * chans : (d + 1) * chans] = w_conv[d]
        res_cat[...] = w_res[...].T
        copies[-1].wait()

    low_half = low_lanes(chans)

    def finish():
        coarse = dot(octants[...], place[...]).astype(BF16)
        coarse_out[0] = coarse
        mixed = dot(w_mix[...], coarse).astype(BF16)
        per_row = VOX // (LANES * lane_tiles)
        for j in range(piece_out.shape[0]):
            chan, part = j // per_row, j % per_row
            for lt in range(lane_tiles):
                lane = (part * lane_tiles + lt) * LANES
                piece_out[j, 0, lt] = mixed[chan * ROWS : (chan + 1) * ROWS, lane : lane + LANES]

    def restrict(first):
        acts = []
        for k in range(first, first + 4):
            shift_into(sources(table, neighbors, q * 8 + k), bricks, views.at[k])
            hidden = dot(conv_cat[...], views[k])
            sig = 0.5 + 0.5 * jnp.tanh(0.5 * hidden)
            act = hidden * sig
            slope_out[0, k * chans : (k + 1) * chans, :] = (sig + act * (1.0 - sig)).astype(BF16)
            acts.append(act.astype(BF16))
        for k in range(0, 4, 2):
            lanes = slice((first + k) * (LANES // 2), (first + k + 2) * (LANES // 2))
            for t in range(4):
                one = acts[k][:, t * LANES : (t + 1) * LANES]
                two = acts[k + 1][:, t * LANES : (t + 1) * LANES]
                parts_out[0, 2 * t * chans : (2 * t + 1) * chans, lanes] = jnp.where(
                    low_half, one, pltpu.roll(two, LANES // 2, 1)
                )
                parts_out[0, (2 * t + 1) * chans : (2 * t + 2) * chans, lanes] = jnp.where(
                    low_half, pltpu.roll(one, LANES // 2, 1), two
                )
        lanes = slice(first * (LANES // 2), (first + 4) * (LANES // 2))
        return dot(res_cat[...], parts_out[0, :, lanes]).astype(BF16)

    @pl.when(q < groups)
    def _():
        finish()
        halves = [restrict(0), restrict(4)]
        octants[...] = jnp.concatenate(halves, axis=1)

    @pl.when(q == groups)
    def _():
        finish()


def backward_kernel(
    lane_tiles, scale, table, neighbors, feat, above, below, pieces, parts, slope, coarse,
    w_mix, w_res, own, other,
    bricks, views, cot, grad_parts, grad_rows, unplace, mix_t, conv_sum, res_sum, mix_sum, packed,
    sem,
):
    q = pl.program_id(0)
    count, chans = feat.shape[:2]
    wide = coarse.shape[1]
    fetch = pltpu.make_async_copy(feat, bricks.at[pl.ds(0, count)], sem)

    @pl.when(q == 0)
    def _():
        fetch.start()
        place_arrivals(above, below, bricks, count)
        unplace[...] = picker(octant_voxel)
        mix_t[...] = w_mix[...].T
        conv_sum[...] = jnp.zeros_like(conv_sum)
        res_sum[...] = jnp.zeros_like(res_sum)
        mix_sum[...] = jnp.zeros_like(mix_sum)
        fetch.wait()

    per_row = VOX // (LANES * lane_tiles)
    for j in range(pieces.shape[0]):
        chan, part = j // per_row, j % per_row
        for lt in range(lane_tiles):
            lane = (part * lane_tiles + lt) * LANES
            cot[chan * ROWS : (chan + 1) * ROWS, lane : lane + LANES] = pieces[j, 0, lt]
    cots = cot[...]
    grad_coarse = (scale * dot(mix_t[...], cots)).astype(BF16)
    grad_fine = dot(grad_coarse, unplace[...]).astype(BF16)
    mix_sum[...] += dot_nt(cots, coarse[0])
    res_sum[...] += dot_nt(parts[0], grad_fine)
    grad_parts[...] = dot(w_res[...], grad_fine)
    low_half = low_lanes(chans)
    for r in range(4):
        for t in range(4):
            cols = slice(r * LANES, (r + 1) * LANES)
            lanes = slice(t * LANES, (t + 1) * LANES)
            one = grad_parts[2 * t * chans : (2 * t + 1) * chans, cols]
            two = grad_parts[(2 * t + 1) * chans : (2 * t + 2) * chans, cols]
            first = slice(2 * r * chans, (2 * r + 1) * chans)
            second = slice((2 * r + 1) * chans, (2 * r + 2) * chans)
            grad_rows[first, lanes] = (
                jnp.where(low_half, one, pltpu.roll(two, LANES // 2, 1))
                * slope[0, first, lanes].astype(F32)
            ).astype(BF16)
            grad_rows[second, lanes] = (
                jnp.where(low_half, pltpu.roll(one, LANES // 2, 1), two)
                * slope[0, second, lanes].astype(F32)
            ).astype(BF16)

    total = None
    for k in range(8):
        shift_into(sources(table, neighbors, q * 8 + k), bricks, views.at[k])
        term = dot_nt(grad_rows[k * chans : (k + 1) * chans, :], views[k])
        total = term if total is None else total + term
    conv_sum[:, : 7 * chans] += total

    @pl.when(q == pl.num_programs(0) - 1)
    def _():
        packed[0:wide] = scale * mix_sum[...]
        at = wide
        packed[at : at + 8 * chans] = res_sum[...]
        at += 8 * chans
        for t in range(4):
            packed[at : at + chans] = conv_sum[:, t * LANES : (t + 1) * LANES]
            at += chans
        if at < packed.shape[0]:
            packed[at:] = jnp.zeros((packed.shape[0] - at, LANES), F32)
        chips, rows = own.shape[:2]
        core = table[4 * count] % 2
        for c in range(chips):
            first = pl.multiple_of((2 * c + core) * rows, 8)
            second = pl.multiple_of((2 * c + 1 - core) * rows, 8)
            own[c] = packed[pl.ds(first, rows), :].astype(BF16)
            other[c] = packed[pl.ds(second, rows), :].astype(BF16)


def join_kernel(kids, shares, pieces, msg):
    devices, groups, lane_tiles = pieces.shape[:3]
    slots = groups
    body_rows = slots * lane_tiles * ROWS
    for s in range(devices):
        for q in range(groups):
            kid = kids[s * groups + q]
            owner, slot = kid // slots, kid % slots
            for lt in range(lane_tiles):
                row = pl.multiple_of((slot * lane_tiles + lt) * ROWS, ROWS)
                msg[owner, pl.ds(row, ROWS), :] = pieces[s, q, lt]
    total = jnp.sum(shares[...].astype(F32), axis=0).astype(BF16)
    for j in range(devices):
        msg[j, body_rows:] = total


def unpack_kernel(lane_tiles, msg, coarse_out, conv, res, mix, packed):
    devices, rows = msg.shape[:2]
    slots = coarse_out.shape[0]
    wide = mix.shape[0]
    chans = conv.shape[1]
    half = LANES // 2
    body_rows = slots * lane_tiles * ROWS
    share = rows - body_rows
    for j in range(devices):
        packed[j * share : (j + 1) * share] = msg[j, body_rows:].astype(F32)
    mix[...] = packed[0:wide]
    at = wide
    for t in range(8):
        res[t] = packed[at : at + chans]
        at += chans
    for t in range(4):
        block = packed[at : at + chans]
        conv[2 * t] = block[:, :half]
        if 2 * t + 1 < 7:
            conv[2 * t + 1] = block[:, half:]
        at += chans
    per_row = VOX // (LANES * lane_tiles)
    for j in range(devices):
        chan, part = j // per_row, j % per_row
        for q in range(slots):
            for lt in range(lane_tiles):
                row = (q * lane_tiles + lt) * ROWS
                lane = (part * lane_tiles + lt) * LANES
                coarse_out[q, chan * ROWS : (chan + 1) * ROWS, lane : lane + LANES] = msg[
                    j, row : row + ROWS
                ]


def kernel_call(kernel, out_shape, grid_spec, flops, moved, vmem=VMEM_BYTES):
    return pl.pallas_call(
        kernel,
        out_shape=out_shape,
        grid_spec=grid_spec,
        compiler_params=pltpu.CompilerParams(vmem_limit_bytes=vmem),
        cost_estimate=pl.CostEstimate(flops=flops, bytes_accessed=moved, transcendentals=0),
    )


def body(features, counts, neighbors, parents, w_conv, w_restrict, w_mix, cotangent):
    devices = lax.axis_size("space")
    position = lax.axis_index("space").astype(jnp.int32).reshape(1)
    slots, wide = cotangent.shape[:2]
    count, chans = features.shape[:2]
    lane_tiles = VOX * 8 // devices // LANES
    tiles = slots * lane_tiles
    groups = count // 8
    whole = lambda shape: pl.BlockSpec(shape, lambda *_: (0,) * len(shape))
    any_spec = pl.BlockSpec(memory_space=pl.ANY)
    smem_spec = pl.BlockSpec(memory_space=pltpu.SMEM)
    smem = lambda size: pltpu.SMEM((size,), jnp.int32)
    vmem = pltpu.VMEM
    ints = lambda size: jax.ShapeDtypeStruct((size,), jnp.int32)

    message_shape = (devices, tiles * ROWS + LABEL_ROWS, LANES)
    message, kids = kernel_call(
        functools.partial(pack_kernel, lane_tiles),
        (jax.ShapeDtypeStruct(message_shape, BF16), ints(groups)),
        pl.GridSpec(
            grid=(1,),
            in_specs=[smem_spec, whole(cotangent.shape)],
            out_specs=[whole(message_shape), smem_spec],
            scratch_shapes=[smem(groups + 1)],
        ),
        1000, 2**20,
    )(parents.T, cotangent)
    spread = lax.all_to_all(message, "space", split_axis=0, concat_axis=0, tiled=True)

    plane = jax.ShapeDtypeStruct((SEND // 2, chans, LANES), BF16)
    up, down, table, ordered = kernel_call(
        table_kernel,
        (plane, plane, ints(4 * count + 1), jax.ShapeDtypeStruct(features.shape, BF16)),
        pl.GridSpec(
            grid=(1,),
            in_specs=[smem_spec] * 5 + [any_spec],
            out_specs=[whole(plane.shape)] * 2 + [smem_spec, any_spec],
            scratch_shapes=[smem(SEND + 1)] * 4
            + [vmem(features.shape, BF16), vmem(features.shape, BF16), vmem((VOX, VOX), BF16),
               pltpu.SemaphoreType.DMA((PARTS,)), pltpu.SemaphoreType.DMA((PARTS,))],
        ),
        1000, 2**20,
    )(position, counts, kids, neighbors.T, parents.T, features)
    below = lax.ppermute(up, "space", [(i, i + 1) for i in range(devices - 1)])
    above = lax.ppermute(down, "space", [(i + 1, i) for i in range(devices - 1)])

    all_kids = spread[:, tiles * ROWS, :groups].astype(jnp.int32).reshape(-1)
    piece_shape = (devices, groups, lane_tiles, ROWS, LANES)
    forward_tiles = kernel_call(
        route_kernel,
        jax.ShapeDtypeStruct(piece_shape, BF16),
        pl.GridSpec(
            grid=(1,),
            in_specs=[smem_spec, whole(message_shape)],
            out_specs=whole(piece_shape),
        ),
        1000, 2**20, SMALL_VMEM_BYTES,
    )(all_kids, spread)
    forward_tiles, above, below = lax.optimization_barrier((forward_tiles, above, below))
    cot_pieces = lax.all_to_all(forward_tiles, "space", split_axis=0, concat_axis=0, tiled=True)

    res_rows = w_restrict.transpose(0, 2, 1).reshape(8 * chans, wide)
    scalars = (table, neighbors.T)
    brick_scratch = vmem((count + SEND + 1, chans, VOX), BF16)
    view_scratch = vmem((8, 7 * chans, VOX), BF16)
    per_group = lambda *shape: pl.BlockSpec((1,) + shape, lambda q: (q,) + (0,) * len(shape))
    piece_spec = pl.BlockSpec((devices, 1, lane_tiles, ROWS, LANES), lambda q: (0, q, 0, 0, 0))
    parts, slope, coarse, pieces = kernel_call(
        functools.partial(forward_kernel, lane_tiles),
        (
            jax.ShapeDtypeStruct((groups, 8 * chans, VOX), BF16),
            jax.ShapeDtypeStruct((groups, 8 * chans, VOX), BF16),
            jax.ShapeDtypeStruct((groups, wide, VOX), BF16),
            jax.ShapeDtypeStruct(piece_shape, BF16),
        ),
        pl.GridSpec(
            grid=(groups + 1,),
            in_specs=[any_spec] * 8,
            out_specs=[
                pl.BlockSpec((1, 8 * chans, VOX), lambda q: (jnp.minimum(q, groups - 1), 0, 0)),
                pl.BlockSpec((1, 8 * chans, VOX), lambda q: (jnp.minimum(q, groups - 1), 0, 0)),
                pl.BlockSpec((1, wide, VOX), lambda q: (jnp.maximum(q - 1, 0), 0, 0)),
                pl.BlockSpec(
                    (devices, 1, lane_tiles, ROWS, LANES),
                    lambda q: (0, jnp.maximum(q - 1, 0), 0, 0, 0),
                ),
            ],
            scratch_shapes=[
                brick_scratch, view_scratch, vmem((VOX, VOX), BF16), vmem(w_conv.shape, BF16),
                vmem(res_rows.shape, BF16), vmem(w_mix.shape, BF16),
                vmem((chans, 7 * chans), BF16), vmem((wide, 8 * chans), BF16),
                vmem((wide, VOX), BF16), smem(4 * count + 1),
                pltpu.SMEM((6, count), jnp.int32), vmem(plane.shape, BF16),
                vmem(plane.shape, BF16), pltpu.SemaphoreType.DMA((8,)),
            ],
        ),
        16 * 10**9, 16 * 2**20,
    )(*scalars, ordered, w_conv, res_rows, w_mix, above, below)
    returned = lax.all_to_all(pieces, "space", split_axis=0, concat_axis=0, tiled=True)

    scale = 1.0 / math.sqrt(devices * slots * VOX)
    used = wide + 8 * chans + 4 * chans
    rows = -(-used // (devices * 8)) * 8
    half = jax.ShapeDtypeStruct((devices // 2, rows, LANES), BF16)
    own, other = kernel_call(
        functools.partial(backward_kernel, lane_tiles, scale),
        (half, half),
        pl.GridSpec(
            grid=(groups,),
            in_specs=[smem_spec] * 2 + [any_spec] + [whole(plane.shape)] * 2
            + [piece_spec, per_group(8 * chans, VOX), per_group(8 * chans, VOX),
               per_group(wide, VOX), whole(w_mix.shape), whole(res_rows.shape)],
            out_specs=[whole(half.shape)] * 2,
            scratch_shapes=[
                brick_scratch, view_scratch, vmem((wide, VOX), BF16),
                vmem((8 * chans, VOX), F32), vmem((8 * chans, VOX), BF16), vmem((VOX, VOX), BF16),
                vmem((wide, wide), BF16), vmem((chans, 8 * chans), F32),
                vmem((8 * chans, wide), F32), vmem((wide, wide), F32),
                vmem((devices * rows, LANES), F32), pltpu.SemaphoreType.DMA,
            ],
        ),
        16 * 10**9, 16 * 2**20,
    )(*scalars, ordered, above, below, cot_pieces, parts, slope, coarse, w_mix, res_rows)

    came = lax.ppermute(other, "space", [(i, i ^ 1) for i in range(devices)])
    paired = (own.astype(F32) + came.astype(F32)).astype(BF16)
    shares = lax.all_to_all(
        paired, "space", split_axis=0, concat_axis=0, tiled=True,
        axis_index_groups=[list(range(core, devices, 2)) for core in range(2)],
    )

    joined_shape = (devices, tiles * ROWS + rows, LANES)
    joined = kernel_call(
        join_kernel,
        jax.ShapeDtypeStruct(joined_shape, BF16),
        pl.GridSpec(
            grid=(1,),
            in_specs=[smem_spec, whole(shares.shape), whole(piece_shape)],
            out_specs=whole(joined_shape),
        ),
        1000, 2**20, SMALL_VMEM_BYTES,
    )(all_kids, shares, returned)
    finished = lax.all_to_all(joined, "space", split_axis=0, concat_axis=0, tiled=True)

    coarse_out, grad_conv, grad_res, grad_mix = kernel_call(
        functools.partial(unpack_kernel, lane_tiles),
        (
            jax.ShapeDtypeStruct((slots, wide, VOX), BF16),
            jax.ShapeDtypeStruct((7, chans, chans), F32),
            jax.ShapeDtypeStruct((8, chans, wide), F32),
            jax.ShapeDtypeStruct((wide, wide), F32),
        ),
        pl.GridSpec(
            grid=(1,),
            in_specs=[whole(joined_shape)],
            out_specs=[whole((slots, wide, VOX)), whole((7, chans, chans)),
                       whole((8, chans, wide)), whole((wide, wide))],
            scratch_shapes=[vmem((devices * rows, LANES), F32)],
        ),
        1000, 2 * 2**20, SMALL_VMEM_BYTES,
    )(finished)
    return coarse_out, grad_conv, grad_res.transpose(0, 2, 1), grad_mix


def solution(mesh):
    return jax.shard_map(
        body,
        mesh=mesh,
        in_specs=(
            P(("groups", "space"), None, None),
            P(("groups", "space")),
            P(("groups", "space"), None),
            P(("groups", "space"), None),
            P(),
            P(),
            P(),
            P(("groups", "space"), None, None),
        ),
        out_specs=(
            P(("groups", "space"), None, None),
            P("groups", None, None),
            P("groups", None, None),
            P("groups", None),
        ),
        check_vma=False,
    )
```

```python
import functools
import math

import jax
import jax.numpy as jnp
from jax import lax
from jax.experimental import pallas as pl
from jax.experimental.pallas import tpu as pltpu
from jax.sharding import PartitionSpec as P

EDGE = 8
HALF = EDGE // 2
VOX = EDGE**3
LANES = 128
ROWS = 16
LABEL_ROWS = 8
SEND = 8
PARTS = 4
BF16 = jnp.bfloat16
F32 = jnp.float32
VMEM_BYTES = 60 * 1024 * 1024
FORWARD_VMEM_BYTES = 58 * 1024 * 1024
SMALL_VMEM_BYTES = 16 * 1024 * 1024


def bits_of(value):
    return [(value >> (8 - k)) & 1 for k in range(9)]


def join_bits(bits):
    value = bits[0]
    for bit in bits[1:]:
        value = value * 2 + bit
    return value


def split_voxel(column):
    ta, tb, tc, a1, a0, b1, b0, c1, c0 = bits_of(column)
    return join_bits([a1, a0, ta, b1, b0, tb, c1, c0, tc])


def octant_voxel(column):
    oa, ob, oc, a1, a0, b1, b0, c1, c0 = bits_of(column)
    return join_bits([oa, a1, a0, ob, b1, b0, oc, c1, c0])


def picker(voxel_of, shape=(VOX, VOX), start=(0, 0), flip=False):
    row = lax.broadcasted_iota(jnp.int32, shape, 0) + start[0]
    column = lax.broadcasted_iota(jnp.int32, shape, 1) + start[1]
    return (column == voxel_of(row) if flip else row == voxel_of(column)).astype(BF16)


def dot(a, b):
    return jnp.dot(a, b, preferred_element_type=F32)


def dot_nt(a, b):
    return lax.dot_general(a, b, (((1,), (1,)), ((), ())), preferred_element_type=F32)


def pack_kernel(lane_tiles, parents, cot, msg, kids_out, kids):
    devices = msg.shape[0]
    slots = cot.shape[0]

    def find(g, found):
        kids[found] = parents[0, g]
        return found + (parents[1, g] == 0).astype(jnp.int32)

    lax.fori_loop(0, parents.shape[1], find, jnp.int32(0), unroll=4)
    lane = lax.broadcasted_iota(jnp.int32, (LABEL_ROWS, LANES), 1)
    label = jnp.zeros((LABEL_ROWS, LANES), jnp.int32)
    for q in range(kids_out.shape[0]):
        kids_out[q] = kids[q]
        label = jnp.where(lane == q, kids[q], label)
    label = label.astype(F32).astype(BF16)
    for j in range(devices):
        msg[j, slots * lane_tiles * ROWS :] = label
    per_row = VOX // (LANES * lane_tiles)
    for j in range(devices):
        chan, part = j // per_row, j % per_row
        for q in range(slots):
            for lt in range(lane_tiles):
                lane = (part * lane_tiles + lt) * LANES
                row = (q * lane_tiles + lt) * ROWS
                msg[j, row : row + ROWS] = cot[
                    q, chan * ROWS : (chan + 1) * ROWS, lane : lane + LANES
                ]


def table_kernel(
    place, counts, kids, neighbors, parents, feat, up, down, table, ordered,
    up_idx, up_far, down_idx, down_far, bricks, done, split, in_sem, out_sem,
):
    count, chans = feat.shape[:2]
    part = count // PARTS
    fetches = [
        pltpu.make_async_copy(
            feat.at[pl.ds(k * part, part)], bricks.at[pl.ds(k * part, part)], in_sem.at[k]
        )
        for k in range(PARTS)
    ]
    for fetch in fetches:
        fetch.start()
    base = place[0] * count
    table[4 * count] = place[0]
    for r in range(SEND + 1):
        up_idx[r] = 0
        down_idx[r] = 0
        up_far[r] = 2 * count
        down_far[r] = 2 * count
    split[...] = picker(split_voxel)

    def scan(g, found):
        n_up, n_down = found
        near_up, near_down = neighbors[0, g], neighbors[1, g]
        far_up, far_down = near_up - base - count, near_down - base + count
        goes_up = (near_up >= 0) & (far_up >= 0)
        goes_down = (near_down >= 0) & (far_down < count)
        up_idx[n_up] = g
        up_far[n_up] = jnp.where(goes_up, far_up, 2 * count)
        down_idx[n_down] = g
        down_far[n_down] = jnp.where(goes_down, far_down, 2 * count)
        q = jnp.int32(0)
        for k in range(1, kids.shape[0]):
            q += jnp.where(kids[k] == parents[0, g], k, 0)
        number = q * 8 + parents[1, g]
        table[number] = g
        table[count + number] = jnp.where(g < counts[0], g, count + SEND)
        return n_up + goes_up.astype(jnp.int32), n_down + goes_down.astype(jnp.int32)

    lax.fori_loop(0, count, scan, (jnp.int32(0), jnp.int32(0)), unroll=4)

    def rank(r, carry):
        for start, far, idx in ((2 * count, up_far, up_idx), (3 * count, down_far, down_idx)):
            earlier = jnp.int32(0)
            for other in range(SEND):
                earlier += (far[other] < far[r]).astype(jnp.int32)

            @pl.when(far[r] < count)
            def _():
                table[start + idx[r]] = count + earlier

        return carry

    lax.fori_loop(0, SEND, rank, jnp.int32(0))
    sends = []
    for k in range(PARTS):
        fetches[k].wait()
        rows = bricks[k * part : (k + 1) * part].reshape(part * chans, VOX)
        done[k * part : (k + 1) * part] = (
            dot(rows, split[...]).astype(BF16).reshape(part, chans, VOX)
        )
        sends.append(
            pltpu.make_async_copy(
                done.at[pl.ds(k * part, part)], ordered.at[pl.ds(k * part, part)], out_sem.at[k]
            )
        )
        sends[-1].start()
    low = low_lanes(chans)
    for r in range(SEND // 2):
        other = r + SEND // 2
        top = slice(VOX - LANES, VOX)
        up[r] = jnp.where(
            low,
            pltpu.roll(bricks[up_idx[r], :, top], LANES // 2, 1),
            bricks[up_idx[other], :, top],
        )
        down[r] = jnp.where(
            low,
            bricks[down_idx[r], :, :LANES],
            pltpu.roll(bricks[down_idx[other], :, :LANES], LANES // 2, 1),
        )
    for send in sends:
        send.wait()


def route_kernel(kids, msg, pieces):
    devices, groups, lane_tiles = pieces.shape[:3]
    slots = groups
    for s in range(devices):
        for q in range(groups):
            kid = kids[s * groups + q]
            owner, slot = kid // slots, kid % slots
            for lt in range(lane_tiles):
                row = pl.multiple_of((slot * lane_tiles + lt) * ROWS, ROWS)
                pieces[s, q, lt] = msg[owner, pl.ds(row, ROWS), :]


def place_arrivals(above, below, bricks, count):
    chans = bricks.shape[1]
    half = VOX // 2
    side = LANES // 2
    shape = (LANES, half)
    pairs = SEND // 2
    for k, shift in ((0, 0), (pairs, -side)):
        slots = slice(count + k, count + k + pairs)
        first = dot(
            above[...].reshape(pairs * chans, LANES), picker(split_voxel, shape, (shift, 0))
        )
        last = dot(
            below[...].reshape(pairs * chans, LANES),
            picker(split_voxel, shape, (VOX - side + shift, half)),
        )
        bricks[slots, :, :half] = first.astype(BF16).reshape(pairs, chans, half)
        bricks[slots, :, half:] = last.astype(BF16).reshape(pairs, chans, half)
    bricks[count + SEND] = jnp.zeros(bricks.shape[1:], BF16)


def sources(table, neighbors, number):
    count = neighbors.shape[1]
    g = table[number]
    found = []
    for d in range(6):
        near = neighbors[d, g]
        local = near - table[4 * count] * count
        if d == 0:
            local = jnp.where(local >= count, table[2 * count + g], local)
        if d == 1:
            local = jnp.where(local < 0, table[3 * count + g], local)
        found.append(jnp.where(near >= 0, local, count + SEND))
    found.append(table[count + number])
    return found


def shift_into(slots, bricks, views):
    chans = bricks.shape[1]
    tiles = VOX // LANES
    lane = lax.broadcasted_iota(jnp.int32, (chans, LANES), 1)
    low = lane < LANES // 2
    a = (lane // 16) % HALF
    b = (lane // 4) % HALF
    c = lane % HALF

    def tile(slot, t):
        return bricks[slot, :, t * LANES : (t + 1) * LANES]

    def turn(value, by):
        return pltpu.roll(value, by % LANES, 1)

    x = [tile(slots[6], t) for t in range(tiles)]
    for t in range(tiles):
        lanes = slice(t * LANES, (t + 1) * LANES)
        if t < 2:
            plus_a = x[t + 2]
            minus_a = jnp.where(a > 0, turn(x[t + 2], 16), turn(tile(slots[1], t + 2), -48))
        else:
            plus_a = jnp.where(a < HALF - 1, turn(x[t - 2], -16), turn(tile(slots[0], t - 2), 48))
            minus_a = x[t - 2]
        if t % 2 == 0:
            plus_b = x[t + 1]
            minus_b = jnp.where(b > 0, turn(x[t + 1], 4), turn(tile(slots[3], t + 1), -12))
        else:
            plus_b = jnp.where(b < HALF - 1, turn(x[t - 1], -4), turn(tile(slots[2], t - 1), 12))
            minus_b = x[t - 1]
        swapped = turn(x[t], 64)
        plus_c = jnp.where(c < HALF - 1, turn(x[t], 63), turn(tile(slots[4], t), 67))
        minus_c = jnp.where(c > 0, turn(x[t], -63), turn(tile(slots[5], t), -67))
        out = [plus_a, minus_a, plus_b, minus_b, jnp.where(low, swapped, plus_c),
               jnp.where(low, minus_c, swapped), x[t]]
        for d in range(7):
            views[d * chans : (d + 1) * chans, lanes] = out[d]


def low_lanes(rows):
    return lax.broadcasted_iota(jnp.int32, (rows, LANES), 1) < LANES // 2


def forward_kernel(
    lane_tiles, table_hbm, neighbors_hbm, feat, w_conv_hbm, w_res_hbm, w_mix_hbm,
    above_hbm, below_hbm,
    parts_out, slope_out, coarse_out, piece_out,
    bricks, views, place, w_conv, w_res, w_mix, conv_cat, res_cat, octants,
    table, neighbors, above, below, sem,
):
    q = pl.program_id(0)
    groups = pl.num_programs(0) - 1
    count, chans = feat.shape[:2]

    @pl.when(q == 0)
    def _():
        copies = [
            pltpu.make_async_copy(source, target, sem.at[k])
            for k, (source, target) in enumerate((
                (above_hbm, above), (below_hbm, below), (w_conv_hbm, w_conv),
                (w_res_hbm, w_res), (w_mix_hbm, w_mix), (table_hbm, table),
                (neighbors_hbm, neighbors), (feat, bricks.at[pl.ds(0, count)]),
            ))
        ]
        for copy in copies:
            copy.start()
        place[...] = picker(octant_voxel, flip=True)
        for copy in copies[:-1]:
            copy.wait()
        place_arrivals(above, below, bricks, count)
        for d in range(7):
            conv_cat[:, d * chans : (d + 1) * chans] = w_conv[d]
        res_cat[...] = w_res[...].T
        copies[-1].wait()

    low_half = low_lanes(chans)

    def finish():
        coarse = dot(octants[...], place[...]).astype(BF16)
        coarse_out[0] = coarse
        mixed = dot(w_mix[...], coarse).astype(BF16)
        per_row = VOX // (LANES * lane_tiles)
        for j in range(piece_out.shape[0]):
            chan, part = j // per_row, j % per_row
            for lt in range(lane_tiles):
                lane = (part * lane_tiles + lt) * LANES
                piece_out[j, 0, lt] = mixed[chan * ROWS : (chan + 1) * ROWS, lane : lane + LANES]

    def restrict(first):
        acts = []
        for k in range(first, first + 4):
            shift_into(sources(table, neighbors, q * 8 + k), bricks, views.at[k])
            hidden = dot(conv_cat[...], views[k])
            sig = 0.5 + 0.5 * jnp.tanh(0.5 * hidden)
            act = hidden * sig
            slope_out[0, k * chans : (k + 1) * chans, :] = (sig + act * (1.0 - sig)).astype(BF16)
            acts.append(act.astype(BF16))
        for k in range(0, 4, 2):
            lanes = slice((first + k) * (LANES // 2), (first + k + 2) * (LANES // 2))
            for t in range(4):
                one = acts[k][:, t * LANES : (t + 1) * LANES]
                two = acts[k + 1][:, t * LANES : (t + 1) * LANES]
                parts_out[0, 2 * t * chans : (2 * t + 1) * chans, lanes] = jnp.where(
                    low_half, one, pltpu.roll(two, LANES // 2, 1)
                )
                parts_out[0, (2 * t + 1) * chans : (2 * t + 2) * chans, lanes] = jnp.where(
                    low_half, pltpu.roll(one, LANES // 2, 1), two
                )
        lanes = slice(first * (LANES // 2), (first + 4) * (LANES // 2))
        return dot(res_cat[...], parts_out[0, :, lanes]).astype(BF16)

    @pl.when(q < groups)
    def _():
        finish()
        halves = [restrict(0), restrict(4)]
        octants[...] = jnp.concatenate(halves, axis=1)

    @pl.when(q == groups)
    def _():
        finish()


def backward_kernel(
    lane_tiles, scale, table, neighbors, feat, above, below, pieces, parts, slope, coarse,
    w_mix, w_res, own, other,
    bricks, views, cot, grad_parts, grad_rows, unplace, mix_t, conv_sum, res_sum, mix_sum, packed,
    sem,
):
    q = pl.program_id(0)
    count, chans = feat.shape[:2]
    wide = coarse.shape[1]
    fetch = pltpu.make_async_copy(feat, bricks.at[pl.ds(0, count)], sem)

    @pl.when(q == 0)
    def _():
        fetch.start()
        place_arrivals(above, below, bricks, count)
        unplace[...] = picker(octant_voxel)
        mix_t[...] = w_mix[...].T
        conv_sum[...] = jnp.zeros_like(conv_sum)
        res_sum[...] = jnp.zeros_like(res_sum)
        mix_sum[...] = jnp.zeros_like(mix_sum)
        fetch.wait()

    per_row = VOX // (LANES * lane_tiles)
    for j in range(pieces.shape[0]):
        chan, part = j // per_row, j % per_row
        for lt in range(lane_tiles):
            lane = (part * lane_tiles + lt) * LANES
            cot[chan * ROWS : (chan + 1) * ROWS, lane : lane + LANES] = pieces[j, 0, lt]
    cots = cot[...]
    grad_coarse = (scale * dot(mix_t[...], cots)).astype(BF16)
    grad_fine = dot(grad_coarse, unplace[...]).astype(BF16)
    mix_sum[...] += dot_nt(cots, coarse[0])
    res_sum[...] += dot_nt(parts[0], grad_fine)
    grad_parts[...] = dot(w_res[...], grad_fine)
    low_half = low_lanes(chans)
    for r in range(4):
        for t in range(4):
            cols = slice(r * LANES, (r + 1) * LANES)
            lanes = slice(t * LANES, (t + 1) * LANES)
            one = grad_parts[2 * t * chans : (2 * t + 1) * chans, cols]
            two = grad_parts[(2 * t + 1) * chans : (2 * t + 2) * chans, cols]
            first = slice(2 * r * chans, (2 * r + 1) * chans)
            second = slice((2 * r + 1) * chans, (2 * r + 2) * chans)
            grad_rows[first, lanes] = (
                jnp.where(low_half, one, pltpu.roll(two, LANES // 2, 1))
                * slope[0, first, lanes].astype(F32)
            ).astype(BF16)
            grad_rows[second, lanes] = (
                jnp.where(low_half, pltpu.roll(one, LANES // 2, 1), two)
                * slope[0, second, lanes].astype(F32)
            ).astype(BF16)

    total = None
    for k in range(8):
        shift_into(sources(table, neighbors, q * 8 + k), bricks, views.at[k])
        term = dot_nt(grad_rows[k * chans : (k + 1) * chans, :], views[k])
        total = term if total is None else total + term
    conv_sum[:, : 7 * chans] += total

    @pl.when(q == pl.num_programs(0) - 1)
    def _():
        packed[0:wide] = scale * mix_sum[...]
        at = wide
        packed[at : at + 8 * chans] = res_sum[...]
        at += 8 * chans
        for t in range(4):
            packed[at : at + chans] = conv_sum[:, t * LANES : (t + 1) * LANES]
            at += chans
        if at < packed.shape[0]:
            packed[at:] = jnp.zeros((packed.shape[0] - at, LANES), F32)
        chips, rows = own.shape[:2]
        core = table[4 * count] % 2
        for c in range(chips):
            first = pl.multiple_of((2 * c + core) * rows, 8)
            second = pl.multiple_of((2 * c + 1 - core) * rows, 8)
            own[c] = packed[pl.ds(first, rows), :]
            other[c] = packed[pl.ds(second, rows), :]


def join_kernel(kids, shares, pieces, msg):
    devices, groups, lane_tiles = pieces.shape[:3]
    slots = groups
    body_rows = slots * lane_tiles * ROWS
    for s in range(devices):
        for q in range(groups):
            kid = kids[s * groups + q]
            owner, slot = kid // slots, kid % slots
            for lt in range(lane_tiles):
                row = pl.multiple_of((slot * lane_tiles + lt) * ROWS, ROWS)
                msg[owner, pl.ds(row, ROWS), :] = pieces[s, q, lt]
    total = jnp.sum(shares[...].astype(F32), axis=0).astype(BF16)
    for j in range(devices):
        msg[j, body_rows:] = total


def unpack_kernel(lane_tiles, msg, coarse_out, conv, res, mix, packed):
    devices, rows = msg.shape[:2]
    slots = coarse_out.shape[0]
    wide = mix.shape[0]
    chans = conv.shape[1]
    half = LANES // 2
    body_rows = slots * lane_tiles * ROWS
    share = rows - body_rows
    for j in range(devices):
        packed[j * share : (j + 1) * share] = msg[j, body_rows:].astype(F32)
    mix[...] = packed[0:wide]
    at = wide
    for t in range(8):
        res[t] = packed[at : at + chans]
        at += chans
    for t in range(4):
        block = packed[at : at + chans]
        conv[2 * t] = block[:, :half]
        if 2 * t + 1 < 7:
            conv[2 * t + 1] = block[:, half:]
        at += chans
    per_row = VOX // (LANES * lane_tiles)
    for j in range(devices):
        chan, part = j // per_row, j % per_row
        for q in range(slots):
            for lt in range(lane_tiles):
                row = (q * lane_tiles + lt) * ROWS
                lane = (part * lane_tiles + lt) * LANES
                coarse_out[q, chan * ROWS : (chan + 1) * ROWS, lane : lane + LANES] = msg[
                    j, row : row + ROWS
                ]


def kernel_call(kernel, out_shape, grid_spec, flops, moved, vmem=VMEM_BYTES):
    return pl.pallas_call(
        kernel,
        out_shape=out_shape,
        grid_spec=grid_spec,
        compiler_params=pltpu.CompilerParams(vmem_limit_bytes=vmem),
        cost_estimate=pl.CostEstimate(flops=flops, bytes_accessed=moved, transcendentals=0),
    )


def body(features, counts, neighbors, parents, w_conv, w_restrict, w_mix, cotangent):
    devices = lax.axis_size("space")
    position = lax.axis_index("space").astype(jnp.int32).reshape(1)
    slots, wide = cotangent.shape[:2]
    count, chans = features.shape[:2]
    lane_tiles = VOX * 8 // devices // LANES
    tiles = slots * lane_tiles
    groups = count // 8
    whole = lambda shape: pl.BlockSpec(shape, lambda *_: (0,) * len(shape))
    any_spec = pl.BlockSpec(memory_space=pl.ANY)
    smem_spec = pl.BlockSpec(memory_space=pltpu.SMEM)
    smem = lambda size: pltpu.SMEM((size,), jnp.int32)
    vmem = pltpu.VMEM
    ints = lambda size: jax.ShapeDtypeStruct((size,), jnp.int32)

    message_shape = (devices, tiles * ROWS + LABEL_ROWS, LANES)
    message, kids = kernel_call(
        functools.partial(pack_kernel, lane_tiles),
        (jax.ShapeDtypeStruct(message_shape, BF16), ints(groups)),
        pl.GridSpec(
            grid=(1,),
            in_specs=[smem_spec, whole(cotangent.shape)],
            out_specs=[whole(message_shape), smem_spec],
            scratch_shapes=[smem(groups + 1)],
        ),
        1000, 2**20,
    )(parents.T, cotangent)
    spread = lax.all_to_all(message, "space", split_axis=0, concat_axis=0, tiled=True)

    plane = jax.ShapeDtypeStruct((SEND // 2, chans, LANES), BF16)
    up, down, table, ordered = kernel_call(
        table_kernel,
        (plane, plane, ints(4 * count + 1), jax.ShapeDtypeStruct(features.shape, BF16)),
        pl.GridSpec(
            grid=(1,),
            in_specs=[smem_spec] * 5 + [any_spec],
            out_specs=[whole(plane.shape)] * 2 + [smem_spec, any_spec],
            scratch_shapes=[smem(SEND + 1)] * 4
            + [vmem(features.shape, BF16), vmem(features.shape, BF16), vmem((VOX, VOX), BF16),
               pltpu.SemaphoreType.DMA((PARTS,)), pltpu.SemaphoreType.DMA((PARTS,))],
        ),
        1000, 2**20,
    )(position, counts, kids, neighbors.T, parents.T, features)
    below = lax.ppermute(up, "space", [(i, i + 1) for i in range(devices - 1)])
    above = lax.ppermute(down, "space", [(i + 1, i) for i in range(devices - 1)])

    all_kids = spread[:, tiles * ROWS, :groups].astype(jnp.int32).reshape(-1)
    piece_shape = (devices, groups, lane_tiles, ROWS, LANES)
    forward_tiles = kernel_call(
        route_kernel,
        jax.ShapeDtypeStruct(piece_shape, BF16),
        pl.GridSpec(
            grid=(1,),
            in_specs=[smem_spec, whole(message_shape)],
            out_specs=whole(piece_shape),
        ),
        1000, 2**20, SMALL_VMEM_BYTES,
    )(all_kids, spread)
    forward_tiles, above, below = lax.optimization_barrier((forward_tiles, above, below))
    cot_pieces = lax.all_to_all(forward_tiles, "space", split_axis=0, concat_axis=0, tiled=True)

    res_rows = w_restrict.transpose(0, 2, 1).reshape(8 * chans, wide)
    scalars = (table, neighbors.T)
    brick_scratch = vmem((count + SEND + 1, chans, VOX), BF16)
    view_scratch = vmem((8, 7 * chans, VOX), BF16)
    per_group = lambda *shape: pl.BlockSpec((1,) + shape, lambda q: (q,) + (0,) * len(shape))
    piece_spec = pl.BlockSpec((devices, 1, lane_tiles, ROWS, LANES), lambda q: (0, q, 0, 0, 0))
    parts, slope, coarse, pieces = kernel_call(
        functools.partial(forward_kernel, lane_tiles),
        (
            jax.ShapeDtypeStruct((groups, 8 * chans, VOX), BF16),
            jax.ShapeDtypeStruct((groups, 8 * chans, VOX), BF16),
            jax.ShapeDtypeStruct((groups, wide, VOX), BF16),
            jax.ShapeDtypeStruct(piece_shape, BF16),
        ),
        pl.GridSpec(
            grid=(groups + 1,),
            in_specs=[any_spec] * 8,
            out_specs=[
                pl.BlockSpec((1, 8 * chans, VOX), lambda q: (jnp.minimum(q, groups - 1), 0, 0)),
                pl.BlockSpec((1, 8 * chans, VOX), lambda q: (jnp.minimum(q, groups - 1), 0, 0)),
                pl.BlockSpec((1, wide, VOX), lambda q: (jnp.maximum(q - 1, 0), 0, 0)),
                pl.BlockSpec(
                    (devices, 1, lane_tiles, ROWS, LANES),
                    lambda q: (0, jnp.maximum(q - 1, 0), 0, 0, 0),
                ),
            ],
            scratch_shapes=[
                brick_scratch, view_scratch, vmem((VOX, VOX), BF16), vmem(w_conv.shape, BF16),
                vmem(res_rows.shape, BF16), vmem(w_mix.shape, BF16),
                vmem((chans, 7 * chans), BF16), vmem((wide, 8 * chans), BF16),
                vmem((wide, VOX), BF16), smem(4 * count + 1),
                pltpu.SMEM((6, count), jnp.int32), vmem(plane.shape, BF16),
                vmem(plane.shape, BF16), pltpu.SemaphoreType.DMA((8,)),
            ],
        ),
        16 * 10**9, 16 * 2**20, FORWARD_VMEM_BYTES,
    )(*scalars, ordered, w_conv, res_rows, w_mix, above, below)
    returned = lax.all_to_all(pieces, "space", split_axis=0, concat_axis=0, tiled=True)

    scale = 1.0 / math.sqrt(devices * slots * VOX)
    used = wide + 8 * chans + 4 * chans
    rows = -(-used // (devices * 8)) * 8
    half = jax.ShapeDtypeStruct((devices // 2, rows, LANES), F32)
    own, other = kernel_call(
        functools.partial(backward_kernel, lane_tiles, scale),
        (half, half),
        pl.GridSpec(
            grid=(groups,),
            in_specs=[smem_spec] * 2 + [any_spec] + [whole(plane.shape)] * 2
            + [piece_spec, per_group(8 * chans, VOX), per_group(8 * chans, VOX),
               per_group(wide, VOX), whole(w_mix.shape), whole(res_rows.shape)],
            out_specs=[whole(half.shape)] * 2,
            scratch_shapes=[
                brick_scratch, view_scratch, vmem((wide, VOX), BF16),
                vmem((8 * chans, VOX), F32), vmem((8 * chans, VOX), BF16), vmem((VOX, VOX), BF16),
                vmem((wide, wide), BF16), vmem((chans, 8 * chans), F32),
                vmem((8 * chans, wide), F32), vmem((wide, wide), F32),
                vmem((devices * rows, LANES), F32), pltpu.SemaphoreType.DMA,
            ],
        ),
        16 * 10**9, 16 * 2**20,
    )(*scalars, ordered, above, below, cot_pieces, parts, slope, coarse, w_mix, res_rows)

    came = lax.ppermute(other, "space", [(i, i ^ 1) for i in range(devices)])
    paired = (own + came).astype(BF16)
    shares = lax.all_to_all(
        paired, "space", split_axis=0, concat_axis=0, tiled=True,
        axis_index_groups=[list(range(core, devices, 2)) for core in range(2)],
    )

    joined_shape = (devices, tiles * ROWS + rows, LANES)
    joined = kernel_call(
        join_kernel,
        jax.ShapeDtypeStruct(joined_shape, BF16),
        pl.GridSpec(
            grid=(1,),
            in_specs=[smem_spec, whole(shares.shape), whole(piece_shape)],
            out_specs=whole(joined_shape),
        ),
        1000, 2**20, SMALL_VMEM_BYTES,
    )(all_kids, shares, returned)
    finished = lax.all_to_all(joined, "space", split_axis=0, concat_axis=0, tiled=True)

    coarse_out, grad_conv, grad_res, grad_mix = kernel_call(
        functools.partial(unpack_kernel, lane_tiles),
        (
            jax.ShapeDtypeStruct((slots, wide, VOX), BF16),
            jax.ShapeDtypeStruct((7, chans, chans), F32),
            jax.ShapeDtypeStruct((8, chans, wide), F32),
            jax.ShapeDtypeStruct((wide, wide), F32),
        ),
        pl.GridSpec(
            grid=(1,),
            in_specs=[whole(joined_shape)],
            out_specs=[whole((slots, wide, VOX)), whole((7, chans, chans)),
                       whole((8, chans, wide)), whole((wide, wide))],
            scratch_shapes=[vmem((devices * rows, LANES), F32)],
        ),
        1000, 2 * 2**20, SMALL_VMEM_BYTES,
    )(finished)
    return coarse_out, grad_conv, grad_res.transpose(0, 2, 1), grad_mix


def solution(mesh):
    return jax.shard_map(
        body,
        mesh=mesh,
        in_specs=(
            P(("groups", "space"), None, None),
            P(("groups", "space")),
            P(("groups", "space"), None),
            P(("groups", "space"), None),
            P(),
            P(),
            P(),
            P(("groups", "space"), None, None),
        ),
        out_specs=(
            P(("groups", "space"), None, None),
            P("groups", None, None),
            P("groups", None, None),
            P("groups", None),
        ),
        check_vma=False,
    )
```

```python
import functools
import math

import jax
import jax.numpy as jnp
from jax import lax
from jax.experimental import pallas as pl
from jax.experimental.pallas import tpu as pltpu
from jax.sharding import PartitionSpec as P

EDGE = 8
HALF = EDGE // 2
VOX = EDGE**3
LANES = 128
ROWS = 16
LABEL_ROWS = 8
SEND = 8
PARTS = 4
BF16 = jnp.bfloat16
F32 = jnp.float32
VMEM_BYTES = 60 * 1024 * 1024
SMALL_VMEM_BYTES = 16 * 1024 * 1024


def bits_of(value):
    return [(value >> (8 - k)) & 1 for k in range(9)]


def join_bits(bits):
    value = bits[0]
    for bit in bits[1:]:
        value = value * 2 + bit
    return value


def split_voxel(column):
    ta, tb, tc, a1, a0, b1, b0, c1, c0 = bits_of(column)
    return join_bits([a1, a0, ta, b1, b0, tb, c1, c0, tc])


def octant_voxel(column):
    oa, ob, oc, a1, a0, b1, b0, c1, c0 = bits_of(column)
    return join_bits([oa, a1, a0, ob, b1, b0, oc, c1, c0])


def picker(voxel_of, shape=(VOX, VOX), start=(0, 0), flip=False):
    row = lax.broadcasted_iota(jnp.int32, shape, 0) + start[0]
    column = lax.broadcasted_iota(jnp.int32, shape, 1) + start[1]
    return (column == voxel_of(row) if flip else row == voxel_of(column)).astype(BF16)


def dot(a, b):
    return jnp.dot(a, b, preferred_element_type=F32)


def dot_nt(a, b):
    return lax.dot_general(a, b, (((1,), (1,)), ((), ())), preferred_element_type=F32)


def pack_kernel(lane_tiles, parents, cot, msg, kids_out, kids):
    devices = msg.shape[0]
    slots = cot.shape[0]

    def find(g, found):
        kids[found] = parents[0, g]
        return found + (parents[1, g] == 0).astype(jnp.int32)

    lax.fori_loop(0, parents.shape[1], find, jnp.int32(0), unroll=4)
    lane = lax.broadcasted_iota(jnp.int32, (LABEL_ROWS, LANES), 1)
    label = jnp.zeros((LABEL_ROWS, LANES), jnp.int32)
    for q in range(kids_out.shape[0]):
        kids_out[q] = kids[q]
        label = jnp.where(lane == q, kids[q], label)
    label = label.astype(F32).astype(BF16)
    for j in range(devices):
        msg[j, slots * lane_tiles * ROWS :] = label
    per_row = VOX // (LANES * lane_tiles)
    for j in range(devices):
        chan, part = j // per_row, j % per_row
        for q in range(slots):
            for lt in range(lane_tiles):
                lane = (part * lane_tiles + lt) * LANES
                row = (q * lane_tiles + lt) * ROWS
                msg[j, row : row + ROWS] = cot[
                    q, chan * ROWS : (chan + 1) * ROWS, lane : lane + LANES
                ]


def table_kernel(
    place, counts, kids, neighbors, parents, feat, up, down, table, ordered,
    up_idx, up_far, down_idx, down_far, bricks, done, split, in_sem, out_sem,
):
    count, chans = feat.shape[:2]
    part = count // PARTS
    fetches = [
        pltpu.make_async_copy(
            feat.at[pl.ds(k * part, part)], bricks.at[pl.ds(k * part, part)], in_sem.at[k]
        )
        for k in range(PARTS)
    ]
    for fetch in fetches:
        fetch.start()
    base = place[0] * count
    table[4 * count] = place[0]
    for r in range(SEND + 1):
        up_idx[r] = 0
        down_idx[r] = 0
        up_far[r] = 2 * count
        down_far[r] = 2 * count
    split[...] = picker(split_voxel)

    def scan(g, found):
        n_up, n_down = found
        near_up, near_down = neighbors[0, g], neighbors[1, g]
        far_up, far_down = near_up - base - count, near_down - base + count
        goes_up = (near_up >= 0) & (far_up >= 0)
        goes_down = (near_down >= 0) & (far_down < count)
        up_idx[n_up] = g
        up_far[n_up] = jnp.where(goes_up, far_up, 2 * count)
        down_idx[n_down] = g
        down_far[n_down] = jnp.where(goes_down, far_down, 2 * count)
        q = jnp.int32(0)
        for k in range(1, kids.shape[0]):
            q += jnp.where(kids[k] == parents[0, g], k, 0)
        number = q * 8 + parents[1, g]
        table[number] = g
        table[count + number] = jnp.where(g < counts[0], g, count + SEND)
        return n_up + goes_up.astype(jnp.int32), n_down + goes_down.astype(jnp.int32)

    lax.fori_loop(0, count, scan, (jnp.int32(0), jnp.int32(0)), unroll=4)

    def rank(r, carry):
        for start, far, idx in ((2 * count, up_far, up_idx), (3 * count, down_far, down_idx)):
            earlier = jnp.int32(0)
            for other in range(SEND):
                earlier += (far[other] < far[r]).astype(jnp.int32)

            @pl.when(far[r] < count)
            def _():
                table[start + idx[r]] = count + earlier

        return carry

    lax.fori_loop(0, SEND, rank, jnp.int32(0))
    sends = []
    for k in range(PARTS):
        fetches[k].wait()
        rows = bricks[k * part : (k + 1) * part].reshape(part * chans, VOX)
        done[k * part : (k + 1) * part] = (
            dot(rows, split[...]).astype(BF16).reshape(part, chans, VOX)
        )
        sends.append(
            pltpu.make_async_copy(
                done.at[pl.ds(k * part, part)], ordered.at[pl.ds(k * part, part)], out_sem.at[k]
            )
        )
        sends[-1].start()
    low = low_lanes(chans)
    for r in range(SEND // 2):
        other = r + SEND // 2
        top = slice(VOX - LANES, VOX)
        up[r] = jnp.where(
            low,
            pltpu.roll(bricks[up_idx[r], :, top], LANES // 2, 1),
            bricks[up_idx[other], :, top],
        )
        down[r] = jnp.where(
            low,
            bricks[down_idx[r], :, :LANES],
            pltpu.roll(bricks[down_idx[other], :, :LANES], LANES // 2, 1),
        )
    for send in sends:
        send.wait()


def route_kernel(kids, msg, pieces):
    devices, groups, lane_tiles = pieces.shape[:3]
    slots = groups
    for s in range(devices):
        for q in range(groups):
            kid = kids[s * groups + q]
            owner, slot = kid // slots, kid % slots
            for lt in range(lane_tiles):
                row = pl.multiple_of((slot * lane_tiles + lt) * ROWS, ROWS)
                pieces[s, q, lt] = msg[owner, pl.ds(row, ROWS), :]


def place_arrivals(above, below, bricks, count):
    chans = bricks.shape[1]
    half = VOX // 2
    side = LANES // 2
    shape = (LANES, half)
    pairs = SEND // 2
    for k, shift in ((0, 0), (pairs, -side)):
        slots = slice(count + k, count + k + pairs)
        first = dot(
            above[...].reshape(pairs * chans, LANES), picker(split_voxel, shape, (shift, 0))
        )
        last = dot(
            below[...].reshape(pairs * chans, LANES),
            picker(split_voxel, shape, (VOX - side + shift, half)),
        )
        bricks[slots, :, :half] = first.astype(BF16).reshape(pairs, chans, half)
        bricks[slots, :, half:] = last.astype(BF16).reshape(pairs, chans, half)
    bricks[count + SEND] = jnp.zeros(bricks.shape[1:], BF16)


def sources(table, neighbors, number):
    count = neighbors.shape[1]
    g = table[number]
    found = []
    for d in range(6):
        near = neighbors[d, g]
        local = near - table[4 * count] * count
        if d == 0:
            local = jnp.where(local >= count, table[2 * count + g], local)
        if d == 1:
            local = jnp.where(local < 0, table[3 * count + g], local)
        found.append(jnp.where(near >= 0, local, count + SEND))
    found.append(table[count + number])
    return found


def shift_into(slots, bricks, views):
    chans = bricks.shape[1]
    tiles = VOX // LANES
    lane = lax.broadcasted_iota(jnp.int32, (chans, LANES), 1)
    low = lane < LANES // 2
    a = (lane // 16) % HALF
    b = (lane // 4) % HALF
    c = lane % HALF

    def tile(slot, t):
        return bricks[slot, :, t * LANES : (t + 1) * LANES]

    def turn(value, by):
        return pltpu.roll(value, by % LANES, 1)

    x = [tile(slots[6], t) for t in range(tiles)]
    for t in range(tiles):
        lanes = slice(t * LANES, (t + 1) * LANES)
        if t < 2:
            plus_a = x[t + 2]
            minus_a = jnp.where(a > 0, turn(x[t + 2], 16), turn(tile(slots[1], t + 2), -48))
        else:
            plus_a = jnp.where(a < HALF - 1, turn(x[t - 2], -16), turn(tile(slots[0], t - 2), 48))
            minus_a = x[t - 2]
        if t % 2 == 0:
            plus_b = x[t + 1]
            minus_b = jnp.where(b > 0, turn(x[t + 1], 4), turn(tile(slots[3], t + 1), -12))
        else:
            plus_b = jnp.where(b < HALF - 1, turn(x[t - 1], -4), turn(tile(slots[2], t - 1), 12))
            minus_b = x[t - 1]
        swapped = turn(x[t], 64)
        plus_c = jnp.where(c < HALF - 1, turn(x[t], 63), turn(tile(slots[4], t), 67))
        minus_c = jnp.where(c > 0, turn(x[t], -63), turn(tile(slots[5], t), -67))
        out = [plus_a, minus_a, plus_b, minus_b, jnp.where(low, swapped, plus_c),
               jnp.where(low, minus_c, swapped), x[t]]
        for d in range(7):
            views[d * chans : (d + 1) * chans, lanes] = out[d]


def low_lanes(rows):
    return lax.broadcasted_iota(jnp.int32, (rows, LANES), 1) < LANES // 2


def forward_kernel(
    lane_tiles, table_hbm, neighbors_hbm, feat, w_conv_hbm, w_res_hbm, w_mix_hbm,
    above_hbm, below_hbm,
    parts_out, slope_out, coarse_out, piece_out,
    bricks, views, place, w_conv, w_res, w_mix, conv_cat, res_cat, octants,
    table, neighbors, above, below, sem,
):
    q = pl.program_id(0)
    groups = pl.num_programs(0) - 1
    count, chans = feat.shape[:2]

    @pl.when(q == 0)
    def _():
        copies = [
            pltpu.make_async_copy(source, target, sem.at[k])
            for k, (source, target) in enumerate((
                (above_hbm, above), (below_hbm, below), (w_conv_hbm, w_conv),
                (w_res_hbm, w_res), (w_mix_hbm, w_mix), (table_hbm, table),
                (neighbors_hbm, neighbors), (feat, bricks.at[pl.ds(0, count)]),
            ))
        ]
        for copy in copies:
            copy.start()
        place[...] = picker(octant_voxel, flip=True)
        for copy in copies[:-1]:
            copy.wait()
        place_arrivals(above, below, bricks, count)
        for d in range(7):
            conv_cat[:, d * chans : (d + 1) * chans] = w_conv[d]
        res_cat[...] = w_res[...].T
        copies[-1].wait()

    low_half = low_lanes(chans)

    def finish():
        coarse = dot(octants[...], place[...]).astype(BF16)
        coarse_out[0] = coarse
        mixed = dot(w_mix[...], coarse).astype(BF16)
        per_row = VOX // (LANES * lane_tiles)
        for j in range(piece_out.shape[0]):
            chan, part = j // per_row, j % per_row
            for lt in range(lane_tiles):
                lane = (part * lane_tiles + lt) * LANES
                piece_out[j, 0, lt] = mixed[chan * ROWS : (chan + 1) * ROWS, lane : lane + LANES]

    def restrict(first):
        acts = []
        for k in range(first, first + 4):
            shift_into(sources(table, neighbors, q * 8 + k), bricks, views.at[k])
            hidden = dot(conv_cat[...], views[k])
            sig = 0.5 + 0.5 * jnp.tanh(0.5 * hidden)
            act = hidden * sig
            slope_out[0, k * chans : (k + 1) * chans, :] = (sig + act * (1.0 - sig)).astype(BF16)
            acts.append(act.astype(BF16))
        for k in range(0, 4, 2):
            lanes = slice((first + k) * (LANES // 2), (first + k + 2) * (LANES // 2))
            for t in range(4):
                one = acts[k][:, t * LANES : (t + 1) * LANES]
                two = acts[k + 1][:, t * LANES : (t + 1) * LANES]
                parts_out[0, 2 * t * chans : (2 * t + 1) * chans, lanes] = jnp.where(
                    low_half, one, pltpu.roll(two, LANES // 2, 1)
                )
                parts_out[0, (2 * t + 1) * chans : (2 * t + 2) * chans, lanes] = jnp.where(
                    low_half, pltpu.roll(one, LANES // 2, 1), two
                )
        lanes = slice(first * (LANES // 2), (first + 4) * (LANES // 2))
        return dot(res_cat[...], parts_out[0, :, lanes]).astype(BF16)

    @pl.when(q < groups)
    def _():
        finish()
        halves = [restrict(0), restrict(4)]
        octants[...] = jnp.concatenate(halves, axis=1)

    @pl.when(q == groups)
    def _():
        finish()


def backward_kernel(
    lane_tiles, scale, table_hbm, neighbors_hbm, feat, above_hbm, below_hbm, pieces, parts, slope,
    coarse, w_mix, w_res, own, other,
    bricks, views, cot, grad_parts, grad_rows, unplace, mix_t, conv_sum, res_sum, mix_sum, packed,
    table, neighbors, above, below, sem,
):
    q = pl.program_id(0)
    count, chans = feat.shape[:2]
    wide = coarse.shape[1]
    part = count // PARTS

    def start_fetches():
        pairs = [(table_hbm, table), (neighbors_hbm, neighbors), (above_hbm, above),
                 (below_hbm, below)]
        for k in range(PARTS):
            slots = pl.ds(k * part, part)
            pairs.append((feat.at[slots], bricks.at[slots]))
        copies = [
            pltpu.make_async_copy(source, target, sem.at[k])
            for k, (source, target) in enumerate(pairs)
        ]
        for copy in copies:
            copy.start()
        return copies

    def gradients():
        per_row = VOX // (LANES * lane_tiles)
        for j in range(pieces.shape[0]):
            chan, half = j // per_row, j % per_row
            for lt in range(lane_tiles):
                lane = (half * lane_tiles + lt) * LANES
                cot[chan * ROWS : (chan + 1) * ROWS, lane : lane + LANES] = pieces[j, 0, lt]
        cots = cot[...]
        grad_coarse = (scale * dot(mix_t[...], cots)).astype(BF16)
        grad_fine = dot(grad_coarse, unplace[...]).astype(BF16)
        mix_sum[...] += dot_nt(cots, coarse[0])
        res_sum[...] += dot_nt(parts[0], grad_fine)
        grad_parts[...] = dot(w_res[...], grad_fine)
        low_half = low_lanes(chans)
        for r in range(4):
            for t in range(4):
                cols = slice(r * LANES, (r + 1) * LANES)
                lanes = slice(t * LANES, (t + 1) * LANES)
                one = grad_parts[2 * t * chans : (2 * t + 1) * chans, cols]
                two = grad_parts[(2 * t + 1) * chans : (2 * t + 2) * chans, cols]
                first = slice(2 * r * chans, (2 * r + 1) * chans)
                second = slice((2 * r + 1) * chans, (2 * r + 2) * chans)
                grad_rows[first, lanes] = (
                    jnp.where(low_half, one, pltpu.roll(two, LANES // 2, 1))
                    * slope[0, first, lanes].astype(F32)
                ).astype(BF16)
                grad_rows[second, lanes] = (
                    jnp.where(low_half, pltpu.roll(one, LANES // 2, 1), two)
                    * slope[0, second, lanes].astype(F32)
                ).astype(BF16)

    def convolution():
        total = None
        for k in range(8):
            shift_into(sources(table, neighbors, q * 8 + k), bricks, views.at[k])
            term = dot_nt(grad_rows[k * chans : (k + 1) * chans, :], views[k])
            total = term if total is None else total + term
        conv_sum[:, : 7 * chans] += total

    @pl.when(q == 0)
    def _():
        copies = start_fetches()
        unplace[...] = picker(octant_voxel)
        mix_t[...] = w_mix[...].T
        conv_sum[...] = jnp.zeros_like(conv_sum)
        res_sum[...] = jnp.zeros_like(res_sum)
        mix_sum[...] = jnp.zeros_like(mix_sum)
        gradients()
        for copy in copies:
            copy.wait()
        place_arrivals(above, below, bricks, count)
        convolution()

    @pl.when(q > 0)
    def _():
        gradients()
        convolution()

    @pl.when(q == pl.num_programs(0) - 1)
    def _():
        packed[0:wide] = scale * mix_sum[...]
        at = wide
        packed[at : at + 8 * chans] = res_sum[...]
        at += 8 * chans
        for t in range(4):
            packed[at : at + chans] = conv_sum[:, t * LANES : (t + 1) * LANES]
            at += chans
        if at < packed.shape[0]:
            packed[at:] = jnp.zeros((packed.shape[0] - at, LANES), F32)
        chips, rows = own.shape[:2]
        core = table[4 * count] % 2
        for c in range(chips):
            first = pl.multiple_of((2 * c + core) * rows, 8)
            second = pl.multiple_of((2 * c + 1 - core) * rows, 8)
            own[c] = packed[pl.ds(first, rows), :]
            other[c] = packed[pl.ds(second, rows), :]


def join_kernel(kids, shares, pieces, msg):
    devices, groups, lane_tiles = pieces.shape[:3]
    slots = groups
    body_rows = slots * lane_tiles * ROWS
    for s in range(devices):
        for q in range(groups):
            kid = kids[s * groups + q]
            owner, slot = kid // slots, kid % slots
            for lt in range(lane_tiles):
                row = pl.multiple_of((slot * lane_tiles + lt) * ROWS, ROWS)
                msg[owner, pl.ds(row, ROWS), :] = pieces[s, q, lt]
    total = jnp.sum(shares[...].astype(F32), axis=0).astype(BF16)
    for j in range(devices):
        msg[j, body_rows:] = total


def unpack_kernel(lane_tiles, msg, coarse_out, conv, res, mix, packed):
    devices, rows = msg.shape[:2]
    slots = coarse_out.shape[0]
    wide = mix.shape[0]
    chans = conv.shape[1]
    half = LANES // 2
    body_rows = slots * lane_tiles * ROWS
    share = rows - body_rows
    for j in range(devices):
        packed[j * share : (j + 1) * share] = msg[j, body_rows:].astype(F32)
    mix[...] = packed[0:wide]
    at = wide
    for t in range(8):
        res[t] = packed[at : at + chans]
        at += chans
    for t in range(4):
        block = packed[at : at + chans]
        conv[2 * t] = block[:, :half]
        if 2 * t + 1 < 7:
            conv[2 * t + 1] = block[:, half:]
        at += chans
    per_row = VOX // (LANES * lane_tiles)
    for j in range(devices):
        chan, part = j // per_row, j % per_row
        for q in range(slots):
            for lt in range(lane_tiles):
                row = (q * lane_tiles + lt) * ROWS
                lane = (part * lane_tiles + lt) * LANES
                coarse_out[q, chan * ROWS : (chan + 1) * ROWS, lane : lane + LANES] = msg[
                    j, row : row + ROWS
                ]


def kernel_call(kernel, out_shape, grid_spec, flops, moved, vmem=VMEM_BYTES):
    return pl.pallas_call(
        kernel,
        out_shape=out_shape,
        grid_spec=grid_spec,
        compiler_params=pltpu.CompilerParams(vmem_limit_bytes=vmem),
        cost_estimate=pl.CostEstimate(flops=flops, bytes_accessed=moved, transcendentals=0),
    )


def body(features, counts, neighbors, parents, w_conv, w_restrict, w_mix, cotangent):
    devices = lax.axis_size("space")
    position = lax.axis_index("space").astype(jnp.int32).reshape(1)
    slots, wide = cotangent.shape[:2]
    count, chans = features.shape[:2]
    lane_tiles = VOX * 8 // devices // LANES
    tiles = slots * lane_tiles
    groups = count // 8
    whole = lambda shape: pl.BlockSpec(shape, lambda *_: (0,) * len(shape))
    any_spec = pl.BlockSpec(memory_space=pl.ANY)
    smem_spec = pl.BlockSpec(memory_space=pltpu.SMEM)
    smem = lambda size: pltpu.SMEM((size,), jnp.int32)
    vmem = pltpu.VMEM
    ints = lambda size: jax.ShapeDtypeStruct((size,), jnp.int32)

    message_shape = (devices, tiles * ROWS + LABEL_ROWS, LANES)
    message, kids = kernel_call(
        functools.partial(pack_kernel, lane_tiles),
        (jax.ShapeDtypeStruct(message_shape, BF16), ints(groups)),
        pl.GridSpec(
            grid=(1,),
            in_specs=[smem_spec, whole(cotangent.shape)],
            out_specs=[whole(message_shape), smem_spec],
            scratch_shapes=[smem(groups + 1)],
        ),
        1000, 2**20,
    )(parents.T, cotangent)
    spread = lax.all_to_all(message, "space", split_axis=0, concat_axis=0, tiled=True)

    plane = jax.ShapeDtypeStruct((SEND // 2, chans, LANES), BF16)
    up, down, table, ordered = kernel_call(
        table_kernel,
        (plane, plane, ints(4 * count + 1), jax.ShapeDtypeStruct(features.shape, BF16)),
        pl.GridSpec(
            grid=(1,),
            in_specs=[smem_spec] * 5 + [any_spec],
            out_specs=[whole(plane.shape)] * 2 + [smem_spec, any_spec],
            scratch_shapes=[smem(SEND + 1)] * 4
            + [vmem(features.shape, BF16), vmem(features.shape, BF16), vmem((VOX, VOX), BF16),
               pltpu.SemaphoreType.DMA((PARTS,)), pltpu.SemaphoreType.DMA((PARTS,))],
        ),
        1000, 2**20,
    )(position, counts, kids, neighbors.T, parents.T, features)
    below = lax.ppermute(up, "space", [(i, i + 1) for i in range(devices - 1)])
    above = lax.ppermute(down, "space", [(i + 1, i) for i in range(devices - 1)])

    all_kids = spread[:, tiles * ROWS, :groups].astype(jnp.int32).reshape(-1)
    piece_shape = (devices, groups, lane_tiles, ROWS, LANES)
    forward_tiles = kernel_call(
        route_kernel,
        jax.ShapeDtypeStruct(piece_shape, BF16),
        pl.GridSpec(
            grid=(1,),
            in_specs=[smem_spec, whole(message_shape)],
            out_specs=whole(piece_shape),
        ),
        1000, 2**20, SMALL_VMEM_BYTES,
    )(all_kids, spread)
    forward_tiles, above, below = lax.optimization_barrier((forward_tiles, above, below))
    cot_pieces = lax.all_to_all(forward_tiles, "space", split_axis=0, concat_axis=0, tiled=True)

    res_rows = w_restrict.transpose(0, 2, 1).reshape(8 * chans, wide)
    scalars = (table, neighbors.T)
    brick_scratch = vmem((count + SEND + 1, chans, VOX), BF16)
    view_scratch = vmem((8, 7 * chans, VOX), BF16)
    per_group = lambda *shape: pl.BlockSpec((1,) + shape, lambda q: (q,) + (0,) * len(shape))
    piece_spec = pl.BlockSpec((devices, 1, lane_tiles, ROWS, LANES), lambda q: (0, q, 0, 0, 0))
    parts, slope, coarse, pieces = kernel_call(
        functools.partial(forward_kernel, lane_tiles),
        (
            jax.ShapeDtypeStruct((groups, 8 * chans, VOX), BF16),
            jax.ShapeDtypeStruct((groups, 8 * chans, VOX), BF16),
            jax.ShapeDtypeStruct((groups, wide, VOX), BF16),
            jax.ShapeDtypeStruct(piece_shape, BF16),
        ),
        pl.GridSpec(
            grid=(groups + 1,),
            in_specs=[any_spec] * 8,
            out_specs=[
                pl.BlockSpec((1, 8 * chans, VOX), lambda q: (jnp.minimum(q, groups - 1), 0, 0)),
                pl.BlockSpec((1, 8 * chans, VOX), lambda q: (jnp.minimum(q, groups - 1), 0, 0)),
                pl.BlockSpec((1, wide, VOX), lambda q: (jnp.maximum(q - 1, 0), 0, 0)),
                pl.BlockSpec(
                    (devices, 1, lane_tiles, ROWS, LANES),
                    lambda q: (0, jnp.maximum(q - 1, 0), 0, 0, 0),
                ),
            ],
            scratch_shapes=[
                brick_scratch, view_scratch, vmem((VOX, VOX), BF16), vmem(w_conv.shape, BF16),
                vmem(res_rows.shape, BF16), vmem(w_mix.shape, BF16),
                vmem((chans, 7 * chans), BF16), vmem((wide, 8 * chans), BF16),
                vmem((wide, VOX), BF16), smem(4 * count + 1),
                pltpu.SMEM((6, count), jnp.int32), vmem(plane.shape, BF16),
                vmem(plane.shape, BF16), pltpu.SemaphoreType.DMA((8,)),
            ],
        ),
        16 * 10**9, 16 * 2**20,
    )(*scalars, ordered, w_conv, res_rows, w_mix, above, below)
    returned = lax.all_to_all(pieces, "space", split_axis=0, concat_axis=0, tiled=True)

    scale = 1.0 / math.sqrt(devices * slots * VOX)
    used = wide + 8 * chans + 4 * chans
    rows = -(-used // (devices * 8)) * 8
    half = jax.ShapeDtypeStruct((devices // 2, rows, LANES), F32)
    own, other = kernel_call(
        functools.partial(backward_kernel, lane_tiles, scale),
        (half, half),
        pl.GridSpec(
            grid=(groups,),
            in_specs=[any_spec] * 5
            + [piece_spec, per_group(8 * chans, VOX), per_group(8 * chans, VOX),
               per_group(wide, VOX), whole(w_mix.shape), whole(res_rows.shape)],
            out_specs=[whole(half.shape)] * 2,
            scratch_shapes=[
                brick_scratch, view_scratch, vmem((wide, VOX), BF16),
                vmem((8 * chans, VOX), F32), vmem((8 * chans, VOX), BF16), vmem((VOX, VOX), BF16),
                vmem((wide, wide), BF16), vmem((chans, 8 * chans), F32),
                vmem((8 * chans, wide), F32), vmem((wide, wide), F32),
                vmem((devices * rows, LANES), F32), smem(4 * count + 1),
                pltpu.SMEM((6, count), jnp.int32), vmem(plane.shape, BF16),
                vmem(plane.shape, BF16), pltpu.SemaphoreType.DMA((4 + PARTS,)),
            ],
        ),
        16 * 10**9, 16 * 2**20,
    )(*scalars, ordered, above, below, cot_pieces, parts, slope, coarse, w_mix, res_rows)

    came = lax.ppermute(other, "space", [(i, i ^ 1) for i in range(devices)])
    paired = (own + came).astype(BF16)
    shares = lax.all_to_all(
        paired, "space", split_axis=0, concat_axis=0, tiled=True,
        axis_index_groups=[list(range(core, devices, 2)) for core in range(2)],
    )

    joined_shape = (devices, tiles * ROWS + rows, LANES)
    joined = kernel_call(
        join_kernel,
        jax.ShapeDtypeStruct(joined_shape, BF16),
        pl.GridSpec(
            grid=(1,),
            in_specs=[smem_spec, whole(shares.shape), whole(piece_shape)],
            out_specs=whole(joined_shape),
        ),
        1000, 2**20, SMALL_VMEM_BYTES,
    )(all_kids, shares, returned)
    finished = lax.all_to_all(joined, "space", split_axis=0, concat_axis=0, tiled=True)

    coarse_out, grad_conv, grad_res, grad_mix = kernel_call(
        functools.partial(unpack_kernel, lane_tiles),
        (
            jax.ShapeDtypeStruct((slots, wide, VOX), BF16),
            jax.ShapeDtypeStruct((7, chans, chans), F32),
            jax.ShapeDtypeStruct((8, chans, wide), F32),
            jax.ShapeDtypeStruct((wide, wide), F32),
        ),
        pl.GridSpec(
            grid=(1,),
            in_specs=[whole(joined_shape)],
            out_specs=[whole((slots, wide, VOX)), whole((7, chans, chans)),
                       whole((8, chans, wide)), whole((wide, wide))],
            scratch_shapes=[vmem((devices * rows, LANES), F32)],
        ),
        1000, 2 * 2**20, SMALL_VMEM_BYTES,
    )(finished)
    return coarse_out, grad_conv, grad_res.transpose(0, 2, 1), grad_mix


def solution(mesh):
    return jax.shard_map(
        body,
        mesh=mesh,
        in_specs=(
            P(("groups", "space"), None, None),
            P(("groups", "space")),
            P(("groups", "space"), None),
            P(("groups", "space"), None),
            P(),
            P(),
            P(),
            P(("groups", "space"), None, None),
        ),
        out_specs=(
            P(("groups", "space"), None, None),
            P("groups", None, None),
            P("groups", None, None),
            P("groups", None),
        ),
        check_vma=False,
    )
```

```python
import functools
import math

import jax
import jax.numpy as jnp
from jax import lax
from jax.experimental import pallas as pl
from jax.experimental.pallas import tpu as pltpu
from jax.sharding import PartitionSpec as P

EDGE = 8
HALF = EDGE // 2
VOX = EDGE**3
LANES = 128
ROWS = 16
LABEL_ROWS = 8
SEND = 8
PARTS = 4
BF16 = jnp.bfloat16
F32 = jnp.float32
VMEM_BYTES = 60 * 1024 * 1024
SMALL_VMEM_BYTES = 16 * 1024 * 1024


def bits_of(value):
    return [(value >> (8 - k)) & 1 for k in range(9)]


def join_bits(bits):
    value = bits[0]
    for bit in bits[1:]:
        value = value * 2 + bit
    return value


def split_voxel(column):
    ta, tb, tc, a1, a0, b1, b0, c1, c0 = bits_of(column)
    return join_bits([a1, a0, ta, b1, b0, tb, c1, c0, tc])


def octant_voxel(column):
    oa, ob, oc, a1, a0, b1, b0, c1, c0 = bits_of(column)
    return join_bits([oa, a1, a0, ob, b1, b0, oc, c1, c0])


def picker(voxel_of, shape=(VOX, VOX), start=(0, 0), flip=False):
    row = lax.broadcasted_iota(jnp.int32, shape, 0) + start[0]
    column = lax.broadcasted_iota(jnp.int32, shape, 1) + start[1]
    return (column == voxel_of(row) if flip else row == voxel_of(column)).astype(BF16)


def dot(a, b):
    return jnp.dot(a, b, preferred_element_type=F32)


def dot_nt(a, b):
    return lax.dot_general(a, b, (((1,), (1,)), ((), ())), preferred_element_type=F32)


def pack_kernel(lane_tiles, parents, cot, msg, kids_out, kids):
    devices = msg.shape[0]
    slots = cot.shape[0]

    def find(g, found):
        kids[found] = parents[0, g]
        return found + (parents[1, g] == 0).astype(jnp.int32)

    lax.fori_loop(0, parents.shape[1], find, jnp.int32(0), unroll=4)
    lane = lax.broadcasted_iota(jnp.int32, (LABEL_ROWS, LANES), 1)
    label = jnp.zeros((LABEL_ROWS, LANES), jnp.int32)
    for q in range(kids_out.shape[0]):
        kids_out[q] = kids[q]
        label = jnp.where(lane == q, kids[q], label)
    label = label.astype(F32).astype(BF16)
    for j in range(devices):
        msg[j, slots * lane_tiles * ROWS :] = label
    per_row = VOX // (LANES * lane_tiles)
    for j in range(devices):
        chan, part = j // per_row, j % per_row
        for q in range(slots):
            for lt in range(lane_tiles):
                lane = (part * lane_tiles + lt) * LANES
                row = (q * lane_tiles + lt) * ROWS
                msg[j, row : row + ROWS] = cot[
                    q, chan * ROWS : (chan + 1) * ROWS, lane : lane + LANES
                ]


def table_kernel(
    place, counts, kids, neighbors, parents, feat, up, down, table, ordered,
    up_idx, up_far, down_idx, down_far, bricks, done, split, in_sem, out_sem,
):
    count, chans = feat.shape[:2]
    part = count // PARTS
    fetches = [
        pltpu.make_async_copy(
            feat.at[pl.ds(k * part, part)], bricks.at[pl.ds(k * part, part)], in_sem.at[k]
        )
        for k in range(PARTS)
    ]
    for fetch in fetches:
        fetch.start()
    base = place[0] * count
    table[4 * count] = place[0]
    for r in range(SEND + 1):
        up_idx[r] = 0
        down_idx[r] = 0
        up_far[r] = 2 * count
        down_far[r] = 2 * count
    split[...] = picker(split_voxel)

    def scan(g, found):
        n_up, n_down = found
        near_up, near_down = neighbors[0, g], neighbors[1, g]
        far_up, far_down = near_up - base - count, near_down - base + count
        goes_up = (near_up >= 0) & (far_up >= 0)
        goes_down = (near_down >= 0) & (far_down < count)
        up_idx[n_up] = g
        up_far[n_up] = jnp.where(goes_up, far_up, 2 * count)
        down_idx[n_down] = g
        down_far[n_down] = jnp.where(goes_down, far_down, 2 * count)
        q = jnp.int32(0)
        for k in range(1, kids.shape[0]):
            q += jnp.where(kids[k] == parents[0, g], k, 0)
        number = q * 8 + parents[1, g]
        table[number] = g
        table[count + number] = jnp.where(g < counts[0], g, count + SEND)
        return n_up + goes_up.astype(jnp.int32), n_down + goes_down.astype(jnp.int32)

    lax.fori_loop(0, count, scan, (jnp.int32(0), jnp.int32(0)), unroll=4)

    def rank(r, carry):
        for start, far, idx in ((2 * count, up_far, up_idx), (3 * count, down_far, down_idx)):
            earlier = jnp.int32(0)
            for other in range(SEND):
                earlier += (far[other] < far[r]).astype(jnp.int32)

            @pl.when(far[r] < count)
            def _():
                table[start + idx[r]] = count + earlier

        return carry

    lax.fori_loop(0, SEND, rank, jnp.int32(0))
    sends = []
    for k in range(PARTS):
        fetches[k].wait()
        rows = bricks[k * part : (k + 1) * part].reshape(part * chans, VOX)
        done[k * part : (k + 1) * part] = (
            dot(rows, split[...]).astype(BF16).reshape(part, chans, VOX)
        )
        sends.append(
            pltpu.make_async_copy(
                done.at[pl.ds(k * part, part)], ordered.at[pl.ds(k * part, part)], out_sem.at[k]
            )
        )
        sends[-1].start()
    low = low_lanes(chans)
    for r in range(SEND // 2):
        other = r + SEND // 2
        top = slice(VOX - LANES, VOX)
        up[r] = jnp.where(
            low,
            pltpu.roll(bricks[up_idx[r], :, top], LANES // 2, 1),
            bricks[up_idx[other], :, top],
        )
        down[r] = jnp.where(
            low,
            bricks[down_idx[r], :, :LANES],
            pltpu.roll(bricks[down_idx[other], :, :LANES], LANES // 2, 1),
        )
    for send in sends:
        send.wait()


def route_kernel(kids, msg, pieces):
    devices, groups, lane_tiles = pieces.shape[:3]
    slots = groups
    for s in range(devices):
        for q in range(groups):
            kid = kids[s * groups + q]
            owner, slot = kid // slots, kid % slots
            for lt in range(lane_tiles):
                row = pl.multiple_of((slot * lane_tiles + lt) * ROWS, ROWS)
                pieces[s, q, lt] = msg[owner, pl.ds(row, ROWS), :]


def place_arrivals(above, below, bricks, count):
    chans = bricks.shape[1]
    half = VOX // 2
    side = LANES // 2
    shape = (LANES, half)
    pairs = SEND // 2
    for k, shift in ((0, 0), (pairs, -side)):
        slots = slice(count + k, count + k + pairs)
        first = dot(
            above[...].reshape(pairs * chans, LANES), picker(split_voxel, shape, (shift, 0))
        )
        last = dot(
            below[...].reshape(pairs * chans, LANES),
            picker(split_voxel, shape, (VOX - side + shift, half)),
        )
        bricks[slots, :, :half] = first.astype(BF16).reshape(pairs, chans, half)
        bricks[slots, :, half:] = last.astype(BF16).reshape(pairs, chans, half)
    bricks[count + SEND] = jnp.zeros(bricks.shape[1:], BF16)


def sources(table, neighbors, number):
    count = neighbors.shape[1]
    g = table[number]
    found = []
    for d in range(6):
        near = neighbors[d, g]
        local = near - table[4 * count] * count
        if d == 0:
            local = jnp.where(local >= count, table[2 * count + g], local)
        if d == 1:
            local = jnp.where(local < 0, table[3 * count + g], local)
        found.append(jnp.where(near >= 0, local, count + SEND))
    found.append(table[count + number])
    return found


def shift_into(slots, bricks, views):
    chans = bricks.shape[1]
    tiles = VOX // LANES
    lane = lax.broadcasted_iota(jnp.int32, (chans, LANES), 1)
    low = lane < LANES // 2
    a = (lane // 16) % HALF
    b = (lane // 4) % HALF
    c = lane % HALF

    def tile(slot, t):
        return bricks[slot, :, t * LANES : (t + 1) * LANES]

    def turn(value, by):
        return pltpu.roll(value, by % LANES, 1)

    x = [tile(slots[6], t) for t in range(tiles)]
    for t in range(tiles):
        lanes = slice(t * LANES, (t + 1) * LANES)
        if t < 2:
            plus_a = x[t + 2]
            minus_a = jnp.where(a > 0, turn(x[t + 2], 16), turn(tile(slots[1], t + 2), -48))
        else:
            plus_a = jnp.where(a < HALF - 1, turn(x[t - 2], -16), turn(tile(slots[0], t - 2), 48))
            minus_a = x[t - 2]
        if t % 2 == 0:
            plus_b = x[t + 1]
            minus_b = jnp.where(b > 0, turn(x[t + 1], 4), turn(tile(slots[3], t + 1), -12))
        else:
            plus_b = jnp.where(b < HALF - 1, turn(x[t - 1], -4), turn(tile(slots[2], t - 1), 12))
            minus_b = x[t - 1]
        swapped = turn(x[t], 64)
        plus_c = jnp.where(c < HALF - 1, turn(x[t], 63), turn(tile(slots[4], t), 67))
        minus_c = jnp.where(c > 0, turn(x[t], -63), turn(tile(slots[5], t), -67))
        out = [plus_a, minus_a, plus_b, minus_b, jnp.where(low, swapped, plus_c),
               jnp.where(low, minus_c, swapped), x[t]]
        for d in range(7):
            views[d * chans : (d + 1) * chans, lanes] = out[d]


def low_lanes(rows):
    return lax.broadcasted_iota(jnp.int32, (rows, LANES), 1) < LANES // 2


def forward_kernel(
    lane_tiles, table_hbm, neighbors_hbm, feat, w_conv_hbm, w_res_hbm, w_mix_hbm,
    above_hbm, below_hbm,
    parts_out, slope_out, coarse_out, piece_out,
    bricks, views, place, w_conv, w_res, w_mix, conv_cat, res_cat, octants,
    table, neighbors, above, below, sem,
):
    q = pl.program_id(0)
    groups = pl.num_programs(0) - 1
    count, chans = feat.shape[:2]
    part = count // PARTS

    @pl.when(q == 0)
    def _():
        copies = [
            pltpu.make_async_copy(source, target, sem.at[k])
            for k, (source, target) in enumerate((
                (above_hbm, above), (below_hbm, below), (w_conv_hbm, w_conv),
                (w_res_hbm, w_res), (w_mix_hbm, w_mix), (table_hbm, table),
                (neighbors_hbm, neighbors),
                *(
                    (feat.at[pl.ds(k * part, part)], bricks.at[pl.ds(k * part, part)])
                    for k in range(PARTS)
                ),
            ))
        ]
        for copy in copies:
            copy.start()
        place[...] = picker(octant_voxel, flip=True)
        for copy in copies[:-PARTS]:
            copy.wait()
        place_arrivals(above, below, bricks, count)
        for d in range(7):
            conv_cat[:, d * chans : (d + 1) * chans] = w_conv[d]
        res_cat[...] = w_res[...].T
        for copy in copies[-PARTS:]:
            copy.wait()

    low_half = low_lanes(chans)

    def finish():
        coarse = dot(octants[...], place[...]).astype(BF16)
        coarse_out[0] = coarse
        mixed = dot(w_mix[...], coarse).astype(BF16)
        per_row = VOX // (LANES * lane_tiles)
        for j in range(piece_out.shape[0]):
            chan, part = j // per_row, j % per_row
            for lt in range(lane_tiles):
                lane = (part * lane_tiles + lt) * LANES
                piece_out[j, 0, lt] = mixed[chan * ROWS : (chan + 1) * ROWS, lane : lane + LANES]

    def restrict(first):
        acts = []
        for k in range(first, first + 4):
            shift_into(sources(table, neighbors, q * 8 + k), bricks, views.at[k])
            hidden = dot(conv_cat[...], views[k])
            sig = 1.0 / (1.0 + jnp.exp(-hidden))
            act = hidden * sig
            slope_out[0, k * chans : (k + 1) * chans, :] = (sig + act * (1.0 - sig)).astype(BF16)
            acts.append(act.astype(BF16))
        for k in range(0, 4, 2):
            lanes = slice((first + k) * (LANES // 2), (first + k + 2) * (LANES // 2))
            for t in range(4):
                one = acts[k][:, t * LANES : (t + 1) * LANES]
                two = acts[k + 1][:, t * LANES : (t + 1) * LANES]
                parts_out[0, 2 * t * chans : (2 * t + 1) * chans, lanes] = jnp.where(
                    low_half, one, pltpu.roll(two, LANES // 2, 1)
                )
                parts_out[0, (2 * t + 1) * chans : (2 * t + 2) * chans, lanes] = jnp.where(
                    low_half, pltpu.roll(one, LANES // 2, 1), two
                )
        lanes = slice(first * (LANES // 2), (first + 4) * (LANES // 2))
        return dot(res_cat[...], parts_out[0, :, lanes]).astype(BF16)

    @pl.when(q < groups)
    def _():
        finish()
        halves = [restrict(0), restrict(4)]
        octants[...] = jnp.concatenate(halves, axis=1)

    @pl.when(q == groups)
    def _():
        finish()


def backward_kernel(
    lane_tiles, scale, table, neighbors, feat, above, below, pieces, parts, slope, coarse, w_mix, w_res, packed,
    bricks, views, cot, grad_parts, grad_rows, unplace, mix_t, conv_sum, res_sum, mix_sum, sem,
):
    q = pl.program_id(0)
    count, chans = feat.shape[:2]
    wide = coarse.shape[1]
    fetch = pltpu.make_async_copy(feat, bricks.at[pl.ds(0, count)], sem)

    @pl.when(q == 0)
    def _():
        fetch.start()
        place_arrivals(above, below, bricks, count)
        unplace[...] = picker(octant_voxel)
        mix_t[...] = w_mix[...].T
        conv_sum[...] = jnp.zeros_like(conv_sum)
        res_sum[...] = jnp.zeros_like(res_sum)
        mix_sum[...] = jnp.zeros_like(mix_sum)
        fetch.wait()

    per_row = VOX // (LANES * lane_tiles)
    for j in range(pieces.shape[0]):
        chan, part = j // per_row, j % per_row
        for lt in range(lane_tiles):
            lane = (part * lane_tiles + lt) * LANES
            cot[chan * ROWS : (chan + 1) * ROWS, lane : lane + LANES] = pieces[j, 0, lt]
    cots = cot[...]
    grad_coarse = (scale * dot(mix_t[...], cots)).astype(BF16)
    grad_fine = dot(grad_coarse, unplace[...]).astype(BF16)
    mix_sum[...] += dot_nt(cots, coarse[0])
    res_sum[...] += dot_nt(parts[0], grad_fine)
    grad_parts[...] = dot(w_res[...], grad_fine)
    low_half = low_lanes(chans)
    for r in range(4):
        for t in range(4):
            cols = slice(r * LANES, (r + 1) * LANES)
            lanes = slice(t * LANES, (t + 1) * LANES)
            one = grad_parts[2 * t * chans : (2 * t + 1) * chans, cols]
            two = grad_parts[(2 * t + 1) * chans : (2 * t + 2) * chans, cols]
            first = slice(2 * r * chans, (2 * r + 1) * chans)
            second = slice((2 * r + 1) * chans, (2 * r + 2) * chans)
            grad_rows[first, lanes] = (
                jnp.where(low_half, one, pltpu.roll(two, LANES // 2, 1))
                * slope[0, first, lanes].astype(F32)
            ).astype(BF16)
            grad_rows[second, lanes] = (
                jnp.where(low_half, pltpu.roll(one, LANES // 2, 1), two)
                * slope[0, second, lanes].astype(F32)
            ).astype(BF16)

    total = None
    for k in range(8):
        shift_into(sources(table, neighbors, q * 8 + k), bricks, views.at[k])
        term = dot_nt(grad_rows[k * chans : (k + 1) * chans, :], views[k])
        total = term if total is None else total + term
    conv_sum[:, : 7 * chans] += total

    @pl.when(q == pl.num_programs(0) - 1)
    def _():
        packed[0:wide] = (scale * mix_sum[...]).astype(BF16)
        at = wide
        packed[at : at + 8 * chans] = res_sum[...].astype(BF16)
        at += 8 * chans
        for t in range(4):
            packed[at : at + chans] = conv_sum[:, t * LANES : (t + 1) * LANES].astype(BF16)
            at += chans
        if at < packed.shape[0]:
            packed[at:] = jnp.zeros((packed.shape[0] - at, LANES), BF16)


def join_kernel(kids, shares, pieces, msg):
    devices, groups, lane_tiles = pieces.shape[:3]
    slots = groups
    body_rows = slots * lane_tiles * ROWS
    for s in range(devices):
        for q in range(groups):
            kid = kids[s * groups + q]
            owner, slot = kid // slots, kid % slots
            for lt in range(lane_tiles):
                row = pl.multiple_of((slot * lane_tiles + lt) * ROWS, ROWS)
                msg[owner, pl.ds(row, ROWS), :] = pieces[s, q, lt]
    total = jnp.sum(shares[...].astype(F32), axis=0).astype(BF16)
    for j in range(devices):
        msg[j, body_rows:] = total


def unpack_kernel(lane_tiles, msg, coarse_out, conv, res, mix, packed):
    devices, rows = msg.shape[:2]
    slots = coarse_out.shape[0]
    wide = mix.shape[0]
    chans = conv.shape[1]
    half = LANES // 2
    body_rows = slots * lane_tiles * ROWS
    share = rows - body_rows
    for j in range(devices):
        packed[j * share : (j + 1) * share] = msg[j, body_rows:].astype(F32)
    mix[...] = packed[0:wide]
    at = wide
    for t in range(8):
        res[t] = packed[at : at + chans]
        at += chans
    for t in range(4):
        block = packed[at : at + chans]
        conv[2 * t] = block[:, :half]
        if 2 * t + 1 < 7:
            conv[2 * t + 1] = block[:, half:]
        at += chans
    per_row = VOX // (LANES * lane_tiles)
    for j in range(devices):
        chan, part = j // per_row, j % per_row
        for q in range(slots):
            for lt in range(lane_tiles):
                row = (q * lane_tiles + lt) * ROWS
                lane = (part * lane_tiles + lt) * LANES
                coarse_out[q, chan * ROWS : (chan + 1) * ROWS, lane : lane + LANES] = msg[
                    j, row : row + ROWS
                ]


def kernel_call(kernel, out_shape, grid_spec, flops, moved, vmem=VMEM_BYTES):
    return pl.pallas_call(
        kernel,
        out_shape=out_shape,
        grid_spec=grid_spec,
        compiler_params=pltpu.CompilerParams(vmem_limit_bytes=vmem),
        cost_estimate=pl.CostEstimate(flops=flops, bytes_accessed=moved, transcendentals=0),
    )


def body(features, counts, neighbors, parents, w_conv, w_restrict, w_mix, cotangent):
    devices = lax.axis_size("space")
    position = lax.axis_index("space").astype(jnp.int32).reshape(1)
    slots, wide = cotangent.shape[:2]
    count, chans = features.shape[:2]
    lane_tiles = VOX * 8 // devices // LANES
    tiles = slots * lane_tiles
    groups = count // 8
    whole = lambda shape: pl.BlockSpec(shape, lambda *_: (0,) * len(shape))
    any_spec = pl.BlockSpec(memory_space=pl.ANY)
    smem_spec = pl.BlockSpec(memory_space=pltpu.SMEM)
    smem = lambda size: pltpu.SMEM((size,), jnp.int32)
    vmem = pltpu.VMEM
    ints = lambda size: jax.ShapeDtypeStruct((size,), jnp.int32)

    message_shape = (devices, tiles * ROWS + LABEL_ROWS, LANES)
    message, kids = kernel_call(
        functools.partial(pack_kernel, lane_tiles),
        (jax.ShapeDtypeStruct(message_shape, BF16), ints(groups)),
        pl.GridSpec(
            grid=(1,),
            in_specs=[smem_spec, whole(cotangent.shape)],
            out_specs=[whole(message_shape), smem_spec],
            scratch_shapes=[smem(groups + 1)],
        ),
        1000, 2**20,
    )(parents.T, cotangent)
    spread = lax.all_to_all(message, "space", split_axis=0, concat_axis=0, tiled=True)

    plane = jax.ShapeDtypeStruct((SEND // 2, chans, LANES), BF16)
    up, down, table, ordered = kernel_call(
        table_kernel,
        (plane, plane, ints(4 * count + 1), jax.ShapeDtypeStruct(features.shape, BF16)),
        pl.GridSpec(
            grid=(1,),
            in_specs=[smem_spec] * 5 + [any_spec],
            out_specs=[whole(plane.shape)] * 2 + [smem_spec, any_spec],
            scratch_shapes=[smem(SEND + 1)] * 4
            + [vmem(features.shape, BF16), vmem(features.shape, BF16), vmem((VOX, VOX), BF16),
               pltpu.SemaphoreType.DMA((PARTS,)), pltpu.SemaphoreType.DMA((PARTS,))],
        ),
        1000, 2**20,
    )(position, counts, kids, neighbors.T, parents.T, features)
    below = lax.ppermute(up, "space", [(i, i + 1) for i in range(devices - 1)])
    above = lax.ppermute(down, "space", [(i + 1, i) for i in range(devices - 1)])

    all_kids = spread[:, tiles * ROWS, :groups].astype(jnp.int32).reshape(-1)
    piece_shape = (devices, groups, lane_tiles, ROWS, LANES)
    forward_tiles = kernel_call(
        route_kernel,
        jax.ShapeDtypeStruct(piece_shape, BF16),
        pl.GridSpec(
            grid=(1,),
            in_specs=[smem_spec, whole(message_shape)],
            out_specs=whole(piece_shape),
        ),
        1000, 2**20, SMALL_VMEM_BYTES,
    )(all_kids, spread)
    forward_tiles, above, below = lax.optimization_barrier((forward_tiles, above, below))
    cot_pieces = lax.all_to_all(forward_tiles, "space", split_axis=0, concat_axis=0, tiled=True)

    res_rows = w_restrict.transpose(0, 2, 1).reshape(8 * chans, wide)
    scalars = (table, neighbors.T)
    brick_scratch = vmem((count + SEND + 1, chans, VOX), BF16)
    view_scratch = vmem((8, 7 * chans, VOX), BF16)
    per_group = lambda *shape: pl.BlockSpec((1,) + shape, lambda q: (q,) + (0,) * len(shape))
    piece_spec = pl.BlockSpec((devices, 1, lane_tiles, ROWS, LANES), lambda q: (0, q, 0, 0, 0))
    parts, slope, coarse, pieces = kernel_call(
        functools.partial(forward_kernel, lane_tiles),
        (
            jax.ShapeDtypeStruct((groups, 8 * chans, VOX), BF16),
            jax.ShapeDtypeStruct((groups, 8 * chans, VOX), BF16),
            jax.ShapeDtypeStruct((groups, wide, VOX), BF16),
            jax.ShapeDtypeStruct(piece_shape, BF16),
        ),
        pl.GridSpec(
            grid=(groups + 1,),
            in_specs=[any_spec] * 8,
            out_specs=[
                pl.BlockSpec((1, 8 * chans, VOX), lambda q: (jnp.minimum(q, groups - 1), 0, 0)),
                pl.BlockSpec((1, 8 * chans, VOX), lambda q: (jnp.minimum(q, groups - 1), 0, 0)),
                pl.BlockSpec((1, wide, VOX), lambda q: (jnp.maximum(q - 1, 0), 0, 0)),
                pl.BlockSpec(
                    (devices, 1, lane_tiles, ROWS, LANES),
                    lambda q: (0, jnp.maximum(q - 1, 0), 0, 0, 0),
                ),
            ],
            scratch_shapes=[
                brick_scratch, view_scratch, vmem((VOX, VOX), BF16), vmem(w_conv.shape, BF16),
                vmem(res_rows.shape, BF16), vmem(w_mix.shape, BF16),
                vmem((chans, 7 * chans), BF16), vmem((wide, 8 * chans), BF16),
                vmem((wide, VOX), BF16), smem(4 * count + 1),
                pltpu.SMEM((6, count), jnp.int32), vmem(plane.shape, BF16),
                vmem(plane.shape, BF16), pltpu.SemaphoreType.DMA((7 + PARTS,)),
            ],
        ),
        16 * 10**9, 16 * 2**20,
    )(*scalars, ordered, w_conv, res_rows, w_mix, above, below)
    returned = lax.all_to_all(pieces, "space", split_axis=0, concat_axis=0, tiled=True)

    scale = 1.0 / math.sqrt(devices * slots * VOX)
    used = wide + 8 * chans + 4 * chans
    rows = -(-used // (devices * 8)) * 8
    packed = kernel_call(
        functools.partial(backward_kernel, lane_tiles, scale),
        jax.ShapeDtypeStruct((devices * rows, LANES), BF16),
        pl.GridSpec(
            grid=(groups,),
            in_specs=[smem_spec] * 2 + [any_spec] + [whole(plane.shape)] * 2
            + [piece_spec, per_group(8 * chans, VOX), per_group(8 * chans, VOX),
               per_group(wide, VOX), whole(w_mix.shape), whole(res_rows.shape)],
            out_specs=whole((devices * rows, LANES)),
            scratch_shapes=[
                brick_scratch, view_scratch, vmem((wide, VOX), BF16),
                vmem((8 * chans, VOX), F32), vmem((8 * chans, VOX), BF16), vmem((VOX, VOX), BF16),
                vmem((wide, wide), BF16), vmem((chans, 8 * chans), F32),
                vmem((8 * chans, wide), F32), vmem((wide, wide), F32), pltpu.SemaphoreType.DMA,
            ],
        ),
        16 * 10**9, 16 * 2**20,
    )(*scalars, ordered, above, below, cot_pieces, parts, slope, coarse, w_mix, res_rows)

    shares = lax.all_to_all(
        packed.reshape(devices, rows, LANES), "space", split_axis=0, concat_axis=0, tiled=True
    )
    joined_shape = (devices, tiles * ROWS + rows, LANES)
    joined = kernel_call(
        join_kernel,
        jax.ShapeDtypeStruct(joined_shape, BF16),
        pl.GridSpec(
            grid=(1,),
            in_specs=[smem_spec, whole(shares.shape), whole(piece_shape)],
            out_specs=whole(joined_shape),
        ),
        1000, 2**20, SMALL_VMEM_BYTES,
    )(all_kids, shares, returned)
    finished = lax.all_to_all(joined, "space", split_axis=0, concat_axis=0, tiled=True)

    coarse_out, grad_conv, grad_res, grad_mix = kernel_call(
        functools.partial(unpack_kernel, lane_tiles),
        (
            jax.ShapeDtypeStruct((slots, wide, VOX), BF16),
            jax.ShapeDtypeStruct((7, chans, chans), F32),
            jax.ShapeDtypeStruct((8, chans, wide), F32),
            jax.ShapeDtypeStruct((wide, wide), F32),
        ),
        pl.GridSpec(
            grid=(1,),
            in_specs=[whole(joined_shape)],
            out_specs=[whole((slots, wide, VOX)), whole((7, chans, chans)),
                       whole((8, chans, wide)), whole((wide, wide))],
            scratch_shapes=[vmem((devices * rows, LANES), F32)],
        ),
        1000, 2 * 2**20, SMALL_VMEM_BYTES,
    )(finished)
    return coarse_out, grad_conv, grad_res.transpose(0, 2, 1), grad_mix


def solution(mesh):
    return jax.shard_map(
        body,
        mesh=mesh,
        in_specs=(
            P(("groups", "space"), None, None),
            P(("groups", "space")),
            P(("groups", "space"), None),
            P(("groups", "space"), None),
            P(),
            P(),
            P(),
            P(("groups", "space"), None, None),
        ),
        out_specs=(
            P(("groups", "space"), None, None),
            P("groups", None, None),
            P("groups", None, None),
            P("groups", None),
        ),
        check_vma=False,
    )
```

```python
import functools
import math

import jax
import jax.numpy as jnp
from jax import lax
from jax.experimental import pallas as pl
from jax.experimental.pallas import tpu as pltpu
from jax.sharding import PartitionSpec as P

EDGE = 8
HALF = EDGE // 2
VOX = EDGE**3
LANES = 128
ROWS = 16
LABEL_ROWS = 8
SEND = 8
PARTS = 4
BF16 = jnp.bfloat16
F32 = jnp.float32
VMEM_BYTES = 60 * 1024 * 1024
SMALL_VMEM_BYTES = 16 * 1024 * 1024


def bits_of(value):
    return [(value >> (8 - k)) & 1 for k in range(9)]


def join_bits(bits):
    value = bits[0]
    for bit in bits[1:]:
        value = value * 2 + bit
    return value


def split_voxel(column):
    ta, tb, tc, a1, a0, b1, b0, c1, c0 = bits_of(column)
    return join_bits([a1, a0, ta, b1, b0, tb, c1, c0, tc])


def octant_voxel(column):
    oa, ob, oc, a1, a0, b1, b0, c1, c0 = bits_of(column)
    return join_bits([oa, a1, a0, ob, b1, b0, oc, c1, c0])


def picker(voxel_of, shape=(VOX, VOX), start=(0, 0), flip=False):
    row = lax.broadcasted_iota(jnp.int32, shape, 0) + start[0]
    column = lax.broadcasted_iota(jnp.int32, shape, 1) + start[1]
    return (column == voxel_of(row) if flip else row == voxel_of(column)).astype(BF16)


def dot(a, b):
    return jnp.dot(a, b, preferred_element_type=F32)


def dot_nt(a, b):
    return lax.dot_general(a, b, (((1,), (1,)), ((), ())), preferred_element_type=F32)


def list_kids(parents, kids):
    def find(g, found):
        kids[found] = parents[0, g]
        return found + (parents[1, g] == 0).astype(jnp.int32)

    lax.fori_loop(0, parents.shape[1], find, jnp.int32(0), unroll=4)


def send_parts(buffer, target, sem, fill):
    size = buffer.shape[0] // PARTS
    sends = []
    for k in range(PARTS):
        for j in range(k * size, (k + 1) * size):
            fill(j)
        part = pl.ds(k * size, size)
        sends.append(pltpu.make_async_copy(buffer.at[part], target.at[part], sem.at[k]))
        sends[-1].start()
    return sends


def pack_kernel(
    lane_tiles, parents_hbm, cot_hbm, msg_hbm, parents, kids, cot, msg, parents_sem, in_sem, out_sem
):
    slots = cot.shape[0]
    listing = pltpu.make_async_copy(parents_hbm, parents, parents_sem)
    listing.start()
    fetches = [
        pltpu.make_async_copy(cot_hbm.at[q], cot.at[q], in_sem.at[q]) for q in range(slots)
    ]
    for fetch in fetches:
        fetch.start()
    listing.wait()
    list_kids(parents, kids)
    lane = lax.broadcasted_iota(jnp.int32, (LABEL_ROWS, LANES), 1)
    label = jnp.zeros((LABEL_ROWS, LANES), jnp.int32)
    for q in range(slots):
        label = jnp.where(lane == q, kids[q], label)
    label = label.astype(F32).astype(BF16)
    for fetch in fetches:
        fetch.wait()
    per_row = VOX // (LANES * lane_tiles)

    def fill(j):
        chan, part = j // per_row, j % per_row
        for q in range(slots):
            for lt in range(lane_tiles):
                lane = (part * lane_tiles + lt) * LANES
                row = (q * lane_tiles + lt) * ROWS
                msg[j, row : row + ROWS] = cot[
                    q, chan * ROWS : (chan + 1) * ROWS, lane : lane + LANES
                ]
        msg[j, slots * lane_tiles * ROWS :] = label

    for send in send_parts(msg, msg_hbm, out_sem, fill):
        send.wait()


def table_kernel(
    place, counts, neighbors, parents, feat, up, down, table, ordered,
    kids, up_idx, up_far, down_idx, down_far, bricks, done, split, in_sem, out_sem,
):
    count, chans = feat.shape[:2]
    part = count // PARTS
    fetches = [
        pltpu.make_async_copy(
            feat.at[pl.ds(k * part, part)], bricks.at[pl.ds(k * part, part)], in_sem.at[k]
        )
        for k in range(PARTS)
    ]
    for fetch in fetches:
        fetch.start()
    base = place[0] * count
    table[4 * count] = place[0]
    for r in range(SEND + 1):
        up_idx[r] = 0
        down_idx[r] = 0
        up_far[r] = 2 * count
        down_far[r] = 2 * count
    split[...] = picker(split_voxel)
    list_kids(parents, kids)

    def scan(g, found):
        n_up, n_down = found
        near_up, near_down = neighbors[0, g], neighbors[1, g]
        far_up, far_down = near_up - base - count, near_down - base + count
        goes_up = (near_up >= 0) & (far_up >= 0)
        goes_down = (near_down >= 0) & (far_down < count)
        up_idx[n_up] = g
        up_far[n_up] = jnp.where(goes_up, far_up, 2 * count)
        down_idx[n_down] = g
        down_far[n_down] = jnp.where(goes_down, far_down, 2 * count)
        q = jnp.int32(0)
        for k in range(1, kids.shape[0] - 1):
            q += jnp.where(kids[k] == parents[0, g], k, 0)
        number = q * 8 + parents[1, g]
        table[number] = g
        table[count + number] = jnp.where(g < counts[0], g, count + SEND)
        return n_up + goes_up.astype(jnp.int32), n_down + goes_down.astype(jnp.int32)

    lax.fori_loop(0, count, scan, (jnp.int32(0), jnp.int32(0)), unroll=4)

    def rank(r, carry):
        for start, far, idx in ((2 * count, up_far, up_idx), (3 * count, down_far, down_idx)):
            earlier = jnp.int32(0)
            for other in range(SEND):
                earlier += (far[other] < far[r]).astype(jnp.int32)

            @pl.when(far[r] < count)
            def _():
                table[start + idx[r]] = count + earlier

        return carry

    lax.fori_loop(0, SEND, rank, jnp.int32(0))
    sends = []
    for k in range(PARTS):
        fetches[k].wait()
        rows = bricks[k * part : (k + 1) * part].reshape(part * chans, VOX)
        done[k * part : (k + 1) * part] = (
            dot(rows, split[...]).astype(BF16).reshape(part, chans, VOX)
        )
        sends.append(
            pltpu.make_async_copy(
                done.at[pl.ds(k * part, part)], ordered.at[pl.ds(k * part, part)], out_sem.at[k]
            )
        )
        sends[-1].start()
    low = low_lanes(chans)
    for r in range(SEND // 2):
        other = r + SEND // 2
        top = slice(VOX - LANES, VOX)
        up[r] = jnp.where(
            low,
            pltpu.roll(bricks[up_idx[r], :, top], LANES // 2, 1),
            bricks[up_idx[other], :, top],
        )
        down[r] = jnp.where(
            low,
            bricks[down_idx[r], :, :LANES],
            pltpu.roll(bricks[down_idx[other], :, :LANES], LANES // 2, 1),
        )
    for send in sends:
        send.wait()


def route_kernel(kids, msg, pieces_hbm, pieces, sem):
    groups, lane_tiles = pieces.shape[1:3]
    slots = groups

    def fill(s):
        for q in range(groups):
            kid = kids[s * groups + q]
            owner, slot = kid // slots, kid % slots
            for lt in range(lane_tiles):
                row = pl.multiple_of((slot * lane_tiles + lt) * ROWS, ROWS)
                pieces[s, q, lt] = msg[owner, pl.ds(row, ROWS), :]

    for send in send_parts(pieces, pieces_hbm, sem, fill):
        send.wait()


def place_arrivals(above, below, bricks, count):
    chans = bricks.shape[1]
    half = VOX // 2
    side = LANES // 2
    shape = (LANES, half)
    pairs = SEND // 2
    for k, shift in ((0, 0), (pairs, -side)):
        slots = slice(count + k, count + k + pairs)
        first = dot(
            above[...].reshape(pairs * chans, LANES), picker(split_voxel, shape, (shift, 0))
        )
        last = dot(
            below[...].reshape(pairs * chans, LANES),
            picker(split_voxel, shape, (VOX - side + shift, half)),
        )
        bricks[slots, :, :half] = first.astype(BF16).reshape(pairs, chans, half)
        bricks[slots, :, half:] = last.astype(BF16).reshape(pairs, chans, half)
    bricks[count + SEND] = jnp.zeros(bricks.shape[1:], BF16)


def sources(table, neighbors, number):
    count = neighbors.shape[1]
    g = table[number]
    found = []
    for d in range(6):
        near = neighbors[d, g]
        local = near - table[4 * count] * count
        if d == 0:
            local = jnp.where(local >= count, table[2 * count + g], local)
        if d == 1:
            local = jnp.where(local < 0, table[3 * count + g], local)
        found.append(jnp.where(near >= 0, local, count + SEND))
    found.append(table[count + number])
    return found


def shift_into(slots, bricks, views):
    chans = bricks.shape[1]
    tiles = VOX // LANES
    lane = lax.broadcasted_iota(jnp.int32, (chans, LANES), 1)
    low = lane < LANES // 2
    a = (lane // 16) % HALF
    b = (lane // 4) % HALF
    c = lane % HALF

    def tile(slot, t):
        return bricks[slot, :, t * LANES : (t + 1) * LANES]

    def turn(value, by):
        return pltpu.roll(value, by % LANES, 1)

    x = [tile(slots[6], t) for t in range(tiles)]
    for t in range(tiles):
        lanes = slice(t * LANES, (t + 1) * LANES)
        if t < 2:
            plus_a = x[t + 2]
            minus_a = jnp.where(a > 0, turn(x[t + 2], 16), turn(tile(slots[1], t + 2), -48))
        else:
            plus_a = jnp.where(a < HALF - 1, turn(x[t - 2], -16), turn(tile(slots[0], t - 2), 48))
            minus_a = x[t - 2]
        if t % 2 == 0:
            plus_b = x[t + 1]
            minus_b = jnp.where(b > 0, turn(x[t + 1], 4), turn(tile(slots[3], t + 1), -12))
        else:
            plus_b = jnp.where(b < HALF - 1, turn(x[t - 1], -4), turn(tile(slots[2], t - 1), 12))
            minus_b = x[t - 1]
        swapped = turn(x[t], 64)
        plus_c = jnp.where(c < HALF - 1, turn(x[t], 63), turn(tile(slots[4], t), 67))
        minus_c = jnp.where(c > 0, turn(x[t], -63), turn(tile(slots[5], t), -67))
        out = [plus_a, minus_a, plus_b, minus_b, jnp.where(low, swapped, plus_c),
               jnp.where(low, minus_c, swapped), x[t]]
        for d in range(7):
            views[d * chans : (d + 1) * chans, lanes] = out[d]


def low_lanes(rows):
    return lax.broadcasted_iota(jnp.int32, (rows, LANES), 1) < LANES // 2


def forward_kernel(
    lane_tiles, table_hbm, neighbors_hbm, feat, w_conv_hbm, w_res_hbm, w_mix_hbm,
    above_hbm, below_hbm,
    parts_out, slope_out, coarse_out, piece_out,
    bricks, views, place, w_conv, w_res, w_mix, conv_cat, res_cat, octants,
    table, neighbors, above, below, sem,
):
    q = pl.program_id(0)
    groups = pl.num_programs(0) - 1
    count, chans = feat.shape[:2]
    part = count // PARTS

    @pl.when(q == 0)
    def _():
        copies = [
            pltpu.make_async_copy(source, target, sem.at[k])
            for k, (source, target) in enumerate((
                (above_hbm, above), (below_hbm, below), (w_conv_hbm, w_conv),
                (w_res_hbm, w_res), (w_mix_hbm, w_mix), (table_hbm, table),
                (neighbors_hbm, neighbors),
                *(
                    (feat.at[pl.ds(k * part, part)], bricks.at[pl.ds(k * part, part)])
                    for k in range(PARTS)
                ),
            ))
        ]
        for copy in copies:
            copy.start()
        place[...] = picker(octant_voxel, flip=True)
        for copy in copies[:-PARTS]:
            copy.wait()
        place_arrivals(above, below, bricks, count)
        for d in range(7):
            conv_cat[:, d * chans : (d + 1) * chans] = w_conv[d]
        res_cat[...] = w_res[...].T
        for copy in copies[-PARTS:]:
            copy.wait()

    low_half = low_lanes(chans)

    def finish():
        coarse = dot(octants[...], place[...]).astype(BF16)
        coarse_out[0] = coarse
        mixed = dot(w_mix[...], coarse).astype(BF16)
        per_row = VOX // (LANES * lane_tiles)
        for j in range(piece_out.shape[0]):
            chan, part = j // per_row, j % per_row
            for lt in range(lane_tiles):
                lane = (part * lane_tiles + lt) * LANES
                piece_out[j, 0, lt] = mixed[chan * ROWS : (chan + 1) * ROWS, lane : lane + LANES]

    def restrict(first):
        acts = []
        for k in range(first, first + 4):
            shift_into(sources(table, neighbors, q * 8 + k), bricks, views.at[k])
            hidden = dot(conv_cat[...], views[k])
            sig = 1.0 / (1.0 + jnp.exp(-hidden))
            act = hidden * sig
            slope_out[0, k * chans : (k + 1) * chans, :] = (sig + act * (1.0 - sig)).astype(BF16)
            acts.append(act.astype(BF16))
        for k in range(0, 4, 2):
            lanes = slice((first + k) * (LANES // 2), (first + k + 2) * (LANES // 2))
            for t in range(4):
                one = acts[k][:, t * LANES : (t + 1) * LANES]
                two = acts[k + 1][:, t * LANES : (t + 1) * LANES]
                parts_out[0, 2 * t * chans : (2 * t + 1) * chans, lanes] = jnp.where(
                    low_half, one, pltpu.roll(two, LANES // 2, 1)
                )
                parts_out[0, (2 * t + 1) * chans : (2 * t + 2) * chans, lanes] = jnp.where(
                    low_half, pltpu.roll(one, LANES // 2, 1), two
                )
        lanes = slice(first * (LANES // 2), (first + 4) * (LANES // 2))
        return dot(res_cat[...], parts_out[0, :, lanes]).astype(BF16)

    @pl.when(q < groups)
    def _():
        finish()
        halves = [restrict(0), restrict(4)]
        octants[...] = jnp.concatenate(halves, axis=1)

    @pl.when(q == groups)
    def _():
        finish()


def backward_kernel(
    lane_tiles, scale, table, neighbors, feat, above, below, pieces, parts, slope, coarse, w_mix, w_res, packed,
    bricks, views, cot, grad_parts, grad_rows, unplace, mix_t, conv_sum, res_sum, mix_sum, sem,
):
    q = pl.program_id(0)
    count, chans = feat.shape[:2]
    wide = coarse.shape[1]
    fetch = pltpu.make_async_copy(feat, bricks.at[pl.ds(0, count)], sem)

    @pl.when(q == 0)
    def _():
        fetch.start()
        place_arrivals(above, below, bricks, count)
        unplace[...] = picker(octant_voxel)
        mix_t[...] = w_mix[...].T
        conv_sum[...] = jnp.zeros_like(conv_sum)
        res_sum[...] = jnp.zeros_like(res_sum)
        mix_sum[...] = jnp.zeros_like(mix_sum)
        fetch.wait()

    per_row = VOX // (LANES * lane_tiles)
    for j in range(pieces.shape[0]):
        chan, part = j // per_row, j % per_row
        for lt in range(lane_tiles):
            lane = (part * lane_tiles + lt) * LANES
            cot[chan * ROWS : (chan + 1) * ROWS, lane : lane + LANES] = pieces[j, 0, lt]
    cots = cot[...]
    grad_coarse = (scale * dot(mix_t[...], cots)).astype(BF16)
    grad_fine = dot(grad_coarse, unplace[...]).astype(BF16)
    mix_sum[...] += dot_nt(cots, coarse[0])
    res_sum[...] += dot_nt(parts[0], grad_fine)
    grad_parts[...] = dot(w_res[...], grad_fine)
    low_half = low_lanes(chans)
    for r in range(4):
        for t in range(4):
            cols = slice(r * LANES, (r + 1) * LANES)
            lanes = slice(t * LANES, (t + 1) * LANES)
            one = grad_parts[2 * t * chans : (2 * t + 1) * chans, cols]
            two = grad_parts[(2 * t + 1) * chans : (2 * t + 2) * chans, cols]
            first = slice(2 * r * chans, (2 * r + 1) * chans)
            second = slice((2 * r + 1) * chans, (2 * r + 2) * chans)
            grad_rows[first, lanes] = (
                jnp.where(low_half, one, pltpu.roll(two, LANES // 2, 1))
                * slope[0, first, lanes].astype(F32)
            ).astype(BF16)
            grad_rows[second, lanes] = (
                jnp.where(low_half, pltpu.roll(one, LANES // 2, 1), two)
                * slope[0, second, lanes].astype(F32)
            ).astype(BF16)

    total = None
    for k in range(8):
        shift_into(sources(table, neighbors, q * 8 + k), bricks, views.at[k])
        term = dot_nt(grad_rows[k * chans : (k + 1) * chans, :], views[k])
        total = term if total is None else total + term
    conv_sum[:, : 7 * chans] += total

    @pl.when(q == pl.num_programs(0) - 1)
    def _():
        packed[0:wide] = (scale * mix_sum[...]).astype(BF16)
        at = wide
        packed[at : at + 8 * chans] = res_sum[...].astype(BF16)
        at += 8 * chans
        for t in range(4):
            packed[at : at + chans] = conv_sum[:, t * LANES : (t + 1) * LANES].astype(BF16)
            at += chans
        if at < packed.shape[0]:
            packed[at:] = jnp.zeros((packed.shape[0] - at, LANES), BF16)


def join_kernel(kids, shares, pieces, msg):
    devices, groups, lane_tiles = pieces.shape[:3]
    slots = groups
    body_rows = slots * lane_tiles * ROWS
    for s in range(devices):
        for q in range(groups):
            kid = kids[s * groups + q]
            owner, slot = kid // slots, kid % slots
            for lt in range(lane_tiles):
                row = pl.multiple_of((slot * lane_tiles + lt) * ROWS, ROWS)
                msg[owner, pl.ds(row, ROWS), :] = pieces[s, q, lt]
    total = jnp.sum(shares[...].astype(F32), axis=0).astype(BF16)
    for j in range(devices):
        msg[j, body_rows:] = total


def unpack_kernel(lane_tiles, msg, coarse_hbm, conv, res, mix, coarse_out, packed, sem):
    devices, rows = msg.shape[:2]
    slots = coarse_out.shape[0]
    wide = mix.shape[0]
    chans = conv.shape[1]
    half = LANES // 2
    per_row = VOX // (LANES * lane_tiles)

    def fill(q):
        for j in range(devices):
            chan, part = j // per_row, j % per_row
            for lt in range(lane_tiles):
                row = (q * lane_tiles + lt) * ROWS
                lane = (part * lane_tiles + lt) * LANES
                coarse_out[q, chan * ROWS : (chan + 1) * ROWS, lane : lane + LANES] = msg[
                    j, row : row + ROWS
                ]

    sends = send_parts(coarse_out, coarse_hbm, sem, fill)
    body_rows = slots * lane_tiles * ROWS
    share = rows - body_rows
    for j in range(devices):
        packed[j * share : (j + 1) * share] = msg[j, body_rows:].astype(F32)
    mix[...] = packed[0:wide]
    at = wide
    for t in range(8):
        res[t] = packed[at : at + chans]
        at += chans
    for t in range(4):
        block = packed[at : at + chans]
        conv[2 * t] = block[:, :half]
        if 2 * t + 1 < 7:
            conv[2 * t + 1] = block[:, half:]
        at += chans
    for send in sends:
        send.wait()


def kernel_call(kernel, out_shape, grid_spec, flops, moved, vmem=VMEM_BYTES):
    return pl.pallas_call(
        kernel,
        out_shape=out_shape,
        grid_spec=grid_spec,
        compiler_params=pltpu.CompilerParams(vmem_limit_bytes=vmem),
        cost_estimate=pl.CostEstimate(flops=flops, bytes_accessed=moved, transcendentals=0),
    )


def body(features, counts, neighbors, parents, w_conv, w_restrict, w_mix, cotangent):
    devices = lax.axis_size("space")
    position = lax.axis_index("space").astype(jnp.int32).reshape(1)
    slots, wide = cotangent.shape[:2]
    count, chans = features.shape[:2]
    lane_tiles = VOX * 8 // devices // LANES
    tiles = slots * lane_tiles
    groups = count // 8
    whole = lambda shape: pl.BlockSpec(shape, lambda *_: (0,) * len(shape))
    any_spec = pl.BlockSpec(memory_space=pl.ANY)
    smem_spec = pl.BlockSpec(memory_space=pltpu.SMEM)
    smem = lambda size: pltpu.SMEM((size,), jnp.int32)
    vmem = pltpu.VMEM
    ints = lambda size: jax.ShapeDtypeStruct((size,), jnp.int32)

    message_shape = (devices, tiles * ROWS + LABEL_ROWS, LANES)
    message = kernel_call(
        functools.partial(pack_kernel, lane_tiles),
        jax.ShapeDtypeStruct(message_shape, BF16),
        pl.GridSpec(
            grid=(1,),
            in_specs=[any_spec] * 2,
            out_specs=any_spec,
            scratch_shapes=[
                pltpu.SMEM((2, count), jnp.int32), smem(groups + 1),
                vmem(cotangent.shape, BF16), vmem(message_shape, BF16),
                pltpu.SemaphoreType.DMA, pltpu.SemaphoreType.DMA((slots,)),
                pltpu.SemaphoreType.DMA((PARTS,)),
            ],
        ),
        1000, 2**20,
    )(parents.T, cotangent)
    spread = lax.all_to_all(message, "space", split_axis=0, concat_axis=0, tiled=True)

    plane = jax.ShapeDtypeStruct((SEND // 2, chans, LANES), BF16)
    up, down, table, ordered = kernel_call(
        table_kernel,
        (plane, plane, ints(4 * count + 1), jax.ShapeDtypeStruct(features.shape, BF16)),
        pl.GridSpec(
            grid=(1,),
            in_specs=[smem_spec] * 4 + [any_spec],
            out_specs=[whole(plane.shape)] * 2 + [smem_spec, any_spec],
            scratch_shapes=[smem(groups + 1)] + [smem(SEND + 1)] * 4
            + [vmem(features.shape, BF16), vmem(features.shape, BF16), vmem((VOX, VOX), BF16),
               pltpu.SemaphoreType.DMA((PARTS,)), pltpu.SemaphoreType.DMA((PARTS,))],
        ),
        1000, 2**20,
    )(position, counts, neighbors.T, parents.T, features)
    below = lax.ppermute(up, "space", [(i, i + 1) for i in range(devices - 1)])
    above = lax.ppermute(down, "space", [(i + 1, i) for i in range(devices - 1)])

    all_kids = spread[:, tiles * ROWS, :groups].astype(jnp.int32).reshape(-1)
    piece_shape = (devices, groups, lane_tiles, ROWS, LANES)
    forward_tiles = kernel_call(
        route_kernel,
        jax.ShapeDtypeStruct(piece_shape, BF16),
        pl.GridSpec(
            grid=(1,),
            in_specs=[smem_spec, whole(message_shape)],
            out_specs=any_spec,
            scratch_shapes=[vmem(piece_shape, BF16), pltpu.SemaphoreType.DMA((PARTS,))],
        ),
        1000, 2**20, SMALL_VMEM_BYTES,
    )(all_kids, spread)
    forward_tiles, above, below = lax.optimization_barrier((forward_tiles, above, below))
    cot_pieces = lax.all_to_all(forward_tiles, "space", split_axis=0, concat_axis=0, tiled=True)

    res_rows = w_restrict.transpose(0, 2, 1).reshape(8 * chans, wide)
    scalars = (table, neighbors.T)
    brick_scratch = vmem((count + SEND + 1, chans, VOX), BF16)
    view_scratch = vmem((8, 7 * chans, VOX), BF16)
    per_group = lambda *shape: pl.BlockSpec((1,) + shape, lambda q: (q,) + (0,) * len(shape))
    piece_spec = pl.BlockSpec((devices, 1, lane_tiles, ROWS, LANES), lambda q: (0, q, 0, 0, 0))
    parts, slope, coarse, pieces = kernel_call(
        functools.partial(forward_kernel, lane_tiles),
        (
            jax.ShapeDtypeStruct((groups, 8 * chans, VOX), BF16),
            jax.ShapeDtypeStruct((groups, 8 * chans, VOX), BF16),
            jax.ShapeDtypeStruct((groups, wide, VOX), BF16),
            jax.ShapeDtypeStruct(piece_shape, BF16),
        ),
        pl.GridSpec(
            grid=(groups + 1,),
            in_specs=[any_spec] * 8,
            out_specs=[
                pl.BlockSpec((1, 8 * chans, VOX), lambda q: (jnp.minimum(q, groups - 1), 0, 0)),
                pl.BlockSpec((1, 8 * chans, VOX), lambda q: (jnp.minimum(q, groups - 1), 0, 0)),
                pl.BlockSpec((1, wide, VOX), lambda q: (jnp.maximum(q - 1, 0), 0, 0)),
                pl.BlockSpec(
                    (devices, 1, lane_tiles, ROWS, LANES),
                    lambda q: (0, jnp.maximum(q - 1, 0), 0, 0, 0),
                ),
            ],
            scratch_shapes=[
                brick_scratch, view_scratch, vmem((VOX, VOX), BF16), vmem(w_conv.shape, BF16),
                vmem(res_rows.shape, BF16), vmem(w_mix.shape, BF16),
                vmem((chans, 7 * chans), BF16), vmem((wide, 8 * chans), BF16),
                vmem((wide, VOX), BF16), smem(4 * count + 1),
                pltpu.SMEM((6, count), jnp.int32), vmem(plane.shape, BF16),
                vmem(plane.shape, BF16), pltpu.SemaphoreType.DMA((7 + PARTS,)),
            ],
        ),
        16 * 10**9, 16 * 2**20,
    )(*scalars, ordered, w_conv, res_rows, w_mix, above, below)
    returned = lax.all_to_all(pieces, "space", split_axis=0, concat_axis=0, tiled=True)

    scale = 1.0 / math.sqrt(devices * slots * VOX)
    used = wide + 8 * chans + 4 * chans
    rows = -(-used // (devices * 8)) * 8
    packed = kernel_call(
        functools.partial(backward_kernel, lane_tiles, scale),
        jax.ShapeDtypeStruct((devices * rows, LANES), BF16),
        pl.GridSpec(
            grid=(groups,),
            in_specs=[smem_spec] * 2 + [any_spec] + [whole(plane.shape)] * 2
            + [piece_spec, per_group(8 * chans, VOX), per_group(8 * chans, VOX),
               per_group(wide, VOX), whole(w_mix.shape), whole(res_rows.shape)],
            out_specs=whole((devices * rows, LANES)),
            scratch_shapes=[
                brick_scratch, view_scratch, vmem((wide, VOX), BF16),
                vmem((8 * chans, VOX), F32), vmem((8 * chans, VOX), BF16), vmem((VOX, VOX), BF16),
                vmem((wide, wide), BF16), vmem((chans, 8 * chans), F32),
                vmem((8 * chans, wide), F32), vmem((wide, wide), F32), pltpu.SemaphoreType.DMA,
            ],
        ),
        16 * 10**9, 16 * 2**20,
    )(*scalars, ordered, above, below, cot_pieces, parts, slope, coarse, w_mix, res_rows)

    shares = lax.all_to_all(
        packed.reshape(devices, rows, LANES), "space", split_axis=0, concat_axis=0, tiled=True
    )
    joined_shape = (devices, tiles * ROWS + rows, LANES)
    joined = kernel_call(
        join_kernel,
        jax.ShapeDtypeStruct(joined_shape, BF16),
        pl.GridSpec(
            grid=(1,),
            in_specs=[smem_spec, whole(shares.shape), whole(piece_shape)],
            out_specs=whole(joined_shape),
        ),
        1000, 2**20, SMALL_VMEM_BYTES,
    )(all_kids, shares, returned)
    finished = lax.all_to_all(joined, "space", split_axis=0, concat_axis=0, tiled=True)

    coarse_out, grad_conv, grad_res, grad_mix = kernel_call(
        functools.partial(unpack_kernel, lane_tiles),
        (
            jax.ShapeDtypeStruct((slots, wide, VOX), BF16),
            jax.ShapeDtypeStruct((7, chans, chans), F32),
            jax.ShapeDtypeStruct((8, chans, wide), F32),
            jax.ShapeDtypeStruct((wide, wide), F32),
        ),
        pl.GridSpec(
            grid=(1,),
            in_specs=[whole(joined_shape)],
            out_specs=[any_spec, whole((7, chans, chans)),
                       whole((8, chans, wide)), whole((wide, wide))],
            scratch_shapes=[
                vmem((slots, wide, VOX), BF16), vmem((devices * rows, LANES), F32),
                pltpu.SemaphoreType.DMA((PARTS,)),
            ],
        ),
        1000, 2 * 2**20, SMALL_VMEM_BYTES,
    )(finished)
    return coarse_out, grad_conv, grad_res.transpose(0, 2, 1), grad_mix


def solution(mesh):
    return jax.shard_map(
        body,
        mesh=mesh,
        in_specs=(
            P(("groups", "space"), None, None),
            P(("groups", "space")),
            P(("groups", "space"), None),
            P(("groups", "space"), None),
            P(),
            P(),
            P(),
            P(("groups", "space"), None, None),
        ),
        out_specs=(
            P(("groups", "space"), None, None),
            P("groups", None, None),
            P("groups", None, None),
            P("groups", None),
        ),
        check_vma=False,
    )
```

```python
import functools
import math

import jax
import jax.numpy as jnp
from jax import lax
from jax.experimental import pallas as pl
from jax.experimental.pallas import tpu as pltpu
from jax.sharding import PartitionSpec as P

EDGE = 8
HALF = EDGE // 2
VOX = EDGE**3
LANES = 128
ROWS = 16
LABEL_ROWS = 8
SEND = 8
PARTS = 4
BF16 = jnp.bfloat16
F32 = jnp.float32
VMEM_BYTES = 60 * 1024 * 1024
SMALL_VMEM_BYTES = 16 * 1024 * 1024


def bits_of(value):
    return [(value >> (8 - k)) & 1 for k in range(9)]


def join_bits(bits):
    value = bits[0]
    for bit in bits[1:]:
        value = value * 2 + bit
    return value


def split_voxel(column):
    ta, tb, tc, a1, a0, b1, b0, c1, c0 = bits_of(column)
    return join_bits([a1, a0, ta, b1, b0, tb, c1, c0, tc])


def octant_voxel(column):
    oa, ob, oc, a1, a0, b1, b0, c1, c0 = bits_of(column)
    return join_bits([oa, a1, a0, ob, b1, b0, oc, c1, c0])


def picker(voxel_of, shape=(VOX, VOX), start=(0, 0), flip=False):
    row = lax.broadcasted_iota(jnp.int32, shape, 0) + start[0]
    column = lax.broadcasted_iota(jnp.int32, shape, 1) + start[1]
    return (column == voxel_of(row) if flip else row == voxel_of(column)).astype(BF16)


def dot(a, b):
    return jnp.dot(a, b, preferred_element_type=F32)


def dot_nt(a, b):
    return lax.dot_general(a, b, (((1,), (1,)), ((), ())), preferred_element_type=F32)


def pack_kernel(lane_tiles, parents, cot, msg, kids_out, kids):
    devices = msg.shape[0]
    slots = cot.shape[0]

    def find(g, found):
        kids[found] = parents[0, g]
        return found + (parents[1, g] == 0).astype(jnp.int32)

    lax.fori_loop(0, parents.shape[1], find, jnp.int32(0), unroll=4)
    lane = lax.broadcasted_iota(jnp.int32, (LABEL_ROWS, LANES), 1)
    label = jnp.zeros((LABEL_ROWS, LANES), jnp.int32)
    for q in range(kids_out.shape[0]):
        kids_out[q] = kids[q]
        label = jnp.where(lane == q, kids[q], label)
    label = label.astype(F32).astype(BF16)
    for j in range(devices):
        msg[j, slots * lane_tiles * ROWS :] = label
    per_row = VOX // (LANES * lane_tiles)
    for j in range(devices):
        chan, part = j // per_row, j % per_row
        for q in range(slots):
            for lt in range(lane_tiles):
                lane = (part * lane_tiles + lt) * LANES
                row = (q * lane_tiles + lt) * ROWS
                msg[j, row : row + ROWS] = cot[
                    q, chan * ROWS : (chan + 1) * ROWS, lane : lane + LANES
                ]


def table_kernel(
    place, counts, kids, neighbors, parents, feat, up, down, table, ordered,
    up_idx, up_far, down_idx, down_far, bricks, done, split, in_sem, out_sem,
):
    count, chans = feat.shape[:2]
    part = count // PARTS
    fetches = [
        pltpu.make_async_copy(
            feat.at[pl.ds(k * part, part)], bricks.at[pl.ds(k * part, part)], in_sem.at[k]
        )
        for k in range(PARTS)
    ]
    for fetch in fetches:
        fetch.start()
    base = place[0] * count
    table[4 * count] = place[0]
    for r in range(SEND + 1):
        up_idx[r] = 0
        down_idx[r] = 0
        up_far[r] = 2 * count
        down_far[r] = 2 * count
    split[...] = picker(split_voxel)

    def scan(g, found):
        n_up, n_down = found
        near_up, near_down = neighbors[0, g], neighbors[1, g]
        far_up, far_down = near_up - base - count, near_down - base + count
        goes_up = (near_up >= 0) & (far_up >= 0)
        goes_down = (near_down >= 0) & (far_down < count)
        up_idx[n_up] = g
        up_far[n_up] = jnp.where(goes_up, far_up, 2 * count)
        down_idx[n_down] = g
        down_far[n_down] = jnp.where(goes_down, far_down, 2 * count)
        q = jnp.int32(0)
        for k in range(1, kids.shape[0]):
            q += jnp.where(kids[k] == parents[0, g], k, 0)
        number = q * 8 + parents[1, g]
        table[number] = g
        table[count + number] = jnp.where(g < counts[0], g, count + SEND)
        return n_up + goes_up.astype(jnp.int32), n_down + goes_down.astype(jnp.int32)

    lax.fori_loop(0, count, scan, (jnp.int32(0), jnp.int32(0)), unroll=4)

    def rank(r, carry):
        for start, far, idx in ((2 * count, up_far, up_idx), (3 * count, down_far, down_idx)):
            earlier = jnp.int32(0)
            for other in range(SEND):
                earlier += (far[other] < far[r]).astype(jnp.int32)

            @pl.when(far[r] < count)
            def _():
                table[start + idx[r]] = count + earlier

        return carry

    lax.fori_loop(0, SEND, rank, jnp.int32(0))
    sends = []
    for k in range(PARTS):
        fetches[k].wait()
        rows = bricks[k * part : (k + 1) * part].reshape(part * chans, VOX)
        done[k * part : (k + 1) * part] = (
            dot(rows, split[...]).astype(BF16).reshape(part, chans, VOX)
        )
        sends.append(
            pltpu.make_async_copy(
                done.at[pl.ds(k * part, part)], ordered.at[pl.ds(k * part, part)], out_sem.at[k]
            )
        )
        sends[-1].start()
    low = low_lanes(chans)
    for r in range(SEND // 2):
        other = r + SEND // 2
        top = slice(VOX - LANES, VOX)
        up[r] = jnp.where(
            low,
            pltpu.roll(bricks[up_idx[r], :, top], LANES // 2, 1),
            bricks[up_idx[other], :, top],
        )
        down[r] = jnp.where(
            low,
            bricks[down_idx[r], :, :LANES],
            pltpu.roll(bricks[down_idx[other], :, :LANES], LANES // 2, 1),
        )
    for send in sends:
        send.wait()


def route_kernel(kids, msg, pieces):
    devices, groups, lane_tiles = pieces.shape[:3]
    slots = groups
    for s in range(devices):
        for q in range(groups):
            kid = kids[s * groups + q]
            owner, slot = kid // slots, kid % slots
            for lt in range(lane_tiles):
                row = pl.multiple_of((slot * lane_tiles + lt) * ROWS, ROWS)
                pieces[s, q, lt] = msg[owner, pl.ds(row, ROWS), :]


def place_arrivals(above, below, bricks, count):
    chans = bricks.shape[1]
    half = VOX // 2
    side = LANES // 2
    shape = (LANES, half)
    pairs = SEND // 2
    for k, shift in ((0, 0), (pairs, -side)):
        slots = slice(count + k, count + k + pairs)
        first = dot(
            above[...].reshape(pairs * chans, LANES), picker(split_voxel, shape, (shift, 0))
        )
        last = dot(
            below[...].reshape(pairs * chans, LANES),
            picker(split_voxel, shape, (VOX - side + shift, half)),
        )
        bricks[slots, :, :half] = first.astype(BF16).reshape(pairs, chans, half)
        bricks[slots, :, half:] = last.astype(BF16).reshape(pairs, chans, half)
    bricks[count + SEND] = jnp.zeros(bricks.shape[1:], BF16)


def sources(table, neighbors, number):
    count = neighbors.shape[1]
    g = table[number]
    found = []
    for d in range(6):
        near = neighbors[d, g]
        local = near - table[4 * count] * count
        if d == 0:
            local = jnp.where(local >= count, table[2 * count + g], local)
        if d == 1:
            local = jnp.where(local < 0, table[3 * count + g], local)
        found.append(jnp.where(near >= 0, local, count + SEND))
    found.append(table[count + number])
    return found


def turn_matrices(turns):
    row = lax.broadcasted_iota(jnp.int32, (2 * LANES, LANES), 0)
    lane = lax.broadcasted_iota(jnp.int32, (2 * LANES, LANES), 1)
    low = lane < LANES // 2
    c = lane % HALF
    plus = jnp.where(low, lane + 64, jnp.where(c < HALF - 1, lane - 63, LANES + lane - 67))
    minus = jnp.where(low, jnp.where(c > 0, lane + 63, LANES + lane + 67), lane - 64)
    turns[0] = (row == plus).astype(BF16)
    turns[1] = (row == minus).astype(BF16)


def shift_into(slots, bricks, turns, views):
    chans = bricks.shape[1]
    tiles = VOX // LANES
    lane = lax.broadcasted_iota(jnp.int32, (chans, LANES), 1)
    a = (lane // 16) % HALF
    b = (lane // 4) % HALF

    def tile(slot, t):
        return bricks[slot, :, t * LANES : (t + 1) * LANES]

    def turn(value, by):
        return pltpu.roll(value, by % LANES, 1)

    x = [tile(slots[6], t) for t in range(tiles)]
    along_c = []
    for k in range(2):
        rows = [
            jnp.concatenate([x[t], tile(slots[4 + k], t)], axis=1) for t in range(tiles)
        ]
        along_c.append(dot(jnp.concatenate(rows, axis=0), turns[k]).astype(BF16))
    for t in range(tiles):
        lanes = slice(t * LANES, (t + 1) * LANES)
        if t < 2:
            plus_a = x[t + 2]
            minus_a = jnp.where(a > 0, turn(x[t + 2], 16), turn(tile(slots[1], t + 2), -48))
        else:
            plus_a = jnp.where(a < HALF - 1, turn(x[t - 2], -16), turn(tile(slots[0], t - 2), 48))
            minus_a = x[t - 2]
        if t % 2 == 0:
            plus_b = x[t + 1]
            minus_b = jnp.where(b > 0, turn(x[t + 1], 4), turn(tile(slots[3], t + 1), -12))
        else:
            plus_b = jnp.where(b < HALF - 1, turn(x[t - 1], -4), turn(tile(slots[2], t - 1), 12))
            minus_b = x[t - 1]
        rows = slice(t * chans, (t + 1) * chans)
        out = [plus_a, minus_a, plus_b, minus_b, along_c[0][rows], along_c[1][rows], x[t]]
        for d in range(7):
            views[d * chans : (d + 1) * chans, lanes] = out[d]


def low_lanes(rows):
    return lax.broadcasted_iota(jnp.int32, (rows, LANES), 1) < LANES // 2


def forward_kernel(
    lane_tiles, table_hbm, neighbors_hbm, feat, w_conv_hbm, w_res_hbm, w_mix_hbm,
    above_hbm, below_hbm,
    parts_out, slope_out, coarse_out, piece_out,
    bricks, views, turns, place, w_conv, w_res, w_mix, conv_cat, res_cat, octants,
    table, neighbors, above, below, sem,
):
    q = pl.program_id(0)
    groups = pl.num_programs(0) - 1
    count, chans = feat.shape[:2]
    part = count // PARTS

    @pl.when(q == 0)
    def _():
        copies = [
            pltpu.make_async_copy(source, target, sem.at[k])
            for k, (source, target) in enumerate((
                (above_hbm, above), (below_hbm, below), (w_conv_hbm, w_conv),
                (w_res_hbm, w_res), (w_mix_hbm, w_mix), (table_hbm, table),
                (neighbors_hbm, neighbors),
                *(
                    (feat.at[pl.ds(k * part, part)], bricks.at[pl.ds(k * part, part)])
                    for k in range(PARTS)
                ),
            ))
        ]
        for copy in copies:
            copy.start()
        place[...] = picker(octant_voxel, flip=True)
        turn_matrices(turns)
        for copy in copies[:-PARTS]:
            copy.wait()
        place_arrivals(above, below, bricks, count)
        for d in range(7):
            conv_cat[:, d * chans : (d + 1) * chans] = w_conv[d]
        res_cat[...] = w_res[...].T
        for copy in copies[-PARTS:]:
            copy.wait()

    low_half = low_lanes(chans)

    def finish():
        coarse = dot(octants[...], place[...]).astype(BF16)
        coarse_out[0] = coarse
        mixed = dot(w_mix[...], coarse).astype(BF16)
        per_row = VOX // (LANES * lane_tiles)
        for j in range(piece_out.shape[0]):
            chan, part = j // per_row, j % per_row
            for lt in range(lane_tiles):
                lane = (part * lane_tiles + lt) * LANES
                piece_out[j, 0, lt] = mixed[chan * ROWS : (chan + 1) * ROWS, lane : lane + LANES]

    def restrict(first):
        acts = []
        for k in range(first, first + 4):
            shift_into(sources(table, neighbors, q * 8 + k), bricks, turns, views.at[k])
            hidden = dot(conv_cat[...], views[k])
            sig = 1.0 / (1.0 + jnp.exp(-hidden))
            act = hidden * sig
            slope_out[0, k * chans : (k + 1) * chans, :] = (sig + act * (1.0 - sig)).astype(BF16)
            acts.append(act.astype(BF16))
        for k in range(0, 4, 2):
            lanes = slice((first + k) * (LANES // 2), (first + k + 2) * (LANES // 2))
            for t in range(4):
                one = acts[k][:, t * LANES : (t + 1) * LANES]
                two = acts[k + 1][:, t * LANES : (t + 1) * LANES]
                parts_out[0, 2 * t * chans : (2 * t + 1) * chans, lanes] = jnp.where(
                    low_half, one, pltpu.roll(two, LANES // 2, 1)
                )
                parts_out[0, (2 * t + 1) * chans : (2 * t + 2) * chans, lanes] = jnp.where(
                    low_half, pltpu.roll(one, LANES // 2, 1), two
                )
        lanes = slice(first * (LANES // 2), (first + 4) * (LANES // 2))
        return dot(res_cat[...], parts_out[0, :, lanes]).astype(BF16)

    @pl.when(q < groups)
    def _():
        finish()
        halves = [restrict(0), restrict(4)]
        octants[...] = jnp.concatenate(halves, axis=1)

    @pl.when(q == groups)
    def _():
        finish()


def backward_kernel(
    lane_tiles, scale, table_hbm, neighbors_hbm, feat, above_hbm, below_hbm, pieces, parts, slope,
    coarse, w_mix, w_res, own, other,
    bricks, views, turns, cot, grad_parts, grad_rows, unplace, mix_t, conv_sum, res_sum, mix_sum, packed,
    table, neighbors, above, below, sem,
):
    q = pl.program_id(0)
    count, chans = feat.shape[:2]
    wide = coarse.shape[1]
    part = count // PARTS

    def start_fetches():
        pairs = [(table_hbm, table), (neighbors_hbm, neighbors), (above_hbm, above),
                 (below_hbm, below)]
        for k in range(PARTS):
            slots = pl.ds(k * part, part)
            pairs.append((feat.at[slots], bricks.at[slots]))
        copies = [
            pltpu.make_async_copy(source, target, sem.at[k])
            for k, (source, target) in enumerate(pairs)
        ]
        for copy in copies:
            copy.start()
        return copies

    def gradients():
        per_row = VOX // (LANES * lane_tiles)
        for j in range(pieces.shape[0]):
            chan, half = j // per_row, j % per_row
            for lt in range(lane_tiles):
                lane = (half * lane_tiles + lt) * LANES
                cot[chan * ROWS : (chan + 1) * ROWS, lane : lane + LANES] = pieces[j, 0, lt]
        cots = cot[...]
        grad_coarse = (scale * dot(mix_t[...], cots)).astype(BF16)
        grad_fine = dot(grad_coarse, unplace[...]).astype(BF16)
        mix_sum[...] += dot_nt(cots, coarse[0])
        res_sum[...] += dot_nt(parts[0], grad_fine)
        grad_parts[...] = dot(w_res[...], grad_fine)
        low_half = low_lanes(chans)
        for r in range(4):
            for t in range(4):
                cols = slice(r * LANES, (r + 1) * LANES)
                lanes = slice(t * LANES, (t + 1) * LANES)
                one = grad_parts[2 * t * chans : (2 * t + 1) * chans, cols]
                two = grad_parts[(2 * t + 1) * chans : (2 * t + 2) * chans, cols]
                first = slice(2 * r * chans, (2 * r + 1) * chans)
                second = slice((2 * r + 1) * chans, (2 * r + 2) * chans)
                grad_rows[first, lanes] = (
                    jnp.where(low_half, one, pltpu.roll(two, LANES // 2, 1))
                    * slope[0, first, lanes].astype(F32)
                ).astype(BF16)
                grad_rows[second, lanes] = (
                    jnp.where(low_half, pltpu.roll(one, LANES // 2, 1), two)
                    * slope[0, second, lanes].astype(F32)
                ).astype(BF16)

    def convolution():
        total = None
        for k in range(8):
            shift_into(sources(table, neighbors, q * 8 + k), bricks, turns, views.at[k])
            term = dot_nt(grad_rows[k * chans : (k + 1) * chans, :], views[k])
            total = term if total is None else total + term
        conv_sum[:, : 7 * chans] += total

    @pl.when(q == 0)
    def _():
        copies = start_fetches()
        unplace[...] = picker(octant_voxel)
        turn_matrices(turns)
        mix_t[...] = w_mix[...].T
        conv_sum[...] = jnp.zeros_like(conv_sum)
        res_sum[...] = jnp.zeros_like(res_sum)
        mix_sum[...] = jnp.zeros_like(mix_sum)
        gradients()
        for copy in copies:
            copy.wait()
        place_arrivals(above, below, bricks, count)
        convolution()

    @pl.when(q > 0)
    def _():
        gradients()
        convolution()

    @pl.when(q == pl.num_programs(0) - 1)
    def _():
        packed[0:wide] = scale * mix_sum[...]
        at = wide
        packed[at : at + 8 * chans] = res_sum[...]
        at += 8 * chans
        for t in range(4):
            packed[at : at + chans] = conv_sum[:, t * LANES : (t + 1) * LANES]
            at += chans
        if at < packed.shape[0]:
            packed[at:] = jnp.zeros((packed.shape[0] - at, LANES), F32)
        chips, rows = own.shape[:2]
        core = table[4 * count] % 2
        for c in range(chips):
            first = pl.multiple_of((2 * c + core) * rows, 8)
            second = pl.multiple_of((2 * c + 1 - core) * rows, 8)
            own[c] = packed[pl.ds(first, rows), :]
            other[c] = packed[pl.ds(second, rows), :]


def join_kernel(kids, shares, pieces, msg):
    devices, groups, lane_tiles = pieces.shape[:3]
    slots = groups
    body_rows = slots * lane_tiles * ROWS
    for s in range(devices):
        for q in range(groups):
            kid = kids[s * groups + q]
            owner, slot = kid // slots, kid % slots
            for lt in range(lane_tiles):
                row = pl.multiple_of((slot * lane_tiles + lt) * ROWS, ROWS)
                msg[owner, pl.ds(row, ROWS), :] = pieces[s, q, lt]
    total = jnp.sum(shares[...].astype(F32), axis=0).astype(BF16)
    for j in range(devices):
        msg[j, body_rows:] = total


def unpack_kernel(lane_tiles, msg, coarse_out, conv, res, mix, packed):
    devices, rows = msg.shape[:2]
    slots = coarse_out.shape[0]
    wide = mix.shape[0]
    chans = conv.shape[1]
    half = LANES // 2
    body_rows = slots * lane_tiles * ROWS
    share = rows - body_rows
    for j in range(devices):
        packed[j * share : (j + 1) * share] = msg[j, body_rows:].astype(F32)
    mix[...] = packed[0:wide]
    at = wide
    for t in range(8):
        res[t] = packed[at : at + chans]
        at += chans
    for t in range(4):
        block = packed[at : at + chans]
        conv[2 * t] = block[:, :half]
        if 2 * t + 1 < 7:
            conv[2 * t + 1] = block[:, half:]
        at += chans
    per_row = VOX // (LANES * lane_tiles)
    for j in range(devices):
        chan, part = j // per_row, j % per_row
        for q in range(slots):
            for lt in range(lane_tiles):
                row = (q * lane_tiles + lt) * ROWS
                lane = (part * lane_tiles + lt) * LANES
                coarse_out[q, chan * ROWS : (chan + 1) * ROWS, lane : lane + LANES] = msg[
                    j, row : row + ROWS
                ]


def kernel_call(kernel, out_shape, grid_spec, flops, moved, vmem=VMEM_BYTES):
    return pl.pallas_call(
        kernel,
        out_shape=out_shape,
        grid_spec=grid_spec,
        compiler_params=pltpu.CompilerParams(vmem_limit_bytes=vmem),
        cost_estimate=pl.CostEstimate(flops=flops, bytes_accessed=moved, transcendentals=0),
    )


def body(features, counts, neighbors, parents, w_conv, w_restrict, w_mix, cotangent):
    devices = lax.axis_size("space")
    position = lax.axis_index("space").astype(jnp.int32).reshape(1)
    slots, wide = cotangent.shape[:2]
    count, chans = features.shape[:2]
    lane_tiles = VOX * 8 // devices // LANES
    tiles = slots * lane_tiles
    groups = count // 8
    whole = lambda shape: pl.BlockSpec(shape, lambda *_: (0,) * len(shape))
    any_spec = pl.BlockSpec(memory_space=pl.ANY)
    smem_spec = pl.BlockSpec(memory_space=pltpu.SMEM)
    smem = lambda size: pltpu.SMEM((size,), jnp.int32)
    vmem = pltpu.VMEM
    ints = lambda size: jax.ShapeDtypeStruct((size,), jnp.int32)

    message_shape = (devices, tiles * ROWS + LABEL_ROWS, LANES)
    message, kids = kernel_call(
        functools.partial(pack_kernel, lane_tiles),
        (jax.ShapeDtypeStruct(message_shape, BF16), ints(groups)),
        pl.GridSpec(
            grid=(1,),
            in_specs=[smem_spec, whole(cotangent.shape)],
            out_specs=[whole(message_shape), smem_spec],
            scratch_shapes=[smem(groups + 1)],
        ),
        1000, 2**20,
    )(parents.T, cotangent)
    spread = lax.all_to_all(message, "space", split_axis=0, concat_axis=0, tiled=True)

    plane = jax.ShapeDtypeStruct((SEND // 2, chans, LANES), BF16)
    up, down, table, ordered = kernel_call(
        table_kernel,
        (plane, plane, ints(4 * count + 1), jax.ShapeDtypeStruct(features.shape, BF16)),
        pl.GridSpec(
            grid=(1,),
            in_specs=[smem_spec] * 5 + [any_spec],
            out_specs=[whole(plane.shape)] * 2 + [smem_spec, any_spec],
            scratch_shapes=[smem(SEND + 1)] * 4
            + [vmem(features.shape, BF16), vmem(features.shape, BF16), vmem((VOX, VOX), BF16),
               pltpu.SemaphoreType.DMA((PARTS,)), pltpu.SemaphoreType.DMA((PARTS,))],
        ),
        1000, 2**20,
    )(position, counts, kids, neighbors.T, parents.T, features)
    below = lax.ppermute(up, "space", [(i, i + 1) for i in range(devices - 1)])
    above = lax.ppermute(down, "space", [(i + 1, i) for i in range(devices - 1)])

    all_kids = spread[:, tiles * ROWS, :groups].astype(jnp.int32).reshape(-1)
    piece_shape = (devices, groups, lane_tiles, ROWS, LANES)
    forward_tiles = kernel_call(
        route_kernel,
        jax.ShapeDtypeStruct(piece_shape, BF16),
        pl.GridSpec(
            grid=(1,),
            in_specs=[smem_spec, whole(message_shape)],
            out_specs=whole(piece_shape),
        ),
        1000, 2**20, SMALL_VMEM_BYTES,
    )(all_kids, spread)
    forward_tiles, above, below = lax.optimization_barrier((forward_tiles, above, below))
    cot_pieces = lax.all_to_all(forward_tiles, "space", split_axis=0, concat_axis=0, tiled=True)

    res_rows = w_restrict.transpose(0, 2, 1).reshape(8 * chans, wide)
    scalars = (table, neighbors.T)
    brick_scratch = vmem((count + SEND + 1, chans, VOX), BF16)
    turn_scratch = vmem((2, 2 * LANES, LANES), BF16)
    view_scratch = vmem((8, 7 * chans, VOX), BF16)
    per_group = lambda *shape: pl.BlockSpec((1,) + shape, lambda q: (q,) + (0,) * len(shape))
    piece_spec = pl.BlockSpec((devices, 1, lane_tiles, ROWS, LANES), lambda q: (0, q, 0, 0, 0))
    parts, slope, coarse, pieces = kernel_call(
        functools.partial(forward_kernel, lane_tiles),
        (
            jax.ShapeDtypeStruct((groups, 8 * chans, VOX), BF16),
            jax.ShapeDtypeStruct((groups, 8 * chans, VOX), BF16),
            jax.ShapeDtypeStruct((groups, wide, VOX), BF16),
            jax.ShapeDtypeStruct(piece_shape, BF16),
        ),
        pl.GridSpec(
            grid=(groups + 1,),
            in_specs=[any_spec] * 8,
            out_specs=[
                pl.BlockSpec((1, 8 * chans, VOX), lambda q: (jnp.minimum(q, groups - 1), 0, 0)),
                pl.BlockSpec((1, 8 * chans, VOX), lambda q: (jnp.minimum(q, groups - 1), 0, 0)),
                pl.BlockSpec((1, wide, VOX), lambda q: (jnp.maximum(q - 1, 0), 0, 0)),
                pl.BlockSpec(
                    (devices, 1, lane_tiles, ROWS, LANES),
                    lambda q: (0, jnp.maximum(q - 1, 0), 0, 0, 0),
                ),
            ],
            scratch_shapes=[
                brick_scratch, view_scratch, turn_scratch, vmem((VOX, VOX), BF16), vmem(w_conv.shape, BF16),
                vmem(res_rows.shape, BF16), vmem(w_mix.shape, BF16),
                vmem((chans, 7 * chans), BF16), vmem((wide, 8 * chans), BF16),
                vmem((wide, VOX), BF16), smem(4 * count + 1),
                pltpu.SMEM((6, count), jnp.int32), vmem(plane.shape, BF16),
                vmem(plane.shape, BF16), pltpu.SemaphoreType.DMA((7 + PARTS,)),
            ],
        ),
        16 * 10**9, 16 * 2**20,
    )(*scalars, ordered, w_conv, res_rows, w_mix, above, below)
    returned = lax.all_to_all(pieces, "space", split_axis=0, concat_axis=0, tiled=True)

    scale = 1.0 / math.sqrt(devices * slots * VOX)
    used = wide + 8 * chans + 4 * chans
    rows = -(-used // (devices * 8)) * 8
    half = jax.ShapeDtypeStruct((devices // 2, rows, LANES), F32)
    own, other = kernel_call(
        functools.partial(backward_kernel, lane_tiles, scale),
        (half, half),
        pl.GridSpec(
            grid=(groups,),
            in_specs=[any_spec] * 5
            + [piece_spec, per_group(8 * chans, VOX), per_group(8 * chans, VOX),
               per_group(wide, VOX), whole(w_mix.shape), whole(res_rows.shape)],
            out_specs=[whole(half.shape)] * 2,
            scratch_shapes=[
                brick_scratch, view_scratch, turn_scratch, vmem((wide, VOX), BF16),
                vmem((8 * chans, VOX), F32), vmem((8 * chans, VOX), BF16), vmem((VOX, VOX), BF16),
                vmem((wide, wide), BF16), vmem((chans, 8 * chans), F32),
                vmem((8 * chans, wide), F32), vmem((wide, wide), F32),
                vmem((devices * rows, LANES), F32), smem(4 * count + 1),
                pltpu.SMEM((6, count), jnp.int32), vmem(plane.shape, BF16),
                vmem(plane.shape, BF16), pltpu.SemaphoreType.DMA((4 + PARTS,)),
            ],
        ),
        16 * 10**9, 16 * 2**20,
    )(*scalars, ordered, above, below, cot_pieces, parts, slope, coarse, w_mix, res_rows)

    came = lax.ppermute(other, "space", [(i, i ^ 1) for i in range(devices)])
    paired = (own + came).astype(BF16)
    shares = lax.all_to_all(
        paired, "space", split_axis=0, concat_axis=0, tiled=True,
        axis_index_groups=[list(range(core, devices, 2)) for core in range(2)],
    )

    joined_shape = (devices, tiles * ROWS + rows, LANES)
    joined = kernel_call(
        join_kernel,
        jax.ShapeDtypeStruct(joined_shape, BF16),
        pl.GridSpec(
            grid=(1,),
            in_specs=[smem_spec, whole(shares.shape), whole(piece_shape)],
            out_specs=whole(joined_shape),
        ),
        1000, 2**20, SMALL_VMEM_BYTES,
    )(all_kids, shares, returned)
    finished = lax.all_to_all(joined, "space", split_axis=0, concat_axis=0, tiled=True)

    coarse_out, grad_conv, grad_res, grad_mix = kernel_call(
        functools.partial(unpack_kernel, lane_tiles),
        (
            jax.ShapeDtypeStruct((slots, wide, VOX), BF16),
            jax.ShapeDtypeStruct((7, chans, chans), F32),
            jax.ShapeDtypeStruct((8, chans, wide), F32),
            jax.ShapeDtypeStruct((wide, wide), F32),
        ),
        pl.GridSpec(
            grid=(1,),
            in_specs=[whole(joined_shape)],
            out_specs=[whole((slots, wide, VOX)), whole((7, chans, chans)),
                       whole((8, chans, wide)), whole((wide, wide))],
            scratch_shapes=[vmem((devices * rows, LANES), F32)],
        ),
        1000, 2 * 2**20, SMALL_VMEM_BYTES,
    )(finished)
    return coarse_out, grad_conv, grad_res.transpose(0, 2, 1), grad_mix


def solution(mesh):
    return jax.shard_map(
        body,
        mesh=mesh,
        in_specs=(
            P(("groups", "space"), None, None),
            P(("groups", "space")),
            P(("groups", "space"), None),
            P(("groups", "space"), None),
            P(),
            P(),
            P(),
            P(("groups", "space"), None, None),
        ),
        out_specs=(
            P(("groups", "space"), None, None),
            P("groups", None, None),
            P("groups", None, None),
            P("groups", None),
        ),
        check_vma=False,
    )
```

```python
import functools
import math

import jax
import jax.numpy as jnp
from jax import lax
from jax.experimental import pallas as pl
from jax.experimental.pallas import tpu as pltpu
from jax.sharding import PartitionSpec as P

EDGE = 8
HALF = EDGE // 2
VOX = EDGE**3
LANES = 128
ROWS = 16
LABEL_ROWS = 8
SEND = 8
PARTS = 4
BF16 = jnp.bfloat16
F32 = jnp.float32
VMEM_BYTES = 60 * 1024 * 1024
SMALL_VMEM_BYTES = 16 * 1024 * 1024


def bits_of(value):
    return [(value >> (8 - k)) & 1 for k in range(9)]


def join_bits(bits):
    value = bits[0]
    for bit in bits[1:]:
        value = value * 2 + bit
    return value


def split_voxel(column):
    ta, tb, tc, a1, a0, b1, b0, c1, c0 = bits_of(column)
    return join_bits([a1, a0, ta, b1, b0, tb, c1, c0, tc])


def octant_voxel(column):
    oa, ob, oc, a1, a0, b1, b0, c1, c0 = bits_of(column)
    return join_bits([oa, a1, a0, ob, b1, b0, oc, c1, c0])


def picker(voxel_of, shape=(VOX, VOX), start=(0, 0), flip=False):
    row = lax.broadcasted_iota(jnp.int32, shape, 0) + start[0]
    column = lax.broadcasted_iota(jnp.int32, shape, 1) + start[1]
    return (column == voxel_of(row) if flip else row == voxel_of(column)).astype(BF16)


def dot(a, b):
    return jnp.dot(a, b, preferred_element_type=F32)


def dot_nt(a, b):
    return lax.dot_general(a, b, (((1,), (1,)), ((), ())), preferred_element_type=F32)


def pack_kernel(lane_tiles, parents, cot, msg, kids_out, kids):
    devices = msg.shape[0]
    slots = cot.shape[0]

    def find(g, found):
        kids[found] = parents[0, g]
        return found + (parents[1, g] == 0).astype(jnp.int32)

    lax.fori_loop(0, parents.shape[1], find, jnp.int32(0), unroll=4)
    lane = lax.broadcasted_iota(jnp.int32, (LABEL_ROWS, LANES), 1)
    label = jnp.zeros((LABEL_ROWS, LANES), jnp.int32)
    for q in range(kids_out.shape[0]):
        kids_out[q] = kids[q]
        label = jnp.where(lane == q, kids[q], label)
    label = label.astype(F32).astype(BF16)
    for j in range(devices):
        msg[j, slots * lane_tiles * ROWS :] = label
    per_row = VOX // (LANES * lane_tiles)
    for j in range(devices):
        chan, part = j // per_row, j % per_row
        for q in range(slots):
            for lt in range(lane_tiles):
                lane = (part * lane_tiles + lt) * LANES
                row = (q * lane_tiles + lt) * ROWS
                msg[j, row : row + ROWS] = cot[
                    q, chan * ROWS : (chan + 1) * ROWS, lane : lane + LANES
                ]


def table_kernel(
    place, counts, kids, neighbors, parents, feat, up, down, table, ordered,
    up_idx, up_far, down_idx, down_far, bricks, done, split, in_sem, out_sem,
):
    count, chans = feat.shape[:2]
    part = count // PARTS
    fetches = [
        pltpu.make_async_copy(
            feat.at[pl.ds(k * part, part)], bricks.at[pl.ds(k * part, part)], in_sem.at[k]
        )
        for k in range(PARTS)
    ]
    for fetch in fetches:
        fetch.start()
    base = place[0] * count
    table[4 * count] = place[0]
    for r in range(SEND + 1):
        up_idx[r] = 0
        down_idx[r] = 0
        up_far[r] = 2 * count
        down_far[r] = 2 * count
    split[...] = picker(split_voxel)

    def scan(g, found):
        n_up, n_down = found
        near_up, near_down = neighbors[0, g], neighbors[1, g]
        far_up, far_down = near_up - base - count, near_down - base + count
        goes_up = (near_up >= 0) & (far_up >= 0)
        goes_down = (near_down >= 0) & (far_down < count)
        up_idx[n_up] = g
        up_far[n_up] = jnp.where(goes_up, far_up, 2 * count)
        down_idx[n_down] = g
        down_far[n_down] = jnp.where(goes_down, far_down, 2 * count)
        q = jnp.int32(0)
        for k in range(1, kids.shape[0]):
            q += jnp.where(kids[k] == parents[0, g], k, 0)
        number = q * 8 + parents[1, g]
        table[number] = g
        table[count + number] = jnp.where(g < counts[0], g, count + SEND)
        return n_up + goes_up.astype(jnp.int32), n_down + goes_down.astype(jnp.int32)

    lax.fori_loop(0, count, scan, (jnp.int32(0), jnp.int32(0)), unroll=4)

    def rank(r, carry):
        for start, far, idx in ((2 * count, up_far, up_idx), (3 * count, down_far, down_idx)):
            earlier = jnp.int32(0)
            for other in range(SEND):
                earlier += (far[other] < far[r]).astype(jnp.int32)

            @pl.when(far[r] < count)
            def _():
                table[start + idx[r]] = count + earlier

        return carry

    lax.fori_loop(0, SEND, rank, jnp.int32(0))
    sends = []
    for k in range(PARTS):
        fetches[k].wait()
        rows = bricks[k * part : (k + 1) * part].reshape(part * chans, VOX)
        done[k * part : (k + 1) * part] = (
            dot(rows, split[...]).astype(BF16).reshape(part, chans, VOX)
        )
        sends.append(
            pltpu.make_async_copy(
                done.at[pl.ds(k * part, part)], ordered.at[pl.ds(k * part, part)], out_sem.at[k]
            )
        )
        sends[-1].start()
    low = low_lanes(chans)
    for r in range(SEND // 2):
        other = r + SEND // 2
        top = slice(VOX - LANES, VOX)
        up[r] = jnp.where(
            low,
            pltpu.roll(bricks[up_idx[r], :, top], LANES // 2, 1),
            bricks[up_idx[other], :, top],
        )
        down[r] = jnp.where(
            low,
            bricks[down_idx[r], :, :LANES],
            pltpu.roll(bricks[down_idx[other], :, :LANES], LANES // 2, 1),
        )
    for send in sends:
        send.wait()


def route_kernel(kids, msg, pieces):
    devices, groups, lane_tiles = pieces.shape[:3]
    slots = groups
    for s in range(devices):
        for q in range(groups):
            kid = kids[s * groups + q]
            owner, slot = kid // slots, kid % slots
            for lt in range(lane_tiles):
                row = pl.multiple_of((slot * lane_tiles + lt) * ROWS, ROWS)
                pieces[s, q, lt] = msg[owner, pl.ds(row, ROWS), :]


def place_arrivals(above, below, bricks, count):
    chans = bricks.shape[1]
    half = VOX // 2
    side = LANES // 2
    shape = (LANES, half)
    pairs = SEND // 2
    for k, shift in ((0, 0), (pairs, -side)):
        slots = slice(count + k, count + k + pairs)
        first = dot(
            above[...].reshape(pairs * chans, LANES), picker(split_voxel, shape, (shift, 0))
        )
        last = dot(
            below[...].reshape(pairs * chans, LANES),
            picker(split_voxel, shape, (VOX - side + shift, half)),
        )
        bricks[slots, :, :half] = first.astype(BF16).reshape(pairs, chans, half)
        bricks[slots, :, half:] = last.astype(BF16).reshape(pairs, chans, half)
    bricks[count + SEND] = jnp.zeros(bricks.shape[1:], BF16)


def sources(table, neighbors, number):
    count = neighbors.shape[1]
    g = table[number]
    found = []
    for d in range(6):
        near = neighbors[d, g]
        local = near - table[4 * count] * count
        if d == 0:
            local = jnp.where(local >= count, table[2 * count + g], local)
        if d == 1:
            local = jnp.where(local < 0, table[3 * count + g], local)
        found.append(jnp.where(near >= 0, local, count + SEND))
    found.append(table[count + number])
    return found


def shift_into(slots, bricks, views):
    chans = bricks.shape[1]
    tiles = VOX // LANES
    lane = lax.broadcasted_iota(jnp.int32, (chans, LANES), 1)
    low = lane < LANES // 2
    a = (lane // 16) % HALF
    b = (lane // 4) % HALF
    c = lane % HALF

    def tile(slot, t):
        return bricks[slot, :, t * LANES : (t + 1) * LANES]

    def turn(value, by):
        return pltpu.roll(value, by % LANES, 1)

    x = [tile(slots[6], t) for t in range(tiles)]
    for t in range(tiles):
        lanes = slice(t * LANES, (t + 1) * LANES)
        if t < 2:
            plus_a = x[t + 2]
            minus_a = jnp.where(a > 0, turn(x[t + 2], 16), turn(tile(slots[1], t + 2), -48))
        else:
            plus_a = jnp.where(a < HALF - 1, turn(x[t - 2], -16), turn(tile(slots[0], t - 2), 48))
            minus_a = x[t - 2]
        if t % 2 == 0:
            plus_b = x[t + 1]
            minus_b = jnp.where(b > 0, turn(x[t + 1], 4), turn(tile(slots[3], t + 1), -12))
        else:
            plus_b = jnp.where(b < HALF - 1, turn(x[t - 1], -4), turn(tile(slots[2], t - 1), 12))
            minus_b = x[t - 1]
        swapped = turn(x[t], 64)
        plus_c = jnp.where(c < HALF - 1, turn(x[t], 63), turn(tile(slots[4], t), 67))
        minus_c = jnp.where(c > 0, turn(x[t], -63), turn(tile(slots[5], t), -67))
        out = [plus_a, minus_a, plus_b, minus_b, jnp.where(low, swapped, plus_c),
               jnp.where(low, minus_c, swapped), x[t]]
        for d in range(7):
            views[d * chans : (d + 1) * chans, lanes] = out[d]


def low_lanes(rows):
    return lax.broadcasted_iota(jnp.int32, (rows, LANES), 1) < LANES // 2


def forward_kernel(
    lane_tiles, table_hbm, neighbors_hbm, feat, w_conv_hbm, w_res_hbm, w_mix_hbm,
    above_hbm, below_hbm,
    parts_out, slope_out, coarse_out, piece_out,
    bricks, views, place, w_conv, w_res, w_mix, conv_cat, res_cat, octants,
    table, neighbors, above, below, sem,
):
    q = pl.program_id(0)
    groups = pl.num_programs(0) - 1
    count, chans = feat.shape[:2]
    part = count // PARTS

    @pl.when(q == 0)
    def _():
        copies = [
            pltpu.make_async_copy(source, target, sem.at[k])
            for k, (source, target) in enumerate((
                (above_hbm, above), (below_hbm, below), (w_conv_hbm, w_conv),
                (w_res_hbm, w_res), (w_mix_hbm, w_mix), (table_hbm, table),
                (neighbors_hbm, neighbors),
                *(
                    (feat.at[pl.ds(k * part, part)], bricks.at[pl.ds(k * part, part)])
                    for k in range(PARTS)
                ),
            ))
        ]
        for copy in copies:
            copy.start()
        place[...] = picker(octant_voxel, flip=True)
        for copy in copies[:-PARTS]:
            copy.wait()
        place_arrivals(above, below, bricks, count)
        for d in range(7):
            conv_cat[:, d * chans : (d + 1) * chans] = w_conv[d]
        res_cat[...] = w_res[...].T
        for copy in copies[-PARTS:]:
            copy.wait()

    low_half = low_lanes(chans)

    def finish():
        coarse = dot(octants[...], place[...]).astype(BF16)
        coarse_out[0] = coarse
        mixed = dot(w_mix[...], coarse).astype(BF16)
        per_row = VOX // (LANES * lane_tiles)
        for j in range(piece_out.shape[0]):
            chan, part = j // per_row, j % per_row
            for lt in range(lane_tiles):
                lane = (part * lane_tiles + lt) * LANES
                piece_out[j, 0, lt] = mixed[chan * ROWS : (chan + 1) * ROWS, lane : lane + LANES]

    def restrict(first):
        acts = []
        for k in range(first, first + 4):
            shift_into(sources(table, neighbors, q * 8 + k), bricks, views.at[k])
            hidden = dot(conv_cat[...], views[k])
            sig = 1.0 / (1.0 + jnp.exp(-hidden))
            act = hidden * sig
            slope_out[0, k * chans : (k + 1) * chans, :] = (sig + act * (1.0 - sig)).astype(BF16)
            acts.append(act.astype(BF16))
        for k in range(0, 4, 2):
            lanes = slice((first + k) * (LANES // 2), (first + k + 2) * (LANES // 2))
            for t in range(4):
                one = acts[k][:, t * LANES : (t + 1) * LANES]
                two = acts[k + 1][:, t * LANES : (t + 1) * LANES]
                parts_out[0, 2 * t * chans : (2 * t + 1) * chans, lanes] = jnp.where(
                    low_half, one, pltpu.roll(two, LANES // 2, 1)
                )
                parts_out[0, (2 * t + 1) * chans : (2 * t + 2) * chans, lanes] = jnp.where(
                    low_half, pltpu.roll(one, LANES // 2, 1), two
                )
        lanes = slice(first * (LANES // 2), (first + 4) * (LANES // 2))
        return dot(res_cat[...], parts_out[0, :, lanes]).astype(BF16)

    @pl.when(q < groups)
    def _():
        finish()
        halves = [restrict(0), restrict(4)]
        octants[...] = jnp.concatenate(halves, axis=1)

    @pl.when(q == groups)
    def _():
        finish()


def backward_kernel(
    lane_tiles, scale, table_hbm, neighbors_hbm, feat, above_hbm, below_hbm, pieces, parts, slope,
    coarse, w_mix, w_res, own, other,
    bricks, views, cot, grad_parts, grad_rows, unplace, mix_t, conv_sum, res_sum, mix_sum, packed,
    table, neighbors, above, below, sem,
):
    q = pl.program_id(0)
    count, chans = feat.shape[:2]
    wide = coarse.shape[1]
    part = count // PARTS

    def start_fetches():
        pairs = [(table_hbm, table), (neighbors_hbm, neighbors), (above_hbm, above),
                 (below_hbm, below)]
        for k in range(PARTS):
            slots = pl.ds(k * part, part)
            pairs.append((feat.at[slots], bricks.at[slots]))
        copies = [
            pltpu.make_async_copy(source, target, sem.at[k])
            for k, (source, target) in enumerate(pairs)
        ]
        for copy in copies:
            copy.start()
        return copies

    def gradients():
        per_row = VOX // (LANES * lane_tiles)
        for j in range(pieces.shape[0]):
            chan, half = j // per_row, j % per_row
            for lt in range(lane_tiles):
                lane = (half * lane_tiles + lt) * LANES
                cot[chan * ROWS : (chan + 1) * ROWS, lane : lane + LANES] = pieces[j, 0, lt]
        cots = cot[...]
        grad_coarse = (scale * dot(mix_t[...], cots)).astype(BF16)
        grad_fine = dot(grad_coarse, unplace[...]).astype(BF16)
        mix_sum[...] += dot_nt(cots, coarse[0])
        res_sum[...] += dot_nt(parts[0], grad_fine)
        grad_parts[...] = dot(w_res[...], grad_fine)
        low_half = low_lanes(chans)
        for r in range(4):
            for t in range(4):
                cols = slice(r * LANES, (r + 1) * LANES)
                lanes = slice(t * LANES, (t + 1) * LANES)
                one = grad_parts[2 * t * chans : (2 * t + 1) * chans, cols]
                two = grad_parts[(2 * t + 1) * chans : (2 * t + 2) * chans, cols]
                first = slice(2 * r * chans, (2 * r + 1) * chans)
                second = slice((2 * r + 1) * chans, (2 * r + 2) * chans)
                grad_rows[first, lanes] = (
                    jnp.where(low_half, one, pltpu.roll(two, LANES // 2, 1))
                    * slope[0, first, lanes].astype(F32)
                ).astype(BF16)
                grad_rows[second, lanes] = (
                    jnp.where(low_half, pltpu.roll(one, LANES // 2, 1), two)
                    * slope[0, second, lanes].astype(F32)
                ).astype(BF16)

    def convolution():
        low_half = low_lanes(7 * chans)
        total = None
        for k in range(0, 8, 2):
            grads = grad_rows[k * chans : (k + 2) * chans, :].T
            terms = []
            for m in (k, k + 1):
                shift_into(sources(table, neighbors, q * 8 + m), bricks, views.at[m])
                terms.append(dot(views[m], grads))
            term = jnp.where(low_half, *terms)
            total = term if total is None else total + term
        conv_sum[...] += total

    @pl.when(q == 0)
    def _():
        copies = start_fetches()
        unplace[...] = picker(octant_voxel)
        mix_t[...] = w_mix[...].T
        conv_sum[...] = jnp.zeros_like(conv_sum)
        res_sum[...] = jnp.zeros_like(res_sum)
        mix_sum[...] = jnp.zeros_like(mix_sum)
        gradients()
        for copy in copies:
            copy.wait()
        place_arrivals(above, below, bricks, count)
        convolution()

    @pl.when(q > 0)
    def _():
        gradients()
        convolution()

    @pl.when(q == pl.num_programs(0) - 1)
    def _():
        packed[0:wide] = scale * mix_sum[...]
        at = wide
        packed[at : at + 8 * chans] = res_sum[...]
        at += 8 * chans
        total = conv_sum[...] + pltpu.roll(conv_sum[...], LANES // 2, 1)
        low = low_lanes(chans)
        for t in range(4):
            one = total[2 * t * chans : (2 * t + 1) * chans]
            two = total[(2 * t + 1) * chans : (2 * t + 2) * chans] if t < 3 else one
            packed[at : at + chans] = jnp.where(low, one, two)
            at += chans
        if at < packed.shape[0]:
            packed[at:] = jnp.zeros((packed.shape[0] - at, LANES), F32)
        chips, rows = own.shape[:2]
        core = table[4 * count] % 2
        for c in range(chips):
            first = pl.multiple_of((2 * c + core) * rows, 8)
            second = pl.multiple_of((2 * c + 1 - core) * rows, 8)
            own[c] = packed[pl.ds(first, rows), :]
            other[c] = packed[pl.ds(second, rows), :]


def join_kernel(kids, shares, pieces, msg):
    devices, groups, lane_tiles = pieces.shape[:3]
    slots = groups
    body_rows = slots * lane_tiles * ROWS
    for s in range(devices):
        for q in range(groups):
            kid = kids[s * groups + q]
            owner, slot = kid // slots, kid % slots
            for lt in range(lane_tiles):
                row = pl.multiple_of((slot * lane_tiles + lt) * ROWS, ROWS)
                msg[owner, pl.ds(row, ROWS), :] = pieces[s, q, lt]
    total = jnp.sum(shares[...].astype(F32), axis=0).astype(BF16)
    for j in range(devices):
        msg[j, body_rows:] = total


def unpack_kernel(lane_tiles, msg, coarse_out, conv, res, mix, packed):
    devices, rows = msg.shape[:2]
    slots = coarse_out.shape[0]
    wide = mix.shape[0]
    chans = conv.shape[1]
    half = LANES // 2
    body_rows = slots * lane_tiles * ROWS
    share = rows - body_rows
    for j in range(devices):
        packed[j * share : (j + 1) * share] = msg[j, body_rows:].astype(F32)
    mix[...] = packed[0:wide]
    at = wide
    for t in range(8):
        res[t] = packed[at : at + chans]
        at += chans
    for t in range(4):
        block = packed[at : at + chans].T
        conv[2 * t] = block[:half]
        if 2 * t + 1 < 7:
            conv[2 * t + 1] = block[half:]
        at += chans
    per_row = VOX // (LANES * lane_tiles)
    for j in range(devices):
        chan, part = j // per_row, j % per_row
        for q in range(slots):
            for lt in range(lane_tiles):
                row = (q * lane_tiles + lt) * ROWS
                lane = (part * lane_tiles + lt) * LANES
                coarse_out[q, chan * ROWS : (chan + 1) * ROWS, lane : lane + LANES] = msg[
                    j, row : row + ROWS
                ]


def kernel_call(kernel, out_shape, grid_spec, flops, moved, vmem=VMEM_BYTES):
    return pl.pallas_call(
        kernel,
        out_shape=out_shape,
        grid_spec=grid_spec,
        compiler_params=pltpu.CompilerParams(vmem_limit_bytes=vmem),
        cost_estimate=pl.CostEstimate(flops=flops, bytes_accessed=moved, transcendentals=0),
    )


def body(features, counts, neighbors, parents, w_conv, w_restrict, w_mix, cotangent):
    devices = lax.axis_size("space")
    position = lax.axis_index("space").astype(jnp.int32).reshape(1)
    slots, wide = cotangent.shape[:2]
    count, chans = features.shape[:2]
    lane_tiles = VOX * 8 // devices // LANES
    tiles = slots * lane_tiles
    groups = count // 8
    whole = lambda shape: pl.BlockSpec(shape, lambda *_: (0,) * len(shape))
    any_spec = pl.BlockSpec(memory_space=pl.ANY)
    smem_spec = pl.BlockSpec(memory_space=pltpu.SMEM)
    smem = lambda size: pltpu.SMEM((size,), jnp.int32)
    vmem = pltpu.VMEM
    ints = lambda size: jax.ShapeDtypeStruct((size,), jnp.int32)

    message_shape = (devices, tiles * ROWS + LABEL_ROWS, LANES)
    message, kids = kernel_call(
        functools.partial(pack_kernel, lane_tiles),
        (jax.ShapeDtypeStruct(message_shape, BF16), ints(groups)),
        pl.GridSpec(
            grid=(1,),
            in_specs=[smem_spec, whole(cotangent.shape)],
            out_specs=[whole(message_shape), smem_spec],
            scratch_shapes=[smem(groups + 1)],
        ),
        1000, 2**20,
    )(parents.T, cotangent)
    spread = lax.all_to_all(message, "space", split_axis=0, concat_axis=0, tiled=True)

    plane = jax.ShapeDtypeStruct((SEND // 2, chans, LANES), BF16)
    up, down, table, ordered = kernel_call(
        table_kernel,
        (plane, plane, ints(4 * count + 1), jax.ShapeDtypeStruct(features.shape, BF16)),
        pl.GridSpec(
            grid=(1,),
            in_specs=[smem_spec] * 5 + [any_spec],
            out_specs=[whole(plane.shape)] * 2 + [smem_spec, any_spec],
            scratch_shapes=[smem(SEND + 1)] * 4
            + [vmem(features.shape, BF16), vmem(features.shape, BF16), vmem((VOX, VOX), BF16),
               pltpu.SemaphoreType.DMA((PARTS,)), pltpu.SemaphoreType.DMA((PARTS,))],
        ),
        1000, 2**20,
    )(position, counts, kids, neighbors.T, parents.T, features)
    below = lax.ppermute(up, "space", [(i, i + 1) for i in range(devices - 1)])
    above = lax.ppermute(down, "space", [(i + 1, i) for i in range(devices - 1)])

    all_kids = spread[:, tiles * ROWS, :groups].astype(jnp.int32).reshape(-1)
    piece_shape = (devices, groups, lane_tiles, ROWS, LANES)
    forward_tiles = kernel_call(
        route_kernel,
        jax.ShapeDtypeStruct(piece_shape, BF16),
        pl.GridSpec(
            grid=(1,),
            in_specs=[smem_spec, whole(message_shape)],
            out_specs=whole(piece_shape),
        ),
        1000, 2**20, SMALL_VMEM_BYTES,
    )(all_kids, spread)
    forward_tiles, above, below = lax.optimization_barrier((forward_tiles, above, below))
    cot_pieces = lax.all_to_all(forward_tiles, "space", split_axis=0, concat_axis=0, tiled=True)

    res_rows = w_restrict.transpose(0, 2, 1).reshape(8 * chans, wide)
    scalars = (table, neighbors.T)
    brick_scratch = vmem((count + SEND + 1, chans, VOX), BF16)
    view_scratch = vmem((8, 7 * chans, VOX), BF16)
    per_group = lambda *shape: pl.BlockSpec((1,) + shape, lambda q: (q,) + (0,) * len(shape))
    piece_spec = pl.BlockSpec((devices, 1, lane_tiles, ROWS, LANES), lambda q: (0, q, 0, 0, 0))
    parts, slope, coarse, pieces = kernel_call(
        functools.partial(forward_kernel, lane_tiles),
        (
            jax.ShapeDtypeStruct((groups, 8 * chans, VOX), BF16),
            jax.ShapeDtypeStruct((groups, 8 * chans, VOX), BF16),
            jax.ShapeDtypeStruct((groups, wide, VOX), BF16),
            jax.ShapeDtypeStruct(piece_shape, BF16),
        ),
        pl.GridSpec(
            grid=(groups + 1,),
            in_specs=[any_spec] * 8,
            out_specs=[
                pl.BlockSpec((1, 8 * chans, VOX), lambda q: (jnp.minimum(q, groups - 1), 0, 0)),
                pl.BlockSpec((1, 8 * chans, VOX), lambda q: (jnp.minimum(q, groups - 1), 0, 0)),
                pl.BlockSpec((1, wide, VOX), lambda q: (jnp.maximum(q - 1, 0), 0, 0)),
                pl.BlockSpec(
                    (devices, 1, lane_tiles, ROWS, LANES),
                    lambda q: (0, jnp.maximum(q - 1, 0), 0, 0, 0),
                ),
            ],
            scratch_shapes=[
                brick_scratch, view_scratch, vmem((VOX, VOX), BF16), vmem(w_conv.shape, BF16),
                vmem(res_rows.shape, BF16), vmem(w_mix.shape, BF16),
                vmem((chans, 7 * chans), BF16), vmem((wide, 8 * chans), BF16),
                vmem((wide, VOX), BF16), smem(4 * count + 1),
                pltpu.SMEM((6, count), jnp.int32), vmem(plane.shape, BF16),
                vmem(plane.shape, BF16), pltpu.SemaphoreType.DMA((7 + PARTS,)),
            ],
        ),
        16 * 10**9, 16 * 2**20,
    )(*scalars, ordered, w_conv, res_rows, w_mix, above, below)
    returned = lax.all_to_all(pieces, "space", split_axis=0, concat_axis=0, tiled=True)

    scale = 1.0 / math.sqrt(devices * slots * VOX)
    used = wide + 8 * chans + 4 * chans
    rows = -(-used // (devices * 8)) * 8
    half = jax.ShapeDtypeStruct((devices // 2, rows, LANES), F32)
    own, other = kernel_call(
        functools.partial(backward_kernel, lane_tiles, scale),
        (half, half),
        pl.GridSpec(
            grid=(groups,),
            in_specs=[any_spec] * 5
            + [piece_spec, per_group(8 * chans, VOX), per_group(8 * chans, VOX),
               per_group(wide, VOX), whole(w_mix.shape), whole(res_rows.shape)],
            out_specs=[whole(half.shape)] * 2,
            scratch_shapes=[
                brick_scratch, view_scratch, vmem((wide, VOX), BF16),
                vmem((8 * chans, VOX), F32), vmem((8 * chans, VOX), BF16), vmem((VOX, VOX), BF16),
                vmem((wide, wide), BF16), vmem((7 * chans, 2 * chans), F32),
                vmem((8 * chans, wide), F32), vmem((wide, wide), F32),
                vmem((devices * rows, LANES), F32), smem(4 * count + 1),
                pltpu.SMEM((6, count), jnp.int32), vmem(plane.shape, BF16),
                vmem(plane.shape, BF16), pltpu.SemaphoreType.DMA((4 + PARTS,)),
            ],
        ),
        16 * 10**9, 16 * 2**20,
    )(*scalars, ordered, above, below, cot_pieces, parts, slope, coarse, w_mix, res_rows)

    came = lax.ppermute(other, "space", [(i, i ^ 1) for i in range(devices)])
    paired = (own + came).astype(BF16)
    shares = lax.all_to_all(
        paired, "space", split_axis=0, concat_axis=0, tiled=True,
        axis_index_groups=[list(range(core, devices, 2)) for core in range(2)],
    )

    joined_shape = (devices, tiles * ROWS + rows, LANES)
    joined = kernel_call(
        join_kernel,
        jax.ShapeDtypeStruct(joined_shape, BF16),
        pl.GridSpec(
            grid=(1,),
            in_specs=[smem_spec, whole(shares.shape), whole(piece_shape)],
            out_specs=whole(joined_shape),
        ),
        1000, 2**20, SMALL_VMEM_BYTES,
    )(all_kids, shares, returned)
    finished = lax.all_to_all(joined, "space", split_axis=0, concat_axis=0, tiled=True)

    coarse_out, grad_conv, grad_res, grad_mix = kernel_call(
        functools.partial(unpack_kernel, lane_tiles),
        (
            jax.ShapeDtypeStruct((slots, wide, VOX), BF16),
            jax.ShapeDtypeStruct((7, chans, chans), F32),
            jax.ShapeDtypeStruct((8, chans, wide), F32),
            jax.ShapeDtypeStruct((wide, wide), F32),
        ),
        pl.GridSpec(
            grid=(1,),
            in_specs=[whole(joined_shape)],
            out_specs=[whole((slots, wide, VOX)), whole((7, chans, chans)),
                       whole((8, chans, wide)), whole((wide, wide))],
            scratch_shapes=[vmem((devices * rows, LANES), F32)],
        ),
        1000, 2 * 2**20, SMALL_VMEM_BYTES,
    )(finished)
    return coarse_out, grad_conv, grad_res.transpose(0, 2, 1), grad_mix


def solution(mesh):
    return jax.shard_map(
        body,
        mesh=mesh,
        in_specs=(
            P(("groups", "space"), None, None),
            P(("groups", "space")),
            P(("groups", "space"), None),
            P(("groups", "space"), None),
            P(),
            P(),
            P(),
            P(("groups", "space"), None, None),
        ),
        out_specs=(
            P(("groups", "space"), None, None),
            P("groups", None, None),
            P("groups", None, None),
            P("groups", None),
        ),
        check_vma=False,
    )
```

```python
import functools
import math

import jax
import jax.numpy as jnp
from jax import lax
from jax.experimental import pallas as pl
from jax.experimental.pallas import tpu as pltpu
from jax.sharding import PartitionSpec as P

EDGE = 8
HALF = EDGE // 2
VOX = EDGE**3
LANES = 128
ROWS = 16
LABEL_ROWS = 8
SEND = 8
PARTS = 4
BF16 = jnp.bfloat16
F32 = jnp.float32
VMEM_BYTES = 60 * 1024 * 1024
SMALL_VMEM_BYTES = 16 * 1024 * 1024


def bits_of(value):
    return [(value >> (8 - k)) & 1 for k in range(9)]


def join_bits(bits):
    value = bits[0]
    for bit in bits[1:]:
        value = value * 2 + bit
    return value


def split_voxel(column):
    ta, tb, tc, a1, a0, b1, b0, c1, c0 = bits_of(column)
    return join_bits([a1, a0, ta, b1, b0, tb, c1, c0, tc])


def octant_voxel(column):
    oa, ob, oc, a1, a0, b1, b0, c1, c0 = bits_of(column)
    return join_bits([oa, a1, a0, ob, b1, b0, oc, c1, c0])


def picker(voxel_of, shape=(VOX, VOX), start=(0, 0), flip=False):
    row = lax.broadcasted_iota(jnp.int32, shape, 0) + start[0]
    column = lax.broadcasted_iota(jnp.int32, shape, 1) + start[1]
    return (column == voxel_of(row) if flip else row == voxel_of(column)).astype(BF16)


def dot(a, b):
    return jnp.dot(a, b, preferred_element_type=F32)


def dot_nt(a, b):
    return lax.dot_general(a, b, (((1,), (1,)), ((), ())), preferred_element_type=F32)


def pack_kernel(lane_tiles, parents, cot, msg, kids_out, kids):
    slots = cot.shape[0]
    body_rows = slots * lane_tiles * ROWS
    rows = body_rows + LABEL_ROWS
    devices = msg.shape[0] // rows

    def find(g, found):
        kids[found] = parents[0, g]
        return found + (parents[1, g] == 0).astype(jnp.int32)

    lax.fori_loop(0, parents.shape[1], find, jnp.int32(0), unroll=4)
    lane = lax.broadcasted_iota(jnp.int32, (LABEL_ROWS, LANES), 1)
    label = jnp.zeros((LABEL_ROWS, LANES), jnp.int32)
    for q in range(kids_out.shape[0]):
        kids_out[q] = kids[q]
        label = jnp.where(lane == q, kids[q], label)
    label = label.astype(F32).astype(BF16)
    for j in range(devices):
        msg[j * rows + body_rows : (j + 1) * rows] = label
    per_row = VOX // (LANES * lane_tiles)
    for j in range(devices):
        chan, part = j // per_row, j % per_row
        for q in range(slots):
            for lt in range(lane_tiles):
                lane = (part * lane_tiles + lt) * LANES
                row = j * rows + (q * lane_tiles + lt) * ROWS
                msg[row : row + ROWS] = cot[
                    q, chan * ROWS : (chan + 1) * ROWS, lane : lane + LANES
                ]


def table_kernel(
    place, counts, kids, neighbors, parents, feat, up, down, table, ordered,
    up_idx, up_far, down_idx, down_far, bricks, done, split, in_sem, out_sem,
):
    count, chans = feat.shape[:2]
    part = count // PARTS
    fetches = [
        pltpu.make_async_copy(
            feat.at[pl.ds(k * part, part)], bricks.at[pl.ds(k * part, part)], in_sem.at[k]
        )
        for k in range(PARTS)
    ]
    for fetch in fetches:
        fetch.start()
    base = place[0] * count
    table[4 * count] = place[0]
    for r in range(SEND + 1):
        up_idx[r] = 0
        down_idx[r] = 0
        up_far[r] = 2 * count
        down_far[r] = 2 * count
    split[...] = picker(split_voxel)

    def scan(g, found):
        n_up, n_down = found
        near_up, near_down = neighbors[0, g], neighbors[1, g]
        far_up, far_down = near_up - base - count, near_down - base + count
        goes_up = (near_up >= 0) & (far_up >= 0)
        goes_down = (near_down >= 0) & (far_down < count)
        up_idx[n_up] = g
        up_far[n_up] = jnp.where(goes_up, far_up, 2 * count)
        down_idx[n_down] = g
        down_far[n_down] = jnp.where(goes_down, far_down, 2 * count)
        q = jnp.int32(0)
        for k in range(1, kids.shape[0]):
            q += jnp.where(kids[k] == parents[0, g], k, 0)
        number = q * 8 + parents[1, g]
        table[number] = g
        table[count + number] = jnp.where(g < counts[0], g, count + SEND)
        return n_up + goes_up.astype(jnp.int32), n_down + goes_down.astype(jnp.int32)

    lax.fori_loop(0, count, scan, (jnp.int32(0), jnp.int32(0)), unroll=4)

    def rank(r, carry):
        for start, far, idx in ((2 * count, up_far, up_idx), (3 * count, down_far, down_idx)):
            earlier = jnp.int32(0)
            for other in range(SEND):
                earlier += (far[other] < far[r]).astype(jnp.int32)

            @pl.when(far[r] < count)
            def _():
                table[start + idx[r]] = count + earlier

        return carry

    lax.fori_loop(0, SEND, rank, jnp.int32(0))
    sends = []
    for k in range(PARTS):
        fetches[k].wait()
        rows = bricks[k * part : (k + 1) * part].reshape(part * chans, VOX)
        done[k * part : (k + 1) * part] = (
            dot(rows, split[...]).astype(BF16).reshape(part, chans, VOX)
        )
        sends.append(
            pltpu.make_async_copy(
                done.at[pl.ds(k * part, part)], ordered.at[pl.ds(k * part, part)], out_sem.at[k]
            )
        )
        sends[-1].start()
    low = low_lanes(chans)
    for r in range(SEND // 2):
        other = r + SEND // 2
        top = slice(VOX - LANES, VOX)
        up[r] = jnp.where(
            low,
            pltpu.roll(bricks[up_idx[r], :, top], LANES // 2, 1),
            bricks[up_idx[other], :, top],
        )
        down[r] = jnp.where(
            low,
            bricks[down_idx[r], :, :LANES],
            pltpu.roll(bricks[down_idx[other], :, :LANES], LANES // 2, 1),
        )
    for send in sends:
        send.wait()


def route_kernel(kids, msg, pieces):
    devices, groups, lane_tiles = pieces.shape[:3]
    slots = groups
    for s in range(devices):
        for q in range(groups):
            kid = kids[s * groups + q]
            owner, slot = kid // slots, kid % slots
            for lt in range(lane_tiles):
                row = pl.multiple_of((slot * lane_tiles + lt) * ROWS, ROWS)
                pieces[s, q, lt] = msg[owner, pl.ds(row, ROWS), :]


def place_arrivals(above, below, bricks, count):
    chans = bricks.shape[1]
    half = VOX // 2
    side = LANES // 2
    shape = (LANES, half)
    pairs = SEND // 2
    for k, shift in ((0, 0), (pairs, -side)):
        slots = slice(count + k, count + k + pairs)
        first = dot(
            above[...].reshape(pairs * chans, LANES), picker(split_voxel, shape, (shift, 0))
        )
        last = dot(
            below[...].reshape(pairs * chans, LANES),
            picker(split_voxel, shape, (VOX - side + shift, half)),
        )
        bricks[slots, :, :half] = first.astype(BF16).reshape(pairs, chans, half)
        bricks[slots, :, half:] = last.astype(BF16).reshape(pairs, chans, half)
    bricks[count + SEND] = jnp.zeros(bricks.shape[1:], BF16)


def sources(table, neighbors, number):
    count = neighbors.shape[1]
    g = table[number]
    found = []
    for d in range(6):
        near = neighbors[d, g]
        local = near - table[4 * count] * count
        if d == 0:
            local = jnp.where(local >= count, table[2 * count + g], local)
        if d == 1:
            local = jnp.where(local < 0, table[3 * count + g], local)
        found.append(jnp.where(near >= 0, local, count + SEND))
    found.append(table[count + number])
    return found


def shift_into(slots, bricks, views):
    chans = bricks.shape[1]
    tiles = VOX // LANES
    lane = lax.broadcasted_iota(jnp.int32, (chans, LANES), 1)
    low = lane < LANES // 2
    a = (lane // 16) % HALF
    b = (lane // 4) % HALF
    c = lane % HALF

    def tile(slot, t):
        return bricks[slot, :, t * LANES : (t + 1) * LANES]

    def turn(value, by):
        return pltpu.roll(value, by % LANES, 1)

    x = [tile(slots[6], t) for t in range(tiles)]
    for t in range(tiles):
        lanes = slice(t * LANES, (t + 1) * LANES)
        if t < 2:
            plus_a = x[t + 2]
            minus_a = jnp.where(a > 0, turn(x[t + 2], 16), turn(tile(slots[1], t + 2), -48))
        else:
            plus_a = jnp.where(a < HALF - 1, turn(x[t - 2], -16), turn(tile(slots[0], t - 2), 48))
            minus_a = x[t - 2]
        if t % 2 == 0:
            plus_b = x[t + 1]
            minus_b = jnp.where(b > 0, turn(x[t + 1], 4), turn(tile(slots[3], t + 1), -12))
        else:
            plus_b = jnp.where(b < HALF - 1, turn(x[t - 1], -4), turn(tile(slots[2], t - 1), 12))
            minus_b = x[t - 1]
        swapped = turn(x[t], 64)
        plus_c = jnp.where(c < HALF - 1, turn(x[t], 63), turn(tile(slots[4], t), 67))
        minus_c = jnp.where(c > 0, turn(x[t], -63), turn(tile(slots[5], t), -67))
        out = [plus_a, minus_a, plus_b, minus_b, jnp.where(low, swapped, plus_c),
               jnp.where(low, minus_c, swapped), x[t]]
        for d in range(7):
            views[d * chans : (d + 1) * chans, lanes] = out[d]


def low_lanes(rows):
    return lax.broadcasted_iota(jnp.int32, (rows, LANES), 1) < LANES // 2


def forward_kernel(
    lane_tiles, table_hbm, neighbors_hbm, feat, w_conv_hbm, w_res_hbm, w_mix_hbm,
    above_hbm, below_hbm,
    parts_out, slope_out, coarse_out, piece_out,
    bricks, views, place, w_conv, w_res, w_mix, conv_cat, res_cat, octants,
    table, neighbors, above, below, sem,
):
    q = pl.program_id(0)
    groups = pl.num_programs(0) - 1
    count, chans = feat.shape[:2]
    part = count // PARTS

    @pl.when(q == 0)
    def _():
        copies = [
            pltpu.make_async_copy(source, target, sem.at[k])
            for k, (source, target) in enumerate((
                (above_hbm, above), (below_hbm, below), (w_conv_hbm, w_conv),
                (w_res_hbm, w_res), (w_mix_hbm, w_mix), (table_hbm, table),
                (neighbors_hbm, neighbors),
                *(
                    (feat.at[pl.ds(k * part, part)], bricks.at[pl.ds(k * part, part)])
                    for k in range(PARTS)
                ),
            ))
        ]
        for copy in copies:
            copy.start()
        place[...] = picker(octant_voxel, flip=True)
        for copy in copies[:-PARTS]:
            copy.wait()
        place_arrivals(above, below, bricks, count)
        for d in range(7):
            conv_cat[:, d * chans : (d + 1) * chans] = w_conv[d]
        res_cat[...] = w_res[...].T
        for copy in copies[-PARTS:]:
            copy.wait()

    low_half = low_lanes(chans)

    def finish():
        coarse = dot(octants[...], place[...]).astype(BF16)
        coarse_out[0] = coarse
        mixed = dot(w_mix[...], coarse).astype(BF16)
        per_row = VOX // (LANES * lane_tiles)
        for j in range(piece_out.shape[0]):
            chan, part = j // per_row, j % per_row
            for lt in range(lane_tiles):
                lane = (part * lane_tiles + lt) * LANES
                piece_out[j, 0, lt] = mixed[chan * ROWS : (chan + 1) * ROWS, lane : lane + LANES]

    def restrict(first):
        acts = []
        for k in range(first, first + 4):
            shift_into(sources(table, neighbors, q * 8 + k), bricks, views.at[k])
            hidden = dot(conv_cat[:, : 7 * chans], views[k])
            sig = 1.0 / (1.0 + jnp.exp(-hidden))
            act = hidden * sig
            slope_out[0, k * chans : (k + 1) * chans, :] = (sig + act * (1.0 - sig)).astype(BF16)
            acts.append(act.astype(BF16))
        for k in range(0, 4, 2):
            lanes = slice((first + k) * (LANES // 2), (first + k + 2) * (LANES // 2))
            for t in range(4):
                one = acts[k][:, t * LANES : (t + 1) * LANES]
                two = acts[k + 1][:, t * LANES : (t + 1) * LANES]
                parts_out[0, 2 * t * chans : (2 * t + 1) * chans, lanes] = jnp.where(
                    low_half, one, pltpu.roll(two, LANES // 2, 1)
                )
                parts_out[0, (2 * t + 1) * chans : (2 * t + 2) * chans, lanes] = jnp.where(
                    low_half, pltpu.roll(one, LANES // 2, 1), two
                )
        lanes = slice(first * (LANES // 2), (first + 4) * (LANES // 2))
        return dot(res_cat[...], parts_out[0, :, lanes]).astype(BF16)

    @pl.when(q < groups)
    def _():
        finish()
        halves = [restrict(0), restrict(4)]
        octants[...] = jnp.concatenate(halves, axis=1)

    @pl.when(q == groups)
    def _():
        finish()


def backward_kernel(
    lane_tiles, scale, table, neighbors, feat, above, below, pieces, parts, slope, coarse, w_mix, w_res, packed,
    bricks, views, cot, grad_parts, grad_rows, unplace, mix_t, conv_sum, res_sum, mix_sum, sem,
):
    q = pl.program_id(0)
    count, chans = feat.shape[:2]
    wide = coarse.shape[1]
    fetch = pltpu.make_async_copy(feat, bricks.at[pl.ds(0, count)], sem)

    @pl.when(q == 0)
    def _():
        fetch.start()
        place_arrivals(above, below, bricks, count)
        unplace[...] = picker(octant_voxel)
        mix_t[...] = w_mix[...].T
        conv_sum[...] = jnp.zeros_like(conv_sum)
        res_sum[...] = jnp.zeros_like(res_sum)
        mix_sum[...] = jnp.zeros_like(mix_sum)
        fetch.wait()

    per_row = VOX // (LANES * lane_tiles)
    for j in range(pieces.shape[0]):
        chan, part = j // per_row, j % per_row
        for lt in range(lane_tiles):
            lane = (part * lane_tiles + lt) * LANES
            cot[chan * ROWS : (chan + 1) * ROWS, lane : lane + LANES] = pieces[j, 0, lt]
    cots = cot[...]
    grad_coarse = (scale * dot(mix_t[...], cots)).astype(BF16)
    grad_fine = dot(grad_coarse, unplace[...]).astype(BF16)
    mix_sum[...] += dot_nt(cots, coarse[0])
    res_sum[...] += dot_nt(parts[0], grad_fine)
    grad_parts[...] = dot(w_res[...], grad_fine)
    low_half = low_lanes(chans)
    for r in range(4):
        for t in range(4):
            cols = slice(r * LANES, (r + 1) * LANES)
            lanes = slice(t * LANES, (t + 1) * LANES)
            one = grad_parts[2 * t * chans : (2 * t + 1) * chans, cols]
            two = grad_parts[(2 * t + 1) * chans : (2 * t + 2) * chans, cols]
            first = slice(2 * r * chans, (2 * r + 1) * chans)
            second = slice((2 * r + 1) * chans, (2 * r + 2) * chans)
            grad_rows[first, lanes] = (
                jnp.where(low_half, one, pltpu.roll(two, LANES // 2, 1))
                * slope[0, first, lanes].astype(F32)
            ).astype(BF16)
            grad_rows[second, lanes] = (
                jnp.where(low_half, pltpu.roll(one, LANES // 2, 1), two)
                * slope[0, second, lanes].astype(F32)
            ).astype(BF16)

    total = None
    for k in range(8):
        shift_into(sources(table, neighbors, q * 8 + k), bricks, views.at[k])
        term = dot_nt(grad_rows[k * chans : (k + 1) * chans, :], views[k])
        total = term if total is None else total + term
    conv_sum[:, : 7 * chans] += total

    @pl.when(q == pl.num_programs(0) - 1)
    def _():
        packed[0:wide] = (scale * mix_sum[...]).astype(BF16)
        at = wide
        packed[at : at + 8 * chans] = res_sum[...].astype(BF16)
        at += 8 * chans
        for t in range(4):
            packed[at : at + chans] = conv_sum[:, t * LANES : (t + 1) * LANES].astype(BF16)
            at += chans
        if at < packed.shape[0]:
            packed[at:] = jnp.zeros((packed.shape[0] - at, LANES), BF16)


def join_kernel(kids, shares, pieces, msg, wanted, wide_shares):
    devices, groups, lane_tiles = pieces.shape[:3]
    slots = groups
    share = shares.shape[0] // devices
    body_rows = slots * lane_tiles * ROWS
    rows = body_rows + share

    def invert(n, carry):
        wanted[kids[n]] = n
        return carry

    lax.fori_loop(0, devices * groups, invert, jnp.int32(0), unroll=4)
    wide_shares[...] = shares[...].astype(F32)
    total = wide_shares[0:share]
    for j in range(1, devices):
        total += wide_shares[j * share : (j + 1) * share]
    total = total.astype(BF16)
    for j in range(devices):
        for slot in range(slots):
            n = wanted[j * slots + slot]
            for lt in range(lane_tiles):
                row = j * rows + (slot * lane_tiles + lt) * ROWS
                msg[row : row + ROWS] = pieces[n // groups, n % groups, lt]
        msg[j * rows + body_rows : (j + 1) * rows] = total


def unpack_kernel(lane_tiles, msg, coarse_out, conv, res, mix, packed):
    slots = coarse_out.shape[0]
    wide = mix.shape[0]
    chans = conv.shape[1]
    half = LANES // 2
    per_row = VOX // (LANES * lane_tiles)
    devices = 8 * per_row
    rows = msg.shape[0] // devices
    body_rows = slots * lane_tiles * ROWS
    share = rows - body_rows
    for j in range(devices):
        packed[j * share : (j + 1) * share] = msg[j * rows + body_rows : (j + 1) * rows].astype(F32)
    mix[...] = packed[0:wide]
    at = wide
    for t in range(8):
        res[t] = packed[at : at + chans]
        at += chans
    for t in range(4):
        block = packed[at : at + chans]
        conv[2 * t] = block[:, :half]
        if 2 * t + 1 < 7:
            conv[2 * t + 1] = block[:, half:]
        at += chans
    for j in range(devices):
        chan, part = j // per_row, j % per_row
        for q in range(slots):
            for lt in range(lane_tiles):
                row = j * rows + (q * lane_tiles + lt) * ROWS
                lane = (part * lane_tiles + lt) * LANES
                coarse_out[q, chan * ROWS : (chan + 1) * ROWS, lane : lane + LANES] = msg[
                    row : row + ROWS
                ]


def kernel_call(kernel, out_shape, grid_spec, flops, moved, vmem=VMEM_BYTES):
    return pl.pallas_call(
        kernel,
        out_shape=out_shape,
        grid_spec=grid_spec,
        compiler_params=pltpu.CompilerParams(vmem_limit_bytes=vmem),
        cost_estimate=pl.CostEstimate(flops=flops, bytes_accessed=moved, transcendentals=0),
    )


def body(features, counts, neighbors, parents, w_conv, w_restrict, w_mix, cotangent):
    devices = lax.axis_size("space")
    position = lax.axis_index("space").astype(jnp.int32).reshape(1)
    slots, wide = cotangent.shape[:2]
    count, chans = features.shape[:2]
    lane_tiles = VOX * 8 // devices // LANES
    tiles = slots * lane_tiles
    groups = count // 8
    whole = lambda shape: pl.BlockSpec(shape, lambda *_: (0,) * len(shape))
    any_spec = pl.BlockSpec(memory_space=pl.ANY)
    smem_spec = pl.BlockSpec(memory_space=pltpu.SMEM)
    smem = lambda size: pltpu.SMEM((size,), jnp.int32)
    vmem = pltpu.VMEM
    ints = lambda size: jax.ShapeDtypeStruct((size,), jnp.int32)

    message_shape = (devices, tiles * ROWS + LABEL_ROWS, LANES)
    flat_shape = (message_shape[0] * message_shape[1], LANES)
    message, kids = kernel_call(
        functools.partial(pack_kernel, lane_tiles),
        (jax.ShapeDtypeStruct(flat_shape, BF16), ints(groups)),
        pl.GridSpec(
            grid=(1,),
            in_specs=[smem_spec, whole(cotangent.shape)],
            out_specs=[whole(flat_shape), smem_spec],
            scratch_shapes=[smem(groups + 1)],
        ),
        1000, 2**20,
    )(parents.T, cotangent)
    spread = lax.all_to_all(
        message.reshape(message_shape), "space", split_axis=0, concat_axis=0, tiled=True
    )

    plane = jax.ShapeDtypeStruct((SEND // 2, chans, LANES), BF16)
    up, down, table, ordered = kernel_call(
        table_kernel,
        (plane, plane, ints(4 * count + 1), jax.ShapeDtypeStruct(features.shape, BF16)),
        pl.GridSpec(
            grid=(1,),
            in_specs=[smem_spec] * 5 + [any_spec],
            out_specs=[whole(plane.shape)] * 2 + [smem_spec, any_spec],
            scratch_shapes=[smem(SEND + 1)] * 4
            + [vmem(features.shape, BF16), vmem(features.shape, BF16), vmem((VOX, VOX), BF16),
               pltpu.SemaphoreType.DMA((PARTS,)), pltpu.SemaphoreType.DMA((PARTS,))],
        ),
        1000, 2**20,
    )(position, counts, kids, neighbors.T, parents.T, features)
    below = lax.ppermute(up, "space", [(i, i + 1) for i in range(devices - 1)])
    above = lax.ppermute(down, "space", [(i + 1, i) for i in range(devices - 1)])

    all_kids = spread[:, tiles * ROWS, :groups].astype(jnp.int32).reshape(-1)
    piece_shape = (devices, groups, lane_tiles, ROWS, LANES)
    forward_tiles = kernel_call(
        route_kernel,
        jax.ShapeDtypeStruct(piece_shape, BF16),
        pl.GridSpec(
            grid=(1,),
            in_specs=[smem_spec, whole(message_shape)],
            out_specs=whole(piece_shape),
        ),
        1000, 2**20, SMALL_VMEM_BYTES,
    )(all_kids, spread)
    forward_tiles, above, below = lax.optimization_barrier((forward_tiles, above, below))
    cot_pieces = lax.all_to_all(forward_tiles, "space", split_axis=0, concat_axis=0, tiled=True)

    res_rows = w_restrict.transpose(0, 2, 1).reshape(8 * chans, wide)
    scalars = (table, neighbors.T)
    brick_scratch = vmem((count + SEND + 1, chans, VOX), BF16)
    view_scratch = vmem((8, 7 * chans, VOX), BF16)
    per_group = lambda *shape: pl.BlockSpec((1,) + shape, lambda q: (q,) + (0,) * len(shape))
    piece_spec = pl.BlockSpec((devices, 1, lane_tiles, ROWS, LANES), lambda q: (0, q, 0, 0, 0))
    parts, slope, coarse, pieces = kernel_call(
        functools.partial(forward_kernel, lane_tiles),
        (
            jax.ShapeDtypeStruct((groups, 8 * chans, VOX), BF16),
            jax.ShapeDtypeStruct((groups, 8 * chans, VOX), BF16),
            jax.ShapeDtypeStruct((groups, wide, VOX), BF16),
            jax.ShapeDtypeStruct(piece_shape, BF16),
        ),
        pl.GridSpec(
            grid=(groups + 1,),
            in_specs=[any_spec] * 8,
            out_specs=[
                pl.BlockSpec((1, 8 * chans, VOX), lambda q: (jnp.minimum(q, groups - 1), 0, 0)),
                pl.BlockSpec((1, 8 * chans, VOX), lambda q: (jnp.minimum(q, groups - 1), 0, 0)),
                pl.BlockSpec((1, wide, VOX), lambda q: (jnp.maximum(q - 1, 0), 0, 0)),
                pl.BlockSpec(
                    (devices, 1, lane_tiles, ROWS, LANES),
                    lambda q: (0, jnp.maximum(q - 1, 0), 0, 0, 0),
                ),
            ],
            scratch_shapes=[
                brick_scratch, view_scratch, vmem((VOX, VOX), BF16), vmem(w_conv.shape, BF16),
                vmem(res_rows.shape, BF16), vmem(w_mix.shape, BF16),
                vmem((chans, 8 * chans), BF16), vmem((wide, 8 * chans), BF16),
                vmem((wide, VOX), BF16), smem(4 * count + 1),
                pltpu.SMEM((6, count), jnp.int32), vmem(plane.shape, BF16),
                vmem(plane.shape, BF16), pltpu.SemaphoreType.DMA((7 + PARTS,)),
            ],
        ),
        16 * 10**9, 16 * 2**20,
    )(*scalars, ordered, w_conv, res_rows, w_mix, above, below)
    returned = lax.all_to_all(pieces, "space", split_axis=0, concat_axis=0, tiled=True)

    scale = 1.0 / math.sqrt(devices * slots * VOX)
    used = wide + 8 * chans + 4 * chans
    rows = -(-used // (devices * 8)) * 8
    packed = kernel_call(
        functools.partial(backward_kernel, lane_tiles, scale),
        jax.ShapeDtypeStruct((devices * rows, LANES), BF16),
        pl.GridSpec(
            grid=(groups,),
            in_specs=[smem_spec] * 2 + [any_spec] + [whole(plane.shape)] * 2
            + [piece_spec, per_group(8 * chans, VOX), per_group(8 * chans, VOX),
               per_group(wide, VOX), whole(w_mix.shape), whole(res_rows.shape)],
            out_specs=whole((devices * rows, LANES)),
            scratch_shapes=[
                brick_scratch, view_scratch, vmem((wide, VOX), BF16),
                vmem((8 * chans, VOX), F32), vmem((8 * chans, VOX), BF16), vmem((VOX, VOX), BF16),
                vmem((wide, wide), BF16), vmem((chans, 8 * chans), F32),
                vmem((8 * chans, wide), F32), vmem((wide, wide), F32), pltpu.SemaphoreType.DMA,
            ],
        ),
        16 * 10**9, 16 * 2**20,
    )(*scalars, ordered, above, below, cot_pieces, parts, slope, coarse, w_mix, res_rows)

    shares = lax.all_to_all(
        packed.reshape(devices, rows, LANES), "space", split_axis=0, concat_axis=0, tiled=True
    )
    joined_shape = (devices, tiles * ROWS + rows, LANES)
    flat_shape = (joined_shape[0] * joined_shape[1], LANES)
    joined = kernel_call(
        join_kernel,
        jax.ShapeDtypeStruct(flat_shape, BF16),
        pl.GridSpec(
            grid=(1,),
            in_specs=[smem_spec, whole((devices * rows, LANES)), whole(piece_shape)],
            out_specs=whole(flat_shape),
            scratch_shapes=[smem(devices * groups), vmem((devices * rows, LANES), F32)],
        ),
        1000, 2**20, SMALL_VMEM_BYTES,
    )(all_kids, shares.reshape(devices * rows, LANES), returned)
    finished = lax.all_to_all(
        joined.reshape(joined_shape), "space", split_axis=0, concat_axis=0, tiled=True
    )

    coarse_out, grad_conv, grad_res, grad_mix = kernel_call(
        functools.partial(unpack_kernel, lane_tiles),
        (
            jax.ShapeDtypeStruct((slots, wide, VOX), BF16),
            jax.ShapeDtypeStruct((7, chans, chans), F32),
            jax.ShapeDtypeStruct((8, chans, wide), F32),
            jax.ShapeDtypeStruct((wide, wide), F32),
        ),
        pl.GridSpec(
            grid=(1,),
            in_specs=[whole(flat_shape)],
            out_specs=[whole((slots, wide, VOX)), whole((7, chans, chans)),
                       whole((8, chans, wide)), whole((wide, wide))],
            scratch_shapes=[vmem((devices * rows, LANES), F32)],
        ),
        1000, 2 * 2**20, SMALL_VMEM_BYTES,
    )(finished.reshape(flat_shape))
    return coarse_out, grad_conv, grad_res.transpose(0, 2, 1), grad_mix


def solution(mesh):
    return jax.shard_map(
        body,
        mesh=mesh,
        in_specs=(
            P(("groups", "space"), None, None),
            P(("groups", "space")),
            P(("groups", "space"), None),
            P(("groups", "space"), None),
            P(),
            P(),
            P(),
            P(("groups", "space"), None, None),
        ),
        out_specs=(
            P(("groups", "space"), None, None),
            P("groups", None, None),
            P("groups", None, None),
            P("groups", None),
        ),
        check_vma=False,
    )
```

```python
import functools
import math

import jax
import jax.numpy as jnp
from jax import lax
from jax.experimental import pallas as pl
from jax.experimental.pallas import tpu as pltpu
from jax.sharding import PartitionSpec as P

EDGE = 8
HALF = EDGE // 2
VOX = EDGE**3
LANES = 128
ROWS = 16
LABEL_ROWS = 8
SEND = 8
PARTS = 4
BF16 = jnp.bfloat16
F32 = jnp.float32
VMEM_BYTES = 60 * 1024 * 1024
SMALL_VMEM_BYTES = 16 * 1024 * 1024


def bits_of(value):
    return [(value >> (8 - k)) & 1 for k in range(9)]


def join_bits(bits):
    value = bits[0]
    for bit in bits[1:]:
        value = value * 2 + bit
    return value


def split_voxel(column):
    ta, tb, tc, a1, a0, b1, b0, c1, c0 = bits_of(column)
    return join_bits([a1, a0, ta, b1, b0, tb, c1, c0, tc])


def octant_voxel(column):
    oa, ob, oc, a1, a0, b1, b0, c1, c0 = bits_of(column)
    return join_bits([oa, a1, a0, ob, b1, b0, oc, c1, c0])


def picker(voxel_of, shape=(VOX, VOX), start=(0, 0), flip=False):
    row = lax.broadcasted_iota(jnp.int32, shape, 0) + start[0]
    column = lax.broadcasted_iota(jnp.int32, shape, 1) + start[1]
    return (column == voxel_of(row) if flip else row == voxel_of(column)).astype(BF16)


def digits(devices):
    radices, left = [], devices // 2
    while left > 1:
        radices.append(4 if left % 4 == 0 else 2)
        left //= radices[-1]
    radices.append(2)
    found, stride = [], devices
    for radix in radices:
        stride //= radix
        found.append((radix, stride))
    return found


def gather_by_digits(own, devices):
    held = own[None]
    for radix, stride in digits(devices):
        came = [held]
        for step in range(1, radix):
            pairs = []
            for i in range(devices):
                digit = i // stride % radix
                pairs.append((i, i + ((digit + step) % radix - digit) * stride))
            came.append(lax.ppermute(held, "space", pairs))
        held = jnp.concatenate(came, axis=0)
    return held


def dot(a, b):
    return jnp.dot(a, b, preferred_element_type=F32)


def dot_nt(a, b):
    return lax.dot_general(a, b, (((1,), (1,)), ((), ())), preferred_element_type=F32)


def pack_kernel(lane_tiles, parents, cot, msg, kids_out, kids):
    slots = cot.shape[0]
    body_rows = slots * lane_tiles * ROWS
    rows = body_rows + LABEL_ROWS
    devices = msg.shape[0] // rows

    def find(g, found):
        kids[found] = parents[0, g]
        return found + (parents[1, g] == 0).astype(jnp.int32)

    lax.fori_loop(0, parents.shape[1], find, jnp.int32(0), unroll=4)
    lane = lax.broadcasted_iota(jnp.int32, (LABEL_ROWS, LANES), 1)
    label = jnp.zeros((LABEL_ROWS, LANES), jnp.int32)
    for q in range(kids_out.shape[0]):
        kids_out[q] = kids[q]
        label = jnp.where(lane == q, kids[q], label)
    label = label.astype(F32).astype(BF16)
    for j in range(devices):
        msg[j * rows + body_rows : (j + 1) * rows] = label
    per_row = VOX // (LANES * lane_tiles)
    for j in range(devices):
        chan, part = j // per_row, j % per_row
        for q in range(slots):
            for lt in range(lane_tiles):
                lane = (part * lane_tiles + lt) * LANES
                row = j * rows + (q * lane_tiles + lt) * ROWS
                msg[row : row + ROWS] = cot[
                    q, chan * ROWS : (chan + 1) * ROWS, lane : lane + LANES
                ]


def table_kernel(
    place, counts, kids, neighbors, parents, feat, up, down, table, ordered,
    up_idx, up_far, down_idx, down_far, bricks, done, split, in_sem, out_sem,
):
    count, chans = feat.shape[:2]
    part = count // PARTS
    fetches = [
        pltpu.make_async_copy(
            feat.at[pl.ds(k * part, part)], bricks.at[pl.ds(k * part, part)], in_sem.at[k]
        )
        for k in range(PARTS)
    ]
    for fetch in fetches:
        fetch.start()
    base = place[0] * count
    table[4 * count] = place[0]
    for r in range(SEND + 1):
        up_idx[r] = 0
        down_idx[r] = 0
        up_far[r] = 2 * count
        down_far[r] = 2 * count
    split[...] = picker(split_voxel)

    def scan(g, found):
        n_up, n_down = found
        near_up, near_down = neighbors[0, g], neighbors[1, g]
        far_up, far_down = near_up - base - count, near_down - base + count
        goes_up = (near_up >= 0) & (far_up >= 0)
        goes_down = (near_down >= 0) & (far_down < count)
        up_idx[n_up] = g
        up_far[n_up] = jnp.where(goes_up, far_up, 2 * count)
        down_idx[n_down] = g
        down_far[n_down] = jnp.where(goes_down, far_down, 2 * count)
        q = jnp.int32(0)
        for k in range(1, kids.shape[0]):
            q += jnp.where(kids[k] == parents[0, g], k, 0)
        number = q * 8 + parents[1, g]
        table[number] = g
        table[count + number] = jnp.where(g < counts[0], g, count + SEND)
        return n_up + goes_up.astype(jnp.int32), n_down + goes_down.astype(jnp.int32)

    lax.fori_loop(0, count, scan, (jnp.int32(0), jnp.int32(0)), unroll=4)

    def rank(r, carry):
        for start, far, idx in ((2 * count, up_far, up_idx), (3 * count, down_far, down_idx)):
            earlier = jnp.int32(0)
            for other in range(SEND):
                earlier += (far[other] < far[r]).astype(jnp.int32)

            @pl.when(far[r] < count)
            def _():
                table[start + idx[r]] = count + earlier

        return carry

    lax.fori_loop(0, SEND, rank, jnp.int32(0))
    sends = []
    for k in range(PARTS):
        fetches[k].wait()
        rows = bricks[k * part : (k + 1) * part].reshape(part * chans, VOX)
        done[k * part : (k + 1) * part] = (
            dot(rows, split[...]).astype(BF16).reshape(part, chans, VOX)
        )
        sends.append(
            pltpu.make_async_copy(
                done.at[pl.ds(k * part, part)], ordered.at[pl.ds(k * part, part)], out_sem.at[k]
            )
        )
        sends[-1].start()
    low = low_lanes(chans)
    for r in range(SEND // 2):
        other = r + SEND // 2
        top = slice(VOX - LANES, VOX)
        up[r] = jnp.where(
            low,
            pltpu.roll(bricks[up_idx[r], :, top], LANES // 2, 1),
            bricks[up_idx[other], :, top],
        )
        down[r] = jnp.where(
            low,
            bricks[down_idx[r], :, :LANES],
            pltpu.roll(bricks[down_idx[other], :, :LANES], LANES // 2, 1),
        )
    for send in sends:
        send.wait()


def route_kernel(kids, msg, pieces):
    devices, groups, lane_tiles = pieces.shape[:3]
    slots = groups
    for s in range(devices):
        for q in range(groups):
            kid = kids[s * groups + q]
            owner, slot = kid // slots, kid % slots
            for lt in range(lane_tiles):
                row = pl.multiple_of((slot * lane_tiles + lt) * ROWS, ROWS)
                pieces[s, q, lt] = msg[owner, pl.ds(row, ROWS), :]


def place_arrivals(above, below, bricks, count):
    chans = bricks.shape[1]
    half = VOX // 2
    side = LANES // 2
    shape = (LANES, half)
    pairs = SEND // 2
    for k, shift in ((0, 0), (pairs, -side)):
        slots = slice(count + k, count + k + pairs)
        first = dot(
            above[...].reshape(pairs * chans, LANES), picker(split_voxel, shape, (shift, 0))
        )
        last = dot(
            below[...].reshape(pairs * chans, LANES),
            picker(split_voxel, shape, (VOX - side + shift, half)),
        )
        bricks[slots, :, :half] = first.astype(BF16).reshape(pairs, chans, half)
        bricks[slots, :, half:] = last.astype(BF16).reshape(pairs, chans, half)
    bricks[count + SEND] = jnp.zeros(bricks.shape[1:], BF16)


def sources(table, neighbors, number):
    count = neighbors.shape[1]
    g = table[number]
    found = []
    for d in range(6):
        near = neighbors[d, g]
        local = near - table[4 * count] * count
        if d == 0:
            local = jnp.where(local >= count, table[2 * count + g], local)
        if d == 1:
            local = jnp.where(local < 0, table[3 * count + g], local)
        found.append(jnp.where(near >= 0, local, count + SEND))
    found.append(table[count + number])
    return found


def shift_into(slots, bricks, views):
    chans = bricks.shape[1]
    tiles = VOX // LANES
    lane = lax.broadcasted_iota(jnp.int32, (chans, LANES), 1)
    low = lane < LANES // 2
    a = (lane // 16) % HALF
    b = (lane // 4) % HALF
    c = lane % HALF

    def tile(slot, t):
        return bricks[slot, :, t * LANES : (t + 1) * LANES]

    def turn(value, by):
        return pltpu.roll(value, by % LANES, 1)

    x = [tile(slots[6], t) for t in range(tiles)]
    for t in range(tiles):
        lanes = slice(t * LANES, (t + 1) * LANES)
        if t < 2:
            plus_a = x[t + 2]
            minus_a = jnp.where(a > 0, turn(x[t + 2], 16), turn(tile(slots[1], t + 2), -48))
        else:
            plus_a = jnp.where(a < HALF - 1, turn(x[t - 2], -16), turn(tile(slots[0], t - 2), 48))
            minus_a = x[t - 2]
        if t % 2 == 0:
            plus_b = x[t + 1]
            minus_b = jnp.where(b > 0, turn(x[t + 1], 4), turn(tile(slots[3], t + 1), -12))
        else:
            plus_b = jnp.where(b < HALF - 1, turn(x[t - 1], -4), turn(tile(slots[2], t - 1), 12))
            minus_b = x[t - 1]
        swapped = turn(x[t], 64)
        plus_c = jnp.where(c < HALF - 1, turn(x[t], 63), turn(tile(slots[4], t), 67))
        minus_c = jnp.where(c > 0, turn(x[t], -63), turn(tile(slots[5], t), -67))
        out = [plus_a, minus_a, plus_b, minus_b, jnp.where(low, swapped, plus_c),
               jnp.where(low, minus_c, swapped), x[t]]
        for d in range(7):
            views[d * chans : (d + 1) * chans, lanes] = out[d]


def low_lanes(rows):
    return lax.broadcasted_iota(jnp.int32, (rows, LANES), 1) < LANES // 2


def forward_kernel(
    lane_tiles, table_hbm, neighbors_hbm, feat, w_conv_hbm, w_res_hbm, w_mix_hbm,
    above_hbm, below_hbm,
    parts_out, slope_out, coarse_out, piece_out,
    bricks, views, place, w_conv, w_res, w_mix, conv_cat, res_cat, octants,
    table, neighbors, above, below, sem,
):
    q = pl.program_id(0)
    groups = pl.num_programs(0) - 1
    count, chans = feat.shape[:2]
    part = count // PARTS

    @pl.when(q == 0)
    def _():
        copies = [
            pltpu.make_async_copy(source, target, sem.at[k])
            for k, (source, target) in enumerate((
                (above_hbm, above), (below_hbm, below), (w_conv_hbm, w_conv),
                (w_res_hbm, w_res), (w_mix_hbm, w_mix), (table_hbm, table),
                (neighbors_hbm, neighbors),
                *(
                    (feat.at[pl.ds(k * part, part)], bricks.at[pl.ds(k * part, part)])
                    for k in range(PARTS)
                ),
            ))
        ]
        for copy in copies:
            copy.start()
        place[...] = picker(octant_voxel, flip=True)
        for copy in copies[:-PARTS]:
            copy.wait()
        place_arrivals(above, below, bricks, count)
        for d in range(7):
            conv_cat[:, d * chans : (d + 1) * chans] = w_conv[d]
        res_cat[...] = w_res[...].T
        for copy in copies[-PARTS:]:
            copy.wait()

    low_half = low_lanes(chans)

    def finish():
        coarse = dot(octants[...], place[...]).astype(BF16)
        coarse_out[0] = coarse
        mixed = dot(w_mix[...], coarse).astype(BF16)
        per_row = VOX // (LANES * lane_tiles)
        for j in range(piece_out.shape[0]):
            chan, part = j // per_row, j % per_row
            for lt in range(lane_tiles):
                lane = (part * lane_tiles + lt) * LANES
                piece_out[j, 0, lt] = mixed[chan * ROWS : (chan + 1) * ROWS, lane : lane + LANES]

    def restrict(first):
        acts = []
        for k in range(first, first + 4):
            shift_into(sources(table, neighbors, q * 8 + k), bricks, views.at[k])
            hidden = dot(conv_cat[:, : 7 * chans], views[k])
            sig = 1.0 / (1.0 + jnp.exp(-hidden))
            act = hidden * sig
            slope_out[0, k * chans : (k + 1) * chans, :] = (sig + act * (1.0 - sig)).astype(BF16)
            acts.append(act.astype(BF16))
        for k in range(0, 4, 2):
            lanes = slice((first + k) * (LANES // 2), (first + k + 2) * (LANES // 2))
            for t in range(4):
                one = acts[k][:, t * LANES : (t + 1) * LANES]
                two = acts[k + 1][:, t * LANES : (t + 1) * LANES]
                parts_out[0, 2 * t * chans : (2 * t + 1) * chans, lanes] = jnp.where(
                    low_half, one, pltpu.roll(two, LANES // 2, 1)
                )
                parts_out[0, (2 * t + 1) * chans : (2 * t + 2) * chans, lanes] = jnp.where(
                    low_half, pltpu.roll(one, LANES // 2, 1), two
                )
        lanes = slice(first * (LANES // 2), (first + 4) * (LANES // 2))
        return dot(res_cat[...], parts_out[0, :, lanes]).astype(BF16)

    @pl.when(q < groups)
    def _():
        finish()
        halves = [restrict(0), restrict(4)]
        octants[...] = jnp.concatenate(halves, axis=1)

    @pl.when(q == groups)
    def _():
        finish()


def backward_kernel(
    lane_tiles, scale, table, neighbors, feat, above, below, pieces, parts, slope, coarse, w_mix, w_res, packed,
    bricks, views, cot, grad_parts, grad_rows, unplace, mix_t, conv_sum, res_sum, mix_sum, sem,
):
    q = pl.program_id(0)
    count, chans = feat.shape[:2]
    wide = coarse.shape[1]
    fetch = pltpu.make_async_copy(feat, bricks.at[pl.ds(0, count)], sem)

    @pl.when(q == 0)
    def _():
        fetch.start()
        place_arrivals(above, below, bricks, count)
        unplace[...] = picker(octant_voxel)
        mix_t[...] = w_mix[...].T
        conv_sum[...] = jnp.zeros_like(conv_sum)
        res_sum[...] = jnp.zeros_like(res_sum)
        mix_sum[...] = jnp.zeros_like(mix_sum)
        fetch.wait()

    per_row = VOX // (LANES * lane_tiles)
    for j in range(pieces.shape[0]):
        chan, part = j // per_row, j % per_row
        for lt in range(lane_tiles):
            lane = (part * lane_tiles + lt) * LANES
            cot[chan * ROWS : (chan + 1) * ROWS, lane : lane + LANES] = pieces[j, 0, lt]
    cots = cot[...]
    grad_coarse = (scale * dot(mix_t[...], cots)).astype(BF16)
    grad_fine = dot(grad_coarse, unplace[...]).astype(BF16)
    mix_sum[...] += dot_nt(cots, coarse[0])
    res_sum[...] += dot_nt(parts[0], grad_fine)
    grad_parts[...] = dot(w_res[...], grad_fine)
    low_half = low_lanes(chans)
    for r in range(4):
        for t in range(4):
            cols = slice(r * LANES, (r + 1) * LANES)
            lanes = slice(t * LANES, (t + 1) * LANES)
            one = grad_parts[2 * t * chans : (2 * t + 1) * chans, cols]
            two = grad_parts[(2 * t + 1) * chans : (2 * t + 2) * chans, cols]
            first = slice(2 * r * chans, (2 * r + 1) * chans)
            second = slice((2 * r + 1) * chans, (2 * r + 2) * chans)
            grad_rows[first, lanes] = (
                jnp.where(low_half, one, pltpu.roll(two, LANES // 2, 1))
                * slope[0, first, lanes].astype(F32)
            ).astype(BF16)
            grad_rows[second, lanes] = (
                jnp.where(low_half, pltpu.roll(one, LANES // 2, 1), two)
                * slope[0, second, lanes].astype(F32)
            ).astype(BF16)

    total = None
    for k in range(8):
        shift_into(sources(table, neighbors, q * 8 + k), bricks, views.at[k])
        term = dot_nt(grad_rows[k * chans : (k + 1) * chans, :], views[k])
        total = term if total is None else total + term
    conv_sum[:, : 7 * chans] += total

    @pl.when(q == pl.num_programs(0) - 1)
    def _():
        packed[0:wide] = (scale * mix_sum[...]).astype(BF16)
        at = wide
        packed[at : at + 8 * chans] = res_sum[...].astype(BF16)
        at += 8 * chans
        for t in range(4):
            packed[at : at + chans] = conv_sum[:, t * LANES : (t + 1) * LANES].astype(BF16)
            at += chans
        if at < packed.shape[0]:
            packed[at:] = jnp.zeros((packed.shape[0] - at, LANES), BF16)


def sort_kernel(kids, pieces, msg, wanted):
    devices, groups, lane_tiles = pieces.shape[:3]
    slots = groups
    rows = slots * lane_tiles * ROWS

    def invert(n, carry):
        wanted[kids[n]] = n
        return carry

    lax.fori_loop(0, devices * groups, invert, jnp.int32(0), unroll=4)
    for j in range(devices):
        for slot in range(slots):
            n = wanted[j * slots + slot]
            for lt in range(lane_tiles):
                row = j * rows + (slot * lane_tiles + lt) * ROWS
                msg[row : row + ROWS] = pieces[n // groups, n % groups, lt]


def unpack_kernel(lane_tiles, place, msg, sums, coarse_out, conv, res, mix, packed, wide_sums):
    slots = coarse_out.shape[0]
    wide = mix.shape[0]
    chans = conv.shape[1]
    half = LANES // 2
    per_row = VOX // (LANES * lane_tiles)
    devices = 8 * per_row
    rows = msg.shape[0] // devices
    share = sums.shape[0] // devices
    wide_sums[...] = sums[...].astype(F32)
    for p in range(devices):
        source, behind = jnp.int32(0), p
        for radix, stride in digits(devices):
            digit = place[0] // stride % radix
            source += (digit + radix - behind % radix) % radix * stride
            behind //= radix
        at = pl.multiple_of(source * share, 8)
        packed[pl.ds(at, share), :] = wide_sums[p * share : (p + 1) * share]
    mix[...] = packed[0:wide]
    at = wide
    for t in range(8):
        res[t] = packed[at : at + chans]
        at += chans
    for t in range(4):
        block = packed[at : at + chans]
        conv[2 * t] = block[:, :half]
        if 2 * t + 1 < 7:
            conv[2 * t + 1] = block[:, half:]
        at += chans
    for j in range(devices):
        chan, part = j // per_row, j % per_row
        for q in range(slots):
            for lt in range(lane_tiles):
                row = j * rows + (q * lane_tiles + lt) * ROWS
                lane = (part * lane_tiles + lt) * LANES
                coarse_out[q, chan * ROWS : (chan + 1) * ROWS, lane : lane + LANES] = msg[
                    row : row + ROWS
                ]


def kernel_call(kernel, out_shape, grid_spec, flops, moved, vmem=VMEM_BYTES):
    return pl.pallas_call(
        kernel,
        out_shape=out_shape,
        grid_spec=grid_spec,
        compiler_params=pltpu.CompilerParams(vmem_limit_bytes=vmem),
        cost_estimate=pl.CostEstimate(flops=flops, bytes_accessed=moved, transcendentals=0),
    )


def body(features, counts, neighbors, parents, w_conv, w_restrict, w_mix, cotangent):
    devices = lax.axis_size("space")
    position = lax.axis_index("space").astype(jnp.int32).reshape(1)
    slots, wide = cotangent.shape[:2]
    count, chans = features.shape[:2]
    lane_tiles = VOX * 8 // devices // LANES
    tiles = slots * lane_tiles
    groups = count // 8
    whole = lambda shape: pl.BlockSpec(shape, lambda *_: (0,) * len(shape))
    any_spec = pl.BlockSpec(memory_space=pl.ANY)
    smem_spec = pl.BlockSpec(memory_space=pltpu.SMEM)
    smem = lambda size: pltpu.SMEM((size,), jnp.int32)
    vmem = pltpu.VMEM
    ints = lambda size: jax.ShapeDtypeStruct((size,), jnp.int32)

    message_shape = (devices, tiles * ROWS + LABEL_ROWS, LANES)
    flat_shape = (message_shape[0] * message_shape[1], LANES)
    message, kids = kernel_call(
        functools.partial(pack_kernel, lane_tiles),
        (jax.ShapeDtypeStruct(flat_shape, BF16), ints(groups)),
        pl.GridSpec(
            grid=(1,),
            in_specs=[smem_spec, whole(cotangent.shape)],
            out_specs=[whole(flat_shape), smem_spec],
            scratch_shapes=[smem(groups + 1)],
        ),
        1000, 2**20,
    )(parents.T, cotangent)
    spread = lax.all_to_all(
        message.reshape(message_shape), "space", split_axis=0, concat_axis=0, tiled=True
    )

    plane = jax.ShapeDtypeStruct((SEND // 2, chans, LANES), BF16)
    up, down, table, ordered = kernel_call(
        table_kernel,
        (plane, plane, ints(4 * count + 1), jax.ShapeDtypeStruct(features.shape, BF16)),
        pl.GridSpec(
            grid=(1,),
            in_specs=[smem_spec] * 5 + [any_spec],
            out_specs=[whole(plane.shape)] * 2 + [smem_spec, any_spec],
            scratch_shapes=[smem(SEND + 1)] * 4
            + [vmem(features.shape, BF16), vmem(features.shape, BF16), vmem((VOX, VOX), BF16),
               pltpu.SemaphoreType.DMA((PARTS,)), pltpu.SemaphoreType.DMA((PARTS,))],
        ),
        1000, 2**20,
    )(position, counts, kids, neighbors.T, parents.T, features)
    below = lax.ppermute(up, "space", [(i, i + 1) for i in range(devices - 1)])
    above = lax.ppermute(down, "space", [(i + 1, i) for i in range(devices - 1)])

    all_kids = spread[:, tiles * ROWS, :groups].astype(jnp.int32).reshape(-1)
    piece_shape = (devices, groups, lane_tiles, ROWS, LANES)
    forward_tiles = kernel_call(
        route_kernel,
        jax.ShapeDtypeStruct(piece_shape, BF16),
        pl.GridSpec(
            grid=(1,),
            in_specs=[smem_spec, whole(message_shape)],
            out_specs=whole(piece_shape),
        ),
        1000, 2**20, SMALL_VMEM_BYTES,
    )(all_kids, spread)
    forward_tiles, above, below = lax.optimization_barrier((forward_tiles, above, below))
    cot_pieces = lax.all_to_all(forward_tiles, "space", split_axis=0, concat_axis=0, tiled=True)

    res_rows = w_restrict.transpose(0, 2, 1).reshape(8 * chans, wide)
    scalars = (table, neighbors.T)
    brick_scratch = vmem((count + SEND + 1, chans, VOX), BF16)
    view_scratch = vmem((8, 7 * chans, VOX), BF16)
    per_group = lambda *shape: pl.BlockSpec((1,) + shape, lambda q: (q,) + (0,) * len(shape))
    piece_spec = pl.BlockSpec((devices, 1, lane_tiles, ROWS, LANES), lambda q: (0, q, 0, 0, 0))
    parts, slope, coarse, pieces = kernel_call(
        functools.partial(forward_kernel, lane_tiles),
        (
            jax.ShapeDtypeStruct((groups, 8 * chans, VOX), BF16),
            jax.ShapeDtypeStruct((groups, 8 * chans, VOX), BF16),
            jax.ShapeDtypeStruct((groups, wide, VOX), BF16),
            jax.ShapeDtypeStruct(piece_shape, BF16),
        ),
        pl.GridSpec(
            grid=(groups + 1,),
            in_specs=[any_spec] * 8,
            out_specs=[
                pl.BlockSpec((1, 8 * chans, VOX), lambda q: (jnp.minimum(q, groups - 1), 0, 0)),
                pl.BlockSpec((1, 8 * chans, VOX), lambda q: (jnp.minimum(q, groups - 1), 0, 0)),
                pl.BlockSpec((1, wide, VOX), lambda q: (jnp.maximum(q - 1, 0), 0, 0)),
                pl.BlockSpec(
                    (devices, 1, lane_tiles, ROWS, LANES),
                    lambda q: (0, jnp.maximum(q - 1, 0), 0, 0, 0),
                ),
            ],
            scratch_shapes=[
                brick_scratch, view_scratch, vmem((VOX, VOX), BF16), vmem(w_conv.shape, BF16),
                vmem(res_rows.shape, BF16), vmem(w_mix.shape, BF16),
                vmem((chans, 8 * chans), BF16), vmem((wide, 8 * chans), BF16),
                vmem((wide, VOX), BF16), smem(4 * count + 1),
                pltpu.SMEM((6, count), jnp.int32), vmem(plane.shape, BF16),
                vmem(plane.shape, BF16), pltpu.SemaphoreType.DMA((7 + PARTS,)),
            ],
        ),
        16 * 10**9, 16 * 2**20,
    )(*scalars, ordered, w_conv, res_rows, w_mix, above, below)
    returned = lax.all_to_all(pieces, "space", split_axis=0, concat_axis=0, tiled=True)

    scale = 1.0 / math.sqrt(devices * slots * VOX)
    used = wide + 8 * chans + 4 * chans
    rows = -(-used // (devices * 8)) * 8
    packed = kernel_call(
        functools.partial(backward_kernel, lane_tiles, scale),
        jax.ShapeDtypeStruct((devices * rows, LANES), BF16),
        pl.GridSpec(
            grid=(groups,),
            in_specs=[smem_spec] * 2 + [any_spec] + [whole(plane.shape)] * 2
            + [piece_spec, per_group(8 * chans, VOX), per_group(8 * chans, VOX),
               per_group(wide, VOX), whole(w_mix.shape), whole(res_rows.shape)],
            out_specs=whole((devices * rows, LANES)),
            scratch_shapes=[
                brick_scratch, view_scratch, vmem((wide, VOX), BF16),
                vmem((8 * chans, VOX), F32), vmem((8 * chans, VOX), BF16), vmem((VOX, VOX), BF16),
                vmem((wide, wide), BF16), vmem((chans, 8 * chans), F32),
                vmem((8 * chans, wide), F32), vmem((wide, wide), F32), pltpu.SemaphoreType.DMA,
            ],
        ),
        16 * 10**9, 16 * 2**20,
    )(*scalars, ordered, above, below, cot_pieces, parts, slope, coarse, w_mix, res_rows)

    shares = lax.all_to_all(
        packed.reshape(devices, rows, LANES), "space", split_axis=0, concat_axis=0, tiled=True
    )
    returned, _ = lax.optimization_barrier((returned, packed))
    flat_shape = (devices * tiles * ROWS, LANES)
    sorted_pieces = kernel_call(
        sort_kernel,
        jax.ShapeDtypeStruct(flat_shape, BF16),
        pl.GridSpec(
            grid=(1,),
            in_specs=[smem_spec, whole(piece_shape)],
            out_specs=whole(flat_shape),
            scratch_shapes=[smem(devices * groups)],
        ),
        1000, 2**20, SMALL_VMEM_BYTES,
    )(all_kids, returned)
    sorted_pieces, shares = lax.optimization_barrier((sorted_pieces, shares))
    finished = lax.all_to_all(
        sorted_pieces.reshape(devices, tiles * ROWS, LANES),
        "space", split_axis=0, concat_axis=0, tiled=True,
    )
    summed = jnp.sum(shares.astype(F32), axis=0).astype(BF16)
    sums = gather_by_digits(summed, devices).reshape(devices * rows, LANES)

    coarse_out, grad_conv, grad_res, grad_mix = kernel_call(
        functools.partial(unpack_kernel, lane_tiles),
        (
            jax.ShapeDtypeStruct((slots, wide, VOX), BF16),
            jax.ShapeDtypeStruct((7, chans, chans), F32),
            jax.ShapeDtypeStruct((8, chans, wide), F32),
            jax.ShapeDtypeStruct((wide, wide), F32),
        ),
        pl.GridSpec(
            grid=(1,),
            in_specs=[smem_spec, whole(flat_shape), whole((devices * rows, LANES))],
            out_specs=[whole((slots, wide, VOX)), whole((7, chans, chans)),
                       whole((8, chans, wide)), whole((wide, wide))],
            scratch_shapes=[vmem((devices * rows, LANES), F32)] * 2,
        ),
        1000, 2 * 2**20, SMALL_VMEM_BYTES,
    )(position, finished.reshape(flat_shape), sums)
    return coarse_out, grad_conv, grad_res.transpose(0, 2, 1), grad_mix


def solution(mesh):
    return jax.shard_map(
        body,
        mesh=mesh,
        in_specs=(
            P(("groups", "space"), None, None),
            P(("groups", "space")),
            P(("groups", "space"), None),
            P(("groups", "space"), None),
            P(),
            P(),
            P(),
            P(("groups", "space"), None, None),
        ),
        out_specs=(
            P(("groups", "space"), None, None),
            P("groups", None, None),
            P("groups", None, None),
            P("groups", None),
        ),
        check_vma=False,
    )
```

```python
import functools
import math

import jax
import jax.numpy as jnp
from jax import lax
from jax.experimental import pallas as pl
from jax.experimental.pallas import tpu as pltpu
from jax.sharding import PartitionSpec as P

EDGE = 8
HALF = EDGE // 2
VOX = EDGE**3
LANES = 128
ROWS = 16
LABEL_ROWS = 8
SEND = 8
PARTS = 4
BF16 = jnp.bfloat16
F32 = jnp.float32
VMEM_BYTES = 60 * 1024 * 1024
SMALL_VMEM_BYTES = 16 * 1024 * 1024


def bits_of(value):
    return [(value >> (8 - k)) & 1 for k in range(9)]


def join_bits(bits):
    value = bits[0]
    for bit in bits[1:]:
        value = value * 2 + bit
    return value


def split_voxel(column):
    ta, tb, tc, a1, a0, b1, b0, c1, c0 = bits_of(column)
    return join_bits([a1, a0, ta, b1, b0, tb, c1, c0, tc])


def octant_voxel(column):
    oa, ob, oc, a1, a0, b1, b0, c1, c0 = bits_of(column)
    return join_bits([oa, a1, a0, ob, b1, b0, oc, c1, c0])


def picker(voxel_of, shape=(VOX, VOX), start=(0, 0), flip=False):
    row = lax.broadcasted_iota(jnp.int32, shape, 0) + start[0]
    column = lax.broadcasted_iota(jnp.int32, shape, 1) + start[1]
    return (column == voxel_of(row) if flip else row == voxel_of(column)).astype(BF16)


def digits(devices):
    found, stride = [], devices
    while stride > 1:
        radix = 4 if stride % 4 == 0 else 2
        stride //= radix
        found.append((radix, stride))
    return found


def gather_by_digits(own, devices):
    held = own[None]
    for radix, stride in digits(devices):
        came = [held]
        for step in range(1, radix):
            pairs = []
            for i in range(devices):
                digit = i // stride % radix
                pairs.append((i, i + ((digit + step) % radix - digit) * stride))
            came.append(lax.ppermute(held, "space", pairs))
        held = jnp.concatenate(came, axis=0)
    return held


def dot(a, b):
    return jnp.dot(a, b, preferred_element_type=F32)


def dot_nt(a, b):
    return lax.dot_general(a, b, (((1,), (1,)), ((), ())), preferred_element_type=F32)


def pack_kernel(lane_tiles, parents, cot, msg, kids_out, kids):
    slots = cot.shape[0]
    body_rows = slots * lane_tiles * ROWS
    rows = body_rows + LABEL_ROWS
    devices = msg.shape[0] // rows

    def find(g, found):
        kids[found] = parents[0, g]
        return found + (parents[1, g] == 0).astype(jnp.int32)

    lax.fori_loop(0, parents.shape[1], find, jnp.int32(0), unroll=4)
    lane = lax.broadcasted_iota(jnp.int32, (LABEL_ROWS, LANES), 1)
    label = jnp.zeros((LABEL_ROWS, LANES), jnp.int32)
    for q in range(kids_out.shape[0]):
        kids_out[q] = kids[q]
        label = jnp.where(lane == q, kids[q], label)
    label = label.astype(F32).astype(BF16)
    for j in range(devices):
        msg[j * rows + body_rows : (j + 1) * rows] = label
    per_row = VOX // (LANES * lane_tiles)
    for j in range(devices):
        chan, part = j // per_row, j % per_row
        for q in range(slots):
            for lt in range(lane_tiles):
                lane = (part * lane_tiles + lt) * LANES
                row = j * rows + (q * lane_tiles + lt) * ROWS
                msg[row : row + ROWS] = cot[
                    q, chan * ROWS : (chan + 1) * ROWS, lane : lane + LANES
                ]


def table_kernel(
    place, counts, kids, neighbors, parents, feat, up, down, table, ordered,
    up_idx, up_far, down_idx, down_far, bricks, done, split, in_sem, out_sem,
):
    count, chans = feat.shape[:2]
    part = count // PARTS
    fetches = [
        pltpu.make_async_copy(
            feat.at[pl.ds(k * part, part)], bricks.at[pl.ds(k * part, part)], in_sem.at[k]
        )
        for k in range(PARTS)
    ]
    for fetch in fetches:
        fetch.start()
    base = place[0] * count
    table[4 * count] = place[0]
    for r in range(SEND + 1):
        up_idx[r] = 0
        down_idx[r] = 0
        up_far[r] = 2 * count
        down_far[r] = 2 * count
    split[...] = picker(split_voxel)

    def scan(g, found):
        n_up, n_down = found
        near_up, near_down = neighbors[0, g], neighbors[1, g]
        far_up, far_down = near_up - base - count, near_down - base + count
        goes_up = (near_up >= 0) & (far_up >= 0)
        goes_down = (near_down >= 0) & (far_down < count)
        up_idx[n_up] = g
        up_far[n_up] = jnp.where(goes_up, far_up, 2 * count)
        down_idx[n_down] = g
        down_far[n_down] = jnp.where(goes_down, far_down, 2 * count)
        q = jnp.int32(0)
        for k in range(1, kids.shape[0]):
            q += jnp.where(kids[k] == parents[0, g], k, 0)
        number = q * 8 + parents[1, g]
        table[number] = g
        table[count + number] = jnp.where(g < counts[0], g, count + SEND)
        return n_up + goes_up.astype(jnp.int32), n_down + goes_down.astype(jnp.int32)

    lax.fori_loop(0, count, scan, (jnp.int32(0), jnp.int32(0)), unroll=4)

    def rank(r, carry):
        for start, far, idx in ((2 * count, up_far, up_idx), (3 * count, down_far, down_idx)):
            earlier = jnp.int32(0)
            for other in range(SEND):
                earlier += (far[other] < far[r]).astype(jnp.int32)

            @pl.when(far[r] < count)
            def _():
                table[start + idx[r]] = count + earlier

        return carry

    lax.fori_loop(0, SEND, rank, jnp.int32(0))
    sends = []
    for k in range(PARTS):
        fetches[k].wait()
        rows = bricks[k * part : (k + 1) * part].reshape(part * chans, VOX)
        done[k * part : (k + 1) * part] = (
            dot(rows, split[...]).astype(BF16).reshape(part, chans, VOX)
        )
        sends.append(
            pltpu.make_async_copy(
                done.at[pl.ds(k * part, part)], ordered.at[pl.ds(k * part, part)], out_sem.at[k]
            )
        )
        sends[-1].start()
    low = low_lanes(chans)
    for r in range(SEND // 2):
        other = r + SEND // 2
        top = slice(VOX - LANES, VOX)
        up[r] = jnp.where(
            low,
            pltpu.roll(bricks[up_idx[r], :, top], LANES // 2, 1),
            bricks[up_idx[other], :, top],
        )
        down[r] = jnp.where(
            low,
            bricks[down_idx[r], :, :LANES],
            pltpu.roll(bricks[down_idx[other], :, :LANES], LANES // 2, 1),
        )
    for send in sends:
        send.wait()


def route_kernel(kids, msg, pieces):
    devices, groups, lane_tiles = pieces.shape[:3]
    slots = groups
    for s in range(devices):
        for q in range(groups):
            kid = kids[s * groups + q]
            owner, slot = kid // slots, kid % slots
            for lt in range(lane_tiles):
                row = pl.multiple_of((slot * lane_tiles + lt) * ROWS, ROWS)
                pieces[s, q, lt] = msg[owner, pl.ds(row, ROWS), :]


def place_arrivals(above, below, bricks, count):
    chans = bricks.shape[1]
    half = VOX // 2
    side = LANES // 2
    shape = (LANES, half)
    pairs = SEND // 2
    for k, shift in ((0, 0), (pairs, -side)):
        slots = slice(count + k, count + k + pairs)
        first = dot(
            above[...].reshape(pairs * chans, LANES), picker(split_voxel, shape, (shift, 0))
        )
        last = dot(
            below[...].reshape(pairs * chans, LANES),
            picker(split_voxel, shape, (VOX - side + shift, half)),
        )
        bricks[slots, :, :half] = first.astype(BF16).reshape(pairs, chans, half)
        bricks[slots, :, half:] = last.astype(BF16).reshape(pairs, chans, half)
    bricks[count + SEND] = jnp.zeros(bricks.shape[1:], BF16)


def sources(table, neighbors, number):
    count = neighbors.shape[1]
    g = table[number]
    found = []
    for d in range(6):
        near = neighbors[d, g]
        local = near - table[4 * count] * count
        if d == 0:
            local = jnp.where(local >= count, table[2 * count + g], local)
        if d == 1:
            local = jnp.where(local < 0, table[3 * count + g], local)
        found.append(jnp.where(near >= 0, local, count + SEND))
    found.append(table[count + number])
    return found


def shift_into(slots, bricks, views):
    chans = bricks.shape[1]
    tiles = VOX // LANES
    lane = lax.broadcasted_iota(jnp.int32, (chans, LANES), 1)
    low = lane < LANES // 2
    a = (lane // 16) % HALF
    b = (lane // 4) % HALF
    c = lane % HALF

    def tile(slot, t):
        return bricks[slot, :, t * LANES : (t + 1) * LANES]

    def turn(value, by):
        return pltpu.roll(value, by % LANES, 1)

    x = [tile(slots[6], t) for t in range(tiles)]
    for t in range(tiles):
        lanes = slice(t * LANES, (t + 1) * LANES)
        if t < 2:
            plus_a = x[t + 2]
            minus_a = jnp.where(a > 0, turn(x[t + 2], 16), turn(tile(slots[1], t + 2), -48))
        else:
            plus_a = jnp.where(a < HALF - 1, turn(x[t - 2], -16), turn(tile(slots[0], t - 2), 48))
            minus_a = x[t - 2]
        if t % 2 == 0:
            plus_b = x[t + 1]
            minus_b = jnp.where(b > 0, turn(x[t + 1], 4), turn(tile(slots[3], t + 1), -12))
        else:
            plus_b = jnp.where(b < HALF - 1, turn(x[t - 1], -4), turn(tile(slots[2], t - 1), 12))
            minus_b = x[t - 1]
        swapped = turn(x[t], 64)
        plus_c = jnp.where(c < HALF - 1, turn(x[t], 63), turn(tile(slots[4], t), 67))
        minus_c = jnp.where(c > 0, turn(x[t], -63), turn(tile(slots[5], t), -67))
        out = [plus_a, minus_a, plus_b, minus_b, jnp.where(low, swapped, plus_c),
               jnp.where(low, minus_c, swapped), x[t]]
        for d in range(7):
            views[d * chans : (d + 1) * chans, lanes] = out[d]


def low_lanes(rows):
    return lax.broadcasted_iota(jnp.int32, (rows, LANES), 1) < LANES // 2


def forward_kernel(
    lane_tiles, table_hbm, neighbors_hbm, feat, w_conv_hbm, w_res_hbm, w_mix_hbm,
    above_hbm, below_hbm,
    parts_out, slope_out, coarse_out, piece_out,
    bricks, views, place, w_conv, w_res, w_mix, conv_cat, res_cat, octants,
    table, neighbors, above, below, sem,
):
    q = pl.program_id(0)
    groups = pl.num_programs(0) - 1
    count, chans = feat.shape[:2]
    part = count // PARTS

    @pl.when(q == 0)
    def _():
        copies = [
            pltpu.make_async_copy(source, target, sem.at[k])
            for k, (source, target) in enumerate((
                (above_hbm, above), (below_hbm, below), (w_conv_hbm, w_conv),
                (w_res_hbm, w_res), (w_mix_hbm, w_mix), (table_hbm, table),
                (neighbors_hbm, neighbors),
                *(
                    (feat.at[pl.ds(k * part, part)], bricks.at[pl.ds(k * part, part)])
                    for k in range(PARTS)
                ),
            ))
        ]
        for copy in copies:
            copy.start()
        place[...] = picker(octant_voxel, flip=True)
        for copy in copies[:-PARTS]:
            copy.wait()
        place_arrivals(above, below, bricks, count)
        for d in range(7):
            conv_cat[:, d * chans : (d + 1) * chans] = w_conv[d]
        res_cat[...] = w_res[...].T
        for copy in copies[-PARTS:]:
            copy.wait()

    low_half = low_lanes(chans)

    def finish():
        coarse = dot(octants[...], place[...]).astype(BF16)
        coarse_out[0] = coarse
        mixed = dot(w_mix[...], coarse).astype(BF16)
        per_row = VOX // (LANES * lane_tiles)
        for j in range(piece_out.shape[0]):
            chan, part = j // per_row, j % per_row
            for lt in range(lane_tiles):
                lane = (part * lane_tiles + lt) * LANES
                piece_out[j, 0, lt] = mixed[chan * ROWS : (chan + 1) * ROWS, lane : lane + LANES]

    def restrict(first):
        acts = []
        for k in range(first, first + 4):
            shift_into(sources(table, neighbors, q * 8 + k), bricks, views.at[k])
            hidden = dot(conv_cat[:, : 7 * chans], views[k])
            sig = 1.0 / (1.0 + jnp.exp(-hidden))
            act = hidden * sig
            slope_out[0, k * chans : (k + 1) * chans, :] = (sig + act * (1.0 - sig)).astype(BF16)
            acts.append(act.astype(BF16))
        for k in range(0, 4, 2):
            lanes = slice((first + k) * (LANES // 2), (first + k + 2) * (LANES // 2))
            for t in range(4):
                one = acts[k][:, t * LANES : (t + 1) * LANES]
                two = acts[k + 1][:, t * LANES : (t + 1) * LANES]
                parts_out[0, 2 * t * chans : (2 * t + 1) * chans, lanes] = jnp.where(
                    low_half, one, pltpu.roll(two, LANES // 2, 1)
                )
                parts_out[0, (2 * t + 1) * chans : (2 * t + 2) * chans, lanes] = jnp.where(
                    low_half, pltpu.roll(one, LANES // 2, 1), two
                )
        lanes = slice(first * (LANES // 2), (first + 4) * (LANES // 2))
        return dot(res_cat[...], parts_out[0, :, lanes]).astype(BF16)

    @pl.when(q < groups)
    def _():
        finish()
        halves = [restrict(0), restrict(4)]
        octants[...] = jnp.concatenate(halves, axis=1)

    @pl.when(q == groups)
    def _():
        finish()


def backward_kernel(
    lane_tiles, scale, table, neighbors, feat, above, below, pieces, parts, slope, coarse, w_mix, w_res, packed,
    bricks, views, cot, grad_parts, grad_rows, unplace, mix_t, conv_sum, res_sum, mix_sum, sem,
):
    q = pl.program_id(0)
    count, chans = feat.shape[:2]
    wide = coarse.shape[1]
    fetch = pltpu.make_async_copy(feat, bricks.at[pl.ds(0, count)], sem)

    @pl.when(q == 0)
    def _():
        fetch.start()
        place_arrivals(above, below, bricks, count)
        unplace[...] = picker(octant_voxel)
        mix_t[...] = w_mix[...].T
        conv_sum[...] = jnp.zeros_like(conv_sum)
        res_sum[...] = jnp.zeros_like(res_sum)
        mix_sum[...] = jnp.zeros_like(mix_sum)
        fetch.wait()

    per_row = VOX // (LANES * lane_tiles)
    for j in range(pieces.shape[0]):
        chan, part = j // per_row, j % per_row
        for lt in range(lane_tiles):
            lane = (part * lane_tiles + lt) * LANES
            cot[chan * ROWS : (chan + 1) * ROWS, lane : lane + LANES] = pieces[j, 0, lt]
    cots = cot[...]
    grad_coarse = (scale * dot(mix_t[...], cots)).astype(BF16)
    grad_fine = dot(grad_coarse, unplace[...]).astype(BF16)
    mix_sum[...] += dot_nt(cots, coarse[0])
    res_sum[...] += dot_nt(parts[0], grad_fine)
    grad_parts[...] = dot(w_res[...], grad_fine)
    low_half = low_lanes(chans)
    for r in range(4):
        for t in range(4):
            cols = slice(r * LANES, (r + 1) * LANES)
            lanes = slice(t * LANES, (t + 1) * LANES)
            one = grad_parts[2 * t * chans : (2 * t + 1) * chans, cols]
            two = grad_parts[(2 * t + 1) * chans : (2 * t + 2) * chans, cols]
            first = slice(2 * r * chans, (2 * r + 1) * chans)
            second = slice((2 * r + 1) * chans, (2 * r + 2) * chans)
            grad_rows[first, lanes] = (
                jnp.where(low_half, one, pltpu.roll(two, LANES // 2, 1))
                * slope[0, first, lanes].astype(F32)
            ).astype(BF16)
            grad_rows[second, lanes] = (
                jnp.where(low_half, pltpu.roll(one, LANES // 2, 1), two)
                * slope[0, second, lanes].astype(F32)
            ).astype(BF16)

    total = None
    for k in range(8):
        shift_into(sources(table, neighbors, q * 8 + k), bricks, views.at[k])
        term = dot_nt(grad_rows[k * chans : (k + 1) * chans, :], views[k])
        total = term if total is None else total + term
    conv_sum[:, : 7 * chans] += total

    @pl.when(q == pl.num_programs(0) - 1)
    def _():
        packed[0:wide] = (scale * mix_sum[...]).astype(BF16)
        at = wide
        packed[at : at + 8 * chans] = res_sum[...].astype(BF16)
        at += 8 * chans
        for t in range(4):
            packed[at : at + chans] = conv_sum[:, t * LANES : (t + 1) * LANES].astype(BF16)
            at += chans
        if at < packed.shape[0]:
            packed[at:] = jnp.zeros((packed.shape[0] - at, LANES), BF16)


def sort_kernel(kids, pieces, msg, wanted):
    devices, groups, lane_tiles = pieces.shape[:3]
    slots = groups
    rows = slots * lane_tiles * ROWS

    def invert(n, carry):
        wanted[kids[n]] = n
        return carry

    lax.fori_loop(0, devices * groups, invert, jnp.int32(0), unroll=4)
    for j in range(devices):
        for slot in range(slots):
            n = wanted[j * slots + slot]
            for lt in range(lane_tiles):
                row = j * rows + (slot * lane_tiles + lt) * ROWS
                msg[row : row + ROWS] = pieces[n // groups, n % groups, lt]


def unpack_kernel(lane_tiles, place, msg, sums, coarse_out, conv, res, mix, packed, wide_sums):
    slots = coarse_out.shape[0]
    wide = mix.shape[0]
    chans = conv.shape[1]
    half = LANES // 2
    per_row = VOX // (LANES * lane_tiles)
    devices = 8 * per_row
    rows = msg.shape[0] // devices
    share = sums.shape[0] // devices
    wide_sums[...] = sums[...].astype(F32)
    for p in range(devices):
        source, behind = jnp.int32(0), p
        for radix, stride in digits(devices):
            digit = place[0] // stride % radix
            source += (digit + radix - behind % radix) % radix * stride
            behind //= radix
        at = pl.multiple_of(source * share, 8)
        packed[pl.ds(at, share), :] = wide_sums[p * share : (p + 1) * share]
    mix[...] = packed[0:wide]
    at = wide
    for t in range(8):
        res[t] = packed[at : at + chans]
        at += chans
    for t in range(4):
        block = packed[at : at + chans]
        conv[2 * t] = block[:, :half]
        if 2 * t + 1 < 7:
            conv[2 * t + 1] = block[:, half:]
        at += chans
    for j in range(devices):
        chan, part = j // per_row, j % per_row
        for q in range(slots):
            for lt in range(lane_tiles):
                row = j * rows + (q * lane_tiles + lt) * ROWS
                lane = (part * lane_tiles + lt) * LANES
                coarse_out[q, chan * ROWS : (chan + 1) * ROWS, lane : lane + LANES] = msg[
                    row : row + ROWS
                ]


def kernel_call(kernel, out_shape, grid_spec, flops, moved, vmem=VMEM_BYTES):
    return pl.pallas_call(
        kernel,
        out_shape=out_shape,
        grid_spec=grid_spec,
        compiler_params=pltpu.CompilerParams(vmem_limit_bytes=vmem),
        cost_estimate=pl.CostEstimate(flops=flops, bytes_accessed=moved, transcendentals=0),
    )


def body(features, counts, neighbors, parents, w_conv, w_restrict, w_mix, cotangent):
    devices = lax.axis_size("space")
    position = lax.axis_index("space").astype(jnp.int32).reshape(1)
    slots, wide = cotangent.shape[:2]
    count, chans = features.shape[:2]
    lane_tiles = VOX * 8 // devices // LANES
    tiles = slots * lane_tiles
    groups = count // 8
    whole = lambda shape: pl.BlockSpec(shape, lambda *_: (0,) * len(shape))
    any_spec = pl.BlockSpec(memory_space=pl.ANY)
    smem_spec = pl.BlockSpec(memory_space=pltpu.SMEM)
    smem = lambda size: pltpu.SMEM((size,), jnp.int32)
    vmem = pltpu.VMEM
    ints = lambda size: jax.ShapeDtypeStruct((size,), jnp.int32)

    message_shape = (devices, tiles * ROWS + LABEL_ROWS, LANES)
    flat_shape = (message_shape[0] * message_shape[1], LANES)
    message, kids = kernel_call(
        functools.partial(pack_kernel, lane_tiles),
        (jax.ShapeDtypeStruct(flat_shape, BF16), ints(groups)),
        pl.GridSpec(
            grid=(1,),
            in_specs=[smem_spec, whole(cotangent.shape)],
            out_specs=[whole(flat_shape), smem_spec],
            scratch_shapes=[smem(groups + 1)],
        ),
        1000, 2**20,
    )(parents.T, cotangent)
    spread = lax.all_to_all(
        message.reshape(message_shape), "space", split_axis=0, concat_axis=0, tiled=True
    )

    plane = jax.ShapeDtypeStruct((SEND // 2, chans, LANES), BF16)
    up, down, table, ordered = kernel_call(
        table_kernel,
        (plane, plane, ints(4 * count + 1), jax.ShapeDtypeStruct(features.shape, BF16)),
        pl.GridSpec(
            grid=(1,),
            in_specs=[smem_spec] * 5 + [any_spec],
            out_specs=[whole(plane.shape)] * 2 + [smem_spec, any_spec],
            scratch_shapes=[smem(SEND + 1)] * 4
            + [vmem(features.shape, BF16), vmem(features.shape, BF16), vmem((VOX, VOX), BF16),
               pltpu.SemaphoreType.DMA((PARTS,)), pltpu.SemaphoreType.DMA((PARTS,))],
        ),
        1000, 2**20,
    )(position, counts, kids, neighbors.T, parents.T, features)
    below = lax.ppermute(up, "space", [(i, i + 1) for i in range(devices - 1)])
    above = lax.ppermute(down, "space", [(i + 1, i) for i in range(devices - 1)])

    all_kids = spread[:, tiles * ROWS, :groups].astype(jnp.int32).reshape(-1)
    piece_shape = (devices, groups, lane_tiles, ROWS, LANES)
    forward_tiles = kernel_call(
        route_kernel,
        jax.ShapeDtypeStruct(piece_shape, BF16),
        pl.GridSpec(
            grid=(1,),
            in_specs=[smem_spec, whole(message_shape)],
            out_specs=whole(piece_shape),
        ),
        1000, 2**20, SMALL_VMEM_BYTES,
    )(all_kids, spread)
    forward_tiles, above, below = lax.optimization_barrier((forward_tiles, above, below))
    cot_pieces = lax.all_to_all(forward_tiles, "space", split_axis=0, concat_axis=0, tiled=True)

    res_rows = w_restrict.transpose(0, 2, 1).reshape(8 * chans, wide)
    scalars = (table, neighbors.T)
    brick_scratch = vmem((count + SEND + 1, chans, VOX), BF16)
    view_scratch = vmem((8, 7 * chans, VOX), BF16)
    per_group = lambda *shape: pl.BlockSpec((1,) + shape, lambda q: (q,) + (0,) * len(shape))
    piece_spec = pl.BlockSpec((devices, 1, lane_tiles, ROWS, LANES), lambda q: (0, q, 0, 0, 0))
    parts, slope, coarse, pieces = kernel_call(
        functools.partial(forward_kernel, lane_tiles),
        (
            jax.ShapeDtypeStruct((groups, 8 * chans, VOX), BF16),
            jax.ShapeDtypeStruct((groups, 8 * chans, VOX), BF16),
            jax.ShapeDtypeStruct((groups, wide, VOX), BF16),
            jax.ShapeDtypeStruct(piece_shape, BF16),
        ),
        pl.GridSpec(
            grid=(groups + 1,),
            in_specs=[any_spec] * 8,
            out_specs=[
                pl.BlockSpec((1, 8 * chans, VOX), lambda q: (jnp.minimum(q, groups - 1), 0, 0)),
                pl.BlockSpec((1, 8 * chans, VOX), lambda q: (jnp.minimum(q, groups - 1), 0, 0)),
                pl.BlockSpec((1, wide, VOX), lambda q: (jnp.maximum(q - 1, 0), 0, 0)),
                pl.BlockSpec(
                    (devices, 1, lane_tiles, ROWS, LANES),
                    lambda q: (0, jnp.maximum(q - 1, 0), 0, 0, 0),
                ),
            ],
            scratch_shapes=[
                brick_scratch, view_scratch, vmem((VOX, VOX), BF16), vmem(w_conv.shape, BF16),
                vmem(res_rows.shape, BF16), vmem(w_mix.shape, BF16),
                vmem((chans, 8 * chans), BF16), vmem((wide, 8 * chans), BF16),
                vmem((wide, VOX), BF16), smem(4 * count + 1),
                pltpu.SMEM((6, count), jnp.int32), vmem(plane.shape, BF16),
                vmem(plane.shape, BF16), pltpu.SemaphoreType.DMA((7 + PARTS,)),
            ],
        ),
        16 * 10**9, 16 * 2**20,
    )(*scalars, ordered, w_conv, res_rows, w_mix, above, below)
    returned = lax.all_to_all(pieces, "space", split_axis=0, concat_axis=0, tiled=True)

    scale = 1.0 / math.sqrt(devices * slots * VOX)
    used = wide + 8 * chans + 4 * chans
    rows = -(-used // (devices * 8)) * 8
    packed = kernel_call(
        functools.partial(backward_kernel, lane_tiles, scale),
        jax.ShapeDtypeStruct((devices * rows, LANES), BF16),
        pl.GridSpec(
            grid=(groups,),
            in_specs=[smem_spec] * 2 + [any_spec] + [whole(plane.shape)] * 2
            + [piece_spec, per_group(8 * chans, VOX), per_group(8 * chans, VOX),
               per_group(wide, VOX), whole(w_mix.shape), whole(res_rows.shape)],
            out_specs=whole((devices * rows, LANES)),
            scratch_shapes=[
                brick_scratch, view_scratch, vmem((wide, VOX), BF16),
                vmem((8 * chans, VOX), F32), vmem((8 * chans, VOX), BF16), vmem((VOX, VOX), BF16),
                vmem((wide, wide), BF16), vmem((chans, 8 * chans), F32),
                vmem((8 * chans, wide), F32), vmem((wide, wide), F32), pltpu.SemaphoreType.DMA,
            ],
        ),
        16 * 10**9, 16 * 2**20,
    )(*scalars, ordered, above, below, cot_pieces, parts, slope, coarse, w_mix, res_rows)

    shares = lax.all_to_all(
        packed.reshape(devices, rows, LANES), "space", split_axis=0, concat_axis=0, tiled=True
    )
    returned, _ = lax.optimization_barrier((returned, packed))
    flat_shape = (devices * tiles * ROWS, LANES)
    sorted_pieces = kernel_call(
        sort_kernel,
        jax.ShapeDtypeStruct(flat_shape, BF16),
        pl.GridSpec(
            grid=(1,),
            in_specs=[smem_spec, whole(piece_shape)],
            out_specs=whole(flat_shape),
            scratch_shapes=[smem(devices * groups)],
        ),
        1000, 2**20, SMALL_VMEM_BYTES,
    )(all_kids, returned)
    sorted_pieces, shares = lax.optimization_barrier((sorted_pieces, shares))
    finished = lax.all_to_all(
        sorted_pieces.reshape(devices, tiles * ROWS, LANES),
        "space", split_axis=0, concat_axis=0, tiled=True,
    )
    summed = jnp.sum(shares.astype(F32), axis=0).astype(BF16)
    sums = gather_by_digits(summed, devices).reshape(devices * rows, LANES)

    coarse_out, grad_conv, grad_res, grad_mix = kernel_call(
        functools.partial(unpack_kernel, lane_tiles),
        (
            jax.ShapeDtypeStruct((slots, wide, VOX), BF16),
            jax.ShapeDtypeStruct((7, chans, chans), F32),
            jax.ShapeDtypeStruct((8, chans, wide), F32),
            jax.ShapeDtypeStruct((wide, wide), F32),
        ),
        pl.GridSpec(
            grid=(1,),
            in_specs=[smem_spec, whole(flat_shape), whole((devices * rows, LANES))],
            out_specs=[whole((slots, wide, VOX)), whole((7, chans, chans)),
                       whole((8, chans, wide)), whole((wide, wide))],
            scratch_shapes=[vmem((devices * rows, LANES), F32)] * 2,
        ),
        1000, 2 * 2**20, SMALL_VMEM_BYTES,
    )(position, finished.reshape(flat_shape), sums)
    return coarse_out, grad_conv, grad_res.transpose(0, 2, 1), grad_mix


def solution(mesh):
    return jax.shard_map(
        body,
        mesh=mesh,
        in_specs=(
            P(("groups", "space"), None, None),
            P(("groups", "space")),
            P(("groups", "space"), None),
            P(("groups", "space"), None),
            P(),
            P(),
            P(),
            P(("groups", "space"), None, None),
        ),
        out_specs=(
            P(("groups", "space"), None, None),
            P("groups", None, None),
            P("groups", None, None),
            P("groups", None),
        ),
        check_vma=False,
    )
```

```python
import functools
import math

import jax
import jax.numpy as jnp
from jax import lax
from jax.experimental import pallas as pl
from jax.experimental.pallas import tpu as pltpu
from jax.sharding import PartitionSpec as P

EDGE = 8
HALF = EDGE // 2
VOX = EDGE**3
LANES = 128
ROWS = 16
LABEL_ROWS = 8
SEND = 8
PARTS = 4
BF16 = jnp.bfloat16
F32 = jnp.float32
VMEM_BYTES = 60 * 1024 * 1024
SMALL_VMEM_BYTES = 16 * 1024 * 1024


def bits_of(value):
    return [(value >> (8 - k)) & 1 for k in range(9)]


def join_bits(bits):
    value = bits[0]
    for bit in bits[1:]:
        value = value * 2 + bit
    return value


def split_voxel(column):
    ta, tb, tc, a1, a0, b1, b0, c1, c0 = bits_of(column)
    return join_bits([a1, a0, ta, b1, b0, tb, c1, c0, tc])


def octant_voxel(column):
    oa, ob, oc, a1, a0, b1, b0, c1, c0 = bits_of(column)
    return join_bits([oa, a1, a0, ob, b1, b0, oc, c1, c0])


def picker(voxel_of, shape=(VOX, VOX), start=(0, 0), flip=False):
    row = lax.broadcasted_iota(jnp.int32, shape, 0) + start[0]
    column = lax.broadcasted_iota(jnp.int32, shape, 1) + start[1]
    return (column == voxel_of(row) if flip else row == voxel_of(column)).astype(BF16)


def digits(devices):
    found, stride = [(2, 1)], devices
    while stride > 2:
        radix = 4 if stride % 8 == 0 else 2
        stride //= radix
        found.append((radix, stride))
    return found


def gather_by_digits(own, devices):
    held = own[None]
    for radix, stride in digits(devices):
        came = [held]
        for step in range(1, radix):
            pairs = []
            for i in range(devices):
                digit = i // stride % radix
                pairs.append((i, i + ((digit + step) % radix - digit) * stride))
            came.append(lax.ppermute(held, "space", pairs))
        held = jnp.concatenate(came, axis=0)
    return held


def dot(a, b):
    return jnp.dot(a, b, preferred_element_type=F32)


def dot_nt(a, b):
    return lax.dot_general(a, b, (((1,), (1,)), ((), ())), preferred_element_type=F32)


def pack_kernel(lane_tiles, parents, cot, msg, kids_out, kids):
    slots = cot.shape[0]
    body_rows = slots * lane_tiles * ROWS
    rows = body_rows + LABEL_ROWS
    devices = msg.shape[0] // rows

    def find(g, found):
        kids[found] = parents[0, g]
        return found + (parents[1, g] == 0).astype(jnp.int32)

    lax.fori_loop(0, parents.shape[1], find, jnp.int32(0), unroll=4)
    lane = lax.broadcasted_iota(jnp.int32, (LABEL_ROWS, LANES), 1)
    label = jnp.zeros((LABEL_ROWS, LANES), jnp.int32)
    for q in range(kids_out.shape[0]):
        kids_out[q] = kids[q]
        label = jnp.where(lane == q, kids[q], label)
    label = label.astype(F32).astype(BF16)
    for j in range(devices):
        msg[j * rows + body_rows : (j + 1) * rows] = label
    per_row = VOX // (LANES * lane_tiles)
    for j in range(devices):
        chan, part = j // per_row, j % per_row
        for q in range(slots):
            for lt in range(lane_tiles):
                lane = (part * lane_tiles + lt) * LANES
                row = j * rows + (q * lane_tiles + lt) * ROWS
                msg[row : row + ROWS] = cot[
                    q, chan * ROWS : (chan + 1) * ROWS, lane : lane + LANES
                ]


def table_kernel(
    place, counts, kids, neighbors, parents, feat, up, down, table, ordered,
    up_idx, up_far, down_idx, down_far, bricks, done, split, in_sem, out_sem,
):
    count, chans = feat.shape[:2]
    part = count // PARTS
    fetches = [
        pltpu.make_async_copy(
            feat.at[pl.ds(k * part, part)], bricks.at[pl.ds(k * part, part)], in_sem.at[k]
        )
        for k in range(PARTS)
    ]
    for fetch in fetches:
        fetch.start()
    base = place[0] * count
    table[4 * count] = place[0]
    for r in range(SEND + 1):
        up_idx[r] = 0
        down_idx[r] = 0
        up_far[r] = 2 * count
        down_far[r] = 2 * count
    split[...] = picker(split_voxel)

    def scan(g, found):
        n_up, n_down = found
        near_up, near_down = neighbors[0, g], neighbors[1, g]
        far_up, far_down = near_up - base - count, near_down - base + count
        goes_up = (near_up >= 0) & (far_up >= 0)
        goes_down = (near_down >= 0) & (far_down < count)
        up_idx[n_up] = g
        up_far[n_up] = jnp.where(goes_up, far_up, 2 * count)
        down_idx[n_down] = g
        down_far[n_down] = jnp.where(goes_down, far_down, 2 * count)
        q = jnp.int32(0)
        for k in range(1, kids.shape[0]):
            q += jnp.where(kids[k] == parents[0, g], k, 0)
        number = q * 8 + parents[1, g]
        table[number] = g
        table[count + number] = jnp.where(g < counts[0], g, count + SEND)
        return n_up + goes_up.astype(jnp.int32), n_down + goes_down.astype(jnp.int32)

    lax.fori_loop(0, count, scan, (jnp.int32(0), jnp.int32(0)), unroll=4)

    def rank(r, carry):
        for start, far, idx in ((2 * count, up_far, up_idx), (3 * count, down_far, down_idx)):
            earlier = jnp.int32(0)
            for other in range(SEND):
                earlier += (far[other] < far[r]).astype(jnp.int32)

            @pl.when(far[r] < count)
            def _():
                table[start + idx[r]] = count + earlier

        return carry

    lax.fori_loop(0, SEND, rank, jnp.int32(0))
    sends = []
    for k in range(PARTS):
        fetches[k].wait()
        rows = bricks[k * part : (k + 1) * part].reshape(part * chans, VOX)
        done[k * part : (k + 1) * part] = (
            dot(rows, split[...]).astype(BF16).reshape(part, chans, VOX)
        )
        sends.append(
            pltpu.make_async_copy(
                done.at[pl.ds(k * part, part)], ordered.at[pl.ds(k * part, part)], out_sem.at[k]
            )
        )
        sends[-1].start()
    low = low_lanes(chans)
    for r in range(SEND // 2):
        other = r + SEND // 2
        top = slice(VOX - LANES, VOX)
        up[r] = jnp.where(
            low,
            pltpu.roll(bricks[up_idx[r], :, top], LANES // 2, 1),
            bricks[up_idx[other], :, top],
        )
        down[r] = jnp.where(
            low,
            bricks[down_idx[r], :, :LANES],
            pltpu.roll(bricks[down_idx[other], :, :LANES], LANES // 2, 1),
        )
    for send in sends:
        send.wait()


def route_kernel(kids, msg, pieces):
    devices, groups, lane_tiles = pieces.shape[:3]
    slots = groups
    for s in range(devices):
        for q in range(groups):
            kid = kids[s * groups + q]
            owner, slot = kid // slots, kid % slots
            for lt in range(lane_tiles):
                row = pl.multiple_of((slot * lane_tiles + lt) * ROWS, ROWS)
                pieces[s, q, lt] = msg[owner, pl.ds(row, ROWS), :]


def place_arrivals(above, below, bricks, count):
    chans = bricks.shape[1]
    half = VOX // 2
    side = LANES // 2
    shape = (LANES, half)
    pairs = SEND // 2
    for k, shift in ((0, 0), (pairs, -side)):
        slots = slice(count + k, count + k + pairs)
        first = dot(
            above[...].reshape(pairs * chans, LANES), picker(split_voxel, shape, (shift, 0))
        )
        last = dot(
            below[...].reshape(pairs * chans, LANES),
            picker(split_voxel, shape, (VOX - side + shift, half)),
        )
        bricks[slots, :, :half] = first.astype(BF16).reshape(pairs, chans, half)
        bricks[slots, :, half:] = last.astype(BF16).reshape(pairs, chans, half)
    bricks[count + SEND] = jnp.zeros(bricks.shape[1:], BF16)


def sources(table, neighbors, number):
    count = neighbors.shape[1]
    g = table[number]
    found = []
    for d in range(6):
        near = neighbors[d, g]
        local = near - table[4 * count] * count
        if d == 0:
            local = jnp.where(local >= count, table[2 * count + g], local)
        if d == 1:
            local = jnp.where(local < 0, table[3 * count + g], local)
        found.append(jnp.where(near >= 0, local, count + SEND))
    found.append(table[count + number])
    return found


def shift_into(slots, bricks, views):
    chans = bricks.shape[1]
    tiles = VOX // LANES
    lane = lax.broadcasted_iota(jnp.int32, (chans, LANES), 1)
    low = lane < LANES // 2
    a = (lane // 16) % HALF
    b = (lane // 4) % HALF
    c = lane % HALF

    def tile(slot, t):
        return bricks[slot, :, t * LANES : (t + 1) * LANES]

    def turn(value, by):
        return pltpu.roll(value, by % LANES, 1)

    x = [tile(slots[6], t) for t in range(tiles)]
    for t in range(tiles):
        lanes = slice(t * LANES, (t + 1) * LANES)
        if t < 2:
            plus_a = x[t + 2]
            minus_a = jnp.where(a > 0, turn(x[t + 2], 16), turn(tile(slots[1], t + 2), -48))
        else:
            plus_a = jnp.where(a < HALF - 1, turn(x[t - 2], -16), turn(tile(slots[0], t - 2), 48))
            minus_a = x[t - 2]
        if t % 2 == 0:
            plus_b = x[t + 1]
            minus_b = jnp.where(b > 0, turn(x[t + 1], 4), turn(tile(slots[3], t + 1), -12))
        else:
            plus_b = jnp.where(b < HALF - 1, turn(x[t - 1], -4), turn(tile(slots[2], t - 1), 12))
            minus_b = x[t - 1]
        swapped = turn(x[t], 64)
        plus_c = jnp.where(c < HALF - 1, turn(x[t], 63), turn(tile(slots[4], t), 67))
        minus_c = jnp.where(c > 0, turn(x[t], -63), turn(tile(slots[5], t), -67))
        out = [plus_a, minus_a, plus_b, minus_b, jnp.where(low, swapped, plus_c),
               jnp.where(low, minus_c, swapped), x[t]]
        for d in range(7):
            views[d * chans : (d + 1) * chans, lanes] = out[d]


def low_lanes(rows):
    return lax.broadcasted_iota(jnp.int32, (rows, LANES), 1) < LANES // 2


def forward_kernel(
    lane_tiles, table_hbm, neighbors_hbm, feat, w_conv_hbm, w_res_hbm, w_mix_hbm,
    above_hbm, below_hbm,
    parts_out, slope_out, coarse_out, piece_out,
    bricks, views, place, w_conv, w_res, w_mix, conv_cat, res_cat, octants,
    table, neighbors, above, below, sem,
):
    q = pl.program_id(0)
    groups = pl.num_programs(0) - 1
    count, chans = feat.shape[:2]
    part = count // PARTS

    @pl.when(q == 0)
    def _():
        copies = [
            pltpu.make_async_copy(source, target, sem.at[k])
            for k, (source, target) in enumerate((
                (above_hbm, above), (below_hbm, below), (w_conv_hbm, w_conv),
                (w_res_hbm, w_res), (w_mix_hbm, w_mix), (table_hbm, table),
                (neighbors_hbm, neighbors),
                *(
                    (feat.at[pl.ds(k * part, part)], bricks.at[pl.ds(k * part, part)])
                    for k in range(PARTS)
                ),
            ))
        ]
        for copy in copies:
            copy.start()
        place[...] = picker(octant_voxel, flip=True)
        for copy in copies[:-PARTS]:
            copy.wait()
        place_arrivals(above, below, bricks, count)
        for d in range(7):
            conv_cat[:, d * chans : (d + 1) * chans] = w_conv[d]
        res_cat[...] = w_res[...].T
        for copy in copies[-PARTS:]:
            copy.wait()

    low_half = low_lanes(chans)

    def finish():
        coarse = dot(octants[...], place[...]).astype(BF16)
        coarse_out[0] = coarse
        mixed = dot(w_mix[...], coarse).astype(BF16)
        per_row = VOX // (LANES * lane_tiles)
        for j in range(piece_out.shape[0]):
            chan, part = j // per_row, j % per_row
            for lt in range(lane_tiles):
                lane = (part * lane_tiles + lt) * LANES
                piece_out[j, 0, lt] = mixed[chan * ROWS : (chan + 1) * ROWS, lane : lane + LANES]

    def restrict(first):
        acts = []
        for k in range(first, first + 4):
            shift_into(sources(table, neighbors, q * 8 + k), bricks, views.at[k])
            hidden = dot(conv_cat[:, : 7 * chans], views[k])
            sig = 1.0 / (1.0 + jnp.exp(-hidden))
            act = hidden * sig
            slope_out[0, k * chans : (k + 1) * chans, :] = (sig + act * (1.0 - sig)).astype(BF16)
            acts.append(act.astype(BF16))
        for k in range(0, 4, 2):
            lanes = slice((first + k) * (LANES // 2), (first + k + 2) * (LANES // 2))
            for t in range(4):
                one = acts[k][:, t * LANES : (t + 1) * LANES]
                two = acts[k + 1][:, t * LANES : (t + 1) * LANES]
                parts_out[0, 2 * t * chans : (2 * t + 1) * chans, lanes] = jnp.where(
                    low_half, one, pltpu.roll(two, LANES // 2, 1)
                )
                parts_out[0, (2 * t + 1) * chans : (2 * t + 2) * chans, lanes] = jnp.where(
                    low_half, pltpu.roll(one, LANES // 2, 1), two
                )
        lanes = slice(first * (LANES // 2), (first + 4) * (LANES // 2))
        return dot(res_cat[...], parts_out[0, :, lanes]).astype(BF16)

    @pl.when(q < groups)
    def _():
        finish()
        halves = [restrict(0), restrict(4)]
        octants[...] = jnp.concatenate(halves, axis=1)

    @pl.when(q == groups)
    def _():
        finish()


def backward_kernel(
    lane_tiles, scale, table, neighbors, feat, above, below, pieces, parts, slope, coarse, w_mix, w_res, packed,
    bricks, views, cot, grad_parts, grad_rows, unplace, mix_t, conv_sum, res_sum, mix_sum, sem,
):
    q = pl.program_id(0)
    count, chans = feat.shape[:2]
    wide = coarse.shape[1]
    fetch = pltpu.make_async_copy(feat, bricks.at[pl.ds(0, count)], sem)

    @pl.when(q == 0)
    def _():
        fetch.start()
        place_arrivals(above, below, bricks, count)
        unplace[...] = picker(octant_voxel)
        mix_t[...] = w_mix[...].T
        conv_sum[...] = jnp.zeros_like(conv_sum)
        res_sum[...] = jnp.zeros_like(res_sum)
        mix_sum[...] = jnp.zeros_like(mix_sum)
        fetch.wait()

    per_row = VOX // (LANES * lane_tiles)
    for j in range(pieces.shape[0]):
        chan, part = j // per_row, j % per_row
        for lt in range(lane_tiles):
            lane = (part * lane_tiles + lt) * LANES
            cot[chan * ROWS : (chan + 1) * ROWS, lane : lane + LANES] = pieces[j, 0, lt]
    cots = cot[...]
    grad_coarse = (scale * dot(mix_t[...], cots)).astype(BF16)
    grad_fine = dot(grad_coarse, unplace[...]).astype(BF16)
    mix_sum[...] += dot_nt(cots, coarse[0])
    res_sum[...] += dot_nt(parts[0], grad_fine)
    grad_parts[...] = dot(w_res[...], grad_fine)
    low_half = low_lanes(chans)
    for r in range(4):
        for t in range(4):
            cols = slice(r * LANES, (r + 1) * LANES)
            lanes = slice(t * LANES, (t + 1) * LANES)
            one = grad_parts[2 * t * chans : (2 * t + 1) * chans, cols]
            two = grad_parts[(2 * t + 1) * chans : (2 * t + 2) * chans, cols]
            first = slice(2 * r * chans, (2 * r + 1) * chans)
            second = slice((2 * r + 1) * chans, (2 * r + 2) * chans)
            grad_rows[first, lanes] = (
                jnp.where(low_half, one, pltpu.roll(two, LANES // 2, 1))
                * slope[0, first, lanes].astype(F32)
            ).astype(BF16)
            grad_rows[second, lanes] = (
                jnp.where(low_half, pltpu.roll(one, LANES // 2, 1), two)
                * slope[0, second, lanes].astype(F32)
            ).astype(BF16)

    total = None
    for k in range(8):
        shift_into(sources(table, neighbors, q * 8 + k), bricks, views.at[k])
        term = dot_nt(grad_rows[k * chans : (k + 1) * chans, :], views[k])
        total = term if total is None else total + term
    conv_sum[:, : 7 * chans] += total

    @pl.when(q == pl.num_programs(0) - 1)
    def _():
        packed[0:wide] = (scale * mix_sum[...]).astype(BF16)
        at = wide
        packed[at : at + 8 * chans] = res_sum[...].astype(BF16)
        at += 8 * chans
        for t in range(4):
            packed[at : at + chans] = conv_sum[:, t * LANES : (t + 1) * LANES].astype(BF16)
            at += chans
        if at < packed.shape[0]:
            packed[at:] = jnp.zeros((packed.shape[0] - at, LANES), BF16)


def sort_kernel(kids, pieces, msg, wanted):
    devices, groups, lane_tiles = pieces.shape[:3]
    slots = groups
    rows = slots * lane_tiles * ROWS

    def invert(n, carry):
        wanted[kids[n]] = n
        return carry

    lax.fori_loop(0, devices * groups, invert, jnp.int32(0), unroll=4)
    for j in range(devices):
        for slot in range(slots):
            n = wanted[j * slots + slot]
            for lt in range(lane_tiles):
                row = j * rows + (slot * lane_tiles + lt) * ROWS
                msg[row : row + ROWS] = pieces[n // groups, n % groups, lt]


def unpack_kernel(lane_tiles, place, msg, sums, coarse_out, conv, res, mix, packed, wide_sums):
    slots = coarse_out.shape[0]
    wide = mix.shape[0]
    chans = conv.shape[1]
    half = LANES // 2
    per_row = VOX // (LANES * lane_tiles)
    devices = 8 * per_row
    rows = msg.shape[0] // devices
    share = sums.shape[0] // devices
    wide_sums[...] = sums[...].astype(F32)
    for p in range(devices):
        source, behind = jnp.int32(0), p
        for radix, stride in digits(devices):
            digit = place[0] // stride % radix
            source += (digit + radix - behind % radix) % radix * stride
            behind //= radix
        at = pl.multiple_of(source * share, 8)
        packed[pl.ds(at, share), :] = wide_sums[p * share : (p + 1) * share]
    mix[...] = packed[0:wide]
    at = wide
    for t in range(8):
        res[t] = packed[at : at + chans]
        at += chans
    for t in range(4):
        block = packed[at : at + chans]
        conv[2 * t] = block[:, :half]
        if 2 * t + 1 < 7:
            conv[2 * t + 1] = block[:, half:]
        at += chans
    for j in range(devices):
        chan, part = j // per_row, j % per_row
        for q in range(slots):
            for lt in range(lane_tiles):
                row = j * rows + (q * lane_tiles + lt) * ROWS
                lane = (part * lane_tiles + lt) * LANES
                coarse_out[q, chan * ROWS : (chan + 1) * ROWS, lane : lane + LANES] = msg[
                    row : row + ROWS
                ]


def kernel_call(kernel, out_shape, grid_spec, flops, moved, vmem=VMEM_BYTES):
    return pl.pallas_call(
        kernel,
        out_shape=out_shape,
        grid_spec=grid_spec,
        compiler_params=pltpu.CompilerParams(vmem_limit_bytes=vmem),
        cost_estimate=pl.CostEstimate(flops=flops, bytes_accessed=moved, transcendentals=0),
    )


def body(features, counts, neighbors, parents, w_conv, w_restrict, w_mix, cotangent):
    devices = lax.axis_size("space")
    position = lax.axis_index("space").astype(jnp.int32).reshape(1)
    slots, wide = cotangent.shape[:2]
    count, chans = features.shape[:2]
    lane_tiles = VOX * 8 // devices // LANES
    tiles = slots * lane_tiles
    groups = count // 8
    whole = lambda shape: pl.BlockSpec(shape, lambda *_: (0,) * len(shape))
    any_spec = pl.BlockSpec(memory_space=pl.ANY)
    smem_spec = pl.BlockSpec(memory_space=pltpu.SMEM)
    smem = lambda size: pltpu.SMEM((size,), jnp.int32)
    vmem = pltpu.VMEM
    ints = lambda size: jax.ShapeDtypeStruct((size,), jnp.int32)

    message_shape = (devices, tiles * ROWS + LABEL_ROWS, LANES)
    flat_shape = (message_shape[0] * message_shape[1], LANES)
    message, kids = kernel_call(
        functools.partial(pack_kernel, lane_tiles),
        (jax.ShapeDtypeStruct(flat_shape, BF16), ints(groups)),
        pl.GridSpec(
            grid=(1,),
            in_specs=[smem_spec, whole(cotangent.shape)],
            out_specs=[whole(flat_shape), smem_spec],
            scratch_shapes=[smem(groups + 1)],
        ),
        1000, 2**20,
    )(parents.T, cotangent)
    spread = lax.all_to_all(
        message.reshape(message_shape), "space", split_axis=0, concat_axis=0, tiled=True
    )

    plane = jax.ShapeDtypeStruct((SEND // 2, chans, LANES), BF16)
    up, down, table, ordered = kernel_call(
        table_kernel,
        (plane, plane, ints(4 * count + 1), jax.ShapeDtypeStruct(features.shape, BF16)),
        pl.GridSpec(
            grid=(1,),
            in_specs=[smem_spec] * 5 + [any_spec],
            out_specs=[whole(plane.shape)] * 2 + [smem_spec, any_spec],
            scratch_shapes=[smem(SEND + 1)] * 4
            + [vmem(features.shape, BF16), vmem(features.shape, BF16), vmem((VOX, VOX), BF16),
               pltpu.SemaphoreType.DMA((PARTS,)), pltpu.SemaphoreType.DMA((PARTS,))],
        ),
        1000, 2**20,
    )(position, counts, kids, neighbors.T, parents.T, features)
    below = lax.ppermute(up, "space", [(i, i + 1) for i in range(devices - 1)])
    above = lax.ppermute(down, "space", [(i + 1, i) for i in range(devices - 1)])

    all_kids = spread[:, tiles * ROWS, :groups].astype(jnp.int32).reshape(-1)
    piece_shape = (devices, groups, lane_tiles, ROWS, LANES)
    forward_tiles = kernel_call(
        route_kernel,
        jax.ShapeDtypeStruct(piece_shape, BF16),
        pl.GridSpec(
            grid=(1,),
            in_specs=[smem_spec, whole(message_shape)],
            out_specs=whole(piece_shape),
        ),
        1000, 2**20, SMALL_VMEM_BYTES,
    )(all_kids, spread)
    forward_tiles, above, below = lax.optimization_barrier((forward_tiles, above, below))
    cot_pieces = lax.all_to_all(forward_tiles, "space", split_axis=0, concat_axis=0, tiled=True)

    res_rows = w_restrict.transpose(0, 2, 1).reshape(8 * chans, wide)
    scalars = (table, neighbors.T)
    brick_scratch = vmem((count + SEND + 1, chans, VOX), BF16)
    view_scratch = vmem((8, 7 * chans, VOX), BF16)
    per_group = lambda *shape: pl.BlockSpec((1,) + shape, lambda q: (q,) + (0,) * len(shape))
    piece_spec = pl.BlockSpec((devices, 1, lane_tiles, ROWS, LANES), lambda q: (0, q, 0, 0, 0))
    parts, slope, coarse, pieces = kernel_call(
        functools.partial(forward_kernel, lane_tiles),
        (
            jax.ShapeDtypeStruct((groups, 8 * chans, VOX), BF16),
            jax.ShapeDtypeStruct((groups, 8 * chans, VOX), BF16),
            jax.ShapeDtypeStruct((groups, wide, VOX), BF16),
            jax.ShapeDtypeStruct(piece_shape, BF16),
        ),
        pl.GridSpec(
            grid=(groups + 1,),
            in_specs=[any_spec] * 8,
            out_specs=[
                pl.BlockSpec((1, 8 * chans, VOX), lambda q: (jnp.minimum(q, groups - 1), 0, 0)),
                pl.BlockSpec((1, 8 * chans, VOX), lambda q: (jnp.minimum(q, groups - 1), 0, 0)),
                pl.BlockSpec((1, wide, VOX), lambda q: (jnp.maximum(q - 1, 0), 0, 0)),
                pl.BlockSpec(
                    (devices, 1, lane_tiles, ROWS, LANES),
                    lambda q: (0, jnp.maximum(q - 1, 0), 0, 0, 0),
                ),
            ],
            scratch_shapes=[
                brick_scratch, view_scratch, vmem((VOX, VOX), BF16), vmem(w_conv.shape, BF16),
                vmem(res_rows.shape, BF16), vmem(w_mix.shape, BF16),
                vmem((chans, 8 * chans), BF16), vmem((wide, 8 * chans), BF16),
                vmem((wide, VOX), BF16), smem(4 * count + 1),
                pltpu.SMEM((6, count), jnp.int32), vmem(plane.shape, BF16),
                vmem(plane.shape, BF16), pltpu.SemaphoreType.DMA((7 + PARTS,)),
            ],
        ),
        16 * 10**9, 16 * 2**20,
    )(*scalars, ordered, w_conv, res_rows, w_mix, above, below)
    returned = lax.all_to_all(pieces, "space", split_axis=0, concat_axis=0, tiled=True)

    scale = 1.0 / math.sqrt(devices * slots * VOX)
    used = wide + 8 * chans + 4 * chans
    rows = -(-used // (devices * 8)) * 8
    packed = kernel_call(
        functools.partial(backward_kernel, lane_tiles, scale),
        jax.ShapeDtypeStruct((devices * rows, LANES), BF16),
        pl.GridSpec(
            grid=(groups,),
            in_specs=[smem_spec] * 2 + [any_spec] + [whole(plane.shape)] * 2
            + [piece_spec, per_group(8 * chans, VOX), per_group(8 * chans, VOX),
               per_group(wide, VOX), whole(w_mix.shape), whole(res_rows.shape)],
            out_specs=whole((devices * rows, LANES)),
            scratch_shapes=[
                brick_scratch, view_scratch, vmem((wide, VOX), BF16),
                vmem((8 * chans, VOX), F32), vmem((8 * chans, VOX), BF16), vmem((VOX, VOX), BF16),
                vmem((wide, wide), BF16), vmem((chans, 8 * chans), F32),
                vmem((8 * chans, wide), F32), vmem((wide, wide), F32), pltpu.SemaphoreType.DMA,
            ],
        ),
        16 * 10**9, 16 * 2**20,
    )(*scalars, ordered, above, below, cot_pieces, parts, slope, coarse, w_mix, res_rows)

    shares = lax.all_to_all(
        packed.reshape(devices, rows, LANES), "space", split_axis=0, concat_axis=0, tiled=True
    )
    returned, _ = lax.optimization_barrier((returned, packed))
    flat_shape = (devices * tiles * ROWS, LANES)
    sorted_pieces = kernel_call(
        sort_kernel,
        jax.ShapeDtypeStruct(flat_shape, BF16),
        pl.GridSpec(
            grid=(1,),
            in_specs=[smem_spec, whole(piece_shape)],
            out_specs=whole(flat_shape),
            scratch_shapes=[smem(devices * groups)],
        ),
        1000, 2**20, SMALL_VMEM_BYTES,
    )(all_kids, returned)
    sorted_pieces, shares = lax.optimization_barrier((sorted_pieces, shares))
    finished = lax.all_to_all(
        sorted_pieces.reshape(devices, tiles * ROWS, LANES),
        "space", split_axis=0, concat_axis=0, tiled=True,
    )
    summed = jnp.sum(shares.astype(F32), axis=0).astype(BF16)
    sums = gather_by_digits(summed, devices).reshape(devices * rows, LANES)

    coarse_out, grad_conv, grad_res, grad_mix = kernel_call(
        functools.partial(unpack_kernel, lane_tiles),
        (
            jax.ShapeDtypeStruct((slots, wide, VOX), BF16),
            jax.ShapeDtypeStruct((7, chans, chans), F32),
            jax.ShapeDtypeStruct((8, chans, wide), F32),
            jax.ShapeDtypeStruct((wide, wide), F32),
        ),
        pl.GridSpec(
            grid=(1,),
            in_specs=[smem_spec, whole(flat_shape), whole((devices * rows, LANES))],
            out_specs=[whole((slots, wide, VOX)), whole((7, chans, chans)),
                       whole((8, chans, wide)), whole((wide, wide))],
            scratch_shapes=[vmem((devices * rows, LANES), F32)] * 2,
        ),
        1000, 2 * 2**20, SMALL_VMEM_BYTES,
    )(position, finished.reshape(flat_shape), sums)
    return coarse_out, grad_conv, grad_res.transpose(0, 2, 1), grad_mix


def solution(mesh):
    return jax.shard_map(
        body,
        mesh=mesh,
        in_specs=(
            P(("groups", "space"), None, None),
            P(("groups", "space")),
            P(("groups", "space"), None),
            P(("groups", "space"), None),
            P(),
            P(),
            P(),
            P(("groups", "space"), None, None),
        ),
        out_specs=(
            P(("groups", "space"), None, None),
            P("groups", None, None),
            P("groups", None, None),
            P("groups", None),
        ),
        check_vma=False,
    )
```

```python
import functools
import math

import jax
import jax.numpy as jnp
from jax import lax
from jax.experimental import pallas as pl
from jax.experimental.pallas import tpu as pltpu
from jax.sharding import PartitionSpec as P

EDGE = 8
HALF = EDGE // 2
VOX = EDGE**3
LANES = 128
ROWS = 16
LABEL_ROWS = 8
SEND = 8
PARTS = 4
BF16 = jnp.bfloat16
F32 = jnp.float32
VMEM_BYTES = 60 * 1024 * 1024
SMALL_VMEM_BYTES = 16 * 1024 * 1024


def bits_of(value):
    return [(value >> (8 - k)) & 1 for k in range(9)]


def join_bits(bits):
    value = bits[0]
    for bit in bits[1:]:
        value = value * 2 + bit
    return value


def split_voxel(column):
    ta, tb, tc, a1, a0, b1, b0, c1, c0 = bits_of(column)
    return join_bits([a1, a0, ta, b1, b0, tb, c1, c0, tc])


def octant_voxel(column):
    oa, ob, oc, a1, a0, b1, b0, c1, c0 = bits_of(column)
    return join_bits([oa, a1, a0, ob, b1, b0, oc, c1, c0])


def picker(voxel_of, shape=(VOX, VOX), start=(0, 0), flip=False):
    row = lax.broadcasted_iota(jnp.int32, shape, 0) + start[0]
    column = lax.broadcasted_iota(jnp.int32, shape, 1) + start[1]
    return (column == voxel_of(row) if flip else row == voxel_of(column)).astype(BF16)


def digits(devices):
    found, stride = [], devices
    while stride > 1:
        stride //= 2
        found.append((2, stride))
    return found


def gather_by_digits(own, devices):
    held = own[None]
    for radix, stride in digits(devices):
        came = [held]
        for step in range(1, radix):
            pairs = []
            for i in range(devices):
                digit = i // stride % radix
                pairs.append((i, i + ((digit + step) % radix - digit) * stride))
            came.append(lax.ppermute(held, "space", pairs))
        held = jnp.concatenate(came, axis=0)
    return held


def dot(a, b):
    return jnp.dot(a, b, preferred_element_type=F32)


def dot_nt(a, b):
    return lax.dot_general(a, b, (((1,), (1,)), ((), ())), preferred_element_type=F32)


def pack_kernel(lane_tiles, parents, cot, msg, kids_out, kids):
    slots = cot.shape[0]
    body_rows = slots * lane_tiles * ROWS
    rows = body_rows + LABEL_ROWS
    devices = msg.shape[0] // rows

    def find(g, found):
        kids[found] = parents[0, g]
        return found + (parents[1, g] == 0).astype(jnp.int32)

    lax.fori_loop(0, parents.shape[1], find, jnp.int32(0), unroll=4)
    lane = lax.broadcasted_iota(jnp.int32, (LABEL_ROWS, LANES), 1)
    label = jnp.zeros((LABEL_ROWS, LANES), jnp.int32)
    for q in range(kids_out.shape[0]):
        kids_out[q] = kids[q]
        label = jnp.where(lane == q, kids[q], label)
    label = label.astype(F32).astype(BF16)
    for j in range(devices):
        msg[j * rows + body_rows : (j + 1) * rows] = label
    per_row = VOX // (LANES * lane_tiles)
    for j in range(devices):
        chan, part = j // per_row, j % per_row
        for q in range(slots):
            for lt in range(lane_tiles):
                lane = (part * lane_tiles + lt) * LANES
                row = j * rows + (q * lane_tiles + lt) * ROWS
                msg[row : row + ROWS] = cot[
                    q, chan * ROWS : (chan + 1) * ROWS, lane : lane + LANES
                ]


def table_kernel(
    place, counts, kids, neighbors, parents, feat, up, down, table, ordered,
    up_idx, up_far, down_idx, down_far, bricks, done, split, in_sem, out_sem,
):
    count, chans = feat.shape[:2]
    part = count // PARTS
    fetches = [
        pltpu.make_async_copy(
            feat.at[pl.ds(k * part, part)], bricks.at[pl.ds(k * part, part)], in_sem.at[k]
        )
        for k in range(PARTS)
    ]
    for fetch in fetches:
        fetch.start()
    base = place[0] * count
    table[4 * count] = place[0]
    for r in range(SEND + 1):
        up_idx[r] = 0
        down_idx[r] = 0
        up_far[r] = 2 * count
        down_far[r] = 2 * count
    split[...] = picker(split_voxel)

    def scan(g, found):
        n_up, n_down = found
        near_up, near_down = neighbors[0, g], neighbors[1, g]
        far_up, far_down = near_up - base - count, near_down - base + count
        goes_up = (near_up >= 0) & (far_up >= 0)
        goes_down = (near_down >= 0) & (far_down < count)
        up_idx[n_up] = g
        up_far[n_up] = jnp.where(goes_up, far_up, 2 * count)
        down_idx[n_down] = g
        down_far[n_down] = jnp.where(goes_down, far_down, 2 * count)
        q = jnp.int32(0)
        for k in range(1, kids.shape[0]):
            q += jnp.where(kids[k] == parents[0, g], k, 0)
        number = q * 8 + parents[1, g]
        table[number] = g
        table[count + number] = jnp.where(g < counts[0], g, count + SEND)
        return n_up + goes_up.astype(jnp.int32), n_down + goes_down.astype(jnp.int32)

    lax.fori_loop(0, count, scan, (jnp.int32(0), jnp.int32(0)), unroll=4)

    def rank(r, carry):
        for start, far, idx in ((2 * count, up_far, up_idx), (3 * count, down_far, down_idx)):
            earlier = jnp.int32(0)
            for other in range(SEND):
                earlier += (far[other] < far[r]).astype(jnp.int32)

            @pl.when(far[r] < count)
            def _():
                table[start + idx[r]] = count + earlier

        return carry

    lax.fori_loop(0, SEND, rank, jnp.int32(0))
    sends = []
    for k in range(PARTS):
        fetches[k].wait()
        rows = bricks[k * part : (k + 1) * part].reshape(part * chans, VOX)
        done[k * part : (k + 1) * part] = (
            dot(rows, split[...]).astype(BF16).reshape(part, chans, VOX)
        )
        sends.append(
            pltpu.make_async_copy(
                done.at[pl.ds(k * part, part)], ordered.at[pl.ds(k * part, part)], out_sem.at[k]
            )
        )
        sends[-1].start()
    low = low_lanes(chans)
    for r in range(SEND // 2):
        other = r + SEND // 2
        top = slice(VOX - LANES, VOX)
        up[r] = jnp.where(
            low,
            pltpu.roll(bricks[up_idx[r], :, top], LANES // 2, 1),
            bricks[up_idx[other], :, top],
        )
        down[r] = jnp.where(
            low,
            bricks[down_idx[r], :, :LANES],
            pltpu.roll(bricks[down_idx[other], :, :LANES], LANES // 2, 1),
        )
    for send in sends:
        send.wait()


def route_kernel(kids, msg, pieces):
    devices, groups, lane_tiles = pieces.shape[:3]
    slots = groups
    for s in range(devices):
        for q in range(groups):
            kid = kids[s * groups + q]
            owner, slot = kid // slots, kid % slots
            for lt in range(lane_tiles):
                row = pl.multiple_of((slot * lane_tiles + lt) * ROWS, ROWS)
                pieces[s, q, lt] = msg[owner, pl.ds(row, ROWS), :]


def place_arrivals(above, below, bricks, count):
    chans = bricks.shape[1]
    half = VOX // 2
    side = LANES // 2
    shape = (LANES, half)
    pairs = SEND // 2
    for k, shift in ((0, 0), (pairs, -side)):
        slots = slice(count + k, count + k + pairs)
        first = dot(
            above[...].reshape(pairs * chans, LANES), picker(split_voxel, shape, (shift, 0))
        )
        last = dot(
            below[...].reshape(pairs * chans, LANES),
            picker(split_voxel, shape, (VOX - side + shift, half)),
        )
        bricks[slots, :, :half] = first.astype(BF16).reshape(pairs, chans, half)
        bricks[slots, :, half:] = last.astype(BF16).reshape(pairs, chans, half)
    bricks[count + SEND] = jnp.zeros(bricks.shape[1:], BF16)


def sources(table, neighbors, number):
    count = neighbors.shape[1]
    g = table[number]
    found = []
    for d in range(6):
        near = neighbors[d, g]
        local = near - table[4 * count] * count
        if d == 0:
            local = jnp.where(local >= count, table[2 * count + g], local)
        if d == 1:
            local = jnp.where(local < 0, table[3 * count + g], local)
        found.append(jnp.where(near >= 0, local, count + SEND))
    found.append(table[count + number])
    return found


def shift_into(slots, bricks, views):
    chans = bricks.shape[1]
    tiles = VOX // LANES
    lane = lax.broadcasted_iota(jnp.int32, (chans, LANES), 1)
    low = lane < LANES // 2
    a = (lane // 16) % HALF
    b = (lane // 4) % HALF
    c = lane % HALF

    def tile(slot, t):
        return bricks[slot, :, t * LANES : (t + 1) * LANES]

    def turn(value, by):
        return pltpu.roll(value, by % LANES, 1)

    x = [tile(slots[6], t) for t in range(tiles)]
    for t in range(tiles):
        lanes = slice(t * LANES, (t + 1) * LANES)
        if t < 2:
            plus_a = x[t + 2]
            minus_a = jnp.where(a > 0, turn(x[t + 2], 16), turn(tile(slots[1], t + 2), -48))
        else:
            plus_a = jnp.where(a < HALF - 1, turn(x[t - 2], -16), turn(tile(slots[0], t - 2), 48))
            minus_a = x[t - 2]
        if t % 2 == 0:
            plus_b = x[t + 1]
            minus_b = jnp.where(b > 0, turn(x[t + 1], 4), turn(tile(slots[3], t + 1), -12))
        else:
            plus_b = jnp.where(b < HALF - 1, turn(x[t - 1], -4), turn(tile(slots[2], t - 1), 12))
            minus_b = x[t - 1]
        swapped = turn(x[t], 64)
        plus_c = jnp.where(c < HALF - 1, turn(x[t], 63), turn(tile(slots[4], t), 67))
        minus_c = jnp.where(c > 0, turn(x[t], -63), turn(tile(slots[5], t), -67))
        out = [plus_a, minus_a, plus_b, minus_b, jnp.where(low, swapped, plus_c),
               jnp.where(low, minus_c, swapped), x[t]]
        for d in range(7):
            views[d * chans : (d + 1) * chans, lanes] = out[d]


def low_lanes(rows):
    return lax.broadcasted_iota(jnp.int32, (rows, LANES), 1) < LANES // 2


def forward_kernel(
    lane_tiles, table_hbm, neighbors_hbm, feat, w_conv_hbm, w_res_hbm, w_mix_hbm,
    above_hbm, below_hbm,
    parts_out, slope_out, coarse_out, piece_out,
    bricks, views, place, w_conv, w_res, w_mix, conv_cat, res_cat, octants,
    table, neighbors, above, below, sem,
):
    q = pl.program_id(0)
    groups = pl.num_programs(0) - 1
    count, chans = feat.shape[:2]
    part = count // PARTS

    @pl.when(q == 0)
    def _():
        copies = [
            pltpu.make_async_copy(source, target, sem.at[k])
            for k, (source, target) in enumerate((
                (above_hbm, above), (below_hbm, below), (w_conv_hbm, w_conv),
                (w_res_hbm, w_res), (w_mix_hbm, w_mix), (table_hbm, table),
                (neighbors_hbm, neighbors),
                *(
                    (feat.at[pl.ds(k * part, part)], bricks.at[pl.ds(k * part, part)])
                    for k in range(PARTS)
                ),
            ))
        ]
        for copy in copies:
            copy.start()
        place[...] = picker(octant_voxel, flip=True)
        for copy in copies[:-PARTS]:
            copy.wait()
        place_arrivals(above, below, bricks, count)
        for d in range(7):
            conv_cat[:, d * chans : (d + 1) * chans] = w_conv[d]
        res_cat[...] = w_res[...].T
        for copy in copies[-PARTS:]:
            copy.wait()

    low_half = low_lanes(chans)

    def finish():
        coarse = dot(octants[...], place[...]).astype(BF16)
        coarse_out[0] = coarse
        mixed = dot(w_mix[...], coarse).astype(BF16)
        per_row = VOX // (LANES * lane_tiles)
        for j in range(piece_out.shape[0]):
            chan, part = j // per_row, j % per_row
            for lt in range(lane_tiles):
                lane = (part * lane_tiles + lt) * LANES
                piece_out[j, 0, lt] = mixed[chan * ROWS : (chan + 1) * ROWS, lane : lane + LANES]

    def restrict(first):
        acts = []
        for k in range(first, first + 4):
            shift_into(sources(table, neighbors, q * 8 + k), bricks, views.at[k])
            hidden = dot(conv_cat[:, : 7 * chans], views[k])
            sig = 1.0 / (1.0 + jnp.exp(-hidden))
            act = hidden * sig
            slope_out[0, k * chans : (k + 1) * chans, :] = (sig + act * (1.0 - sig)).astype(BF16)
            acts.append(act.astype(BF16))
        for k in range(0, 4, 2):
            lanes = slice((first + k) * (LANES // 2), (first + k + 2) * (LANES // 2))
            for t in range(4):
                one = acts[k][:, t * LANES : (t + 1) * LANES]
                two = acts[k + 1][:, t * LANES : (t + 1) * LANES]
                parts_out[0, 2 * t * chans : (2 * t + 1) * chans, lanes] = jnp.where(
                    low_half, one, pltpu.roll(two, LANES // 2, 1)
                )
                parts_out[0, (2 * t + 1) * chans : (2 * t + 2) * chans, lanes] = jnp.where(
                    low_half, pltpu.roll(one, LANES // 2, 1), two
                )
        lanes = slice(first * (LANES // 2), (first + 4) * (LANES // 2))
        return dot(res_cat[...], parts_out[0, :, lanes]).astype(BF16)

    @pl.when(q < groups)
    def _():
        finish()
        halves = [restrict(0), restrict(4)]
        octants[...] = jnp.concatenate(halves, axis=1)

    @pl.when(q == groups)
    def _():
        finish()


def backward_kernel(
    lane_tiles, scale, table, neighbors, feat, above, below, pieces, parts, slope, coarse, w_mix, w_res, packed,
    bricks, views, cot, grad_parts, grad_rows, unplace, mix_t, conv_sum, res_sum, mix_sum, sem,
):
    q = pl.program_id(0)
    count, chans = feat.shape[:2]
    wide = coarse.shape[1]
    fetch = pltpu.make_async_copy(feat, bricks.at[pl.ds(0, count)], sem)

    @pl.when(q == 0)
    def _():
        fetch.start()
        place_arrivals(above, below, bricks, count)
        unplace[...] = picker(octant_voxel)
        mix_t[...] = w_mix[...].T
        conv_sum[...] = jnp.zeros_like(conv_sum)
        res_sum[...] = jnp.zeros_like(res_sum)
        mix_sum[...] = jnp.zeros_like(mix_sum)
        fetch.wait()

    per_row = VOX // (LANES * lane_tiles)
    for j in range(pieces.shape[0]):
        chan, part = j // per_row, j % per_row
        for lt in range(lane_tiles):
            lane = (part * lane_tiles + lt) * LANES
            cot[chan * ROWS : (chan + 1) * ROWS, lane : lane + LANES] = pieces[j, 0, lt]
    cots = cot[...]
    grad_coarse = (scale * dot(mix_t[...], cots)).astype(BF16)
    grad_fine = dot(grad_coarse, unplace[...]).astype(BF16)
    mix_sum[...] += dot_nt(cots, coarse[0])
    res_sum[...] += dot_nt(parts[0], grad_fine)
    grad_parts[...] = dot(w_res[...], grad_fine)
    low_half = low_lanes(chans)
    for r in range(4):
        for t in range(4):
            cols = slice(r * LANES, (r + 1) * LANES)
            lanes = slice(t * LANES, (t + 1) * LANES)
            one = grad_parts[2 * t * chans : (2 * t + 1) * chans, cols]
            two = grad_parts[(2 * t + 1) * chans : (2 * t + 2) * chans, cols]
            first = slice(2 * r * chans, (2 * r + 1) * chans)
            second = slice((2 * r + 1) * chans, (2 * r + 2) * chans)
            grad_rows[first, lanes] = (
                jnp.where(low_half, one, pltpu.roll(two, LANES // 2, 1))
                * slope[0, first, lanes].astype(F32)
            ).astype(BF16)
            grad_rows[second, lanes] = (
                jnp.where(low_half, pltpu.roll(one, LANES // 2, 1), two)
                * slope[0, second, lanes].astype(F32)
            ).astype(BF16)

    total = None
    for k in range(8):
        shift_into(sources(table, neighbors, q * 8 + k), bricks, views.at[k])
        term = dot_nt(grad_rows[k * chans : (k + 1) * chans, :], views[k])
        total = term if total is None else total + term
    conv_sum[:, : 7 * chans] += total

    @pl.when(q == pl.num_programs(0) - 1)
    def _():
        packed[0:wide] = (scale * mix_sum[...]).astype(BF16)
        at = wide
        packed[at : at + 8 * chans] = res_sum[...].astype(BF16)
        at += 8 * chans
        for t in range(4):
            packed[at : at + chans] = conv_sum[:, t * LANES : (t + 1) * LANES].astype(BF16)
            at += chans
        if at < packed.shape[0]:
            packed[at:] = jnp.zeros((packed.shape[0] - at, LANES), BF16)


def sort_kernel(kids, pieces, msg, wanted):
    devices, groups, lane_tiles = pieces.shape[:3]
    slots = groups
    rows = slots * lane_tiles * ROWS

    def invert(n, carry):
        wanted[kids[n]] = n
        return carry

    lax.fori_loop(0, devices * groups, invert, jnp.int32(0), unroll=4)
    for j in range(devices):
        for slot in range(slots):
            n = wanted[j * slots + slot]
            for lt in range(lane_tiles):
                row = j * rows + (slot * lane_tiles + lt) * ROWS
                msg[row : row + ROWS] = pieces[n // groups, n % groups, lt]


def unpack_kernel(lane_tiles, place, msg, sums, coarse_out, conv, res, mix, packed, wide_sums):
    slots = coarse_out.shape[0]
    wide = mix.shape[0]
    chans = conv.shape[1]
    half = LANES // 2
    per_row = VOX // (LANES * lane_tiles)
    devices = 8 * per_row
    rows = msg.shape[0] // devices
    share = sums.shape[0] // devices
    wide_sums[...] = sums[...].astype(F32)
    for p in range(devices):
        source, behind = jnp.int32(0), p
        for radix, stride in digits(devices):
            digit = place[0] // stride % radix
            source += (digit + radix - behind % radix) % radix * stride
            behind //= radix
        at = pl.multiple_of(source * share, 8)
        packed[pl.ds(at, share), :] = wide_sums[p * share : (p + 1) * share]
    mix[...] = packed[0:wide]
    at = wide
    for t in range(8):
        res[t] = packed[at : at + chans]
        at += chans
    for t in range(4):
        block = packed[at : at + chans]
        conv[2 * t] = block[:, :half]
        if 2 * t + 1 < 7:
            conv[2 * t + 1] = block[:, half:]
        at += chans
    for j in range(devices):
        chan, part = j // per_row, j % per_row
        for q in range(slots):
            for lt in range(lane_tiles):
                row = j * rows + (q * lane_tiles + lt) * ROWS
                lane = (part * lane_tiles + lt) * LANES
                coarse_out[q, chan * ROWS : (chan + 1) * ROWS, lane : lane + LANES] = msg[
                    row : row + ROWS
                ]


def kernel_call(kernel, out_shape, grid_spec, flops, moved, vmem=VMEM_BYTES):
    return pl.pallas_call(
        kernel,
        out_shape=out_shape,
        grid_spec=grid_spec,
        compiler_params=pltpu.CompilerParams(vmem_limit_bytes=vmem),
        cost_estimate=pl.CostEstimate(flops=flops, bytes_accessed=moved, transcendentals=0),
    )


def body(features, counts, neighbors, parents, w_conv, w_restrict, w_mix, cotangent):
    devices = lax.axis_size("space")
    position = lax.axis_index("space").astype(jnp.int32).reshape(1)
    slots, wide = cotangent.shape[:2]
    count, chans = features.shape[:2]
    lane_tiles = VOX * 8 // devices // LANES
    tiles = slots * lane_tiles
    groups = count // 8
    whole = lambda shape: pl.BlockSpec(shape, lambda *_: (0,) * len(shape))
    any_spec = pl.BlockSpec(memory_space=pl.ANY)
    smem_spec = pl.BlockSpec(memory_space=pltpu.SMEM)
    smem = lambda size: pltpu.SMEM((size,), jnp.int32)
    vmem = pltpu.VMEM
    ints = lambda size: jax.ShapeDtypeStruct((size,), jnp.int32)

    message_shape = (devices, tiles * ROWS + LABEL_ROWS, LANES)
    flat_shape = (message_shape[0] * message_shape[1], LANES)
    message, kids = kernel_call(
        functools.partial(pack_kernel, lane_tiles),
        (jax.ShapeDtypeStruct(flat_shape, BF16), ints(groups)),
        pl.GridSpec(
            grid=(1,),
            in_specs=[smem_spec, whole(cotangent.shape)],
            out_specs=[whole(flat_shape), smem_spec],
            scratch_shapes=[smem(groups + 1)],
        ),
        1000, 2**20,
    )(parents.T, cotangent)
    spread = lax.all_to_all(
        message.reshape(message_shape), "space", split_axis=0, concat_axis=0, tiled=True
    )

    plane = jax.ShapeDtypeStruct((SEND // 2, chans, LANES), BF16)
    up, down, table, ordered = kernel_call(
        table_kernel,
        (plane, plane, ints(4 * count + 1), jax.ShapeDtypeStruct(features.shape, BF16)),
        pl.GridSpec(
            grid=(1,),
            in_specs=[smem_spec] * 5 + [any_spec],
            out_specs=[whole(plane.shape)] * 2 + [smem_spec, any_spec],
            scratch_shapes=[smem(SEND + 1)] * 4
            + [vmem(features.shape, BF16), vmem(features.shape, BF16), vmem((VOX, VOX), BF16),
               pltpu.SemaphoreType.DMA((PARTS,)), pltpu.SemaphoreType.DMA((PARTS,))],
        ),
        1000, 2**20,
    )(position, counts, kids, neighbors.T, parents.T, features)
    below = lax.ppermute(up, "space", [(i, i + 1) for i in range(devices - 1)])
    above = lax.ppermute(down, "space", [(i + 1, i) for i in range(devices - 1)])

    all_kids = spread[:, tiles * ROWS, :groups].astype(jnp.int32).reshape(-1)
    piece_shape = (devices, groups, lane_tiles, ROWS, LANES)
    forward_tiles = kernel_call(
        route_kernel,
        jax.ShapeDtypeStruct(piece_shape, BF16),
        pl.GridSpec(
            grid=(1,),
            in_specs=[smem_spec, whole(message_shape)],
            out_specs=whole(piece_shape),
        ),
        1000, 2**20, SMALL_VMEM_BYTES,
    )(all_kids, spread)
    forward_tiles, above, below = lax.optimization_barrier((forward_tiles, above, below))
    cot_pieces = lax.all_to_all(forward_tiles, "space", split_axis=0, concat_axis=0, tiled=True)

    res_rows = w_restrict.transpose(0, 2, 1).reshape(8 * chans, wide)
    scalars = (table, neighbors.T)
    brick_scratch = vmem((count + SEND + 1, chans, VOX), BF16)
    view_scratch = vmem((8, 7 * chans, VOX), BF16)
    per_group = lambda *shape: pl.BlockSpec((1,) + shape, lambda q: (q,) + (0,) * len(shape))
    piece_spec = pl.BlockSpec((devices, 1, lane_tiles, ROWS, LANES), lambda q: (0, q, 0, 0, 0))
    parts, slope, coarse, pieces = kernel_call(
        functools.partial(forward_kernel, lane_tiles),
        (
            jax.ShapeDtypeStruct((groups, 8 * chans, VOX), BF16),
            jax.ShapeDtypeStruct((groups, 8 * chans, VOX), BF16),
            jax.ShapeDtypeStruct((groups, wide, VOX), BF16),
            jax.ShapeDtypeStruct(piece_shape, BF16),
        ),
        pl.GridSpec(
            grid=(groups + 1,),
            in_specs=[any_spec] * 8,
            out_specs=[
                pl.BlockSpec((1, 8 * chans, VOX), lambda q: (jnp.minimum(q, groups - 1), 0, 0)),
                pl.BlockSpec((1, 8 * chans, VOX), lambda q: (jnp.minimum(q, groups - 1), 0, 0)),
                pl.BlockSpec((1, wide, VOX), lambda q: (jnp.maximum(q - 1, 0), 0, 0)),
                pl.BlockSpec(
                    (devices, 1, lane_tiles, ROWS, LANES),
                    lambda q: (0, jnp.maximum(q - 1, 0), 0, 0, 0),
                ),
            ],
            scratch_shapes=[
                brick_scratch, view_scratch, vmem((VOX, VOX), BF16), vmem(w_conv.shape, BF16),
                vmem(res_rows.shape, BF16), vmem(w_mix.shape, BF16),
                vmem((chans, 8 * chans), BF16), vmem((wide, 8 * chans), BF16),
                vmem((wide, VOX), BF16), smem(4 * count + 1),
                pltpu.SMEM((6, count), jnp.int32), vmem(plane.shape, BF16),
                vmem(plane.shape, BF16), pltpu.SemaphoreType.DMA((7 + PARTS,)),
            ],
        ),
        16 * 10**9, 16 * 2**20,
    )(*scalars, ordered, w_conv, res_rows, w_mix, above, below)
    returned = lax.all_to_all(pieces, "space", split_axis=0, concat_axis=0, tiled=True)

    scale = 1.0 / math.sqrt(devices * slots * VOX)
    used = wide + 8 * chans + 4 * chans
    rows = -(-used // (devices * 8)) * 8
    packed = kernel_call(
        functools.partial(backward_kernel, lane_tiles, scale),
        jax.ShapeDtypeStruct((devices * rows, LANES), BF16),
        pl.GridSpec(
            grid=(groups,),
            in_specs=[smem_spec] * 2 + [any_spec] + [whole(plane.shape)] * 2
            + [piece_spec, per_group(8 * chans, VOX), per_group(8 * chans, VOX),
               per_group(wide, VOX), whole(w_mix.shape), whole(res_rows.shape)],
            out_specs=whole((devices * rows, LANES)),
            scratch_shapes=[
                brick_scratch, view_scratch, vmem((wide, VOX), BF16),
                vmem((8 * chans, VOX), F32), vmem((8 * chans, VOX), BF16), vmem((VOX, VOX), BF16),
                vmem((wide, wide), BF16), vmem((chans, 8 * chans), F32),
                vmem((8 * chans, wide), F32), vmem((wide, wide), F32), pltpu.SemaphoreType.DMA,
            ],
        ),
        16 * 10**9, 16 * 2**20,
    )(*scalars, ordered, above, below, cot_pieces, parts, slope, coarse, w_mix, res_rows)

    shares = lax.all_to_all(
        packed.reshape(devices, rows, LANES), "space", split_axis=0, concat_axis=0, tiled=True
    )
    returned, _ = lax.optimization_barrier((returned, packed))
    flat_shape = (devices * tiles * ROWS, LANES)
    sorted_pieces = kernel_call(
        sort_kernel,
        jax.ShapeDtypeStruct(flat_shape, BF16),
        pl.GridSpec(
            grid=(1,),
            in_specs=[smem_spec, whole(piece_shape)],
            out_specs=whole(flat_shape),
            scratch_shapes=[smem(devices * groups)],
        ),
        1000, 2**20, SMALL_VMEM_BYTES,
    )(all_kids, returned)
    sorted_pieces, shares = lax.optimization_barrier((sorted_pieces, shares))
    finished = lax.all_to_all(
        sorted_pieces.reshape(devices, tiles * ROWS, LANES),
        "space", split_axis=0, concat_axis=0, tiled=True,
    )
    summed = jnp.sum(shares.astype(F32), axis=0).astype(BF16)
    sums = gather_by_digits(summed, devices).reshape(devices * rows, LANES)

    coarse_out, grad_conv, grad_res, grad_mix = kernel_call(
        functools.partial(unpack_kernel, lane_tiles),
        (
            jax.ShapeDtypeStruct((slots, wide, VOX), BF16),
            jax.ShapeDtypeStruct((7, chans, chans), F32),
            jax.ShapeDtypeStruct((8, chans, wide), F32),
            jax.ShapeDtypeStruct((wide, wide), F32),
        ),
        pl.GridSpec(
            grid=(1,),
            in_specs=[smem_spec, whole(flat_shape), whole((devices * rows, LANES))],
            out_specs=[whole((slots, wide, VOX)), whole((7, chans, chans)),
                       whole((8, chans, wide)), whole((wide, wide))],
            scratch_shapes=[vmem((devices * rows, LANES), F32)] * 2,
        ),
        1000, 2 * 2**20, SMALL_VMEM_BYTES,
    )(position, finished.reshape(flat_shape), sums)
    return coarse_out, grad_conv, grad_res.transpose(0, 2, 1), grad_mix


def solution(mesh):
    return jax.shard_map(
        body,
        mesh=mesh,
        in_specs=(
            P(("groups", "space"), None, None),
            P(("groups", "space")),
            P(("groups", "space"), None),
            P(("groups", "space"), None),
            P(),
            P(),
            P(),
            P(("groups", "space"), None, None),
        ),
        out_specs=(
            P(("groups", "space"), None, None),
            P("groups", None, None),
            P("groups", None, None),
            P("groups", None),
        ),
        check_vma=False,
    )
```

```python
import functools
import math

import jax
import jax.numpy as jnp
from jax import lax
from jax.experimental import pallas as pl
from jax.experimental.pallas import tpu as pltpu
from jax.sharding import PartitionSpec as P

EDGE = 8
HALF = EDGE // 2
VOX = EDGE**3
LANES = 128
ROWS = 16
LABEL_ROWS = 8
SEND = 8
PARTS = 4
BF16 = jnp.bfloat16
F32 = jnp.float32
VMEM_BYTES = 60 * 1024 * 1024
SMALL_VMEM_BYTES = 16 * 1024 * 1024


def bits_of(value):
    return [(value >> (8 - k)) & 1 for k in range(9)]


def join_bits(bits):
    value = bits[0]
    for bit in bits[1:]:
        value = value * 2 + bit
    return value


def split_voxel(column):
    ta, tb, tc, a1, a0, b1, b0, c1, c0 = bits_of(column)
    return join_bits([a1, a0, ta, b1, b0, tb, c1, c0, tc])


def octant_voxel(column):
    oa, ob, oc, a1, a0, b1, b0, c1, c0 = bits_of(column)
    return join_bits([oa, a1, a0, ob, b1, b0, oc, c1, c0])


def picker(voxel_of, shape=(VOX, VOX), start=(0, 0), flip=False):
    row = lax.broadcasted_iota(jnp.int32, shape, 0) + start[0]
    column = lax.broadcasted_iota(jnp.int32, shape, 1) + start[1]
    return (column == voxel_of(row) if flip else row == voxel_of(column)).astype(BF16)


def digits(devices):
    strides = [devices // 2]
    for stride in (2, 1, *(1 << k for k in range(2, devices.bit_length()))):
        if stride < devices // 2:
            strides.append(stride)
    return [(2, stride) for stride in strides]


def gather_by_digits(own, devices):
    held = own[None]
    for radix, stride in digits(devices):
        came = [held]
        for step in range(1, radix):
            pairs = []
            for i in range(devices):
                digit = i // stride % radix
                pairs.append((i, i + ((digit + step) % radix - digit) * stride))
            came.append(lax.ppermute(held, "space", pairs))
        held = jnp.concatenate(came, axis=0)
    return held


def dot(a, b):
    return jnp.dot(a, b, preferred_element_type=F32)


def dot_nt(a, b):
    return lax.dot_general(a, b, (((1,), (1,)), ((), ())), preferred_element_type=F32)


def pack_kernel(lane_tiles, parents, cot, msg, kids_out, kids):
    slots = cot.shape[0]
    body_rows = slots * lane_tiles * ROWS
    rows = body_rows + LABEL_ROWS
    devices = msg.shape[0] // rows

    def find(g, found):
        kids[found] = parents[0, g]
        return found + (parents[1, g] == 0).astype(jnp.int32)

    lax.fori_loop(0, parents.shape[1], find, jnp.int32(0), unroll=4)
    lane = lax.broadcasted_iota(jnp.int32, (LABEL_ROWS, LANES), 1)
    label = jnp.zeros((LABEL_ROWS, LANES), jnp.int32)
    for q in range(kids_out.shape[0]):
        kids_out[q] = kids[q]
        label = jnp.where(lane == q, kids[q], label)
    label = label.astype(F32).astype(BF16)
    for j in range(devices):
        msg[j * rows + body_rows : (j + 1) * rows] = label
    per_row = VOX // (LANES * lane_tiles)
    for j in range(devices):
        chan, part = j // per_row, j % per_row
        for q in range(slots):
            for lt in range(lane_tiles):
                lane = (part * lane_tiles + lt) * LANES
                row = j * rows + (q * lane_tiles + lt) * ROWS
                msg[row : row + ROWS] = cot[
                    q, chan * ROWS : (chan + 1) * ROWS, lane : lane + LANES
                ]


def table_kernel(
    place, counts, kids, neighbors, parents, feat, up, down, table, ordered,
    up_idx, up_far, down_idx, down_far, bricks, done, split, in_sem, out_sem,
):
    count, chans = feat.shape[:2]
    part = count // PARTS
    fetches = [
        pltpu.make_async_copy(
            feat.at[pl.ds(k * part, part)], bricks.at[pl.ds(k * part, part)], in_sem.at[k]
        )
        for k in range(PARTS)
    ]
    for fetch in fetches:
        fetch.start()
    base = place[0] * count
    table[4 * count] = place[0]
    for r in range(SEND + 1):
        up_idx[r] = 0
        down_idx[r] = 0
        up_far[r] = 2 * count
        down_far[r] = 2 * count
    split[...] = picker(split_voxel)

    def scan(g, found):
        n_up, n_down = found
        near_up, near_down = neighbors[0, g], neighbors[1, g]
        far_up, far_down = near_up - base - count, near_down - base + count
        goes_up = (near_up >= 0) & (far_up >= 0)
        goes_down = (near_down >= 0) & (far_down < count)
        up_idx[n_up] = g
        up_far[n_up] = jnp.where(goes_up, far_up, 2 * count)
        down_idx[n_down] = g
        down_far[n_down] = jnp.where(goes_down, far_down, 2 * count)
        q = jnp.int32(0)
        for k in range(1, kids.shape[0]):
            q += jnp.where(kids[k] == parents[0, g], k, 0)
        number = q * 8 + parents[1, g]
        table[number] = g
        table[count + number] = jnp.where(g < counts[0], g, count + SEND)
        return n_up + goes_up.astype(jnp.int32), n_down + goes_down.astype(jnp.int32)

    lax.fori_loop(0, count, scan, (jnp.int32(0), jnp.int32(0)), unroll=4)

    def rank(r, carry):
        for start, far, idx in ((2 * count, up_far, up_idx), (3 * count, down_far, down_idx)):
            earlier = jnp.int32(0)
            for other in range(SEND):
                earlier += (far[other] < far[r]).astype(jnp.int32)

            @pl.when(far[r] < count)
            def _():
                table[start + idx[r]] = count + earlier

        return carry

    lax.fori_loop(0, SEND, rank, jnp.int32(0))
    sends = []
    for k in range(PARTS):
        fetches[k].wait()
        rows = bricks[k * part : (k + 1) * part].reshape(part * chans, VOX)
        done[k * part : (k + 1) * part] = (
            dot(rows, split[...]).astype(BF16).reshape(part, chans, VOX)
        )
        sends.append(
            pltpu.make_async_copy(
                done.at[pl.ds(k * part, part)], ordered.at[pl.ds(k * part, part)], out_sem.at[k]
            )
        )
        sends[-1].start()
    low = low_lanes(chans)
    for r in range(SEND // 2):
        other = r + SEND // 2
        top = slice(VOX - LANES, VOX)
        up[r] = jnp.where(
            low,
            pltpu.roll(bricks[up_idx[r], :, top], LANES // 2, 1),
            bricks[up_idx[other], :, top],
        )
        down[r] = jnp.where(
            low,
            bricks[down_idx[r], :, :LANES],
            pltpu.roll(bricks[down_idx[other], :, :LANES], LANES // 2, 1),
        )
    for send in sends:
        send.wait()


def route_kernel(kids, msg, pieces):
    devices, groups, lane_tiles = pieces.shape[:3]
    slots = groups
    for s in range(devices):
        for q in range(groups):
            kid = kids[s * groups + q]
            owner, slot = kid // slots, kid % slots
            for lt in range(lane_tiles):
                row = pl.multiple_of((slot * lane_tiles + lt) * ROWS, ROWS)
                pieces[s, q, lt] = msg[owner, pl.ds(row, ROWS), :]


def place_arrivals(above, below, bricks, count):
    chans = bricks.shape[1]
    half = VOX // 2
    side = LANES // 2
    shape = (LANES, half)
    pairs = SEND // 2
    for k, shift in ((0, 0), (pairs, -side)):
        slots = slice(count + k, count + k + pairs)
        first = dot(
            above[...].reshape(pairs * chans, LANES), picker(split_voxel, shape, (shift, 0))
        )
        last = dot(
            below[...].reshape(pairs * chans, LANES),
            picker(split_voxel, shape, (VOX - side + shift, half)),
        )
        bricks[slots, :, :half] = first.astype(BF16).reshape(pairs, chans, half)
        bricks[slots, :, half:] = last.astype(BF16).reshape(pairs, chans, half)
    bricks[count + SEND] = jnp.zeros(bricks.shape[1:], BF16)


def sources(table, neighbors, number):
    count = neighbors.shape[1]
    g = table[number]
    found = []
    for d in range(6):
        near = neighbors[d, g]
        local = near - table[4 * count] * count
        if d == 0:
            local = jnp.where(local >= count, table[2 * count + g], local)
        if d == 1:
            local = jnp.where(local < 0, table[3 * count + g], local)
        found.append(jnp.where(near >= 0, local, count + SEND))
    found.append(table[count + number])
    return found


def shift_into(slots, bricks, views):
    chans = bricks.shape[1]
    tiles = VOX // LANES
    lane = lax.broadcasted_iota(jnp.int32, (chans, LANES), 1)
    low = lane < LANES // 2
    a = (lane // 16) % HALF
    b = (lane // 4) % HALF
    c = lane % HALF

    def tile(slot, t):
        return bricks[slot, :, t * LANES : (t + 1) * LANES]

    def turn(value, by):
        return pltpu.roll(value, by % LANES, 1)

    x = [tile(slots[6], t) for t in range(tiles)]
    for t in range(tiles):
        lanes = slice(t * LANES, (t + 1) * LANES)
        if t < 2:
            plus_a = x[t + 2]
            minus_a = jnp.where(a > 0, turn(x[t + 2], 16), turn(tile(slots[1], t + 2), -48))
        else:
            plus_a = jnp.where(a < HALF - 1, turn(x[t - 2], -16), turn(tile(slots[0], t - 2), 48))
            minus_a = x[t - 2]
        if t % 2 == 0:
            plus_b = x[t + 1]
            minus_b = jnp.where(b > 0, turn(x[t + 1], 4), turn(tile(slots[3], t + 1), -12))
        else:
            plus_b = jnp.where(b < HALF - 1, turn(x[t - 1], -4), turn(tile(slots[2], t - 1), 12))
            minus_b = x[t - 1]
        swapped = turn(x[t], 64)
        plus_c = jnp.where(c < HALF - 1, turn(x[t], 63), turn(tile(slots[4], t), 67))
        minus_c = jnp.where(c > 0, turn(x[t], -63), turn(tile(slots[5], t), -67))
        out = [plus_a, minus_a, plus_b, minus_b, jnp.where(low, swapped, plus_c),
               jnp.where(low, minus_c, swapped), x[t]]
        for d in range(7):
            views[d * chans : (d + 1) * chans, lanes] = out[d]


def low_lanes(rows):
    return lax.broadcasted_iota(jnp.int32, (rows, LANES), 1) < LANES // 2


def forward_kernel(
    lane_tiles, table_hbm, neighbors_hbm, feat, w_conv_hbm, w_res_hbm, w_mix_hbm,
    above_hbm, below_hbm,
    parts_out, slope_out, coarse_out, piece_out,
    bricks, views, place, w_conv, w_res, w_mix, conv_cat, res_cat, octants,
    table, neighbors, above, below, sem,
):
    q = pl.program_id(0)
    groups = pl.num_programs(0) - 1
    count, chans = feat.shape[:2]
    part = count // PARTS

    @pl.when(q == 0)
    def _():
        copies = [
            pltpu.make_async_copy(source, target, sem.at[k])
            for k, (source, target) in enumerate((
                (above_hbm, above), (below_hbm, below), (w_conv_hbm, w_conv),
                (w_res_hbm, w_res), (w_mix_hbm, w_mix), (table_hbm, table),
                (neighbors_hbm, neighbors),
                *(
                    (feat.at[pl.ds(k * part, part)], bricks.at[pl.ds(k * part, part)])
                    for k in range(PARTS)
                ),
            ))
        ]
        for copy in copies:
            copy.start()
        place[...] = picker(octant_voxel, flip=True)
        for copy in copies[:-PARTS]:
            copy.wait()
        place_arrivals(above, below, bricks, count)
        for d in range(7):
            conv_cat[:, d * chans : (d + 1) * chans] = w_conv[d]
        res_cat[...] = w_res[...].T
        for copy in copies[-PARTS:]:
            copy.wait()

    low_half = low_lanes(chans)

    def finish():
        coarse = dot(octants[...], place[...]).astype(BF16)
        coarse_out[0] = coarse
        mixed = dot(w_mix[...], coarse).astype(BF16)
        per_row = VOX // (LANES * lane_tiles)
        for j in range(piece_out.shape[0]):
            chan, part = j // per_row, j % per_row
            for lt in range(lane_tiles):
                lane = (part * lane_tiles + lt) * LANES
                piece_out[j, 0, lt] = mixed[chan * ROWS : (chan + 1) * ROWS, lane : lane + LANES]

    def restrict(first):
        acts = []
        for k in range(first, first + 4):
            shift_into(sources(table, neighbors, q * 8 + k), bricks, views.at[k])
            hidden = dot(conv_cat[:, : 7 * chans], views[k])
            sig = 1.0 / (1.0 + jnp.exp(-hidden))
            act = hidden * sig
            slope_out[0, k * chans : (k + 1) * chans, :] = (sig + act * (1.0 - sig)).astype(BF16)
            acts.append(act.astype(BF16))
        for k in range(0, 4, 2):
            lanes = slice((first + k) * (LANES // 2), (first + k + 2) * (LANES // 2))
            for t in range(4):
                one = acts[k][:, t * LANES : (t + 1) * LANES]
                two = acts[k + 1][:, t * LANES : (t + 1) * LANES]
                parts_out[0, 2 * t * chans : (2 * t + 1) * chans, lanes] = jnp.where(
                    low_half, one, pltpu.roll(two, LANES // 2, 1)
                )
                parts_out[0, (2 * t + 1) * chans : (2 * t + 2) * chans, lanes] = jnp.where(
                    low_half, pltpu.roll(one, LANES // 2, 1), two
                )
        lanes = slice(first * (LANES // 2), (first + 4) * (LANES // 2))
        return dot(res_cat[...], parts_out[0, :, lanes]).astype(BF16)

    @pl.when(q < groups)
    def _():
        finish()
        halves = [restrict(0), restrict(4)]
        octants[...] = jnp.concatenate(halves, axis=1)

    @pl.when(q == groups)
    def _():
        finish()


def backward_kernel(
    lane_tiles, scale, table, neighbors, feat, above, below, pieces, parts, slope, coarse, w_mix, w_res, packed,
    bricks, views, cot, grad_parts, grad_rows, unplace, mix_t, conv_sum, res_sum, mix_sum, sem,
):
    q = pl.program_id(0)
    count, chans = feat.shape[:2]
    wide = coarse.shape[1]
    fetch = pltpu.make_async_copy(feat, bricks.at[pl.ds(0, count)], sem)

    @pl.when(q == 0)
    def _():
        fetch.start()
        place_arrivals(above, below, bricks, count)
        unplace[...] = picker(octant_voxel)
        mix_t[...] = w_mix[...].T
        conv_sum[...] = jnp.zeros_like(conv_sum)
        res_sum[...] = jnp.zeros_like(res_sum)
        mix_sum[...] = jnp.zeros_like(mix_sum)
        fetch.wait()

    per_row = VOX // (LANES * lane_tiles)
    for j in range(pieces.shape[0]):
        chan, part = j // per_row, j % per_row
        for lt in range(lane_tiles):
            lane = (part * lane_tiles + lt) * LANES
            cot[chan * ROWS : (chan + 1) * ROWS, lane : lane + LANES] = pieces[j, 0, lt]
    cots = cot[...]
    grad_coarse = (scale * dot(mix_t[...], cots)).astype(BF16)
    grad_fine = dot(grad_coarse, unplace[...]).astype(BF16)
    mix_sum[...] += dot_nt(cots, coarse[0])
    res_sum[...] += dot_nt(parts[0], grad_fine)
    grad_parts[...] = dot(w_res[...], grad_fine)
    low_half = low_lanes(chans)
    for r in range(4):
        for t in range(4):
            cols = slice(r * LANES, (r + 1) * LANES)
            lanes = slice(t * LANES, (t + 1) * LANES)
            one = grad_parts[2 * t * chans : (2 * t + 1) * chans, cols]
            two = grad_parts[(2 * t + 1) * chans : (2 * t + 2) * chans, cols]
            first = slice(2 * r * chans, (2 * r + 1) * chans)
            second = slice((2 * r + 1) * chans, (2 * r + 2) * chans)
            grad_rows[first, lanes] = (
                jnp.where(low_half, one, pltpu.roll(two, LANES // 2, 1))
                * slope[0, first, lanes].astype(F32)
            ).astype(BF16)
            grad_rows[second, lanes] = (
                jnp.where(low_half, pltpu.roll(one, LANES // 2, 1), two)
                * slope[0, second, lanes].astype(F32)
            ).astype(BF16)

    total = None
    for k in range(8):
        shift_into(sources(table, neighbors, q * 8 + k), bricks, views.at[k])
        term = dot_nt(grad_rows[k * chans : (k + 1) * chans, :], views[k])
        total = term if total is None else total + term
    conv_sum[:, : 7 * chans] += total

    @pl.when(q == pl.num_programs(0) - 1)
    def _():
        packed[0:wide] = (scale * mix_sum[...]).astype(BF16)
        at = wide
        packed[at : at + 8 * chans] = res_sum[...].astype(BF16)
        at += 8 * chans
        for t in range(4):
            packed[at : at + chans] = conv_sum[:, t * LANES : (t + 1) * LANES].astype(BF16)
            at += chans
        if at < packed.shape[0]:
            packed[at:] = jnp.zeros((packed.shape[0] - at, LANES), BF16)


def sort_kernel(kids, pieces, msg, wanted):
    devices, groups, lane_tiles = pieces.shape[:3]
    slots = groups
    rows = slots * lane_tiles * ROWS

    def invert(n, carry):
        wanted[kids[n]] = n
        return carry

    lax.fori_loop(0, devices * groups, invert, jnp.int32(0), unroll=4)
    for j in range(devices):
        for slot in range(slots):
            n = wanted[j * slots + slot]
            for lt in range(lane_tiles):
                row = j * rows + (slot * lane_tiles + lt) * ROWS
                msg[row : row + ROWS] = pieces[n // groups, n % groups, lt]


def unpack_kernel(lane_tiles, place, msg, sums, coarse_out, conv, res, mix, packed, wide_sums):
    slots = coarse_out.shape[0]
    wide = mix.shape[0]
    chans = conv.shape[1]
    half = LANES // 2
    per_row = VOX // (LANES * lane_tiles)
    devices = 8 * per_row
    rows = msg.shape[0] // devices
    share = sums.shape[0] // devices
    wide_sums[...] = sums[...].astype(F32)
    for p in range(devices):
        source, behind = jnp.int32(0), p
        for radix, stride in digits(devices):
            digit = place[0] // stride % radix
            source += (digit + radix - behind % radix) % radix * stride
            behind //= radix
        at = pl.multiple_of(source * share, 8)
        packed[pl.ds(at, share), :] = wide_sums[p * share : (p + 1) * share]
    mix[...] = packed[0:wide]
    at = wide
    for t in range(8):
        res[t] = packed[at : at + chans]
        at += chans
    for t in range(4):
        block = packed[at : at + chans]
        conv[2 * t] = block[:, :half]
        if 2 * t + 1 < 7:
            conv[2 * t + 1] = block[:, half:]
        at += chans
    for j in range(devices):
        chan, part = j // per_row, j % per_row
        for q in range(slots):
            for lt in range(lane_tiles):
                row = j * rows + (q * lane_tiles + lt) * ROWS
                lane = (part * lane_tiles + lt) * LANES
                coarse_out[q, chan * ROWS : (chan + 1) * ROWS, lane : lane + LANES] = msg[
                    row : row + ROWS
                ]


def kernel_call(kernel, out_shape, grid_spec, flops, moved, vmem=VMEM_BYTES):
    return pl.pallas_call(
        kernel,
        out_shape=out_shape,
        grid_spec=grid_spec,
        compiler_params=pltpu.CompilerParams(vmem_limit_bytes=vmem),
        cost_estimate=pl.CostEstimate(flops=flops, bytes_accessed=moved, transcendentals=0),
    )


def body(features, counts, neighbors, parents, w_conv, w_restrict, w_mix, cotangent):
    devices = lax.axis_size("space")
    position = lax.axis_index("space").astype(jnp.int32).reshape(1)
    slots, wide = cotangent.shape[:2]
    count, chans = features.shape[:2]
    lane_tiles = VOX * 8 // devices // LANES
    tiles = slots * lane_tiles
    groups = count // 8
    whole = lambda shape: pl.BlockSpec(shape, lambda *_: (0,) * len(shape))
    any_spec = pl.BlockSpec(memory_space=pl.ANY)
    smem_spec = pl.BlockSpec(memory_space=pltpu.SMEM)
    smem = lambda size: pltpu.SMEM((size,), jnp.int32)
    vmem = pltpu.VMEM
    ints = lambda size: jax.ShapeDtypeStruct((size,), jnp.int32)

    message_shape = (devices, tiles * ROWS + LABEL_ROWS, LANES)
    flat_shape = (message_shape[0] * message_shape[1], LANES)
    message, kids = kernel_call(
        functools.partial(pack_kernel, lane_tiles),
        (jax.ShapeDtypeStruct(flat_shape, BF16), ints(groups)),
        pl.GridSpec(
            grid=(1,),
            in_specs=[smem_spec, whole(cotangent.shape)],
            out_specs=[whole(flat_shape), smem_spec],
            scratch_shapes=[smem(groups + 1)],
        ),
        1000, 2**20,
    )(parents.T, cotangent)
    spread = lax.all_to_all(
        message.reshape(message_shape), "space", split_axis=0, concat_axis=0, tiled=True
    )

    plane = jax.ShapeDtypeStruct((SEND // 2, chans, LANES), BF16)
    up, down, table, ordered = kernel_call(
        table_kernel,
        (plane, plane, ints(4 * count + 1), jax.ShapeDtypeStruct(features.shape, BF16)),
        pl.GridSpec(
            grid=(1,),
            in_specs=[smem_spec] * 5 + [any_spec],
            out_specs=[whole(plane.shape)] * 2 + [smem_spec, any_spec],
            scratch_shapes=[smem(SEND + 1)] * 4
            + [vmem(features.shape, BF16), vmem(features.shape, BF16), vmem((VOX, VOX), BF16),
               pltpu.SemaphoreType.DMA((PARTS,)), pltpu.SemaphoreType.DMA((PARTS,))],
        ),
        1000, 2**20,
    )(position, counts, kids, neighbors.T, parents.T, features)
    below = lax.ppermute(up, "space", [(i, i + 1) for i in range(devices - 1)])
    above = lax.ppermute(down, "space", [(i + 1, i) for i in range(devices - 1)])

    all_kids = spread[:, tiles * ROWS, :groups].astype(jnp.int32).reshape(-1)
    piece_shape = (devices, groups, lane_tiles, ROWS, LANES)
    forward_tiles = kernel_call(
        route_kernel,
        jax.ShapeDtypeStruct(piece_shape, BF16),
        pl.GridSpec(
            grid=(1,),
            in_specs=[smem_spec, whole(message_shape)],
            out_specs=whole(piece_shape),
        ),
        1000, 2**20, SMALL_VMEM_BYTES,
    )(all_kids, spread)
    forward_tiles, above, below = lax.optimization_barrier((forward_tiles, above, below))
    cot_pieces = lax.all_to_all(forward_tiles, "space", split_axis=0, concat_axis=0, tiled=True)

    res_rows = w_restrict.transpose(0, 2, 1).reshape(8 * chans, wide)
    scalars = (table, neighbors.T)
    brick_scratch = vmem((count + SEND + 1, chans, VOX), BF16)
    view_scratch = vmem((8, 7 * chans, VOX), BF16)
    per_group = lambda *shape: pl.BlockSpec((1,) + shape, lambda q: (q,) + (0,) * len(shape))
    piece_spec = pl.BlockSpec((devices, 1, lane_tiles, ROWS, LANES), lambda q: (0, q, 0, 0, 0))
    parts, slope, coarse, pieces = kernel_call(
        functools.partial(forward_kernel, lane_tiles),
        (
            jax.ShapeDtypeStruct((groups, 8 * chans, VOX), BF16),
            jax.ShapeDtypeStruct((groups, 8 * chans, VOX), BF16),
            jax.ShapeDtypeStruct((groups, wide, VOX), BF16),
            jax.ShapeDtypeStruct(piece_shape, BF16),
        ),
        pl.GridSpec(
            grid=(groups + 1,),
            in_specs=[any_spec] * 8,
            out_specs=[
                pl.BlockSpec((1, 8 * chans, VOX), lambda q: (jnp.minimum(q, groups - 1), 0, 0)),
                pl.BlockSpec((1, 8 * chans, VOX), lambda q: (jnp.minimum(q, groups - 1), 0, 0)),
                pl.BlockSpec((1, wide, VOX), lambda q: (jnp.maximum(q - 1, 0), 0, 0)),
                pl.BlockSpec(
                    (devices, 1, lane_tiles, ROWS, LANES),
                    lambda q: (0, jnp.maximum(q - 1, 0), 0, 0, 0),
                ),
            ],
            scratch_shapes=[
                brick_scratch, view_scratch, vmem((VOX, VOX), BF16), vmem(w_conv.shape, BF16),
                vmem(res_rows.shape, BF16), vmem(w_mix.shape, BF16),
                vmem((chans, 8 * chans), BF16), vmem((wide, 8 * chans), BF16),
                vmem((wide, VOX), BF16), smem(4 * count + 1),
                pltpu.SMEM((6, count), jnp.int32), vmem(plane.shape, BF16),
                vmem(plane.shape, BF16), pltpu.SemaphoreType.DMA((7 + PARTS,)),
            ],
        ),
        16 * 10**9, 16 * 2**20,
    )(*scalars, ordered, w_conv, res_rows, w_mix, above, below)
    returned = lax.all_to_all(pieces, "space", split_axis=0, concat_axis=0, tiled=True)

    scale = 1.0 / math.sqrt(devices * slots * VOX)
    used = wide + 8 * chans + 4 * chans
    rows = -(-used // (devices * 8)) * 8
    packed = kernel_call(
        functools.partial(backward_kernel, lane_tiles, scale),
        jax.ShapeDtypeStruct((devices * rows, LANES), BF16),
        pl.GridSpec(
            grid=(groups,),
            in_specs=[smem_spec] * 2 + [any_spec] + [whole(plane.shape)] * 2
            + [piece_spec, per_group(8 * chans, VOX), per_group(8 * chans, VOX),
               per_group(wide, VOX), whole(w_mix.shape), whole(res_rows.shape)],
            out_specs=whole((devices * rows, LANES)),
            scratch_shapes=[
                brick_scratch, view_scratch, vmem((wide, VOX), BF16),
                vmem((8 * chans, VOX), F32), vmem((8 * chans, VOX), BF16), vmem((VOX, VOX), BF16),
                vmem((wide, wide), BF16), vmem((chans, 8 * chans), F32),
                vmem((8 * chans, wide), F32), vmem((wide, wide), F32), pltpu.SemaphoreType.DMA,
            ],
        ),
        16 * 10**9, 16 * 2**20,
    )(*scalars, ordered, above, below, cot_pieces, parts, slope, coarse, w_mix, res_rows)

    shares = lax.all_to_all(
        packed.reshape(devices, rows, LANES), "space", split_axis=0, concat_axis=0, tiled=True
    )
    returned, _ = lax.optimization_barrier((returned, packed))
    flat_shape = (devices * tiles * ROWS, LANES)
    sorted_pieces = kernel_call(
        sort_kernel,
        jax.ShapeDtypeStruct(flat_shape, BF16),
        pl.GridSpec(
            grid=(1,),
            in_specs=[smem_spec, whole(piece_shape)],
            out_specs=whole(flat_shape),
            scratch_shapes=[smem(devices * groups)],
        ),
        1000, 2**20, SMALL_VMEM_BYTES,
    )(all_kids, returned)
    sorted_pieces, shares = lax.optimization_barrier((sorted_pieces, shares))
    finished = lax.all_to_all(
        sorted_pieces.reshape(devices, tiles * ROWS, LANES),
        "space", split_axis=0, concat_axis=0, tiled=True,
    )
    summed = jnp.sum(shares.astype(F32), axis=0).astype(BF16)
    sums = gather_by_digits(summed, devices).reshape(devices * rows, LANES)

    coarse_out, grad_conv, grad_res, grad_mix = kernel_call(
        functools.partial(unpack_kernel, lane_tiles),
        (
            jax.ShapeDtypeStruct((slots, wide, VOX), BF16),
            jax.ShapeDtypeStruct((7, chans, chans), F32),
            jax.ShapeDtypeStruct((8, chans, wide), F32),
            jax.ShapeDtypeStruct((wide, wide), F32),
        ),
        pl.GridSpec(
            grid=(1,),
            in_specs=[smem_spec, whole(flat_shape), whole((devices * rows, LANES))],
            out_specs=[whole((slots, wide, VOX)), whole((7, chans, chans)),
                       whole((8, chans, wide)), whole((wide, wide))],
            scratch_shapes=[vmem((devices * rows, LANES), F32)] * 2,
        ),
        1000, 2 * 2**20, SMALL_VMEM_BYTES,
    )(position, finished.reshape(flat_shape), sums)
    return coarse_out, grad_conv, grad_res.transpose(0, 2, 1), grad_mix


def solution(mesh):
    return jax.shard_map(
        body,
        mesh=mesh,
        in_specs=(
            P(("groups", "space"), None, None),
            P(("groups", "space")),
            P(("groups", "space"), None),
            P(("groups", "space"), None),
            P(),
            P(),
            P(),
            P(("groups", "space"), None, None),
        ),
        out_specs=(
            P(("groups", "space"), None, None),
            P("groups", None, None),
            P("groups", None, None),
            P("groups", None),
        ),
        check_vma=False,
    )
```

```python
import functools
import math

import jax
import jax.numpy as jnp
from jax import lax
from jax.experimental import pallas as pl
from jax.experimental.pallas import tpu as pltpu
from jax.sharding import PartitionSpec as P

EDGE = 8
HALF = EDGE // 2
VOX = EDGE**3
LANES = 128
ROWS = 16
LABEL_ROWS = 8
SEND = 8
PARTS = 4
BF16 = jnp.bfloat16
F32 = jnp.float32
VMEM_BYTES = 60 * 1024 * 1024
SMALL_VMEM_BYTES = 16 * 1024 * 1024


def bits_of(value):
    return [(value >> (8 - k)) & 1 for k in range(9)]


def join_bits(bits):
    value = bits[0]
    for bit in bits[1:]:
        value = value * 2 + bit
    return value


def split_voxel(column):
    ta, tb, tc, a1, a0, b1, b0, c1, c0 = bits_of(column)
    return join_bits([a1, a0, ta, b1, b0, tb, c1, c0, tc])


def octant_voxel(column):
    oa, ob, oc, a1, a0, b1, b0, c1, c0 = bits_of(column)
    return join_bits([oa, a1, a0, ob, b1, b0, oc, c1, c0])


def picker(voxel_of, shape=(VOX, VOX), start=(0, 0), flip=False):
    row = lax.broadcasted_iota(jnp.int32, shape, 0) + start[0]
    column = lax.broadcasted_iota(jnp.int32, shape, 1) + start[1]
    return (column == voxel_of(row) if flip else row == voxel_of(column)).astype(BF16)


def digits(devices):
    strides = [devices // 2]
    for stride in (2, 1, *(1 << k for k in range(2, devices.bit_length()))):
        if stride < devices // 2:
            strides.append(stride)
    return [(2, stride) for stride in strides]


def gather_by_digits(own, devices):
    held = own[None]
    for radix, stride in digits(devices):
        came = [held]
        for step in range(1, radix):
            pairs = []
            for i in range(devices):
                digit = i // stride % radix
                pairs.append((i, i + ((digit + step) % radix - digit) * stride))
            came.append(lax.ppermute(held, "space", pairs))
        held = jnp.concatenate(came, axis=0)
    return held


def dot(a, b):
    return jnp.dot(a, b, preferred_element_type=F32)


def dot_nt(a, b):
    return lax.dot_general(a, b, (((1,), (1,)), ((), ())), preferred_element_type=F32)


def pack_kernel(lane_tiles, parents, cot, msg, kids_out, kids):
    slots = cot.shape[0]
    body_rows = slots * lane_tiles * ROWS
    rows = body_rows + LABEL_ROWS
    devices = msg.shape[0] // rows

    def find(g, found):
        kids[found] = parents[0, g]
        return found + (parents[1, g] == 0).astype(jnp.int32)

    lax.fori_loop(0, parents.shape[1], find, jnp.int32(0), unroll=4)
    lane = lax.broadcasted_iota(jnp.int32, (LABEL_ROWS, LANES), 1)
    label = jnp.zeros((LABEL_ROWS, LANES), jnp.int32)
    for q in range(kids_out.shape[0]):
        kids_out[q] = kids[q]
        label = jnp.where(lane == q, kids[q], label)
    label = label.astype(F32).astype(BF16)
    for j in range(devices):
        msg[j * rows + body_rows : (j + 1) * rows] = label
    per_row = VOX // (LANES * lane_tiles)
    for j in range(devices):
        chan, part = j // per_row, j % per_row
        for q in range(slots):
            for lt in range(lane_tiles):
                lane = (part * lane_tiles + lt) * LANES
                row = j * rows + (q * lane_tiles + lt) * ROWS
                msg[row : row + ROWS] = cot[
                    q, chan * ROWS : (chan + 1) * ROWS, lane : lane + LANES
                ]


def table_kernel(
    place, counts, kids, neighbors, parents, feat, up, down, table, ordered,
    up_idx, up_far, down_idx, down_far, bricks, done, split, in_sem, out_sem,
):
    count, chans = feat.shape[:2]
    part = count // PARTS
    fetches = [
        pltpu.make_async_copy(
            feat.at[pl.ds(k * part, part)], bricks.at[pl.ds(k * part, part)], in_sem.at[k]
        )
        for k in range(PARTS)
    ]
    for fetch in fetches:
        fetch.start()
    base = place[0] * count
    table[4 * count] = place[0]
    for r in range(SEND + 1):
        up_idx[r] = 0
        down_idx[r] = 0
        up_far[r] = 2 * count
        down_far[r] = 2 * count
    split[...] = picker(split_voxel)

    def scan(g, found):
        n_up, n_down = found
        near_up, near_down = neighbors[0, g], neighbors[1, g]
        far_up, far_down = near_up - base - count, near_down - base + count
        goes_up = (near_up >= 0) & (far_up >= 0)
        goes_down = (near_down >= 0) & (far_down < count)
        up_idx[n_up] = g
        up_far[n_up] = jnp.where(goes_up, far_up, 2 * count)
        down_idx[n_down] = g
        down_far[n_down] = jnp.where(goes_down, far_down, 2 * count)
        q = jnp.int32(0)
        for k in range(1, kids.shape[0]):
            q += jnp.where(kids[k] == parents[0, g], k, 0)
        number = q * 8 + parents[1, g]
        table[number] = g
        table[count + number] = jnp.where(g < counts[0], g, count + SEND)
        return n_up + goes_up.astype(jnp.int32), n_down + goes_down.astype(jnp.int32)

    lax.fori_loop(0, count, scan, (jnp.int32(0), jnp.int32(0)), unroll=4)

    def rank(r, carry):
        for start, far, idx in ((2 * count, up_far, up_idx), (3 * count, down_far, down_idx)):
            earlier = jnp.int32(0)
            for other in range(SEND):
                earlier += (far[other] < far[r]).astype(jnp.int32)

            @pl.when(far[r] < count)
            def _():
                table[start + idx[r]] = count + earlier

        return carry

    lax.fori_loop(0, SEND, rank, jnp.int32(0))
    sends = []
    for k in range(PARTS):
        fetches[k].wait()
        rows = bricks[k * part : (k + 1) * part].reshape(part * chans, VOX)
        done[k * part : (k + 1) * part] = (
            dot(rows, split[...]).astype(BF16).reshape(part, chans, VOX)
        )
        sends.append(
            pltpu.make_async_copy(
                done.at[pl.ds(k * part, part)], ordered.at[pl.ds(k * part, part)], out_sem.at[k]
            )
        )
        sends[-1].start()
    low = low_lanes(chans)
    for r in range(SEND // 2):
        other = r + SEND // 2
        top = slice(VOX - LANES, VOX)
        up[r] = jnp.where(
            low,
            pltpu.roll(bricks[up_idx[r], :, top], LANES // 2, 1),
            bricks[up_idx[other], :, top],
        )
        down[r] = jnp.where(
            low,
            bricks[down_idx[r], :, :LANES],
            pltpu.roll(bricks[down_idx[other], :, :LANES], LANES // 2, 1),
        )
    for send in sends:
        send.wait()


def route_kernel(kids, msg, pieces):
    devices, groups, lane_tiles = pieces.shape[:3]
    slots = groups
    for s in range(devices):
        for q in range(groups):
            kid = kids[s * groups + q]
            owner, slot = kid // slots, kid % slots
            for lt in range(lane_tiles):
                row = pl.multiple_of((slot * lane_tiles + lt) * ROWS, ROWS)
                pieces[s, q, lt] = msg[owner, pl.ds(row, ROWS), :]


def place_arrivals(above, below, bricks, count):
    chans = bricks.shape[1]
    half = VOX // 2
    side = LANES // 2
    shape = (LANES, half)
    pairs = SEND // 2
    for k, shift in ((0, 0), (pairs, -side)):
        slots = slice(count + k, count + k + pairs)
        first = dot(
            above[...].reshape(pairs * chans, LANES), picker(split_voxel, shape, (shift, 0))
        )
        last = dot(
            below[...].reshape(pairs * chans, LANES),
            picker(split_voxel, shape, (VOX - side + shift, half)),
        )
        bricks[slots, :, :half] = first.astype(BF16).reshape(pairs, chans, half)
        bricks[slots, :, half:] = last.astype(BF16).reshape(pairs, chans, half)
    bricks[count + SEND] = jnp.zeros(bricks.shape[1:], BF16)


def sources(table, neighbors, number):
    count = neighbors.shape[1]
    g = table[number]
    found = []
    for d in range(6):
        near = neighbors[d, g]
        local = near - table[4 * count] * count
        if d == 0:
            local = jnp.where(local >= count, table[2 * count + g], local)
        if d == 1:
            local = jnp.where(local < 0, table[3 * count + g], local)
        found.append(jnp.where(near >= 0, local, count + SEND))
    found.append(table[count + number])
    return found


def shift_into(slots, bricks, views):
    chans = bricks.shape[1]
    tiles = VOX // LANES
    lane = lax.broadcasted_iota(jnp.int32, (chans, LANES), 1)
    low = lane < LANES // 2
    a = (lane // 16) % HALF
    b = (lane // 4) % HALF
    c = lane % HALF

    def tile(slot, t):
        return bricks[slot, :, t * LANES : (t + 1) * LANES]

    def turn(value, by):
        return pltpu.roll(value, by % LANES, 1)

    x = [tile(slots[6], t) for t in range(tiles)]
    for t in range(tiles):
        lanes = slice(t * LANES, (t + 1) * LANES)
        if t < 2:
            plus_a = x[t + 2]
            minus_a = jnp.where(a > 0, turn(x[t + 2], 16), turn(tile(slots[1], t + 2), -48))
        else:
            plus_a = jnp.where(a < HALF - 1, turn(x[t - 2], -16), turn(tile(slots[0], t - 2), 48))
            minus_a = x[t - 2]
        if t % 2 == 0:
            plus_b = x[t + 1]
            minus_b = jnp.where(b > 0, turn(x[t + 1], 4), turn(tile(slots[3], t + 1), -12))
        else:
            plus_b = jnp.where(b < HALF - 1, turn(x[t - 1], -4), turn(tile(slots[2], t - 1), 12))
            minus_b = x[t - 1]
        swapped = turn(x[t], 64)
        plus_c = jnp.where(c < HALF - 1, turn(x[t], 63), turn(tile(slots[4], t), 67))
        minus_c = jnp.where(c > 0, turn(x[t], -63), turn(tile(slots[5], t), -67))
        out = [plus_a, minus_a, plus_b, minus_b, jnp.where(low, swapped, plus_c),
               jnp.where(low, minus_c, swapped), x[t]]
        for d in range(7):
            views[d * chans : (d + 1) * chans, lanes] = out[d]


def low_lanes(rows):
    return lax.broadcasted_iota(jnp.int32, (rows, LANES), 1) < LANES // 2


def forward_kernel(
    lane_tiles, table_hbm, neighbors_hbm, feat, w_conv_hbm, w_res_hbm, w_mix_hbm,
    above_hbm, below_hbm,
    parts_out, slope_out, coarse_out, piece_out,
    bricks, views, place, w_conv, w_res, w_mix, conv_cat, res_cat, octants,
    table, neighbors, above, below, sem,
):
    q = pl.program_id(0)
    groups = pl.num_programs(0) - 1
    count, chans = feat.shape[:2]
    part = count // PARTS

    @pl.when(q == 0)
    def _():
        copies = [
            pltpu.make_async_copy(source, target, sem.at[k])
            for k, (source, target) in enumerate((
                (above_hbm, above), (below_hbm, below), (w_conv_hbm, w_conv),
                (w_res_hbm, w_res), (w_mix_hbm, w_mix), (table_hbm, table),
                (neighbors_hbm, neighbors),
                *(
                    (feat.at[pl.ds(k * part, part)], bricks.at[pl.ds(k * part, part)])
                    for k in range(PARTS)
                ),
            ))
        ]
        for copy in copies:
            copy.start()
        place[...] = picker(octant_voxel, flip=True)
        for copy in copies[:-PARTS]:
            copy.wait()
        place_arrivals(above, below, bricks, count)
        for d in range(7):
            conv_cat[:, d * chans : (d + 1) * chans] = w_conv[d]
        res_cat[...] = w_res[...].T
        for copy in copies[-PARTS:]:
            copy.wait()

    low_half = low_lanes(chans)

    def finish():
        coarse = dot(octants[...], place[...]).astype(BF16)
        coarse_out[0] = coarse
        mixed = dot(w_mix[...], coarse).astype(BF16)
        per_row = VOX // (LANES * lane_tiles)
        for j in range(piece_out.shape[0]):
            chan, part = j // per_row, j % per_row
            for lt in range(lane_tiles):
                lane = (part * lane_tiles + lt) * LANES
                piece_out[j, 0, lt] = mixed[chan * ROWS : (chan + 1) * ROWS, lane : lane + LANES]

    def restrict(first):
        acts = []
        for k in range(first, first + 4):
            shift_into(sources(table, neighbors, q * 8 + k), bricks, views.at[k])
            hidden = dot(conv_cat[:, : 7 * chans], views[k])
            sig = 1.0 / (1.0 + jnp.exp(-hidden))
            act = hidden * sig
            slope_out[0, k * chans : (k + 1) * chans, :] = (sig + act * (1.0 - sig)).astype(BF16)
            acts.append(act.astype(BF16))
        for k in range(0, 4, 2):
            lanes = slice((first + k) * (LANES // 2), (first + k + 2) * (LANES // 2))
            for t in range(4):
                one = acts[k][:, t * LANES : (t + 1) * LANES]
                two = acts[k + 1][:, t * LANES : (t + 1) * LANES]
                parts_out[0, 2 * t * chans : (2 * t + 1) * chans, lanes] = jnp.where(
                    low_half, one, pltpu.roll(two, LANES // 2, 1)
                )
                parts_out[0, (2 * t + 1) * chans : (2 * t + 2) * chans, lanes] = jnp.where(
                    low_half, pltpu.roll(one, LANES // 2, 1), two
                )
        lanes = slice(first * (LANES // 2), (first + 4) * (LANES // 2))
        return dot(res_cat[...], parts_out[0, :, lanes]).astype(BF16)

    @pl.when(q < groups)
    def _():
        finish()
        halves = [restrict(0), restrict(4)]
        octants[...] = jnp.concatenate(halves, axis=1)

    @pl.when(q == groups)
    def _():
        finish()


def backward_kernel(
    lane_tiles, scale, table, neighbors, feat, above, below, pieces, parts, slope, coarse, w_mix, w_res, packed,
    bricks, views, cot, grad_parts, grad_rows, unplace, mix_t, conv_sum, res_sum, mix_sum, sem,
):
    q = pl.program_id(0)
    count, chans = feat.shape[:2]
    wide = coarse.shape[1]
    fetch = pltpu.make_async_copy(feat, bricks.at[pl.ds(0, count)], sem)

    @pl.when(q == 0)
    def _():
        fetch.start()
        place_arrivals(above, below, bricks, count)
        unplace[...] = picker(octant_voxel)
        mix_t[...] = w_mix[...].T
        conv_sum[...] = jnp.zeros_like(conv_sum)
        res_sum[...] = jnp.zeros_like(res_sum)
        mix_sum[...] = jnp.zeros_like(mix_sum)
        fetch.wait()

    per_row = VOX // (LANES * lane_tiles)
    for j in range(pieces.shape[0]):
        chan, part = j // per_row, j % per_row
        for lt in range(lane_tiles):
            lane = (part * lane_tiles + lt) * LANES
            cot[chan * ROWS : (chan + 1) * ROWS, lane : lane + LANES] = pieces[j, 0, lt]
    cots = cot[...]
    grad_coarse = (scale * dot(mix_t[...], cots)).astype(BF16)
    grad_fine = dot(grad_coarse, unplace[...]).astype(BF16)
    mix_sum[...] += dot_nt(cots, coarse[0])
    res_sum[...] += dot_nt(parts[0], grad_fine)
    grad_parts[...] = dot(w_res[...], grad_fine)
    low_half = low_lanes(chans)
    for r in range(4):
        for t in range(4):
            cols = slice(r * LANES, (r + 1) * LANES)
            lanes = slice(t * LANES, (t + 1) * LANES)
            one = grad_parts[2 * t * chans : (2 * t + 1) * chans, cols]
            two = grad_parts[(2 * t + 1) * chans : (2 * t + 2) * chans, cols]
            first = slice(2 * r * chans, (2 * r + 1) * chans)
            second = slice((2 * r + 1) * chans, (2 * r + 2) * chans)
            grad_rows[first, lanes] = (
                jnp.where(low_half, one, pltpu.roll(two, LANES // 2, 1))
                * slope[0, first, lanes].astype(F32)
            ).astype(BF16)
            grad_rows[second, lanes] = (
                jnp.where(low_half, pltpu.roll(one, LANES // 2, 1), two)
                * slope[0, second, lanes].astype(F32)
            ).astype(BF16)

    total = None
    for k in range(8):
        shift_into(sources(table, neighbors, q * 8 + k), bricks, views.at[k])
        term = dot_nt(grad_rows[k * chans : (k + 1) * chans, :], views[k])
        total = term if total is None else total + term
    conv_sum[:, : 7 * chans] += total

    @pl.when(q == pl.num_programs(0) - 1)
    def _():
        packed[0:wide] = (scale * mix_sum[...]).astype(BF16)
        at = wide
        packed[at : at + 8 * chans] = res_sum[...].astype(BF16)
        at += 8 * chans
        for t in range(4):
            packed[at : at + chans] = conv_sum[:, t * LANES : (t + 1) * LANES].astype(BF16)
            at += chans
        if at < packed.shape[0]:
            packed[at:] = jnp.zeros((packed.shape[0] - at, LANES), BF16)


def sort_kernel(kids, pieces, msg, wanted):
    devices, groups, lane_tiles = pieces.shape[:3]
    slots = groups
    rows = slots * lane_tiles * ROWS

    def invert(n, carry):
        wanted[kids[n]] = n
        return carry

    lax.fori_loop(0, devices * groups, invert, jnp.int32(0), unroll=4)
    for j in range(devices):
        for slot in range(slots):
            n = wanted[j * slots + slot]
            for lt in range(lane_tiles):
                row = j * rows + (slot * lane_tiles + lt) * ROWS
                msg[row : row + ROWS] = pieces[n // groups, n % groups, lt]


def coarse_kernel(lane_tiles, msg, coarse_out):
    slots = coarse_out.shape[0]
    per_row = VOX // (LANES * lane_tiles)
    devices = 8 * per_row
    rows = msg.shape[0] // devices
    for j in range(devices):
        chan, part = j // per_row, j % per_row
        for q in range(slots):
            for lt in range(lane_tiles):
                row = j * rows + (q * lane_tiles + lt) * ROWS
                lane = (part * lane_tiles + lt) * LANES
                coarse_out[q, chan * ROWS : (chan + 1) * ROWS, lane : lane + LANES] = msg[
                    row : row + ROWS
                ]


def gradient_kernel(devices, place, sums, conv, res, mix, packed, wide_sums):
    wide = mix.shape[0]
    chans = conv.shape[1]
    half = LANES // 2
    share = sums.shape[0] // devices
    wide_sums[...] = sums[...].astype(F32)
    for p in range(devices):
        source, behind = jnp.int32(0), p
        for radix, stride in digits(devices):
            digit = place[0] // stride % radix
            source += (digit + radix - behind % radix) % radix * stride
            behind //= radix
        at = pl.multiple_of(source * share, 8)
        packed[pl.ds(at, share), :] = wide_sums[p * share : (p + 1) * share]
    mix[...] = packed[0:wide]
    at = wide
    for t in range(8):
        res[t] = packed[at : at + chans]
        at += chans
    for t in range(4):
        block = packed[at : at + chans]
        conv[2 * t] = block[:, :half]
        if 2 * t + 1 < 7:
            conv[2 * t + 1] = block[:, half:]
        at += chans


def kernel_call(kernel, out_shape, grid_spec, flops, moved, vmem=VMEM_BYTES):
    return pl.pallas_call(
        kernel,
        out_shape=out_shape,
        grid_spec=grid_spec,
        compiler_params=pltpu.CompilerParams(vmem_limit_bytes=vmem),
        cost_estimate=pl.CostEstimate(flops=flops, bytes_accessed=moved, transcendentals=0),
    )


def body(features, counts, neighbors, parents, w_conv, w_restrict, w_mix, cotangent):
    devices = lax.axis_size("space")
    position = lax.axis_index("space").astype(jnp.int32).reshape(1)
    slots, wide = cotangent.shape[:2]
    count, chans = features.shape[:2]
    lane_tiles = VOX * 8 // devices // LANES
    tiles = slots * lane_tiles
    groups = count // 8
    whole = lambda shape: pl.BlockSpec(shape, lambda *_: (0,) * len(shape))
    any_spec = pl.BlockSpec(memory_space=pl.ANY)
    smem_spec = pl.BlockSpec(memory_space=pltpu.SMEM)
    smem = lambda size: pltpu.SMEM((size,), jnp.int32)
    vmem = pltpu.VMEM
    ints = lambda size: jax.ShapeDtypeStruct((size,), jnp.int32)

    message_shape = (devices, tiles * ROWS + LABEL_ROWS, LANES)
    flat_shape = (message_shape[0] * message_shape[1], LANES)
    message, kids = kernel_call(
        functools.partial(pack_kernel, lane_tiles),
        (jax.ShapeDtypeStruct(flat_shape, BF16), ints(groups)),
        pl.GridSpec(
            grid=(1,),
            in_specs=[smem_spec, whole(cotangent.shape)],
            out_specs=[whole(flat_shape), smem_spec],
            scratch_shapes=[smem(groups + 1)],
        ),
        1000, 2**20,
    )(parents.T, cotangent)
    spread = lax.all_to_all(
        message.reshape(message_shape), "space", split_axis=0, concat_axis=0, tiled=True
    )

    plane = jax.ShapeDtypeStruct((SEND // 2, chans, LANES), BF16)
    up, down, table, ordered = kernel_call(
        table_kernel,
        (plane, plane, ints(4 * count + 1), jax.ShapeDtypeStruct(features.shape, BF16)),
        pl.GridSpec(
            grid=(1,),
            in_specs=[smem_spec] * 5 + [any_spec],
            out_specs=[whole(plane.shape)] * 2 + [smem_spec, any_spec],
            scratch_shapes=[smem(SEND + 1)] * 4
            + [vmem(features.shape, BF16), vmem(features.shape, BF16), vmem((VOX, VOX), BF16),
               pltpu.SemaphoreType.DMA((PARTS,)), pltpu.SemaphoreType.DMA((PARTS,))],
        ),
        1000, 2**20,
    )(position, counts, kids, neighbors.T, parents.T, features)
    below = lax.ppermute(up, "space", [(i, i + 1) for i in range(devices - 1)])
    above = lax.ppermute(down, "space", [(i + 1, i) for i in range(devices - 1)])

    all_kids = spread[:, tiles * ROWS, :groups].astype(jnp.int32).reshape(-1)
    piece_shape = (devices, groups, lane_tiles, ROWS, LANES)
    forward_tiles = kernel_call(
        route_kernel,
        jax.ShapeDtypeStruct(piece_shape, BF16),
        pl.GridSpec(
            grid=(1,),
            in_specs=[smem_spec, whole(message_shape)],
            out_specs=whole(piece_shape),
        ),
        1000, 2**20, SMALL_VMEM_BYTES,
    )(all_kids, spread)
    forward_tiles, above, below = lax.optimization_barrier((forward_tiles, above, below))
    cot_pieces = lax.all_to_all(forward_tiles, "space", split_axis=0, concat_axis=0, tiled=True)

    res_rows = w_restrict.transpose(0, 2, 1).reshape(8 * chans, wide)
    scalars = (table, neighbors.T)
    brick_scratch = vmem((count + SEND + 1, chans, VOX), BF16)
    view_scratch = vmem((8, 7 * chans, VOX), BF16)
    per_group = lambda *shape: pl.BlockSpec((1,) + shape, lambda q: (q,) + (0,) * len(shape))
    piece_spec = pl.BlockSpec((devices, 1, lane_tiles, ROWS, LANES), lambda q: (0, q, 0, 0, 0))
    parts, slope, coarse, pieces = kernel_call(
        functools.partial(forward_kernel, lane_tiles),
        (
            jax.ShapeDtypeStruct((groups, 8 * chans, VOX), BF16),
            jax.ShapeDtypeStruct((groups, 8 * chans, VOX), BF16),
            jax.ShapeDtypeStruct((groups, wide, VOX), BF16),
            jax.ShapeDtypeStruct(piece_shape, BF16),
        ),
        pl.GridSpec(
            grid=(groups + 1,),
            in_specs=[any_spec] * 8,
            out_specs=[
                pl.BlockSpec((1, 8 * chans, VOX), lambda q: (jnp.minimum(q, groups - 1), 0, 0)),
                pl.BlockSpec((1, 8 * chans, VOX), lambda q: (jnp.minimum(q, groups - 1), 0, 0)),
                pl.BlockSpec((1, wide, VOX), lambda q: (jnp.maximum(q - 1, 0), 0, 0)),
                pl.BlockSpec(
                    (devices, 1, lane_tiles, ROWS, LANES),
                    lambda q: (0, jnp.maximum(q - 1, 0), 0, 0, 0),
                ),
            ],
            scratch_shapes=[
                brick_scratch, view_scratch, vmem((VOX, VOX), BF16), vmem(w_conv.shape, BF16),
                vmem(res_rows.shape, BF16), vmem(w_mix.shape, BF16),
                vmem((chans, 8 * chans), BF16), vmem((wide, 8 * chans), BF16),
                vmem((wide, VOX), BF16), smem(4 * count + 1),
                pltpu.SMEM((6, count), jnp.int32), vmem(plane.shape, BF16),
                vmem(plane.shape, BF16), pltpu.SemaphoreType.DMA((7 + PARTS,)),
            ],
        ),
        16 * 10**9, 16 * 2**20,
    )(*scalars, ordered, w_conv, res_rows, w_mix, above, below)
    returned = lax.all_to_all(pieces, "space", split_axis=0, concat_axis=0, tiled=True)

    scale = 1.0 / math.sqrt(devices * slots * VOX)
    used = wide + 8 * chans + 4 * chans
    rows = -(-used // (devices * 8)) * 8
    packed = kernel_call(
        functools.partial(backward_kernel, lane_tiles, scale),
        jax.ShapeDtypeStruct((devices * rows, LANES), BF16),
        pl.GridSpec(
            grid=(groups,),
            in_specs=[smem_spec] * 2 + [any_spec] + [whole(plane.shape)] * 2
            + [piece_spec, per_group(8 * chans, VOX), per_group(8 * chans, VOX),
               per_group(wide, VOX), whole(w_mix.shape), whole(res_rows.shape)],
            out_specs=whole((devices * rows, LANES)),
            scratch_shapes=[
                brick_scratch, view_scratch, vmem((wide, VOX), BF16),
                vmem((8 * chans, VOX), F32), vmem((8 * chans, VOX), BF16), vmem((VOX, VOX), BF16),
                vmem((wide, wide), BF16), vmem((chans, 8 * chans), F32),
                vmem((8 * chans, wide), F32), vmem((wide, wide), F32), pltpu.SemaphoreType.DMA,
            ],
        ),
        16 * 10**9, 16 * 2**20,
    )(*scalars, ordered, above, below, cot_pieces, parts, slope, coarse, w_mix, res_rows)

    shares = lax.all_to_all(
        packed.reshape(devices, rows, LANES), "space", split_axis=0, concat_axis=0, tiled=True
    )
    returned, _ = lax.optimization_barrier((returned, packed))
    flat_shape = (devices * tiles * ROWS, LANES)
    sorted_pieces = kernel_call(
        sort_kernel,
        jax.ShapeDtypeStruct(flat_shape, BF16),
        pl.GridSpec(
            grid=(1,),
            in_specs=[smem_spec, whole(piece_shape)],
            out_specs=whole(flat_shape),
            scratch_shapes=[smem(devices * groups)],
        ),
        1000, 2**20, SMALL_VMEM_BYTES,
    )(all_kids, returned)
    sorted_pieces, shares = lax.optimization_barrier((sorted_pieces, shares))
    finished = lax.all_to_all(
        sorted_pieces.reshape(devices, tiles * ROWS, LANES),
        "space", split_axis=0, concat_axis=0, tiled=True,
    )
    summed = jnp.sum(shares.astype(F32), axis=0).astype(BF16)
    sums = gather_by_digits(summed, devices).reshape(devices * rows, LANES)

    coarse_out = kernel_call(
        functools.partial(coarse_kernel, lane_tiles),
        jax.ShapeDtypeStruct((slots, wide, VOX), BF16),
        pl.GridSpec(
            grid=(1,), in_specs=[whole(flat_shape)], out_specs=whole((slots, wide, VOX))
        ),
        1000, 2**20, SMALL_VMEM_BYTES,
    )(finished.reshape(flat_shape))
    grad_conv, grad_res, grad_mix = kernel_call(
        functools.partial(gradient_kernel, devices),
        (
            jax.ShapeDtypeStruct((7, chans, chans), F32),
            jax.ShapeDtypeStruct((8, chans, wide), F32),
            jax.ShapeDtypeStruct((wide, wide), F32),
        ),
        pl.GridSpec(
            grid=(1,),
            in_specs=[smem_spec, whole((devices * rows, LANES))],
            out_specs=[whole((7, chans, chans)), whole((8, chans, wide)), whole((wide, wide))],
            scratch_shapes=[vmem((devices * rows, LANES), F32)] * 2,
        ),
        1000, 2**20, SMALL_VMEM_BYTES,
    )(position, sums)
    return coarse_out, grad_conv, grad_res.transpose(0, 2, 1), grad_mix


def solution(mesh):
    return jax.shard_map(
        body,
        mesh=mesh,
        in_specs=(
            P(("groups", "space"), None, None),
            P(("groups", "space")),
            P(("groups", "space"), None),
            P(("groups", "space"), None),
            P(),
            P(),
            P(),
            P(("groups", "space"), None, None),
        ),
        out_specs=(
            P(("groups", "space"), None, None),
            P("groups", None, None),
            P("groups", None, None),
            P("groups", None),
        ),
        check_vma=False,
    )
```
